32 devices in a mesh: dp: 8 (over z, x), fsdp: 4 (over y, core).
Axes of the slice: x: 2, y: 2, z: 4, core: 2. Of those that a mesh axis runs over, the one named last changes fastest.
Arguments:
- tokens: bfloat16 [262144, 128], P(('dp', 'fsdp')), may hold values from -6 to 6
- points: bfloat16 [64, 3, 1024, 128], P(('dp', 'fsdp')), may hold values from -6 to 6
- coords: float32 [2, 262144], P(None, ('dp', 'fsdp')), may hold values from -1 to 1
- presence: int32 [64, 3], P(('dp', 'fsdp')), may hold values from 0 to 1, as said below
- counts: int32 [64, 3], P(('dp', 'fsdp')), may hold values from 256 to 1024, as said below
- cotangent: bfloat16 [262144, 128], P(('dp', 'fsdp')), may hold values from -6 to 6
- gain_first: bfloat16 [128], P('fsdp'), may hold values from 0.5 to 1.5
- bias_first: bfloat16 [128], P('fsdp'), may hold values from -2.5 to 2.5
- query_first: bfloat16 [128, 128], P('fsdp'), may hold values from -0.5 to 0.5
- key_first: bfloat16 [128, 128], P('fsdp'), may hold values from -0.5 to 0.5
- value_first: bfloat16 [128, 128], P('fsdp'), may hold values from -0.5 to 0.5
- out_first: bfloat16 [128, 128], P('fsdp'), may hold values from -6 to 6
- query_second: bfloat16 [128, 128], P('fsdp'), may hold values from -0.5 to 0.5
- key_second: bfloat16 [128, 128], P('fsdp'), may hold values from -0.5 to 0.5
- value_second: bfloat16 [128, 128], P('fsdp'), may hold values from -0.5 to 0.5
- out_second: bfloat16 [128, 128], P('fsdp'), may hold values from -6 to 6
- gain_second: bfloat16 [128], P('fsdp'), may hold values from 0.5 to 1.5
- bias_second: bfloat16 [128], P('fsdp'), may hold values from -2.5 to 2.5
- expert_in: bfloat16 [4, 128, 256], P(None, 'fsdp'), may hold values from -0.5 to 0.5
- expert_out: bfloat16 [4, 256, 128], P(None, 'fsdp'), may hold values from -0.375 to 0.375
- gate_weight: bfloat16 [2, 4], P(None, 'fsdp'), may hold values from -3 to 3
Outputs:
- result: bfloat16 [262144, 128], P(('dp', 'fsdp'))
- grad_tokens: float32 [262144, 128], P(('dp', 'fsdp'))
- grad_gain_first: float32 [128], P('fsdp')
- grad_bias_first: float32 [128], P('fsdp')
- grad_query_first: float32 [128, 128], P('fsdp')
- grad_key_first: float32 [128, 128], P('fsdp')
- grad_value_first: float32 [128, 128], P('fsdp')
- grad_out_first: float32 [128, 128], P('fsdp')
- grad_query_second: float32 [128, 128], P('fsdp')
- grad_key_second: float32 [128, 128], P('fsdp')
- grad_value_second: float32 [128, 128], P('fsdp')
- grad_out_second: float32 [128, 128], P('fsdp')
- grad_gain_second: float32 [128], P('fsdp')
- grad_bias_second: float32 [128], P('fsdp')
- grad_expert_in: float32 [4, 128, 256], P(None, 'fsdp')
- grad_expert_out: float32 [4, 256, 128], P(None, 'fsdp')
- grad_gate_weight: float32 [2, 4], P(None, 'fsdp')
The draws below stay inside these ranges and needn't reach their ends.
Inputs may be any that keep to these rules, and one draw needn't show every extreme that they name: `presence`: each item has at least one of its 3 input functions present. `counts`: slots of an input function from its count on are padding; the count 1024 occurs in every draw.
All inputs are finite; a program needn't handle non-finite values.
Results may differ from the reference program's by a relative error of at most 0.029.
Values may be sent and summed in bfloat16 or wider, within the bound.
No kernel may reach another device: no remote copies, remote signals or barrier semaphores. Data moves between devices by JAX's collectives and lax.ppermute only.
A program may use at most 256 MiB of HBM per device.

```python
import jax
import jax.numpy as jnp
from jax import lax

D = 128
HEADS = 8
HID = 256
E = 4
F = 3
MAXP = 1024
PTS = 4096
ITEMS = 64
TOKENS = 262144


def draw_presence(key, part):
    key = jax.random.fold_in(key, 11)
    first, second = jax.random.split(key)
    present = (jax.random.randint(first, (ITEMS, F), 0, 3) < 2).astype(jnp.int32)
    chosen = jax.random.randint(second, (ITEMS, 1), 0, F)
    column = jnp.arange(F, dtype=jnp.int32)[None, :]
    return jnp.where(column == chosen, 1, present).astype(jnp.int32)


def draw_counts(key, part):
    key = jax.random.fold_in(key, 12)
    first, second = jax.random.split(key)
    drawn = jax.random.randint(first, (ITEMS, F), MAXP // 4, MAXP + 1)
    chosen = jax.random.randint(second, (), 0, F)
    row = jnp.arange(ITEMS, dtype=jnp.int32)[:, None]
    column = jnp.arange(F, dtype=jnp.int32)[None, :]
    return jnp.where((row == 0) & (column == chosen), MAXP, drawn).astype(jnp.int32)


def block_levels(own_key, shape, cuts, smallest, largest):
    def one(axis_at, blocks):
        heights = jax.random.uniform(jax.random.fold_in(jax.random.fold_in(own_key, 6), axis_at), (blocks,), jnp.float32, smallest / len(cuts), largest / len(cuts))
        return jnp.repeat(jnp.exp(heights), shape[axis_at] // blocks).reshape((-1,) + (1,) * (len(shape) - axis_at - 1))

    factor_of = one(*cuts[0])
    for cut in cuts[1:]:
        factor_of = factor_of * one(*cut)
    return factor_of


def centred(key, extent, width, limit, pieces=(), held_as=jnp.bfloat16):
    loudness = block_levels(key, extent, pieces, -0.22, 0.18) if pieces else 1.0
    entries = jax.random.normal(key, extent, jnp.float32) * width * loudness
    return jnp.minimum(jnp.maximum(entries, -limit), limit).astype(held_as)


def setup_inputs(seed: int = 0) -> dict:
    seeds = jax.random.split(jax.random.key(seed), 22)
    return {
        "tokens": centred(seeds[0], (TOKENS, D), 1.0, 6.0, ((0, 32),)),
        "points": centred(seeds[1], (ITEMS, F, MAXP, D), 1.0, 6.0, ((0, 32),)),
        "coords": jnp.clip(jax.random.uniform(seeds[2], (2, TOKENS), jnp.float32, -1.0, 1.0) * block_levels(seeds[2], (2, TOKENS), ((1, 32),), -0.4, 0.0), -1.0, 1.0),
        "presence": draw_presence(jax.random.fold_in(seeds[21], 71), 0),
        "counts": draw_counts(jax.random.fold_in(seeds[21], 71), 0),
        "cotangent": centred(seeds[5], (TOKENS, D), 1.0, 6.0, ((0, 32),)),
        "gain_first": jnp.clip(1.0 + 0.1 * jax.random.normal(seeds[6], (D,), jnp.float32), 0.5, 1.5).astype(jnp.bfloat16),
        "bias_first": centred(seeds[7], (D,), 0.2, 2.5, ((0, 4),)),
        "query_first": centred(seeds[8], (D, D), D ** -0.5, 0.5, ((0, 4),)),
        "key_first": centred(seeds[9], (D, D), D ** -0.5, 0.5, ((0, 4),)),
        "value_first": centred(seeds[10], (D, D), D ** -0.5, 0.5, ((0, 4),)),
        "out_first": centred(seeds[11], (D, D), 1 ** -0.5, 6.0, ((0, 4),)),
        "query_second": centred(seeds[12], (D, D), D ** -0.5, 0.5, ((0, 4),)),
        "key_second": centred(seeds[13], (D, D), D ** -0.5, 0.5, ((0, 4),)),
        "value_second": centred(seeds[14], (D, D), D ** -0.5, 0.5, ((0, 4),)),
        "out_second": centred(seeds[15], (D, D), 1 ** -0.5, 6.0, ((0, 4),)),
        "gain_second": jnp.clip(1.0 + 0.1 * jax.random.normal(seeds[16], (D,), jnp.float32), 0.5, 1.5).astype(jnp.bfloat16),
        "bias_second": centred(seeds[17], (D,), 0.2, 2.5, ((0, 4),)),
        "expert_in": centred(seeds[18], (E, D, HID), D ** -0.5, 0.5, ((1, 4),)),
        "expert_out": centred(seeds[19], (E, HID, D), HID ** -0.5, 0.375, ((1, 4),)),
        "gate_weight": centred(seeds[20], (2, E), 0.7, 3.0, ((1, 4),)),
    }


eps = 1e-05
highest = lax.Precision.HIGHEST

@jax.custom_vjp
def low(v):
    return lax.optimization_barrier(v.astype(jnp.bfloat16)).astype(jnp.float32)

@jax.custom_vjp
def low_back(v):
    return v

def low_keep(v):
    return (low(v), None)

def low_pass(kept, grad):
    return (grad,)

def back_keep(v):
    return (v, None)

def back_low(kept, grad):
    return (low(grad),)
low.defvjp(low_keep, low_pass)
low_back.defvjp(back_keep, back_low)

def layer_norm(value, gain, bias):
    centre = value - lax.optimization_barrier(jnp.mean(value, axis=-1, keepdims=True))
    spread = lax.optimization_barrier(jnp.mean(centre * centre, axis=-1, keepdims=True))
    return centre * lax.rsqrt(spread + eps) * gain + bias

def matmul(left, right):
    return jnp.dot(left, right, precision=highest)

def head_softmax(value):
    shape = value.shape
    split = value.reshape(shape[:-1] + (HEADS, D // HEADS))
    return jax.nn.softmax(split, axis=-1).reshape(shape)

def readout(queries, keys, values, weights):
    head = D // HEADS
    query_heads = queries.reshape(queries.shape[0], HEADS, head)
    key_heads = keys.reshape(keys.shape[0], keys.shape[1], HEADS, head)
    value_heads = values.reshape(values.shape[0], values.shape[1], HEADS, head)
    state = jnp.einsum('fphd,fphe->fhde', key_heads, value_heads, precision=highest)
    state = low(low_back(state))
    totals = lax.optimization_barrier(jnp.sum(key_heads, axis=1))
    numerator = low_back(jnp.einsum('thd,fhde->fthe', query_heads, state, precision=highest))
    denominator = jnp.einsum('thd,fhd->fth', query_heads, totals, precision=highest)
    share = numerator / denominator[..., None]
    mixed = jnp.einsum('f,fthe->the', weights, share, precision=highest)
    return mixed.reshape(queries.shape)

def block(token_rows, point_rows, coord_rows, valid_rows, weight_rows, params):
    gain_first, bias_first, query_first, key_first, value_first, out_first, query_second, key_second, value_second, out_second, gain_second, bias_second, expert_in, expert_out, gate_weight = params
    normed = low(layer_norm(token_rows, gain_first, bias_first))
    queries = low(head_softmax(low_back(matmul(normed, query_first))))
    flat_points = point_rows.reshape(-1, D)
    keys = low(head_softmax(low_back(matmul(flat_points, key_first)))).reshape(F, MAXP, D) * valid_rows[..., None]
    values = low(low_back(matmul(flat_points, value_first))).reshape(F, MAXP, D)
    cross = low(readout(queries, keys, values, weight_rows))
    first = token_rows + low_back(matmul(cross, out_first))
    rounded = low(first)
    queries = low(head_softmax(low_back(matmul(rounded, query_second))))
    keys = low(head_softmax(low_back(matmul(rounded, key_second))))
    values = low(low_back(matmul(rounded, value_second)))
    own = low(readout(queries, keys[None], values[None], jnp.ones((1,), jnp.float32)))
    second = first + low_back(matmul(own, out_second))
    normed = low(layer_norm(second, gain_second, bias_second))
    gates = jax.nn.softmax(jnp.dot(coord_rows.T, gate_weight, precision=highest), axis=-1)
    total = second
    for expert in range(E):
        hidden = low(jax.nn.gelu(low_back(matmul(normed, expert_in[expert])), approximate=True))
        total = total + gates[:, expert:expert + 1] * low_back(matmul(hidden, expert_out[expert]))
    return total

def reference(tokens, points, coords, presence, counts, cotangent, gain_first, bias_first, query_first, key_first, value_first, out_first, query_second, key_second, value_second, out_second, gain_second, bias_second, expert_in, expert_out, gate_weight):
    params = tuple((weight.astype(jnp.float32) for weight in (gain_first, bias_first, query_first, key_first, value_first, out_first, query_second, key_second, value_second, out_second, gain_second, bias_second, expert_in, expert_out, gate_weight)))
    token_items = tokens.astype(jnp.float32).reshape(ITEMS, PTS, D)
    point_items = points.astype(jnp.float32)
    coord_items = coords.astype(jnp.float32).reshape(2, ITEMS, PTS).transpose(1, 0, 2)
    cot_items = cotangent.astype(jnp.float32).reshape(ITEMS, PTS, D)
    slots = jnp.arange(MAXP, dtype=jnp.int32)
    valid = (slots[None, None, :] < counts.astype(jnp.int32)[:, :, None]).astype(jnp.float32)
    present = presence.astype(jnp.float32)
    weights = present / lax.optimization_barrier(jnp.sum(present, axis=1, keepdims=True))

    def one_item(carry, item):
        token_rows, point_rows, coord_rows, valid_rows, weight_rows, cot_rows = item

        def forward(rows, inner_params):
            return block(rows, point_rows, coord_rows, valid_rows, weight_rows, inner_params)
        output, pullback = jax.vjp(forward, token_rows, params)
        grad_rows, grad_params = pullback(cot_rows)
        carry = jax.tree.map(lambda total, grad: total + grad, carry, grad_params)
        return (carry, (output, grad_rows))
    zeros = jax.tree.map(jnp.zeros_like, params)
    grads, (outputs, grad_rows) = lax.scan(one_item, zeros, (token_items, point_items, coord_items, valid, weights, cot_items))
    grad_gain_first, grad_bias_first, grad_query_first, grad_key_first, grad_value_first, grad_out_first, grad_query_second, grad_key_second, grad_value_second, grad_out_second, grad_gain_second, grad_bias_second, grad_expert_in, grad_expert_out, grad_gate_weight = grads
    return (outputs.reshape(-1, D).astype(jnp.bfloat16), grad_rows.reshape(-1, D), grad_gain_first, grad_bias_first, grad_query_first, grad_key_first, grad_value_first, grad_out_first, grad_query_second, grad_key_second, grad_value_second, grad_out_second, grad_gain_second, grad_bias_second, grad_expert_in, grad_expert_out, grad_gate_weight)
```

```python
from functools import partial

import jax
import jax.numpy as jnp
from jax import lax
from jax.experimental import pallas as pl
from jax.experimental.pallas import tpu as pltpu
from jax.sharding import PartitionSpec as P


HEADS = 8
eps = 1e-05
f32 = jnp.float32
bf16 = jnp.bfloat16
TILE = 512
VMEM = 56 * 1024 * 1024


def nn(left, right):
    return jnp.dot(left, right, preferred_element_type=f32)


def nt(left, right):
    return lax.dot_general(left, right, (((1,), (1,)), ((), ())), preferred_element_type=f32)


def flip(value):
    return value.T


def inverse(value):
    return pl.reciprocal(value, approx=True)


def head_softmax(value):
    width, rows = value.shape
    split = value.reshape(HEADS, width // HEADS, rows)
    raised = jnp.exp(split - jnp.max(split, axis=1, keepdims=True))
    return (raised * inverse(jnp.sum(raised, axis=1, keepdims=True))).reshape(width, rows)


def softmax_back(probs, grad):
    width, rows = grad.shape
    probs = probs.astype(f32).reshape(HEADS, width // HEADS, rows)
    grad = grad.reshape(HEADS, width // HEADS, rows)
    inner = jnp.sum(probs * grad, axis=1, keepdims=True)
    return (probs * (grad - inner)).reshape(width, rows)


def standardize(value):
    centre = value - jnp.mean(value, axis=0, keepdims=True)
    scale = lax.rsqrt(jnp.mean(centre * centre, axis=0, keepdims=True) + eps)
    return centre * scale, scale


def norm_back(grad, hat, scale):
    return scale * (
        grad
        - jnp.mean(grad, axis=0, keepdims=True)
        - hat * jnp.mean(grad * hat, axis=0, keepdims=True)
    )


def same_head(rows, columns, width):
    head = width // HEADS
    row = lax.rem(lax.broadcasted_iota(jnp.int32, (rows, columns), 0), width)
    column = lax.rem(lax.broadcasted_iota(jnp.int32, (rows, columns), 1), width)
    return lax.div(row, head) == lax.div(column, head)


def whole(gathered, start, rows):
    shards = gathered.shape[0]
    return gathered[:, start : start + rows, :].reshape(shards * rows, gathered.shape[2])


def function_weight(presence, item, func, funcs, shape):
    total = presence[item, 0]
    for other in range(1, funcs):
        total = total + presence[item, other]
    own = jnp.full(shape, presence[item, func], jnp.int32).astype(f32)
    return own / jnp.full(shape, total, jnp.int32).astype(f32)


def points_forward(
    counts, presence, points, params, state_t, state, keys_out, values_out, weight, *, funcs, at
):
    step = pl.program_id(0)
    item, func = lax.div(step, funcs), lax.rem(step, funcs)
    width = points.shape[2]
    slots = points.shape[1]
    piece = width // params.shape[0]

    @pl.when(step == 0)
    def _():
        weight[:width] = flip(whole(params, at["key_first"], piece))
        weight[width:] = flip(whole(params, at["value_first"], piece))

    both = nt(weight[...], points[0])
    probs = head_softmax(both[:width])
    slot = lax.broadcasted_iota(jnp.int32, (1, slots), 1)
    keys = jnp.where(slot < counts[item, func], probs, 0.0).astype(bf16)
    values = both[width:].astype(bf16)
    keys_out[0] = keys
    values_out[0] = values
    extended = jnp.concatenate([values, jnp.ones_like(values)], axis=0)
    share = function_weight(presence, item, func, funcs, (1, width))
    one = jnp.ones_like(share)
    mask = same_head(width, width, width)
    summed = nt(keys, extended)
    left = jnp.where(mask, summed[:, :width], 0.0) * share
    right = jnp.where(mask, summed[:, width:], 0.0) * one
    state[0, :, :width] = left.astype(bf16)
    state[0, :, width:] = (-right).astype(bf16)
    state_t[0, :width] = flip(left).astype(bf16)
    state_t[0, width:] = flip(right).astype(bf16)


def main_kernel(
    tokens,
    cotangent,
    coords,
    state_t,
    params,
    result,
    queries_out,
    cross_out,
    first_out,
    keys_out,
    values_out,
    grad_q_out,
    grad_second_out,
    grad_state_out,
    grads_out,
    first_keep,
    query_keep,
    state_sum,
    self_t,
    self_state,
    grad_state_sum,
    w_query,
    w_out_one,
    w_self,
    w_out_two_t,
    w_out_two,
    w_in_t,
    w_in,
    w_exit,
    w_exit_t,
    gain_one,
    bias_one,
    gain_two,
    bias_two,
    hidden_keep,
    inner_keep,
    sum_in,
    sum_exit,
    sum_out_two,
    sum_gain,
    sum_bias,
    sum_gate,
    *,
    funcs,
    experts,
    at,
):
    item = pl.program_id(0)
    phase = pl.program_id(1)
    step = pl.program_id(2)
    steps = pl.num_programs(2)
    width = tokens.shape[1]
    rows = tokens.shape[0]
    shards = params.shape[0]
    piece = width // shards
    hidden = w_in.shape[1] // experts
    exit_piece = hidden // shards

    @pl.when((item == 0) & (phase == 0) & (step == 0))
    def _():
        w_query[...] = flip(whole(params, at["query_first"], piece))
        w_out_one[...] = flip(whole(params, at["out_first"], piece))
        w_self[:width] = flip(whole(params, at["query_second"], piece))
        w_self[width : 2 * width] = flip(whole(params, at["key_second"], piece))
        w_self[2 * width :] = flip(whole(params, at["value_second"], piece))
        out_two = whole(params, at["out_second"], piece)
        w_out_two[...] = out_two
        w_out_two_t[...] = flip(out_two)
        for block in range(experts * hidden // width):
            part = whole(params, at["expert_in"] + block * piece, piece)
            w_in[:, block * width : (block + 1) * width] = part
            w_in_t[block * width : (block + 1) * width] = flip(part)
        for expert in range(experts):
            part = whole(params, at["expert_out"] + expert * exit_piece, exit_piece)
            w_exit[expert * hidden : (expert + 1) * hidden] = part
            w_exit_t[:, expert * hidden : (expert + 1) * hidden] = flip(part)
        vectors = whole(params, at["vectors"], piece).astype(f32)
        for place, vector in enumerate((gain_one, bias_one, gain_two, bias_two)):
            column = vectors[:, place * piece : place * piece + 1]
            vector[...] = jnp.broadcast_to(column, vector.shape)
        sum_in[...] = jnp.zeros_like(sum_in)
        sum_exit[...] = jnp.zeros_like(sum_exit)
        sum_out_two[...] = jnp.zeros_like(sum_out_two)
        sum_gain[...] = jnp.zeros_like(sum_gain)
        sum_bias[...] = jnp.zeros_like(sum_bias)
        sum_gate[...] = jnp.zeros_like(sum_gate)

    @pl.when(phase == 0)
    def _():
        rows_t = flip(tokens[...]).astype(f32)
        hat, _scale = standardize(rows_t)
        normed = (hat * gain_one[...] + bias_one[...]).astype(bf16)
        queries = head_softmax(nn(w_query[...], normed)).astype(bf16)
        queries_out[0] = queries
        mixed = jnp.zeros((width, rows), f32)
        for func in range(funcs):
            both = nn(state_t[func], queries)
            mixed = mixed + both[:width] * inverse(both[width:])
        cross = mixed.astype(bf16)
        cross_out[0] = cross
        first = rows_t + nn(w_out_one[...], cross)
        first_keep[step] = first
        first_low = first.astype(bf16)
        first_out[0] = first_low
        three = nn(w_self[...], first_low)
        query_keep[step] = head_softmax(three[:width]).astype(bf16)
        keys = head_softmax(three[width : 2 * width]).astype(bf16)
        values = three[2 * width :].astype(bf16)
        keys_out[0] = keys
        values_out[0] = values
        extended = jnp.concatenate([values, jnp.ones_like(values)], axis=0)
        found = nt(keys, extended)

        @pl.when(step == 0)
        def _():
            state_sum[...] = found

        @pl.when(step > 0)
        def _():
            state_sum[...] += found

        @pl.when(step == steps - 1)
        def _():
            mask = same_head(width, width, width)
            left = jnp.where(mask, state_sum[:, :width], 0.0)
            right = jnp.where(mask, state_sum[:, width:], 0.0)
            self_state[:, :width] = left.astype(bf16)
            self_state[:, width:] = (-right).astype(bf16)
            self_t[:width] = flip(left).astype(bf16)
            self_t[width:] = flip(right).astype(bf16)

    @pl.when(phase == 1)
    def _():
        queries = query_keep[step]
        both = nn(self_t[...], queries)
        undo = inverse(both[width:])
        own = both[:width] * undo
        own_low = own.astype(bf16)
        second = first_keep[step] + nn(w_out_two_t[...], own_low)
        hat, scale = standardize(second)
        normed = (hat * gain_two[...] + bias_two[...]).astype(bf16)
        grad = flip(cotangent[...])
        across, down = coords[0:1, :], coords[1:2, :]
        logits = []
        for expert in range(experts):
            pair = params[expert, at["gate"] : at["gate"] + 16, 0:1].astype(f32)
            logits.append(across * pair[0:1] + down * pair[8:9])
        peak = logits[0]
        for logit in logits[1:]:
            peak = jnp.maximum(peak, logit)
        raised = [jnp.exp(logit - peak) for logit in logits]
        total = raised[0]
        for other in raised[1:]:
            total = total + other
        gates = [other / total for other in raised]
        grad_gates = []
        for expert in range(experts):
            span = slice(expert * hidden, (expert + 1) * hidden)
            inner = nn(w_in_t[span], normed)
            back = nn(w_exit[span], grad)
            square = inner * inner
            tanh = jnp.tanh(inner * (0.7978845608028654 + 0.035677408136300125 * square))
            half = 0.5 + 0.5 * tanh
            active = inner * half
            grad_gates.append(jnp.sum(active * back, axis=0, keepdims=True))
            hidden_keep[span] = (active * gates[expert]).astype(bf16)
            slope = half + active * (1.0 - half) * (
                1.5957691216057308 + 0.21406444881780074 * square
            )
            inner_keep[span] = (slope * (back * gates[expert])).astype(bf16)
        total = second + nn(w_exit_t[...], hidden_keep[...])
        result[...] = flip(total.astype(bf16))
        grad_normed = nn(w_in[...], inner_keep[...])
        sum_exit[...] += nt(grad, hidden_keep[...])
        sum_in[...] += nt(normed, inner_keep[...])
        mean_gate = gates[0] * grad_gates[0]
        for expert in range(1, experts):
            mean_gate = mean_gate + gates[expert] * grad_gates[expert]
        for expert in range(experts):
            change = gates[expert] * (grad_gates[expert] - mean_gate)
            sum_gate[expert : expert + 1] += across * change
            sum_gate[experts + expert : experts + expert + 1] += down * change
        sum_gain[...] += grad_normed * hat
        sum_bias[...] += grad_normed
        grad_second = grad.astype(f32) + norm_back(grad_normed * gain_two[...], hat, scale)
        grad_second_out[0] = grad_second.astype(bf16)
        grad_own = grad_second.astype(bf16)
        sum_out_two[...] += nt(own_low, grad_own)
        share = nn(w_out_two[...], grad_own) * undo
        pair = jnp.concatenate([share.astype(bf16), (share * own).astype(bf16)], axis=0)
        grad_q = nn(self_state[...], pair)
        found = nt(queries, pair)

        @pl.when(step == 0)
        def _():
            grad_state_sum[...] = found

        @pl.when(step > 0)
        def _():
            grad_state_sum[...] += found

        grad_q_out[0] = softmax_back(queries, grad_q).astype(bf16)

        @pl.when(step == steps - 1)
        def _():
            grad_state_out[0] = grad_state_sum[...]

    @pl.when((item == pl.num_programs(0) - 1) & (phase == 1) & (step == steps - 1))
    def _():
        gain = flip(jnp.broadcast_to(jnp.sum(sum_gain[...], axis=1, keepdims=True), (width, width)))
        bias = flip(jnp.broadcast_to(jnp.sum(sum_bias[...], axis=1, keepdims=True), (width, width)))
        gate = jnp.broadcast_to(jnp.sum(sum_gate[...], axis=1, keepdims=True), (8, width))
        row = lax.broadcasted_iota(jnp.int32, (8, width), 0)
        vectors = jnp.where(row == 0, gain[:8], bias[:8])
        small = jnp.concatenate([vectors, gate], axis=0).astype(bf16)
        blocks = experts * hidden // width
        for block in range(blocks):
            part = sum_in[:, block * width : (block + 1) * width].astype(bf16)
            grads_out[:, block * piece : (block + 1) * piece, :] = part.reshape(
                shards, piece, width
            )
        start = blocks * piece
        for expert in range(experts):
            part = flip(sum_exit[:, expert * hidden : (expert + 1) * hidden]).astype(bf16)
            grads_out[:, start : start + exit_piece, :] = part.reshape(shards, exit_piece, width)
            start += exit_piece
        grads_out[:, start : start + piece, :] = (
            sum_out_two[...].astype(bf16).reshape(shards, piece, width)
        )
        start += piece
        for shard in range(shards):
            grads_out[shard, start : start + 16, :] = small


def rest_kernel(
    presence,
    tokens,
    queries_in,
    cross_in,
    first_in,
    keys_in,
    values_in,
    grad_q_in,
    grad_second_in,
    grad_state_in,
    state_t,
    state,
    params,
    grad_tokens,
    grad_cross_state_out,
    grad_totals_out,
    grads_out,
    w_self,
    w_out_one,
    w_query,
    gain_one,
    bias_one,
    grad_self_state,
    grad_totals,
    grad_state_sum,
    sum_self,
    sum_out_one,
    sum_query,
    sum_gain,
    sum_bias,
    *,
    funcs,
    at,
):
    item = pl.program_id(0)
    step = pl.program_id(1)
    steps = pl.num_programs(1)
    width = tokens.shape[1]
    shards = params.shape[0]
    piece = width // shards

    @pl.when((item == 0) & (step == 0))
    def _():
        w_query[...] = whole(params, at["query_first"], piece)
        w_out_one[...] = whole(params, at["out_first"], piece)
        w_self[:, :width] = whole(params, at["query_second"], piece)
        w_self[:, width : 2 * width] = whole(params, at["key_second"], piece)
        w_self[:, 2 * width :] = whole(params, at["value_second"], piece)
        vectors = whole(params, at["vectors"], piece).astype(f32)
        for place, vector in enumerate((gain_one, bias_one)):
            column = vectors[:, place * piece : place * piece + 1]
            vector[...] = jnp.broadcast_to(column, vector.shape)
        sum_self[...] = jnp.zeros_like(sum_self)
        sum_out_one[...] = jnp.zeros_like(sum_out_one)
        sum_query[...] = jnp.zeros_like(sum_query)
        sum_gain[...] = jnp.zeros_like(sum_gain)
        sum_bias[...] = jnp.zeros_like(sum_bias)

    @pl.when(step == 0)
    def _():
        mask = same_head(width, width, width)
        left = jnp.where(mask, grad_state_in[0, :, :width], 0.0)
        right = jnp.where(mask, grad_state_in[0, :, width:], 0.0)
        grad_self_state[0] = left.astype(bf16)
        grad_self_state[1] = flip(left).astype(bf16)
        grad_totals[...] = jnp.broadcast_to(
            -jnp.sum(right, axis=1, keepdims=True), grad_totals.shape
        )

    first_low = first_in[0]
    keys, values = keys_in[0], values_in[0]
    grad_k = softmax_back(keys, nn(grad_self_state[0], values) + grad_totals[...]).astype(bf16)
    grad_v = nn(grad_self_state[1], keys).astype(bf16)
    three = jnp.concatenate([grad_q_in[0], grad_k, grad_v], axis=0)
    sum_self[...] += nt(first_low, three)
    grad_first = grad_second_in[0].astype(f32) + nn(w_self[...], three)
    grad_cross = grad_first.astype(bf16)
    sum_out_one[...] += nt(cross_in[0], grad_cross)
    share = nn(w_out_one[...], grad_cross)
    queries = queries_in[0]
    pieces = []
    for func in range(funcs):
        both = nn(state_t[func], queries)
        undo = inverse(both[width:])
        part = share * undo
        pieces.append(part.astype(bf16))
        pieces.append((part * (both[:width] * undo)).astype(bf16))
    stack = jnp.concatenate(pieces, axis=0)
    found = nt(queries, stack)

    @pl.when(step == 0)
    def _():
        grad_state_sum[...] = found

    @pl.when(step > 0)
    def _():
        grad_state_sum[...] += found

    joined = jnp.concatenate([state[func] for func in range(funcs)], axis=1)
    grad_q = softmax_back(queries, nn(joined, stack)).astype(bf16)
    rows_t = flip(tokens[...]).astype(f32)
    hat, scale = standardize(rows_t)
    normed = (hat * gain_one[...] + bias_one[...]).astype(bf16)
    sum_query[...] += nt(normed, grad_q)
    grad_normed = nn(w_query[...], grad_q)
    sum_gain[...] += grad_normed * hat
    sum_bias[...] += grad_normed
    grad_rows = grad_first + norm_back(grad_normed * gain_one[...], hat, scale)
    grad_tokens[...] = flip(grad_rows)

    @pl.when(step == steps - 1)
    def _():
        mask = same_head(width, width, width)
        for func in range(funcs):
            weight = function_weight(presence, item, func, funcs, (1, width))
            start = 2 * func * width
            left = jnp.where(mask, grad_state_sum[:, start : start + width], 0.0) * weight
            right = jnp.where(mask, grad_state_sum[:, start + width : start + 2 * width], 0.0)
            grad_cross_state_out[func] = left.astype(bf16)
            grad_totals_out[func] = jnp.broadcast_to(
                -jnp.sum(right, axis=1, keepdims=True), (width, width)
            )

    @pl.when((item == pl.num_programs(0) - 1) & (step == steps - 1))
    def _():
        gain = flip(jnp.broadcast_to(jnp.sum(sum_gain[...], axis=1, keepdims=True), (width, width)))
        bias = flip(jnp.broadcast_to(jnp.sum(sum_bias[...], axis=1, keepdims=True), (width, width)))
        row = lax.broadcasted_iota(jnp.int32, (16, width), 0)
        small = jnp.where(row == 0, gain[:16], bias[:16]).astype(bf16)
        for place in range(3):
            part = sum_self[:, place * width : (place + 1) * width].astype(bf16)
            grads_out[:, place * piece : (place + 1) * piece, :] = part.reshape(
                shards, piece, width
            )
        grads_out[:, 3 * piece : 4 * piece, :] = (
            sum_out_one[...].astype(bf16).reshape(shards, piece, width)
        )
        grads_out[:, 4 * piece : 5 * piece, :] = (
            sum_query[...].astype(bf16).reshape(shards, piece, width)
        )
        for shard in range(shards):
            grads_out[shard, 5 * piece : 5 * piece + 16, :] = small


def points_back(points, keys_in, values_in, grad_state, grad_totals, grads_out, sums):
    step = pl.program_id(0)
    width = points.shape[2]
    shards = grads_out.shape[0]
    piece = width // shards
    keys, values = keys_in[0], values_in[0]
    left = grad_state[0]
    grad_keys = nn(left, values) + grad_totals[0, :, 0:1]
    grad_k = softmax_back(keys, grad_keys).astype(bf16)
    grad_v = nn(flip(left), keys).astype(bf16)
    found = nn(jnp.concatenate([grad_k, grad_v], axis=0), points[0])

    @pl.when(step == 0)
    def _():
        sums[...] = found

    @pl.when(step > 0)
    def _():
        sums[...] += found

    @pl.when(step == pl.num_programs(0) - 1)
    def _():
        for place in range(2):
            part = flip(sums[place * width : (place + 1) * width]).astype(bf16)
            grads_out[:, place * piece : (place + 1) * piece, :] = part.reshape(
                shards, piece, width
            )


def shards_fn(
    shards,
    tokens,
    points,
    coords,
    presence,
    counts,
    cotangent,
    gain_first,
    bias_first,
    query_first,
    key_first,
    value_first,
    out_first,
    query_second,
    key_second,
    value_second,
    out_second,
    gain_second,
    bias_second,
    expert_in,
    expert_out,
    gate_weight,
):
    count, width = tokens.shape
    items, funcs, slots, _ = points.shape
    length = count // items
    experts, piece, hidden = expert_in.shape
    exit_piece = expert_out.shape[1]
    tile = min(TILE, length)
    steps = length // tile
    halves = hidden // width

    at = {}
    blocks = []
    place = 0

    def put(name, block):
        nonlocal place
        at[name] = place
        blocks.append(block)
        place += block.shape[0]

    put("key_first", key_first)
    put("value_first", value_first)
    put("query_first", query_first)
    put("out_first", out_first)
    put("query_second", query_second)
    put("key_second", key_second)
    put("value_second", value_second)
    put("out_second", out_second)
    put(
        "expert_in",
        expert_in.reshape(experts, piece, halves, width)
        .transpose(0, 2, 1, 3)
        .reshape(experts * halves * piece, width),
    )
    put("expert_out", expert_out.reshape(experts * exit_piece, width))
    vectors = jnp.stack([gain_first, bias_first, gain_second, bias_second], axis=1)
    vectors = jnp.broadcast_to(vectors[:, :, None], (piece, 4, width // 4))
    put("vectors", vectors.reshape(piece, width))
    put(
        "gate",
        jnp.broadcast_to(gate_weight[:, None, :], (2, 8, width)).reshape(16, width),
    )
    packed = jnp.concatenate(blocks, axis=0)
    params = lax.all_gather(packed, "fsdp", axis=0, tiled=False)
    total_rows = packed.shape[0]

    smem = pl.BlockSpec(memory_space=pltpu.SMEM)
    units = items * funcs
    flat_points = points.reshape(units, slots, width)
    state_t, state, keys_one, values_one = pl.pallas_call(
        partial(points_forward, funcs=funcs, at=at),
        grid=(units,),
        in_specs=[
            smem,
            smem,
            pl.BlockSpec((1, slots, width), lambda u: (u, 0, 0)),
            pl.BlockSpec((shards, total_rows, width), lambda u: (0, 0, 0)),
        ],
        out_specs=[
            pl.BlockSpec((1, 2 * width, width), lambda u: (u, 0, 0)),
            pl.BlockSpec((1, width, 2 * width), lambda u: (u, 0, 0)),
            pl.BlockSpec((1, width, slots), lambda u: (u, 0, 0)),
            pl.BlockSpec((1, width, slots), lambda u: (u, 0, 0)),
        ],
        out_shape=[
            jax.ShapeDtypeStruct((units, 2 * width, width), bf16),
            jax.ShapeDtypeStruct((units, width, 2 * width), bf16),
            jax.ShapeDtypeStruct((units, width, slots), bf16),
            jax.ShapeDtypeStruct((units, width, slots), bf16),
        ],
        scratch_shapes=[pltpu.VMEM((2 * width, width), bf16)],
        compiler_params=pltpu.CompilerParams(vmem_limit_bytes=VMEM),
        name="points_forward",
    )(counts, presence, flat_points, params)

    inner = experts * hidden
    kept = jax.ShapeDtypeStruct((items * steps, width, tile), bf16)
    main_rows = (experts * halves + 1) * piece + experts * exit_piece + 16

    def early(i, p, j):
        return i * steps + jnp.where(p == 0, j, steps - 1)

    def late(i, p, j):
        return i * steps + jnp.where(p == 0, 0, j)

    early_keep = pl.BlockSpec((1, width, tile), lambda i, p, j: (early(i, p, j), 0, 0))
    late_keep = pl.BlockSpec((1, width, tile), lambda i, p, j: (late(i, p, j), 0, 0))
    late_rows = pl.BlockSpec((tile, width), lambda i, p, j: (late(i, p, j), 0))
    (
        result,
        queries_one,
        cross,
        first,
        keys_two,
        values_two,
        grad_q_two,
        grad_second,
        grad_state_two,
        main_grads,
    ) = pl.pallas_call(
        partial(main_kernel, funcs=funcs, experts=experts, at=at),
        grid=(items, 2, steps),
        in_specs=[
            pl.BlockSpec((tile, width), lambda i, p, j: (early(i, p, j), 0)),
            late_rows,
            pl.BlockSpec((2, tile), lambda i, p, j: (0, late(i, p, j))),
            pl.BlockSpec((funcs, 2 * width, width), lambda i, p, j: (i, 0, 0)),
            pl.BlockSpec((shards, total_rows, width), lambda i, p, j: (0, 0, 0)),
        ],
        out_specs=[
            late_rows,
            early_keep,
            early_keep,
            early_keep,
            early_keep,
            early_keep,
            late_keep,
            late_keep,
            pl.BlockSpec((1, width, 2 * width), lambda i, p, j: (i, 0, 0)),
            pl.BlockSpec((shards, main_rows, width), lambda i, p, j: (0, 0, 0)),
        ],
        out_shape=[
            jax.ShapeDtypeStruct((count, width), bf16),
            kept,
            kept,
            kept,
            kept,
            kept,
            kept,
            kept,
            jax.ShapeDtypeStruct((items, width, 2 * width), f32),
            jax.ShapeDtypeStruct((shards, main_rows, width), bf16),
        ],
        scratch_shapes=[
            pltpu.VMEM((steps, width, tile), f32),
            pltpu.VMEM((steps, width, tile), bf16),
            pltpu.VMEM((width, 2 * width), f32),
            pltpu.VMEM((2 * width, width), bf16),
            pltpu.VMEM((width, 2 * width), bf16),
            pltpu.VMEM((width, 2 * width), f32),
            pltpu.VMEM((width, width), bf16),
            pltpu.VMEM((width, width), bf16),
            pltpu.VMEM((3 * width, width), bf16),
            pltpu.VMEM((width, width), bf16),
            pltpu.VMEM((width, width), bf16),
            pltpu.VMEM((inner, width), bf16),
            pltpu.VMEM((width, inner), bf16),
            pltpu.VMEM((inner, width), bf16),
            pltpu.VMEM((width, inner), bf16),
            pltpu.VMEM((width, tile), f32),
            pltpu.VMEM((width, tile), f32),
            pltpu.VMEM((width, tile), f32),
            pltpu.VMEM((width, tile), f32),
            pltpu.VMEM((inner, tile), bf16),
            pltpu.VMEM((inner, tile), bf16),
            pltpu.VMEM((width, inner), f32),
            pltpu.VMEM((width, inner), f32),
            pltpu.VMEM((width, width), f32),
            pltpu.VMEM((width, tile), f32),
            pltpu.VMEM((width, tile), f32),
            pltpu.VMEM((8, tile), f32),
        ],
        compiler_params=pltpu.CompilerParams(vmem_limit_bytes=VMEM),
        name="main",
    )(tokens, cotangent, coords, state_t, params)

    rest_rows = 5 * piece + 16
    keep_spec = pl.BlockSpec((1, width, tile), lambda i, j: (i * steps + j, 0, 0))
    row_spec = pl.BlockSpec((tile, width), lambda i, j: (i * steps + j, 0))
    grad_tokens, grad_state_one, grad_totals_one, rest_grads = pl.pallas_call(
        partial(rest_kernel, funcs=funcs, at=at),
        grid=(items, steps),
        in_specs=[
            smem,
            row_spec,
            keep_spec,
            keep_spec,
            keep_spec,
            keep_spec,
            keep_spec,
            keep_spec,
            keep_spec,
            pl.BlockSpec((1, width, 2 * width), lambda i, j: (i, 0, 0)),
            pl.BlockSpec((funcs, 2 * width, width), lambda i, j: (i, 0, 0)),
            pl.BlockSpec((funcs, width, 2 * width), lambda i, j: (i, 0, 0)),
            pl.BlockSpec((shards, total_rows, width), lambda i, j: (0, 0, 0)),
        ],
        out_specs=[
            row_spec,
            pl.BlockSpec((funcs, width, width), lambda i, j: (i, 0, 0)),
            pl.BlockSpec((funcs, width, width), lambda i, j: (i, 0, 0)),
            pl.BlockSpec((shards, rest_rows, width), lambda i, j: (0, 0, 0)),
        ],
        out_shape=[
            jax.ShapeDtypeStruct((count, width), f32),
            jax.ShapeDtypeStruct((units, width, width), bf16),
            jax.ShapeDtypeStruct((units, width, width), f32),
            jax.ShapeDtypeStruct((shards, rest_rows, width), bf16),
        ],
        scratch_shapes=[
            pltpu.VMEM((width, 3 * width), bf16),
            pltpu.VMEM((width, width), bf16),
            pltpu.VMEM((width, width), bf16),
            pltpu.VMEM((width, tile), f32),
            pltpu.VMEM((width, tile), f32),
            pltpu.VMEM((2, width, width), bf16),
            pltpu.VMEM((width, tile), f32),
            pltpu.VMEM((width, 2 * funcs * width), f32),
            pltpu.VMEM((width, 3 * width), f32),
            pltpu.VMEM((width, width), f32),
            pltpu.VMEM((width, width), f32),
            pltpu.VMEM((width, tile), f32),
            pltpu.VMEM((width, tile), f32),
        ],
        compiler_params=pltpu.CompilerParams(vmem_limit_bytes=VMEM),
        name="rest",
    )(
        presence,
        tokens,
        queries_one,
        cross,
        first,
        keys_two,
        values_two,
        grad_q_two,
        grad_second,
        grad_state_two,
        state_t,
        state,
        params,
    )

    points_grads = pl.pallas_call(
        points_back,
        grid=(units,),
        in_specs=[
            pl.BlockSpec((1, slots, width), lambda u: (u, 0, 0)),
            pl.BlockSpec((1, width, slots), lambda u: (u, 0, 0)),
            pl.BlockSpec((1, width, slots), lambda u: (u, 0, 0)),
            pl.BlockSpec((1, width, width), lambda u: (u, 0, 0)),
            pl.BlockSpec((1, width, width), lambda u: (u, 0, 0)),
        ],
        out_specs=pl.BlockSpec((shards, 2 * piece, width), lambda u: (0, 0, 0)),
        out_shape=jax.ShapeDtypeStruct((shards, 2 * piece, width), bf16),
        scratch_shapes=[pltpu.VMEM((2 * width, width), f32)],
        compiler_params=pltpu.CompilerParams(vmem_limit_bytes=VMEM),
        name="points_back",
    )(flat_points, keys_one, values_one, grad_state_one, grad_totals_one)

    grads = jnp.concatenate([main_grads, rest_grads, points_grads], axis=1)
    grads = lax.psum_scatter(grads, "fsdp", scatter_dimension=0, tiled=False)
    grads = lax.psum(grads.astype(f32), "dp")

    shard = lax.axis_index("fsdp")
    spots = {}
    place = 0
    for name, size in (
        ("expert_in", experts * halves * piece),
        ("expert_out", experts * exit_piece),
        ("out_second", piece),
        ("small_second", 16),
        ("query_second", piece),
        ("key_second", piece),
        ("value_second", piece),
        ("out_first", piece),
        ("query_first", piece),
        ("small_first", 16),
        ("key_first", piece),
        ("value_first", piece),
    ):
        spots[name] = grads[place : place + size]
        place += size

    def vector(name, row):
        return lax.dynamic_slice(spots[name][row], (shard * piece,), (piece,))

    gate = spots["small_second"][8:, 0].reshape(2, experts)
    return (
        result,
        grad_tokens,
        vector("small_first", 0),
        vector("small_first", 1),
        spots["query_first"],
        spots["key_first"],
        spots["value_first"],
        spots["out_first"],
        spots["query_second"],
        spots["key_second"],
        spots["value_second"],
        spots["out_second"],
        vector("small_second", 0),
        vector("small_second", 1),
        spots["expert_in"]
        .reshape(experts, halves, piece, width)
        .transpose(0, 2, 1, 3)
        .reshape(experts, piece, hidden),
        spots["expert_out"].reshape(experts, exit_piece, width),
        lax.dynamic_slice(gate, (0, shard * gate_weight.shape[1]), (2, gate_weight.shape[1])),
    )


def solution(mesh):
    rows = P(("dp", "fsdp"), None)
    matrix = P("fsdp", None)
    vector = P("fsdp")
    expert = P(None, "fsdp", None)
    parameters = (
        (vector, vector)
        + (matrix,) * 8
        + (vector, vector, expert, expert, P(None, "fsdp"))
    )
    return jax.shard_map(
        partial(shards_fn, mesh.shape["fsdp"]),
        mesh=mesh,
        in_specs=(
            rows,
            P(("dp", "fsdp"), None, None, None),
            P(None, ("dp", "fsdp")),
            rows,
            rows,
            rows,
        )
        + parameters,
        out_specs=(rows, rows) + parameters,
        check_vma=False,
    )
```

```python
from functools import partial

import jax
import jax.numpy as jnp
from jax import lax
from jax.experimental import pallas as pl
from jax.experimental.pallas import tpu as pltpu
from jax.sharding import PartitionSpec as P


HEADS = 8
eps = 1e-05
f32 = jnp.float32
bf16 = jnp.bfloat16
TILE = 512
VMEM = 56 * 1024 * 1024


def cost(microseconds):
    return pl.CostEstimate(flops=microseconds * 10**9, bytes_accessed=10**6, transcendentals=0)


def nn(left, right):
    return jnp.dot(left, right, preferred_element_type=f32)


def nt(left, right):
    return lax.dot_general(left, right, (((1,), (1,)), ((), ())), preferred_element_type=f32)


def flip(value):
    return value.T


def inverse(value):
    return pl.reciprocal(value, approx=True)


def head_softmax(value):
    width, rows = value.shape
    split = value.reshape(HEADS, width // HEADS, rows)
    raised = jnp.exp(split - jnp.max(split, axis=1, keepdims=True))
    return (raised * inverse(jnp.sum(raised, axis=1, keepdims=True))).reshape(width, rows)


def softmax_back(probs, grad):
    width, rows = grad.shape
    probs = probs.astype(f32).reshape(HEADS, width // HEADS, rows)
    grad = grad.reshape(HEADS, width // HEADS, rows)
    inner = jnp.sum(probs * grad, axis=1, keepdims=True)
    return (probs * (grad - inner)).reshape(width, rows)


def standardize(value):
    centre = value - jnp.mean(value, axis=0, keepdims=True)
    scale = lax.rsqrt(jnp.mean(centre * centre, axis=0, keepdims=True) + eps)
    return centre * scale, scale


def norm_back(grad, hat, scale):
    return scale * (
        grad
        - jnp.mean(grad, axis=0, keepdims=True)
        - hat * jnp.mean(grad * hat, axis=0, keepdims=True)
    )


def same_head(rows, columns, width):
    head = width // HEADS
    row = lax.rem(lax.broadcasted_iota(jnp.int32, (rows, columns), 0), width)
    column = lax.rem(lax.broadcasted_iota(jnp.int32, (rows, columns), 1), width)
    return lax.div(row, head) == lax.div(column, head)


def assemble(parts, gathered):
    shards = len(parts)
    here = lax.axis_index("fsdp")
    for place, part in enumerate(parts):
        gathered[lax.rem(here + shards - place, shards)] = part[...]


def columns(gathered, start, count):
    shards, _, width = gathered.shape
    piece = width // shards
    small = [gathered[shard, start : start + 16, :].astype(f32) for shard in range(shards)]
    joined = jnp.concatenate([part[:, :piece] for part in small], axis=1)
    return [
        flip(jnp.broadcast_to(joined[place : place + 1], (width, width)))[:, 0:1]
        for place in range(count)
    ]


def lane_fold(value):
    width = value.shape[0]
    total = value[:, :width]
    for start in range(width, value.shape[1], width):
        total = total + value[:, start : start + width]
    return total


def as_row(value):
    width = value.shape[0]
    return flip(jnp.broadcast_to(jnp.sum(value, axis=1, keepdims=True), (width, width)))


def scatter_blocks(stage, outs):
    shards = len(outs)
    here = lax.axis_index("fsdp")
    for place, out in enumerate(outs):
        out[...] = stage[lax.rem(here + place, shards)]


def whole(gathered, start, rows):
    shards = gathered.shape[0]
    return gathered[:, start : start + rows, :].reshape(shards * rows, gathered.shape[2])


def function_weight(presence, item, func, funcs, shape):
    total = presence[item, 0]
    for other in range(1, funcs):
        total = total + presence[item, other]
    own = jnp.full(shape, presence[item, func], jnp.int32).astype(f32)
    return own / jnp.full(shape, total, jnp.int32).astype(f32)


def pack_kernel(*refs):
    weights, vectors, gate = refs[:10], refs[10:14], refs[14]
    early, late = refs[15:]
    keys, values, query, out, query_two, key_two, value_two, out_two, enter, leave = weights
    start = 0
    for weight in (keys, values):
        early[start : start + weight.shape[0]] = weight[...]
        start += weight.shape[0]
    start = 0
    for weight in (query, out, query_two, key_two, value_two, out_two):
        late[start : start + weight.shape[0]] = weight[...]
        start += weight.shape[0]
    experts, piece, hidden = enter.shape
    width = late.shape[1]
    for expert in range(experts):
        for half in range(hidden // width):
            late[start : start + piece] = enter[expert, :, half * width : (half + 1) * width]
            start += piece
    for expert in range(experts):
        late[start : start + leave.shape[1]] = leave[expert]
        start += leave.shape[1]
    rest = jnp.zeros((1, width - piece), f32)
    rows = [
        jnp.concatenate([vector[...].astype(f32), rest], axis=1) for vector in vectors
    ]
    rows.append(jnp.zeros((4, width), f32))
    for row in range(2):
        rows.append(jnp.broadcast_to(gate[row : row + 1, 0:1].astype(f32), (1, width)))
    rows.append(jnp.zeros((6, width), f32))
    late[start : start + 16] = jnp.concatenate(rows, axis=0).astype(bf16)


def points_forward(counts, presence, points, *refs, funcs, shards):
    parts = refs[:shards]
    state_t, state, keys_out, values_out, gathered, weight = refs[shards:]
    step = pl.program_id(0)
    item, func = lax.div(step, funcs), lax.rem(step, funcs)
    width = points.shape[2]
    slots = points.shape[1]
    piece = width // shards

    @pl.when(step == 0)
    def _():
        assemble(parts, gathered)
        weight[:width] = flip(whole(gathered, 0, piece))
        weight[width:] = flip(whole(gathered, piece, piece))

    both = nt(weight[...], points[0])
    probs = head_softmax(both[:width])
    slot = lax.broadcasted_iota(jnp.int32, (1, slots), 1)
    keys = jnp.where(slot < counts[item, func], probs, 0.0).astype(bf16)
    values = both[width:].astype(bf16)
    keys_out[0] = keys
    values_out[0] = values
    extended = jnp.concatenate([values, jnp.ones_like(values)], axis=0)
    share = function_weight(presence, item, func, funcs, (1, width))
    mask = same_head(width, width, width)
    summed = nt(keys, extended)
    left = jnp.where(mask, summed[:, :width], 0.0) * share
    right = jnp.where(mask, summed[:, width:], 0.0)
    state[0, :, :width] = left.astype(bf16)
    state[0, :, width:] = (-right).astype(bf16)
    state_t[0, :width] = flip(left).astype(bf16)
    state_t[0, width:] = flip(right).astype(bf16)


def main_kernel(tokens, cotangent, coords, state_t, *refs, funcs, experts, shards, at):
    parts, outs, scratch = refs[:shards], refs[shards : 2 * shards + 9], refs[2 * shards + 9 :]
    (
        result,
        queries_out,
        cross_out,
        first_out,
        keys_out,
        values_out,
        grad_q_out,
        grad_second_out,
        grad_state_out,
    ) = outs[:9]
    grads_out = outs[9:]
    (
        params,
        grads_stage,
        first_keep,
        query_keep,
        state_sum,
        self_t,
        self_state,
        grad_state_sum,
        w_query,
        w_out_one,
        w_self,
        w_out_two_t,
        w_out_two,
        w_in_t,
        w_in,
        w_exit,
        w_exit_t,
        gain_one,
        bias_one,
        gain_two,
        bias_two,
        hidden_keep,
        inner_keep,
        sum_in,
        sum_exit,
        sum_out_two,
        sum_gain,
        sum_bias,
        sum_gate,
    ) = scratch
    item = pl.program_id(0)
    phase = pl.program_id(1)
    step = pl.program_id(2)
    steps = pl.num_programs(2)
    width = tokens.shape[1]
    rows = tokens.shape[0]
    piece = width // shards
    hidden = w_in.shape[1] // experts
    exit_piece = hidden // shards

    @pl.when((item == 0) & (phase == 0) & (step == 0))
    def _():
        assemble(parts, params)
        w_query[...] = flip(whole(params, at["query_first"], piece))
        w_out_one[...] = flip(whole(params, at["out_first"], piece))
        w_self[:width] = flip(whole(params, at["query_second"], piece))
        w_self[width : 2 * width] = flip(whole(params, at["key_second"], piece))
        w_self[2 * width :] = flip(whole(params, at["value_second"], piece))
        out_two = whole(params, at["out_second"], piece)
        w_out_two[...] = out_two
        w_out_two_t[...] = flip(out_two)
        for block in range(experts * hidden // width):
            part = whole(params, at["expert_in"] + block * piece, piece)
            w_in[:, block * width : (block + 1) * width] = part
            w_in_t[block * width : (block + 1) * width] = flip(part)
        for expert in range(experts):
            part = whole(params, at["expert_out"] + expert * exit_piece, exit_piece)
            w_exit[expert * hidden : (expert + 1) * hidden] = part
            w_exit_t[:, expert * hidden : (expert + 1) * hidden] = flip(part)
        found = columns(params, at["small"], 4)
        for vector, column in zip((gain_one, bias_one, gain_two, bias_two), found):
            vector[...] = jnp.broadcast_to(column, vector.shape)
        sum_in[...] = jnp.zeros_like(sum_in)
        sum_exit[...] = jnp.zeros_like(sum_exit)
        sum_out_two[...] = jnp.zeros_like(sum_out_two)
        sum_gain[...] = jnp.zeros_like(sum_gain)
        sum_bias[...] = jnp.zeros_like(sum_bias)
        sum_gate[...] = jnp.zeros_like(sum_gate)

    @pl.when(phase == 0)
    def _():
        rows_t = flip(tokens[...]).astype(f32)
        hat, _scale = standardize(rows_t)
        normed = (hat * gain_one[...] + bias_one[...]).astype(bf16)
        queries = head_softmax(nn(w_query[...], normed)).astype(bf16)
        queries_out[0] = queries
        mixed = jnp.zeros((width, rows), f32)
        for func in range(funcs):
            both = nn(state_t[func], queries)
            mixed = mixed + both[:width] * inverse(both[width:])
        cross = mixed.astype(bf16)
        cross_out[0] = cross
        first = rows_t + nn(w_out_one[...], cross)
        first_keep[step] = first
        first_low = first.astype(bf16)
        first_out[0] = first_low
        three = nn(w_self[...], first_low)
        query_keep[step] = head_softmax(three[:width]).astype(bf16)
        keys = head_softmax(three[width : 2 * width]).astype(bf16)
        values = three[2 * width :].astype(bf16)
        keys_out[0] = keys
        values_out[0] = values
        extended = jnp.concatenate([values, jnp.ones_like(values)], axis=0)
        found = nt(keys, extended)

        @pl.when(step == 0)
        def _():
            state_sum[...] = found

        @pl.when(step > 0)
        def _():
            state_sum[...] += found

        @pl.when(step == steps - 1)
        def _():
            mask = same_head(width, width, width)
            left = jnp.where(mask, state_sum[:, :width], 0.0)
            right = jnp.where(mask, state_sum[:, width:], 0.0)
            self_state[:, :width] = left.astype(bf16)
            self_state[:, width:] = (-right).astype(bf16)
            self_t[:width] = flip(left).astype(bf16)
            self_t[width:] = flip(right).astype(bf16)

    @pl.when(phase == 1)
    def _():
        queries = query_keep[step]
        both = nn(self_t[...], queries)
        undo = inverse(both[width:])
        own = both[:width] * undo
        own_low = own.astype(bf16)
        second = first_keep[step] + nn(w_out_two_t[...], own_low)
        hat, scale = standardize(second)
        normed = (hat * gain_two[...] + bias_two[...]).astype(bf16)
        grad = flip(cotangent[...])
        across, down = coords[0:1, :], coords[1:2, :]
        logits = []
        for expert in range(experts):
            pair = params[expert, at["small"] : at["small"] + 16, 0:1].astype(f32)
            logits.append(across * pair[8:9] + down * pair[9:10])
        peak = logits[0]
        for logit in logits[1:]:
            peak = jnp.maximum(peak, logit)
        raised = [jnp.exp(logit - peak) for logit in logits]
        total = raised[0]
        for other in raised[1:]:
            total = total + other
        gates = [other / total for other in raised]
        grad_gates = []
        for expert in range(experts):
            span = slice(expert * hidden, (expert + 1) * hidden)
            inner = nn(w_in_t[span], normed)
            back = nn(w_exit[span], grad)
            square = inner * inner
            tanh = jnp.tanh(inner * (0.7978845608028654 + 0.035677408136300125 * square))
            half = 0.5 + 0.5 * tanh
            active = inner * half
            grad_gates.append(jnp.sum(active * back, axis=0, keepdims=True))
            hidden_keep[span] = (active * gates[expert]).astype(bf16)
            slope = half + active * (1.0 - half) * (
                1.5957691216057308 + 0.21406444881780074 * square
            )
            inner_keep[span] = (slope * (back * gates[expert])).astype(bf16)
        total = second + nn(w_exit_t[...], hidden_keep[...])
        result[...] = flip(total.astype(bf16))
        grad_normed = nn(w_in[...], inner_keep[...])
        sum_exit[...] += nt(grad, hidden_keep[...])
        sum_in[...] += nt(normed, inner_keep[...])
        mean_gate = gates[0] * grad_gates[0]
        for expert in range(1, experts):
            mean_gate = mean_gate + gates[expert] * grad_gates[expert]
        for expert in range(experts):
            change = gates[expert] * (grad_gates[expert] - mean_gate)
            sum_gate[expert : expert + 1] += across * change
            sum_gate[experts + expert : experts + expert + 1] += down * change
        sum_gain[...] += lane_fold(grad_normed * hat)
        sum_bias[...] += lane_fold(grad_normed)
        grad_second = grad.astype(f32) + norm_back(grad_normed * gain_two[...], hat, scale)
        grad_second_out[0] = grad_second.astype(bf16)
        grad_own = grad_second.astype(bf16)
        sum_out_two[...] += nt(own_low, grad_own)
        share = nn(w_out_two[...], grad_own) * undo
        pair = jnp.concatenate([share.astype(bf16), (share * own).astype(bf16)], axis=0)
        grad_q = nn(self_state[...], pair)
        found = nt(queries, pair)

        @pl.when(step == 0)
        def _():
            grad_state_sum[...] = found

        @pl.when(step > 0)
        def _():
            grad_state_sum[...] += found

        grad_q_out[0] = softmax_back(queries, grad_q).astype(bf16)

        @pl.when(step == steps - 1)
        def _():
            grad_state_out[0] = grad_state_sum[...]

    @pl.when((item == pl.num_programs(0) - 1) & (phase == 1) & (step == steps - 1))
    def _():
        gain, bias = as_row(sum_gain[...]), as_row(sum_bias[...])
        gate = jnp.broadcast_to(jnp.sum(sum_gate[...], axis=1, keepdims=True), (8, width))
        row = lax.broadcasted_iota(jnp.int32, (8, width), 0)
        vectors = jnp.where(row == 0, gain[:8], bias[:8])
        small = jnp.concatenate([vectors, gate], axis=0).astype(bf16)
        start = 0
        for block in range(experts * hidden // width):
            part = sum_in[:, block * width : (block + 1) * width].astype(bf16)
            grads_stage[:, start : start + piece, :] = part.reshape(shards, piece, width)
            start += piece
        for expert in range(experts):
            part = flip(sum_exit[:, expert * hidden : (expert + 1) * hidden]).astype(bf16)
            grads_stage[:, start : start + exit_piece, :] = part.reshape(shards, exit_piece, width)
            start += exit_piece
        part = sum_out_two[...].astype(bf16)
        grads_stage[:, start : start + piece, :] = part.reshape(shards, piece, width)
        start += piece
        for shard in range(shards):
            grads_stage[shard, start : start + 16, :] = small
        start += 16
        if start < grads_stage.shape[1]:
            grads_stage[:, start:, :] = jnp.zeros_like(grads_stage[:, start:, :])
        scatter_blocks(grads_stage, grads_out)


def rest_kernel(
    presence,
    tokens,
    queries_in,
    cross_in,
    first_in,
    keys_in,
    values_in,
    grad_q_in,
    grad_second_in,
    grad_state_in,
    state_t,
    state,
    *refs,
    funcs,
    item,
    shards,
    at,
    first_call,
    last_call,
):
    parts, refs = refs[:shards], refs[shards:]
    if not first_call:
        carry, refs = refs[3], refs[5:]
    grad_tokens, grad_cross_state_out, grad_totals_out = refs[:3]
    outs = refs[3 : 3 + shards] if last_call else refs[3:4]
    refs = refs[3 + len(outs) :]
    (
        params,
        grads_stage,
        w_self,
        w_out_one,
        w_query,
        gain_one,
        bias_one,
        grad_self_state,
        grad_totals,
        grad_state_sum,
        sums,
    ) = refs
    step = pl.program_id(0)
    steps = pl.num_programs(0)
    width = tokens.shape[1]
    piece = width // shards
    self_part = slice(0, 3 * width)
    out_part = slice(3 * width, 4 * width)
    query_part = slice(4 * width, 5 * width)
    gain_part = slice(5 * width, 6 * width)
    bias_part = slice(6 * width, 7 * width)

    @pl.when(step == 0)
    def _():
        assemble(parts, params)
        w_query[...] = whole(params, at["query_first"], piece)
        w_out_one[...] = whole(params, at["out_first"], piece)
        w_self[:, :width] = whole(params, at["query_second"], piece)
        w_self[:, width : 2 * width] = whole(params, at["key_second"], piece)
        w_self[:, 2 * width :] = whole(params, at["value_second"], piece)
        for vector, column in zip((gain_one, bias_one), columns(params, at["small"], 2)):
            vector[...] = jnp.broadcast_to(column, vector.shape)
        sums[...] = jnp.zeros_like(sums) if first_call else carry[...]
        mask = same_head(width, width, width)
        left = jnp.where(mask, grad_state_in[0, :, :width], 0.0)
        right = jnp.where(mask, grad_state_in[0, :, width:], 0.0)
        grad_self_state[0] = left.astype(bf16)
        grad_self_state[1] = flip(left).astype(bf16)
        grad_totals[...] = jnp.broadcast_to(
            -jnp.sum(right, axis=1, keepdims=True), grad_totals.shape
        )

    first_low = first_in[0]
    keys, values = keys_in[0], values_in[0]
    grad_k = softmax_back(keys, nn(grad_self_state[0], values) + grad_totals[...]).astype(bf16)
    grad_v = nn(grad_self_state[1], keys).astype(bf16)
    three = jnp.concatenate([grad_q_in[0], grad_k, grad_v], axis=0)
    sums[:, self_part] += nt(first_low, three)
    grad_first = grad_second_in[0].astype(f32) + nn(w_self[...], three)
    grad_cross = grad_first.astype(bf16)
    sums[:, out_part] += nt(cross_in[0], grad_cross)
    share = nn(w_out_one[...], grad_cross)
    queries = queries_in[0]
    pieces = []
    for func in range(funcs):
        both = nn(state_t[func], queries)
        undo = inverse(both[width:])
        part = share * undo
        pieces.append(part.astype(bf16))
        pieces.append((part * (both[:width] * undo)).astype(bf16))
    stack = jnp.concatenate(pieces, axis=0)
    found = nt(queries, stack)

    @pl.when(step == 0)
    def _():
        grad_state_sum[...] = found

    @pl.when(step > 0)
    def _():
        grad_state_sum[...] += found

    joined = jnp.concatenate([state[func] for func in range(funcs)], axis=1)
    grad_q = softmax_back(queries, nn(joined, stack)).astype(bf16)
    rows_t = flip(tokens[...]).astype(f32)
    hat, scale = standardize(rows_t)
    normed = (hat * gain_one[...] + bias_one[...]).astype(bf16)
    sums[:, query_part] += nt(normed, grad_q)
    grad_normed = nn(w_query[...], grad_q)
    sums[:, gain_part] += lane_fold(grad_normed * hat)
    sums[:, bias_part] += lane_fold(grad_normed)
    grad_rows = grad_first + norm_back(grad_normed * gain_one[...], hat, scale)
    grad_tokens[...] = flip(grad_rows)

    @pl.when(step == steps - 1)
    def _():
        mask = same_head(width, width, width)
        for func in range(funcs):
            weight = function_weight(presence, item, func, funcs, (1, width))
            start = 2 * func * width
            left = jnp.where(mask, grad_state_sum[:, start : start + width], 0.0) * weight
            right = jnp.where(mask, grad_state_sum[:, start + width : start + 2 * width], 0.0)
            grad_cross_state_out[func] = left.astype(bf16)
            grad_totals_out[func] = jnp.broadcast_to(
                -jnp.sum(right, axis=1, keepdims=True), (width, width)
            )
        if not last_call:
            outs[0][...] = sums[...]
        else:
            gain, bias = as_row(sums[:, gain_part]), as_row(sums[:, bias_part])
            row = lax.broadcasted_iota(jnp.int32, (16, width), 0)
            small = jnp.where(row == 0, gain[:16], bias[:16]).astype(bf16)
            for place in range(5):
                part = sums[:, place * width : (place + 1) * width].astype(bf16)
                grads_stage[:, place * piece : (place + 1) * piece, :] = part.reshape(
                    shards, piece, width
                )
            for shard in range(shards):
                grads_stage[shard, 5 * piece : 5 * piece + 16, :] = small
            start = 5 * piece + 16
            if start < grads_stage.shape[1]:
                grads_stage[:, start:, :] = jnp.zeros_like(grads_stage[:, start:, :])
            scatter_blocks(grads_stage, outs)


def points_back(points, keys_in, values_in, grad_state, grad_totals, *refs, shards):
    outs = refs[:shards]
    sums, stage = refs[shards:]
    step = pl.program_id(0)
    width = points.shape[2]
    piece = width // shards
    keys, values = keys_in[0], values_in[0]
    left = grad_state[0]
    grad_keys = nn(left, values) + grad_totals[0, :, 0:1]
    grad_k = softmax_back(keys, grad_keys).astype(bf16)
    grad_v = nn(flip(left), keys).astype(bf16)
    found = nn(jnp.concatenate([grad_k, grad_v], axis=0), points[0])

    @pl.when(step == 0)
    def _():
        sums[...] = found

    @pl.when(step > 0)
    def _():
        sums[...] += found

    @pl.when(step == pl.num_programs(0) - 1)
    def _():
        for place in range(2):
            part = flip(sums[place * width : (place + 1) * width]).astype(bf16)
            stage[:, place * piece : (place + 1) * piece, :] = part.reshape(shards, piece, width)
        scatter_blocks(stage, outs)


def sum_kernel(*refs, count, pieces, axis):
    parts, outs, total = refs[:count], refs[count : count + pieces], refs[count + pieces]
    value = parts[0][...].astype(f32)
    for part in parts[1:]:
        value = value + part[...].astype(f32)
    size = outs[0].shape[0]
    total[...] = value.astype(bf16).reshape(total.shape)
    here = lax.axis_index(axis)
    for place, out in enumerate(outs):
        out[...] = total[lax.rem(here + place, pieces)].reshape(size, out.shape[1])


def unpack_kernel(*refs, dp, experts, piece, exit_piece, hidden):
    main, rest, last = refs[:dp], refs[dp : 2 * dp], refs[2 * dp : 3 * dp]
    outs = refs[3 * dp : 3 * dp + 15]
    main_all, rest_all, small = refs[3 * dp + 15 :]
    width = main_all.shape[2]
    here = lax.axis_index("dp")
    for place in range(dp):
        spot = lax.rem(here + dp - place, dp)
        main_all[spot] = main[place][...].astype(f32)
        rest_all[spot] = rest[place][...].astype(f32)
    (
        gain_one,
        bias_one,
        query_one,
        key_one,
        value_one,
        out_one,
        query_two,
        key_two,
        value_two,
        out_two,
        gain_two,
        bias_two,
        enter,
        leave,
        gate,
    ) = outs
    flat = main_all[...].reshape(-1, width)
    start = 0
    for expert in range(experts):
        for half in range(hidden // width):
            enter[expert, :, half * width : (half + 1) * width] = flat[start : start + piece]
            start += piece
    for expert in range(experts):
        leave[expert] = flat[start : start + exit_piece]
        start += exit_piece
    out_two[...] = flat[start : start + piece]
    start += piece
    small[:16] = flat[start : start + 16]
    flat = rest_all[...].reshape(-1, width)
    start = 0
    for out in (query_two, key_two, value_two, out_one, query_one):
        out[...] = flat[start : start + piece]
        start += piece
    small[16:] = flat[start : start + 16]
    shard = lax.axis_index("fsdp")
    turned = pltpu.roll(small[...], lax.rem(width - shard * piece, width), 1)
    gain_two[...] = turned[0:1, :piece]
    bias_two[...] = turned[1:2, :piece]
    gain_one[...] = turned[16:17, :piece]
    bias_one[...] = turned[17:18, :piece]
    for row in range(2):
        gate[row : row + 1, :] = small[pl.ds(8 + row * experts + shard, 1), 0:1]
    total = last[0][...].astype(f32)
    for part in last[1:]:
        total = total + part[...].astype(f32)
    key_one[...] = total[:piece]
    value_one[...] = total[piece:]


def whole_spec(shape):
    return pl.BlockSpec(shape, lambda *_: (0,) * len(shape))


def spread(value, axis, size):
    got = [value]
    for shift in range(1, size):
        got.append(lax.ppermute(value, axis, [(i, (i + shift) % size) for i in range(size)]))
    return got


def exchange(values, axis):
    size = len(values)
    got = [values[0]]
    for shift in range(1, size):
        route = [(i, (i + shift) % size) for i in range(size)]
        got.append(lax.ppermute(values[shift], axis, route))
    return got


def sum_pieces(parts, pieces, axis, name):
    rows, width = parts[0].shape
    size = rows // pieces
    return pl.pallas_call(
        partial(sum_kernel, count=len(parts), pieces=pieces, axis=axis),
        out_shape=[jax.ShapeDtypeStruct((size, width), bf16)] * pieces,
        scratch_shapes=[pltpu.VMEM((pieces, size, width), bf16)],
        name=name,
    )(*parts)


def padded(rows, pieces):
    unit = 16 * pieces
    return -(-rows // unit) * unit


def shards_fn(
    dp,
    shards,
    tokens,
    points,
    coords,
    presence,
    counts,
    cotangent,
    gain_first,
    bias_first,
    query_first,
    key_first,
    value_first,
    out_first,
    query_second,
    key_second,
    value_second,
    out_second,
    gain_second,
    bias_second,
    expert_in,
    expert_out,
    gate_weight,
):
    count, width = tokens.shape
    items, funcs, slots, _ = points.shape
    length = count // items
    experts, piece, hidden = expert_in.shape
    exit_piece = expert_out.shape[1]
    tile = min(TILE, length)
    steps = length // tile
    inner = experts * hidden
    enter_rows = experts * piece * (hidden // width)
    limit = pltpu.CompilerParams(vmem_limit_bytes=VMEM)

    at = {}
    place = 0
    for name, size in (
        ("query_first", piece),
        ("out_first", piece),
        ("query_second", piece),
        ("key_second", piece),
        ("value_second", piece),
        ("out_second", piece),
        ("expert_in", enter_rows),
        ("expert_out", experts * exit_piece),
        ("small", 16),
    ):
        at[name] = place
        place += size
    late_rows_count = place
    early_pack, late_pack = pl.pallas_call(
        pack_kernel,
        out_shape=[
            jax.ShapeDtypeStruct((2 * piece, width), bf16),
            jax.ShapeDtypeStruct((late_rows_count, width), bf16),
        ],
        name="pack",
    )(
        key_first,
        value_first,
        query_first,
        out_first,
        query_second,
        key_second,
        value_second,
        out_second,
        expert_in,
        expert_out,
        *(
            vector.reshape(1, piece)
            for vector in (gain_first, bias_first, gain_second, bias_second)
        ),
        gate_weight,
    )
    early_parts = spread(early_pack, "fsdp", shards)
    late_parts = spread(late_pack, "fsdp", shards)
    late_specs = [whole_spec((late_rows_count, width))] * shards
    gathered = pltpu.VMEM((shards, late_rows_count, width), bf16)

    smem = pl.BlockSpec(memory_space=pltpu.SMEM)
    units = items * funcs
    flat_points = points.reshape(units, slots, width)
    state_t, state, keys_one, values_one = pl.pallas_call(
        partial(points_forward, funcs=funcs, shards=shards),
        grid=(units,),
        in_specs=[smem, smem, pl.BlockSpec((1, slots, width), lambda u: (u, 0, 0))]
        + [whole_spec((2 * piece, width))] * shards,
        out_specs=[
            pl.BlockSpec((1, 2 * width, width), lambda u: (u, 0, 0)),
            pl.BlockSpec((1, width, 2 * width), lambda u: (u, 0, 0)),
            pl.BlockSpec((1, width, slots), lambda u: (u, 0, 0)),
            pl.BlockSpec((1, width, slots), lambda u: (u, 0, 0)),
        ],
        out_shape=[
            jax.ShapeDtypeStruct((units, 2 * width, width), bf16),
            jax.ShapeDtypeStruct((units, width, 2 * width), bf16),
            jax.ShapeDtypeStruct((units, width, slots), bf16),
            jax.ShapeDtypeStruct((units, width, slots), bf16),
        ],
        scratch_shapes=[
            pltpu.VMEM((shards, 2 * piece, width), bf16),
            pltpu.VMEM((2 * width, width), bf16),
        ],
        compiler_params=limit,
        cost_estimate=cost(8),
        name="points_forward",
    )(counts, presence, flat_points, *early_parts)

    kept = jax.ShapeDtypeStruct((items * steps, width, tile), bf16)
    main_rows = padded(enter_rows + experts * exit_piece + piece + 16, dp)

    def early(i, p, j):
        return i * steps + jnp.where(p == 0, j, steps - 1)

    def late(i, p, j):
        return i * steps + jnp.where(p == 0, 0, j)

    early_keep = pl.BlockSpec((1, width, tile), lambda i, p, j: (early(i, p, j), 0, 0))
    late_keep = pl.BlockSpec((1, width, tile), lambda i, p, j: (late(i, p, j), 0, 0))
    late_rows = pl.BlockSpec((tile, width), lambda i, p, j: (late(i, p, j), 0))
    (
        result,
        queries_one,
        cross,
        first,
        keys_two,
        values_two,
        grad_q_two,
        grad_second,
        grad_state_two,
        *main_grads,
    ) = pl.pallas_call(
        partial(main_kernel, funcs=funcs, experts=experts, shards=shards, at=at),
        grid=(items, 2, steps),
        in_specs=[
            pl.BlockSpec((tile, width), lambda i, p, j: (early(i, p, j), 0)),
            late_rows,
            pl.BlockSpec((2, tile), lambda i, p, j: (0, late(i, p, j))),
            pl.BlockSpec((funcs, 2 * width, width), lambda i, p, j: (i, 0, 0)),
        ]
        + late_specs,
        out_specs=[
            late_rows,
            early_keep,
            early_keep,
            early_keep,
            early_keep,
            early_keep,
            late_keep,
            late_keep,
            pl.BlockSpec((1, width, 2 * width), lambda i, p, j: (i, 0, 0)),
        ]
        + [whole_spec((main_rows, width))] * shards,
        out_shape=[
            jax.ShapeDtypeStruct((count, width), bf16),
            kept,
            kept,
            kept,
            kept,
            kept,
            kept,
            kept,
            jax.ShapeDtypeStruct((items, width, 2 * width), f32),
        ]
        + [jax.ShapeDtypeStruct((main_rows, width), bf16)] * shards,
        scratch_shapes=[
            gathered,
            pltpu.VMEM((shards, main_rows, width), bf16),
            pltpu.VMEM((steps, width, tile), f32),
            pltpu.VMEM((steps, width, tile), bf16),
            pltpu.VMEM((width, 2 * width), f32),
            pltpu.VMEM((2 * width, width), bf16),
            pltpu.VMEM((width, 2 * width), bf16),
            pltpu.VMEM((width, 2 * width), f32),
            pltpu.VMEM((width, width), bf16),
            pltpu.VMEM((width, width), bf16),
            pltpu.VMEM((3 * width, width), bf16),
            pltpu.VMEM((width, width), bf16),
            pltpu.VMEM((width, width), bf16),
            pltpu.VMEM((inner, width), bf16),
            pltpu.VMEM((width, inner), bf16),
            pltpu.VMEM((inner, width), bf16),
            pltpu.VMEM((width, inner), bf16),
            pltpu.VMEM((width, tile), f32),
            pltpu.VMEM((width, tile), f32),
            pltpu.VMEM((width, tile), f32),
            pltpu.VMEM((width, tile), f32),
            pltpu.VMEM((inner, tile), bf16),
            pltpu.VMEM((inner, tile), bf16),
            pltpu.VMEM((width, inner), f32),
            pltpu.VMEM((width, inner), f32),
            pltpu.VMEM((width, width), f32),
            pltpu.VMEM((width, width), f32),
            pltpu.VMEM((width, width), f32),
            pltpu.VMEM((2 * experts, tile), f32),
        ],
        compiler_params=limit,
        cost_estimate=cost(80),
        name="main",
    )(tokens, cotangent, coords, state_t, *late_parts)

    rest_rows = padded(5 * piece + 16, dp)

    def rest_call(item, earlier, after):
        first_call, last_call = item == 0, item == items - 1
        keep_spec = pl.BlockSpec((1, width, tile), lambda j: (item * steps + j, 0, 0))
        row_spec = pl.BlockSpec((tile, width), lambda j: (item * steps + j, 0))
        unit_spec = pl.BlockSpec((funcs, width, width), lambda j: (item, 0, 0))
        anywhere = pl.BlockSpec(memory_space=pl.ANY)
        in_specs = [
            smem,
            row_spec,
            keep_spec,
            keep_spec,
            keep_spec,
            keep_spec,
            keep_spec,
            keep_spec,
            keep_spec,
            pl.BlockSpec((1, width, 2 * width), lambda j: (item, 0, 0)),
            pl.BlockSpec((funcs, 2 * width, width), lambda j: (item, 0, 0)),
            pl.BlockSpec((funcs, width, 2 * width), lambda j: (item, 0, 0)),
        ] + late_specs
        operands = [
            presence,
            tokens,
            queries_one,
            cross,
            first,
            keys_two,
            values_two,
            grad_q_two,
            grad_second,
            grad_state_two,
            state_t,
            state,
            *late_parts,
        ]
        aliases = {}
        if not first_call:
            aliases = {len(operands) + k: k for k in range(3)}
            in_specs += [anywhere] * 3 + [whole_spec((width, 7 * width)), anywhere]
            operands += [*earlier[:4], after]
        out_specs = [row_spec, unit_spec, unit_spec]
        out_shape = [
            jax.ShapeDtypeStruct((count, width), f32),
            jax.ShapeDtypeStruct((units, width, width), bf16),
            jax.ShapeDtypeStruct((units, width, width), f32),
        ]
        if last_call:
            out_specs += [whole_spec((rest_rows, width))] * shards
            out_shape += [jax.ShapeDtypeStruct((rest_rows, width), bf16)] * shards
        else:
            out_specs.append(whole_spec((width, 7 * width)))
            out_shape.append(jax.ShapeDtypeStruct((width, 7 * width), f32))
        return pl.pallas_call(
            partial(
                rest_kernel,
                funcs=funcs,
                item=item,
                shards=shards,
                at=at,
                first_call=first_call,
                last_call=last_call,
            ),
            grid=(steps,),
            in_specs=in_specs,
            out_specs=out_specs,
            out_shape=out_shape,
            input_output_aliases=aliases,
            scratch_shapes=[
                gathered,
                pltpu.VMEM((shards, rest_rows, width), bf16),
                pltpu.VMEM((width, 3 * width), bf16),
                pltpu.VMEM((width, width), bf16),
                pltpu.VMEM((width, width), bf16),
                pltpu.VMEM((width, tile), f32),
                pltpu.VMEM((width, tile), f32),
                pltpu.VMEM((2, width, width), bf16),
                pltpu.VMEM((width, tile), f32),
                pltpu.VMEM((width, 2 * funcs * width), f32),
                pltpu.VMEM((width, 7 * width), f32),
            ],
            compiler_params=limit,
            cost_estimate=cost(18),
            name="rest",
        )(*operands)

    got = exchange(main_grads, "fsdp")
    found = rest_call(0, None, None)
    main_pieces = None
    for item in range(1, items):
        if main_pieces is None:
            main_pieces = sum_pieces(got, dp, "dp", "sum_main")
        found = rest_call(item, found, main_pieces[0])
    if main_pieces is None:
        main_pieces = sum_pieces(got, dp, "dp", "sum_main")
    grad_tokens, grad_state_one, grad_totals_one, *rest_grads = found
    (main_own,) = sum_pieces(exchange(main_pieces, "dp"), 1, "dp", "sum_main_own")
    main_all = spread(main_own, "dp", dp)
    rest_got = exchange(rest_grads, "fsdp")

    point_grads = pl.pallas_call(
        partial(points_back, shards=shards),
        grid=(units,),
        in_specs=[
            pl.BlockSpec((1, slots, width), lambda u: (u, 0, 0)),
            pl.BlockSpec((1, width, slots), lambda u: (u, 0, 0)),
            pl.BlockSpec((1, width, slots), lambda u: (u, 0, 0)),
            pl.BlockSpec((1, width, width), lambda u: (u, 0, 0)),
            pl.BlockSpec((1, width, width), lambda u: (u, 0, 0)),
        ],
        out_specs=[whole_spec((2 * piece, width))] * shards,
        out_shape=[jax.ShapeDtypeStruct((2 * piece, width), bf16)] * shards,
        scratch_shapes=[
            pltpu.VMEM((2 * width, width), f32),
            pltpu.VMEM((shards, 2 * piece, width), bf16),
        ],
        compiler_params=limit,
        cost_estimate=cost(7),
        name="points_back",
    )(flat_points, keys_one, values_one, grad_state_one, grad_totals_one)

    point_got = exchange(point_grads, "fsdp")
    rest_pieces = sum_pieces(rest_got, dp, "dp", "sum_rest")
    rest_exchanged = exchange(rest_pieces, "dp")
    (point_own,) = sum_pieces(point_got, 1, "dp", "sum_points")
    (rest_own,) = sum_pieces(rest_exchanged, 1, "dp", "sum_rest_own")
    point_all = spread(point_own, "dp", dp)
    rest_all = spread(rest_own, "dp", dp)

    matrix = jax.ShapeDtypeStruct((piece, width), f32)
    vector = jax.ShapeDtypeStruct((1, piece), f32)
    outs = pl.pallas_call(
        partial(
            unpack_kernel,
            dp=dp,
            experts=experts,
            piece=piece,
            exit_piece=exit_piece,
            hidden=hidden,
        ),
        out_shape=[vector] * 2
        + [matrix] * 8
        + [vector] * 2
        + [
            jax.ShapeDtypeStruct(expert_in.shape, f32),
            jax.ShapeDtypeStruct(expert_out.shape, f32),
            jax.ShapeDtypeStruct(gate_weight.shape, f32),
        ],
        scratch_shapes=[
            pltpu.VMEM((dp, main_rows // dp, width), f32),
            pltpu.VMEM((dp, rest_rows // dp, width), f32),
            pltpu.VMEM((32, width), f32),
        ],
        name="unpack",
    )(*main_all, *rest_all, *point_all)
    outs = [out.reshape(piece) if out.shape == (1, piece) else out for out in outs]
    return (result, grad_tokens, *outs)


def solution(mesh):
    rows = P(("dp", "fsdp"), None)
    matrix = P("fsdp", None)
    vector = P("fsdp")
    expert = P(None, "fsdp", None)
    parameters = (
        (vector, vector)
        + (matrix,) * 8
        + (vector, vector, expert, expert, P(None, "fsdp"))
    )
    return jax.shard_map(
        partial(shards_fn, mesh.shape["dp"], mesh.shape["fsdp"]),
        mesh=mesh,
        in_specs=(
            rows,
            P(("dp", "fsdp"), None, None, None),
            P(None, ("dp", "fsdp")),
            rows,
            rows,
            rows,
        )
        + parameters,
        out_specs=(rows, rows) + parameters,
        check_vma=False,
    )
```

```python
from functools import partial

import jax
import jax.numpy as jnp
from jax import lax
from jax.experimental import pallas as pl
from jax.experimental.pallas import tpu as pltpu
from jax.sharding import PartitionSpec as P


HEADS = 8
eps = 1e-05
f32 = jnp.float32
bf16 = jnp.bfloat16
TILE = 1024
VMEM = 56 * 1024 * 1024


def cost(microseconds):
    return pl.CostEstimate(flops=microseconds * 10**9, bytes_accessed=10**6, transcendentals=0)


def nn(left, right):
    return jnp.dot(left, right, preferred_element_type=f32)


def nt(left, right):
    return lax.dot_general(left, right, (((1,), (1,)), ((), ())), preferred_element_type=f32)


def flip(value):
    return value.T


def inverse(value):
    return pl.reciprocal(value, approx=True)


def head_softmax(value):
    width, rows = value.shape
    split = value.reshape(HEADS, width // HEADS, rows)
    raised = jnp.exp(split - jnp.max(split, axis=1, keepdims=True))
    return (raised * inverse(jnp.sum(raised, axis=1, keepdims=True))).reshape(width, rows)


def softmax_back(probs, grad):
    width, rows = grad.shape
    probs = probs.astype(f32).reshape(HEADS, width // HEADS, rows)
    grad = grad.reshape(HEADS, width // HEADS, rows)
    inner = jnp.sum(probs * grad, axis=1, keepdims=True)
    return (probs * (grad - inner)).reshape(width, rows)


def standardize(value):
    centre = value - jnp.mean(value, axis=0, keepdims=True)
    scale = lax.rsqrt(jnp.mean(centre * centre, axis=0, keepdims=True) + eps)
    return centre * scale, scale


def norm_back(grad, hat, scale):
    return scale * (
        grad
        - jnp.mean(grad, axis=0, keepdims=True)
        - hat * jnp.mean(grad * hat, axis=0, keepdims=True)
    )


def same_head(rows, columns, width):
    head = width // HEADS
    row = lax.rem(lax.broadcasted_iota(jnp.int32, (rows, columns), 0), width)
    column = lax.rem(lax.broadcasted_iota(jnp.int32, (rows, columns), 1), width)
    return lax.div(row, head) == lax.div(column, head)


def assemble(parts, gathered):
    shards = len(parts)
    here = lax.axis_index("fsdp")
    for place, part in enumerate(parts):
        gathered[lax.rem(here + shards - place, shards)] = part[...]


def columns(gathered, start, count):
    shards, _, width = gathered.shape
    piece = width // shards
    small = [gathered[shard, start : start + 16, :].astype(f32) for shard in range(shards)]
    joined = jnp.concatenate([part[:, :piece] for part in small], axis=1)
    return [
        flip(jnp.broadcast_to(joined[place : place + 1], (width, width)))[:, 0:1]
        for place in range(count)
    ]


def lane_fold(value):
    width = value.shape[0]
    total = value[:, :width]
    for start in range(width, value.shape[1], width):
        total = total + value[:, start : start + width]
    return total


def as_row(value):
    width = value.shape[0]
    return flip(jnp.broadcast_to(jnp.sum(value, axis=1, keepdims=True), (width, width)))


def scatter_blocks(stage, outs):
    shards = len(outs)
    here = lax.axis_index("fsdp")
    for place, out in enumerate(outs):
        out[...] = stage[lax.rem(here + place, shards)]


def whole(gathered, start, rows):
    shards = gathered.shape[0]
    return gathered[:, start : start + rows, :].reshape(shards * rows, gathered.shape[2])


def function_weight(presence, item, func, funcs, shape):
    total = presence[item, 0]
    for other in range(1, funcs):
        total = total + presence[item, other]
    own = jnp.full(shape, presence[item, func], jnp.int32).astype(f32)
    return own / jnp.full(shape, total, jnp.int32).astype(f32)


def pack_kernel(*refs):
    weights, vectors, gate = refs[:10], refs[10:14], refs[14]
    early, late = refs[15:]
    keys, values, query, out, query_two, key_two, value_two, out_two, enter, leave = weights
    start = 0
    for weight in (keys, values):
        early[start : start + weight.shape[0]] = weight[...]
        start += weight.shape[0]
    start = 0
    for weight in (query, out, query_two, key_two, value_two, out_two):
        late[start : start + weight.shape[0]] = weight[...]
        start += weight.shape[0]
    experts, piece, hidden = enter.shape
    width = late.shape[1]
    for expert in range(experts):
        for half in range(hidden // width):
            late[start : start + piece] = enter[expert, :, half * width : (half + 1) * width]
            start += piece
    for expert in range(experts):
        late[start : start + leave.shape[1]] = leave[expert]
        start += leave.shape[1]
    rest = jnp.zeros((1, width - piece), f32)
    rows = [
        jnp.concatenate([vector[...].astype(f32), rest], axis=1) for vector in vectors
    ]
    rows.append(jnp.zeros((4, width), f32))
    for row in range(2):
        rows.append(jnp.broadcast_to(gate[row : row + 1, 0:1].astype(f32), (1, width)))
    rows.append(jnp.zeros((6, width), f32))
    late[start : start + 16] = jnp.concatenate(rows, axis=0).astype(bf16)


def points_forward(counts, presence, points, *refs, funcs, shards):
    parts = refs[:shards]
    state_t, state, keys_out, values_out, gathered, weight = refs[shards:]
    step = pl.program_id(0)
    item, func = lax.div(step, funcs), lax.rem(step, funcs)
    width = points.shape[2]
    slots = points.shape[1]
    piece = width // shards

    @pl.when(step == 0)
    def _():
        assemble(parts, gathered)
        weight[:width] = flip(whole(gathered, 0, piece))
        weight[width:] = flip(whole(gathered, piece, piece))

    both = nt(weight[...], points[0])
    probs = head_softmax(both[:width])
    slot = lax.broadcasted_iota(jnp.int32, (1, slots), 1)
    keys = jnp.where(slot < counts[item, func], probs, 0.0).astype(bf16)
    values = both[width:].astype(bf16)
    keys_out[0] = keys
    values_out[0] = values
    extended = jnp.concatenate([values, jnp.ones_like(values)], axis=0)
    share = function_weight(presence, item, func, funcs, (1, width))
    mask = same_head(width, width, width)
    summed = nt(keys, extended)
    left = jnp.where(mask, summed[:, :width], 0.0) * share
    right = jnp.where(mask, summed[:, width:], 0.0)
    state[0, :, :width] = left.astype(bf16)
    state[0, :, width:] = (-right).astype(bf16)
    state_t[0, :width] = flip(left).astype(bf16)
    state_t[0, width:] = flip(right).astype(bf16)


def main_kernel(tokens, cotangent, coords, state_t, *refs, funcs, experts, shards, at):
    parts, outs, scratch = refs[:shards], refs[shards : 2 * shards + 9], refs[2 * shards + 9 :]
    (
        result,
        queries_out,
        cross_out,
        first_out,
        keys_out,
        values_out,
        grad_q_out,
        grad_second_out,
        grad_state_out,
    ) = outs[:9]
    grads_out = outs[9:]
    (
        params,
        grads_stage,
        first_keep,
        query_keep,
        state_sum,
        self_t,
        self_state,
        grad_state_sum,
        w_query,
        w_out_one,
        w_self,
        w_out_two_t,
        w_out_two,
        w_in_t,
        w_in,
        w_exit,
        w_exit_t,
        gain_one,
        bias_one,
        gain_two,
        bias_two,
        hidden_keep,
        inner_keep,
        sum_in,
        sum_exit,
        sum_out_two,
        sum_gain,
        sum_bias,
        sum_gate,
    ) = scratch
    item = pl.program_id(0)
    phase = pl.program_id(1)
    step = pl.program_id(2)
    steps = pl.num_programs(2)
    width = tokens.shape[1]
    rows = tokens.shape[0]
    piece = width // shards
    hidden = w_in.shape[1] // experts
    exit_piece = hidden // shards

    @pl.when((item == 0) & (phase == 0) & (step == 0))
    def _():
        assemble(parts, params)
        w_query[...] = flip(whole(params, at["query_first"], piece))
        w_out_one[...] = flip(whole(params, at["out_first"], piece))
        w_self[:width] = flip(whole(params, at["query_second"], piece))
        w_self[width : 2 * width] = flip(whole(params, at["key_second"], piece))
        w_self[2 * width :] = flip(whole(params, at["value_second"], piece))
        out_two = whole(params, at["out_second"], piece)
        w_out_two[...] = out_two
        w_out_two_t[...] = flip(out_two)
        for block in range(experts * hidden // width):
            part = whole(params, at["expert_in"] + block * piece, piece)
            w_in[:, block * width : (block + 1) * width] = part
            w_in_t[block * width : (block + 1) * width] = flip(part)
        for expert in range(experts):
            part = whole(params, at["expert_out"] + expert * exit_piece, exit_piece)
            w_exit[expert * hidden : (expert + 1) * hidden] = part
            w_exit_t[:, expert * hidden : (expert + 1) * hidden] = flip(part)
        found = columns(params, at["small"], 4)
        for vector, column in zip((gain_one, bias_one, gain_two, bias_two), found):
            vector[...] = jnp.broadcast_to(column, vector.shape)
        sum_in[...] = jnp.zeros_like(sum_in)
        sum_exit[...] = jnp.zeros_like(sum_exit)
        sum_out_two[...] = jnp.zeros_like(sum_out_two)
        sum_gain[...] = jnp.zeros_like(sum_gain)
        sum_bias[...] = jnp.zeros_like(sum_bias)
        sum_gate[...] = jnp.zeros_like(sum_gate)

    @pl.when(phase == 0)
    def _():
        rows_t = flip(tokens[...]).astype(f32)
        hat, _scale = standardize(rows_t)
        normed = (hat * gain_one[...] + bias_one[...]).astype(bf16)
        queries = head_softmax(nn(w_query[...], normed)).astype(bf16)
        queries_out[0] = queries
        mixed = jnp.zeros((width, rows), f32)
        for func in range(funcs):
            both = nn(state_t[func], queries)
            mixed = mixed + both[:width] * inverse(both[width:])
        cross = mixed.astype(bf16)
        cross_out[0] = cross
        first = rows_t + nn(w_out_one[...], cross)
        first_keep[step] = first
        first_low = first.astype(bf16)
        first_out[0] = first_low
        three = nn(w_self[...], first_low)
        query_keep[step] = head_softmax(three[:width]).astype(bf16)
        keys = head_softmax(three[width : 2 * width]).astype(bf16)
        values = three[2 * width :].astype(bf16)
        keys_out[0] = keys
        values_out[0] = values
        extended = jnp.concatenate([values, jnp.ones_like(values)], axis=0)
        found = nt(keys, extended)

        @pl.when(step == 0)
        def _():
            state_sum[...] = found

        @pl.when(step > 0)
        def _():
            state_sum[...] += found

        @pl.when(step == steps - 1)
        def _():
            mask = same_head(width, width, width)
            left = jnp.where(mask, state_sum[:, :width], 0.0)
            right = jnp.where(mask, state_sum[:, width:], 0.0)
            self_state[:, :width] = left.astype(bf16)
            self_state[:, width:] = (-right).astype(bf16)
            self_t[:width] = flip(left).astype(bf16)
            self_t[width:] = flip(right).astype(bf16)

    @pl.when(phase == 1)
    def _():
        queries = query_keep[step]
        both = nn(self_t[...], queries)
        undo = inverse(both[width:])
        own = both[:width] * undo
        own_low = own.astype(bf16)
        second = first_keep[step] + nn(w_out_two_t[...], own_low)
        hat, scale = standardize(second)
        normed = (hat * gain_two[...] + bias_two[...]).astype(bf16)
        grad = flip(cotangent[...])
        across, down = coords[0:1, :], coords[1:2, :]
        logits = []
        for expert in range(experts):
            pair = params[expert, at["small"] : at["small"] + 16, 0:1].astype(f32)
            logits.append(across * pair[8:9] + down * pair[9:10])
        peak = logits[0]
        for logit in logits[1:]:
            peak = jnp.maximum(peak, logit)
        raised = [jnp.exp(logit - peak) for logit in logits]
        total = raised[0]
        for other in raised[1:]:
            total = total + other
        gates = [other / total for other in raised]
        grad_gates = []
        for expert in range(experts):
            span = slice(expert * hidden, (expert + 1) * hidden)
            inner = nn(w_in_t[span], normed)
            back = nn(w_exit[span], grad)
            square = inner * inner
            tanh = jnp.tanh(inner * (0.7978845608028654 + 0.035677408136300125 * square))
            half = 0.5 + 0.5 * tanh
            active = inner * half
            grad_gates.append(jnp.sum(active * back, axis=0, keepdims=True))
            hidden_keep[span] = (active * gates[expert]).astype(bf16)
            slope = half + active * (1.0 - half) * (
                1.5957691216057308 + 0.21406444881780074 * square
            )
            inner_keep[span] = (slope * (back * gates[expert])).astype(bf16)
        total = second + nn(w_exit_t[...], hidden_keep[...])
        result[...] = flip(total.astype(bf16))
        grad_normed = nn(w_in[...], inner_keep[...])
        sum_exit[...] += nt(grad, hidden_keep[...])
        sum_in[...] += nt(normed, inner_keep[...])
        mean_gate = gates[0] * grad_gates[0]
        for expert in range(1, experts):
            mean_gate = mean_gate + gates[expert] * grad_gates[expert]
        for expert in range(experts):
            change = gates[expert] * (grad_gates[expert] - mean_gate)
            sum_gate[expert : expert + 1] += across * change
            sum_gate[experts + expert : experts + expert + 1] += down * change
        sum_gain[...] += lane_fold(grad_normed * hat)
        sum_bias[...] += lane_fold(grad_normed)
        grad_second = grad.astype(f32) + norm_back(grad_normed * gain_two[...], hat, scale)
        grad_second_out[0] = grad_second.astype(bf16)
        grad_own = grad_second.astype(bf16)
        sum_out_two[...] += nt(own_low, grad_own)
        share = nn(w_out_two[...], grad_own) * undo
        pair = jnp.concatenate([share.astype(bf16), (share * own).astype(bf16)], axis=0)
        grad_q = nn(self_state[...], pair)
        found = nt(queries, pair)

        @pl.when(step == 0)
        def _():
            grad_state_sum[...] = found

        @pl.when(step > 0)
        def _():
            grad_state_sum[...] += found

        grad_q_out[0] = softmax_back(queries, grad_q).astype(bf16)

        @pl.when(step == steps - 1)
        def _():
            grad_state_out[0] = grad_state_sum[...]

    @pl.when((item == pl.num_programs(0) - 1) & (phase == 1) & (step == steps - 1))
    def _():
        gain, bias = as_row(sum_gain[...]), as_row(sum_bias[...])
        gate = jnp.broadcast_to(jnp.sum(sum_gate[...], axis=1, keepdims=True), (8, width))
        row = lax.broadcasted_iota(jnp.int32, (8, width), 0)
        vectors = jnp.where(row == 0, gain[:8], bias[:8])
        small = jnp.concatenate([vectors, gate], axis=0).astype(bf16)
        start = 0
        for block in range(experts * hidden // width):
            part = sum_in[:, block * width : (block + 1) * width].astype(bf16)
            grads_stage[:, start : start + piece, :] = part.reshape(shards, piece, width)
            start += piece
        for expert in range(experts):
            part = flip(sum_exit[:, expert * hidden : (expert + 1) * hidden]).astype(bf16)
            grads_stage[:, start : start + exit_piece, :] = part.reshape(shards, exit_piece, width)
            start += exit_piece
        part = sum_out_two[...].astype(bf16)
        grads_stage[:, start : start + piece, :] = part.reshape(shards, piece, width)
        start += piece
        for shard in range(shards):
            grads_stage[shard, start : start + 16, :] = small
        scatter_blocks(grads_stage, grads_out)


def rest_kernel(
    presence,
    tokens,
    queries_in,
    cross_in,
    first_in,
    keys_in,
    values_in,
    grad_q_in,
    grad_second_in,
    grad_state_in,
    state_t,
    state,
    *refs,
    funcs,
    item,
    shards,
    at,
    first_call,
    last_call,
):
    parts, refs = refs[:shards], refs[shards:]
    if not first_call:
        carry, refs = refs[3], refs[4:]
    grad_tokens, grad_cross_state_out, grad_totals_out = refs[:3]
    outs = refs[3 : 3 + shards] if last_call else refs[3:4]
    refs = refs[3 + len(outs) :]
    (
        params,
        grads_stage,
        w_self,
        w_out_one,
        w_query,
        gain_one,
        bias_one,
        grad_self_state,
        grad_totals,
        grad_state_sum,
        sums,
    ) = refs
    step = pl.program_id(0)
    steps = pl.num_programs(0)
    width = tokens.shape[1]
    piece = width // shards
    self_part = slice(0, 3 * width)
    out_part = slice(3 * width, 4 * width)
    query_part = slice(4 * width, 5 * width)
    gain_part = slice(5 * width, 6 * width)
    bias_part = slice(6 * width, 7 * width)

    @pl.when(step == 0)
    def _():
        assemble(parts, params)
        w_query[...] = whole(params, at["query_first"], piece)
        w_out_one[...] = whole(params, at["out_first"], piece)
        w_self[:, :width] = whole(params, at["query_second"], piece)
        w_self[:, width : 2 * width] = whole(params, at["key_second"], piece)
        w_self[:, 2 * width :] = whole(params, at["value_second"], piece)
        for vector, column in zip((gain_one, bias_one), columns(params, at["small"], 2)):
            vector[...] = jnp.broadcast_to(column, vector.shape)
        sums[...] = jnp.zeros_like(sums) if first_call else carry[...]
        mask = same_head(width, width, width)
        left = jnp.where(mask, grad_state_in[0, :, :width], 0.0)
        right = jnp.where(mask, grad_state_in[0, :, width:], 0.0)
        grad_self_state[0] = left.astype(bf16)
        grad_self_state[1] = flip(left).astype(bf16)
        grad_totals[...] = jnp.broadcast_to(
            -jnp.sum(right, axis=1, keepdims=True), grad_totals.shape
        )

    first_low = first_in[0]
    keys, values = keys_in[0], values_in[0]
    grad_k = softmax_back(keys, nn(grad_self_state[0], values) + grad_totals[...]).astype(bf16)
    grad_v = nn(grad_self_state[1], keys).astype(bf16)
    three = jnp.concatenate([grad_q_in[0], grad_k, grad_v], axis=0)
    sums[:, self_part] += nt(first_low, three)
    grad_first = grad_second_in[0].astype(f32) + nn(w_self[...], three)
    grad_cross = grad_first.astype(bf16)
    sums[:, out_part] += nt(cross_in[0], grad_cross)
    share = nn(w_out_one[...], grad_cross)
    queries = queries_in[0]
    pieces = []
    for func in range(funcs):
        both = nn(state_t[func], queries)
        undo = inverse(both[width:])
        part = share * undo
        pieces.append(part.astype(bf16))
        pieces.append((part * (both[:width] * undo)).astype(bf16))
    stack = jnp.concatenate(pieces, axis=0)
    found = nt(queries, stack)

    @pl.when(step == 0)
    def _():
        grad_state_sum[...] = found

    @pl.when(step > 0)
    def _():
        grad_state_sum[...] += found

    joined = jnp.concatenate([state[func] for func in range(funcs)], axis=1)
    grad_q = softmax_back(queries, nn(joined, stack)).astype(bf16)
    rows_t = flip(tokens[...]).astype(f32)
    hat, scale = standardize(rows_t)
    normed = (hat * gain_one[...] + bias_one[...]).astype(bf16)
    sums[:, query_part] += nt(normed, grad_q)
    grad_normed = nn(w_query[...], grad_q)
    sums[:, gain_part] += lane_fold(grad_normed * hat)
    sums[:, bias_part] += lane_fold(grad_normed)
    grad_rows = grad_first + norm_back(grad_normed * gain_one[...], hat, scale)
    grad_tokens[...] = flip(grad_rows)

    @pl.when(step == steps - 1)
    def _():
        mask = same_head(width, width, width)
        for func in range(funcs):
            weight = function_weight(presence, item, func, funcs, (1, width))
            start = 2 * func * width
            left = jnp.where(mask, grad_state_sum[:, start : start + width], 0.0) * weight
            right = jnp.where(mask, grad_state_sum[:, start + width : start + 2 * width], 0.0)
            grad_cross_state_out[func] = left.astype(bf16)
            grad_totals_out[func] = jnp.broadcast_to(
                -jnp.sum(right, axis=1, keepdims=True), (width, width)
            )
        if not last_call:
            outs[0][...] = sums[...]
        else:
            gain, bias = as_row(sums[:, gain_part]), as_row(sums[:, bias_part])
            row = lax.broadcasted_iota(jnp.int32, (16, width), 0)
            small = jnp.where(row == 0, gain[:16], bias[:16]).astype(bf16)
            for place in range(5):
                part = sums[:, place * width : (place + 1) * width].astype(bf16)
                grads_stage[:, place * piece : (place + 1) * piece, :] = part.reshape(
                    shards, piece, width
                )
            for shard in range(shards):
                grads_stage[shard, 5 * piece : 5 * piece + 16, :] = small
            scatter_blocks(grads_stage, outs)


def points_back(points, keys_in, values_in, grad_state, grad_totals, *refs, shards):
    outs = refs[:shards]
    sums, stage = refs[shards:]
    step = pl.program_id(0)
    width = points.shape[2]
    piece = width // shards
    keys, values = keys_in[0], values_in[0]
    left = grad_state[0]
    grad_keys = nn(left, values) + grad_totals[0, :, 0:1]
    grad_k = softmax_back(keys, grad_keys).astype(bf16)
    grad_v = nn(flip(left), keys).astype(bf16)
    found = nn(jnp.concatenate([grad_k, grad_v], axis=0), points[0])

    @pl.when(step == 0)
    def _():
        sums[...] = found

    @pl.when(step > 0)
    def _():
        sums[...] += found

    @pl.when(step == pl.num_programs(0) - 1)
    def _():
        for place in range(2):
            part = flip(sums[place * width : (place + 1) * width]).astype(bf16)
            stage[:, place * piece : (place + 1) * piece, :] = part.reshape(shards, piece, width)
        scatter_blocks(stage, outs)


def join_kernel(*refs, counts):
    out = refs[-1]
    start = 0
    for count in counts:
        group, refs = refs[:count], refs[count:]
        value = group[0][...].astype(f32)
        for part in group[1:]:
            value = value + part[...].astype(f32)
        out[start : start + value.shape[0]] = value.astype(bf16)
        start += value.shape[0]
    if start < out.shape[0]:
        out[start:] = jnp.zeros_like(out[start:])


def sum_kernel(parts, out):
    value = parts[0].astype(f32)
    for part in range(1, parts.shape[0]):
        value = value + parts[part].astype(f32)
    out[...] = value.astype(bf16)


def unpack_kernel(joined, *refs, experts, piece, exit_piece, hidden, spots):
    outs, (small,) = refs[:15], refs[15:]
    width = joined.shape[1]
    (
        gain_one,
        bias_one,
        query_one,
        key_one,
        value_one,
        out_one,
        query_two,
        key_two,
        value_two,
        out_two,
        gain_two,
        bias_two,
        enter,
        leave,
        gate,
    ) = outs
    start = spots[0]
    for expert in range(experts):
        for half in range(hidden // width):
            block = joined[start : start + piece].astype(f32)
            enter[expert, :, half * width : (half + 1) * width] = block
            start += piece
    for expert in range(experts):
        leave[expert] = joined[start : start + exit_piece].astype(f32)
        start += exit_piece
    out_two[...] = joined[start : start + piece].astype(f32)
    start += piece
    small[:16] = joined[start : start + 16].astype(f32)
    start = spots[1]
    for out in (query_two, key_two, value_two, out_one, query_one):
        out[...] = joined[start : start + piece].astype(f32)
        start += piece
    small[16:] = joined[start : start + 16].astype(f32)
    start = spots[2]
    for out in (key_one, value_one):
        out[...] = joined[start : start + piece].astype(f32)
        start += piece
    shard = lax.axis_index("fsdp")
    turned = pltpu.roll(small[...], lax.rem(width - shard * piece, width), 1)
    gain_two[...] = turned[0:1, :piece]
    bias_two[...] = turned[1:2, :piece]
    gain_one[...] = turned[16:17, :piece]
    bias_one[...] = turned[17:18, :piece]
    for row in range(2):
        gate[row : row + 1, :] = small[pl.ds(8 + row * experts + shard, 1), 0:1]


def whole_spec(shape):
    return pl.BlockSpec(shape, lambda *_: (0,) * len(shape))


def spread(value, axis, size):
    got = [value]
    for shift in range(1, size):
        got.append(lax.ppermute(value, axis, [(i, (i + shift) % size) for i in range(size)]))
    return got


def exchange(values, axis):
    size = len(values)
    got = [values[0]]
    for shift in range(1, size):
        route = [(i, (i + shift) % size) for i in range(size)]
        got.append(lax.ppermute(values[shift], axis, route))
    return got


def padded(rows, pieces):
    unit = 16 * pieces
    return -(-rows // unit) * unit


def shards_fn(
    dp,
    shards,
    tokens,
    points,
    coords,
    presence,
    counts,
    cotangent,
    gain_first,
    bias_first,
    query_first,
    key_first,
    value_first,
    out_first,
    query_second,
    key_second,
    value_second,
    out_second,
    gain_second,
    bias_second,
    expert_in,
    expert_out,
    gate_weight,
):
    count, width = tokens.shape
    items, funcs, slots, _ = points.shape
    length = count // items
    experts, piece, hidden = expert_in.shape
    exit_piece = expert_out.shape[1]
    tile = min(TILE, length)
    steps = length // tile
    inner = experts * hidden
    enter_rows = experts * piece * (hidden // width)
    limit = pltpu.CompilerParams(vmem_limit_bytes=VMEM)

    at = {}
    place = 0
    for name, size in (
        ("query_first", piece),
        ("out_first", piece),
        ("query_second", piece),
        ("key_second", piece),
        ("value_second", piece),
        ("out_second", piece),
        ("expert_in", enter_rows),
        ("expert_out", experts * exit_piece),
        ("small", 16),
    ):
        at[name] = place
        place += size
    late_rows_count = place
    early_pack, late_pack = pl.pallas_call(
        pack_kernel,
        out_shape=[
            jax.ShapeDtypeStruct((2 * piece, width), bf16),
            jax.ShapeDtypeStruct((late_rows_count, width), bf16),
        ],
        name="pack",
    )(
        key_first,
        value_first,
        query_first,
        out_first,
        query_second,
        key_second,
        value_second,
        out_second,
        expert_in,
        expert_out,
        *(
            vector.reshape(1, piece)
            for vector in (gain_first, bias_first, gain_second, bias_second)
        ),
        gate_weight,
    )
    early_parts = spread(early_pack, "fsdp", shards)
    late_parts = spread(late_pack, "fsdp", shards)
    late_specs = [whole_spec((late_rows_count, width))] * shards
    gathered = pltpu.VMEM((shards, late_rows_count, width), bf16)

    smem = pl.BlockSpec(memory_space=pltpu.SMEM)
    units = items * funcs
    flat_points = points.reshape(units, slots, width)
    state_t, state, keys_one, values_one = pl.pallas_call(
        partial(points_forward, funcs=funcs, shards=shards),
        grid=(units,),
        in_specs=[smem, smem, pl.BlockSpec((1, slots, width), lambda u: (u, 0, 0))]
        + [whole_spec((2 * piece, width))] * shards,
        out_specs=[
            pl.BlockSpec((1, 2 * width, width), lambda u: (u, 0, 0)),
            pl.BlockSpec((1, width, 2 * width), lambda u: (u, 0, 0)),
            pl.BlockSpec((1, width, slots), lambda u: (u, 0, 0)),
            pl.BlockSpec((1, width, slots), lambda u: (u, 0, 0)),
        ],
        out_shape=[
            jax.ShapeDtypeStruct((units, 2 * width, width), bf16),
            jax.ShapeDtypeStruct((units, width, 2 * width), bf16),
            jax.ShapeDtypeStruct((units, width, slots), bf16),
            jax.ShapeDtypeStruct((units, width, slots), bf16),
        ],
        scratch_shapes=[
            pltpu.VMEM((shards, 2 * piece, width), bf16),
            pltpu.VMEM((2 * width, width), bf16),
        ],
        compiler_params=limit,
        cost_estimate=cost(8),
        name="points_forward",
    )(counts, presence, flat_points, *early_parts)

    kept = jax.ShapeDtypeStruct((items * steps, width, tile), bf16)
    main_rows = enter_rows + experts * exit_piece + piece + 16

    def early(i, p, j):
        return i * steps + jnp.where(p == 0, j, steps - 1)

    def late(i, p, j):
        return i * steps + jnp.where(p == 0, 0, j)

    early_keep = pl.BlockSpec((1, width, tile), lambda i, p, j: (early(i, p, j), 0, 0))
    late_keep = pl.BlockSpec((1, width, tile), lambda i, p, j: (late(i, p, j), 0, 0))
    late_rows = pl.BlockSpec((tile, width), lambda i, p, j: (late(i, p, j), 0))
    (
        result,
        queries_one,
        cross,
        first,
        keys_two,
        values_two,
        grad_q_two,
        grad_second,
        grad_state_two,
        *main_grads,
    ) = pl.pallas_call(
        partial(main_kernel, funcs=funcs, experts=experts, shards=shards, at=at),
        grid=(items, 2, steps),
        in_specs=[
            pl.BlockSpec((tile, width), lambda i, p, j: (early(i, p, j), 0)),
            late_rows,
            pl.BlockSpec((2, tile), lambda i, p, j: (0, late(i, p, j))),
            pl.BlockSpec((funcs, 2 * width, width), lambda i, p, j: (i, 0, 0)),
        ]
        + late_specs,
        out_specs=[
            late_rows,
            early_keep,
            early_keep,
            early_keep,
            early_keep,
            early_keep,
            late_keep,
            late_keep,
            pl.BlockSpec((1, width, 2 * width), lambda i, p, j: (i, 0, 0)),
        ]
        + [whole_spec((main_rows, width))] * shards,
        out_shape=[
            jax.ShapeDtypeStruct((count, width), bf16),
            kept,
            kept,
            kept,
            kept,
            kept,
            kept,
            kept,
            jax.ShapeDtypeStruct((items, width, 2 * width), f32),
        ]
        + [jax.ShapeDtypeStruct((main_rows, width), bf16)] * shards,
        scratch_shapes=[
            gathered,
            pltpu.VMEM((shards, main_rows, width), bf16),
            pltpu.VMEM((steps, width, tile), f32),
            pltpu.VMEM((steps, width, tile), bf16),
            pltpu.VMEM((width, 2 * width), f32),
            pltpu.VMEM((2 * width, width), bf16),
            pltpu.VMEM((width, 2 * width), bf16),
            pltpu.VMEM((width, 2 * width), f32),
            pltpu.VMEM((width, width), bf16),
            pltpu.VMEM((width, width), bf16),
            pltpu.VMEM((3 * width, width), bf16),
            pltpu.VMEM((width, width), bf16),
            pltpu.VMEM((width, width), bf16),
            pltpu.VMEM((inner, width), bf16),
            pltpu.VMEM((width, inner), bf16),
            pltpu.VMEM((inner, width), bf16),
            pltpu.VMEM((width, inner), bf16),
            pltpu.VMEM((width, tile), f32),
            pltpu.VMEM((width, tile), f32),
            pltpu.VMEM((width, tile), f32),
            pltpu.VMEM((width, tile), f32),
            pltpu.VMEM((inner, tile), bf16),
            pltpu.VMEM((inner, tile), bf16),
            pltpu.VMEM((width, inner), f32),
            pltpu.VMEM((width, inner), f32),
            pltpu.VMEM((width, width), f32),
            pltpu.VMEM((width, width), f32),
            pltpu.VMEM((width, width), f32),
            pltpu.VMEM((2 * experts, tile), f32),
        ],
        compiler_params=limit,
        cost_estimate=cost(80),
        name="main",
    )(tokens, cotangent, coords, state_t, *late_parts)

    rest_rows = 5 * piece + 16

    def rest_call(item, earlier):
        first_call, last_call = item == 0, item == items - 1
        keep_spec = pl.BlockSpec((1, width, tile), lambda j: (item * steps + j, 0, 0))
        row_spec = pl.BlockSpec((tile, width), lambda j: (item * steps + j, 0))
        unit_spec = pl.BlockSpec((funcs, width, width), lambda j: (item, 0, 0))
        anywhere = pl.BlockSpec(memory_space=pl.ANY)
        in_specs = [
            smem,
            row_spec,
            keep_spec,
            keep_spec,
            keep_spec,
            keep_spec,
            keep_spec,
            keep_spec,
            keep_spec,
            pl.BlockSpec((1, width, 2 * width), lambda j: (item, 0, 0)),
            pl.BlockSpec((funcs, 2 * width, width), lambda j: (item, 0, 0)),
            pl.BlockSpec((funcs, width, 2 * width), lambda j: (item, 0, 0)),
        ] + late_specs
        operands = [
            presence,
            tokens,
            queries_one,
            cross,
            first,
            keys_two,
            values_two,
            grad_q_two,
            grad_second,
            grad_state_two,
            state_t,
            state,
            *late_parts,
        ]
        aliases = {}
        if not first_call:
            aliases = {len(operands) + k: k for k in range(3)}
            in_specs += [anywhere] * 3 + [whole_spec((width, 7 * width))]
            operands += earlier
        out_specs = [row_spec, unit_spec, unit_spec]
        out_shape = [
            jax.ShapeDtypeStruct((count, width), f32),
            jax.ShapeDtypeStruct((units, width, width), bf16),
            jax.ShapeDtypeStruct((units, width, width), f32),
        ]
        if last_call:
            out_specs += [whole_spec((rest_rows, width))] * shards
            out_shape += [jax.ShapeDtypeStruct((rest_rows, width), bf16)] * shards
        else:
            out_specs.append(whole_spec((width, 7 * width)))
            out_shape.append(jax.ShapeDtypeStruct((width, 7 * width), f32))
        return pl.pallas_call(
            partial(
                rest_kernel,
                funcs=funcs,
                item=item,
                shards=shards,
                at=at,
                first_call=first_call,
                last_call=last_call,
            ),
            grid=(steps,),
            in_specs=in_specs,
            out_specs=out_specs,
            out_shape=out_shape,
            input_output_aliases=aliases,
            scratch_shapes=[
                gathered,
                pltpu.VMEM((shards, rest_rows, width), bf16),
                pltpu.VMEM((width, 3 * width), bf16),
                pltpu.VMEM((width, width), bf16),
                pltpu.VMEM((width, width), bf16),
                pltpu.VMEM((width, tile), f32),
                pltpu.VMEM((width, tile), f32),
                pltpu.VMEM((2, width, width), bf16),
                pltpu.VMEM((width, tile), f32),
                pltpu.VMEM((width, 2 * funcs * width), f32),
                pltpu.VMEM((width, 7 * width), f32),
            ],
            compiler_params=limit,
            cost_estimate=cost(18),
            name="rest",
        )(*operands)

    main_got = exchange(main_grads, "fsdp")
    found = None
    for item in range(items):
        found = rest_call(item, found)
    grad_tokens, grad_state_one, grad_totals_one, *rest_grads = found
    rest_got = exchange(rest_grads, "fsdp")

    point_grads = pl.pallas_call(
        partial(points_back, shards=shards),
        grid=(units,),
        in_specs=[
            pl.BlockSpec((1, slots, width), lambda u: (u, 0, 0)),
            pl.BlockSpec((1, width, slots), lambda u: (u, 0, 0)),
            pl.BlockSpec((1, width, slots), lambda u: (u, 0, 0)),
            pl.BlockSpec((1, width, width), lambda u: (u, 0, 0)),
            pl.BlockSpec((1, width, width), lambda u: (u, 0, 0)),
        ],
        out_specs=[whole_spec((2 * piece, width))] * shards,
        out_shape=[jax.ShapeDtypeStruct((2 * piece, width), bf16)] * shards,
        scratch_shapes=[
            pltpu.VMEM((2 * width, width), f32),
            pltpu.VMEM((shards, 2 * piece, width), bf16),
        ],
        compiler_params=limit,
        cost_estimate=cost(7),
        name="points_back",
    )(flat_points, keys_one, values_one, grad_state_one, grad_totals_one)

    point_got = exchange(point_grads, "fsdp")
    spots = (0, main_rows, main_rows + rest_rows)
    all_rows = padded(main_rows + rest_rows + 2 * piece, dp)
    joined = pl.pallas_call(
        partial(join_kernel, counts=(shards, shards, shards)),
        out_shape=jax.ShapeDtypeStruct((all_rows, width), bf16),
        name="join",
    )(*main_got, *rest_got, *point_got)
    split = joined.reshape(dp, all_rows // dp, width)
    split = lax.all_to_all(split, "dp", 0, 0, tiled=True)
    own = pl.pallas_call(
        sum_kernel,
        out_shape=jax.ShapeDtypeStruct((all_rows // dp, width), bf16),
        name="sum",
    )(split)
    joined = lax.all_gather(own, "dp", axis=0, tiled=True)

    matrix = jax.ShapeDtypeStruct((piece, width), f32)
    vector = jax.ShapeDtypeStruct((1, piece), f32)
    outs = pl.pallas_call(
        partial(
            unpack_kernel,
            experts=experts,
            piece=piece,
            exit_piece=exit_piece,
            hidden=hidden,
            spots=spots,
        ),
        out_shape=[vector] * 2
        + [matrix] * 8
        + [vector] * 2
        + [
            jax.ShapeDtypeStruct(expert_in.shape, f32),
            jax.ShapeDtypeStruct(expert_out.shape, f32),
            jax.ShapeDtypeStruct(gate_weight.shape, f32),
        ],
        scratch_shapes=[
            pltpu.VMEM((32, width), f32),
        ],
        name="unpack",
    )(joined)
    outs = [out.reshape(piece) if out.shape == (1, piece) else out for out in outs]
    return (result, grad_tokens, *outs)


def solution(mesh):
    rows = P(("dp", "fsdp"), None)
    matrix = P("fsdp", None)
    vector = P("fsdp")
    expert = P(None, "fsdp", None)
    parameters = (
        (vector, vector)
        + (matrix,) * 8
        + (vector, vector, expert, expert, P(None, "fsdp"))
    )
    return jax.shard_map(
        partial(shards_fn, mesh.shape["dp"], mesh.shape["fsdp"]),
        mesh=mesh,
        in_specs=(
            rows,
            P(("dp", "fsdp"), None, None, None),
            P(None, ("dp", "fsdp")),
            rows,
            rows,
            rows,
        )
        + parameters,
        out_specs=(rows, rows) + parameters,
        check_vma=False,
    )
```

```python
from functools import partial

import jax
import jax.numpy as jnp
from jax import lax
from jax.experimental import pallas as pl
from jax.experimental.pallas import tpu as pltpu
from jax.sharding import PartitionSpec as P


HEADS = 8
eps = 1e-05
f32 = jnp.float32
bf16 = jnp.bfloat16
TILE = 1024
VMEM = 56 * 1024 * 1024


def cost(microseconds):
    return pl.CostEstimate(flops=microseconds * 10**9, bytes_accessed=10**6, transcendentals=0)


def nn(left, right):
    return jnp.dot(left, right, preferred_element_type=f32)


def nt(left, right):
    return lax.dot_general(left, right, (((1,), (1,)), ((), ())), preferred_element_type=f32)


def flip(value):
    return value.T


def inverse(value):
    return pl.reciprocal(value, approx=True)


def head_softmax(value):
    width, rows = value.shape
    split = value.reshape(HEADS, width // HEADS, rows)
    raised = jnp.exp(split - jnp.max(split, axis=1, keepdims=True))
    return (raised * inverse(jnp.sum(raised, axis=1, keepdims=True))).reshape(width, rows)


def softmax_back(probs, grad):
    width, rows = grad.shape
    probs = probs.astype(f32).reshape(HEADS, width // HEADS, rows)
    grad = grad.reshape(HEADS, width // HEADS, rows)
    inner = jnp.sum(probs * grad, axis=1, keepdims=True)
    return (probs * (grad - inner)).reshape(width, rows)


def standardize(value):
    centre = value - jnp.mean(value, axis=0, keepdims=True)
    scale = lax.rsqrt(jnp.mean(centre * centre, axis=0, keepdims=True) + eps)
    return centre * scale, scale


def norm_back(grad, hat, scale):
    return scale * (
        grad
        - jnp.mean(grad, axis=0, keepdims=True)
        - hat * jnp.mean(grad * hat, axis=0, keepdims=True)
    )


def same_head(rows, columns, width):
    head = width // HEADS
    row = lax.rem(lax.broadcasted_iota(jnp.int32, (rows, columns), 0), width)
    column = lax.rem(lax.broadcasted_iota(jnp.int32, (rows, columns), 1), width)
    return lax.div(row, head) == lax.div(column, head)


def assemble(parts, gathered):
    shards = len(parts)
    here = lax.axis_index("fsdp")
    for place, part in enumerate(parts):
        gathered[lax.rem(here + shards - place, shards)] = part[...]


def columns(gathered, start, count):
    shards, _, width = gathered.shape
    piece = width // shards
    small = [gathered[shard, start : start + 16, :].astype(f32) for shard in range(shards)]
    joined = jnp.concatenate([part[:, :piece] for part in small], axis=1)
    return [
        flip(jnp.broadcast_to(joined[place : place + 1], (width, width)))[:, 0:1]
        for place in range(count)
    ]


def lane_fold(value):
    width = value.shape[0]
    total = value[:, :width]
    for start in range(width, value.shape[1], width):
        total = total + value[:, start : start + width]
    return total


def as_row(value):
    width = value.shape[0]
    return flip(jnp.broadcast_to(jnp.sum(value, axis=1, keepdims=True), (width, width)))


def scatter_blocks(stage, outs):
    shards = len(outs)
    here = lax.axis_index("fsdp")
    for place, out in enumerate(outs):
        out[...] = stage[lax.rem(here + place, shards)]


def whole(gathered, start, rows):
    shards = gathered.shape[0]
    return gathered[:, start : start + rows, :].reshape(shards * rows, gathered.shape[2])


def function_weight(presence, item, func, funcs, shape):
    total = presence[item, 0]
    for other in range(1, funcs):
        total = total + presence[item, other]
    own = jnp.full(shape, presence[item, func], jnp.int32).astype(f32)
    return own / jnp.full(shape, total, jnp.int32).astype(f32)


def pack_kernel(*refs):
    weights, vectors, gate = refs[:10], refs[10:14], refs[14]
    early, late = refs[15:]
    keys, values, query, out, query_two, key_two, value_two, out_two, enter, leave = weights
    start = 0
    for weight in (keys, values):
        early[start : start + weight.shape[0]] = weight[...]
        start += weight.shape[0]
    start = 0
    for weight in (query, out, query_two, key_two, value_two, out_two):
        late[start : start + weight.shape[0]] = weight[...]
        start += weight.shape[0]
    experts, piece, hidden = enter.shape
    width = late.shape[1]
    for expert in range(experts):
        for half in range(hidden // width):
            late[start : start + piece] = enter[expert, :, half * width : (half + 1) * width]
            start += piece
    for expert in range(experts):
        late[start : start + leave.shape[1]] = leave[expert]
        start += leave.shape[1]
    rest = jnp.zeros((1, width - piece), f32)
    rows = [
        jnp.concatenate([vector[...].astype(f32), rest], axis=1) for vector in vectors
    ]
    rows.append(jnp.zeros((4, width), f32))
    for row in range(2):
        rows.append(jnp.broadcast_to(gate[row : row + 1, 0:1].astype(f32), (1, width)))
    rows.append(jnp.zeros((6, width), f32))
    late[start : start + 16] = jnp.concatenate(rows, axis=0).astype(bf16)


def points_forward(counts, presence, points, *refs, funcs, shards):
    parts = refs[:shards]
    state_t, state, keys_out, values_out, gathered, weight = refs[shards:]
    step = pl.program_id(0)
    item, func = lax.div(step, funcs), lax.rem(step, funcs)
    width = points.shape[2]
    slots = points.shape[1]
    piece = width // shards

    @pl.when(step == 0)
    def _():
        assemble(parts, gathered)
        weight[:width] = flip(whole(gathered, 0, piece))
        weight[width:] = flip(whole(gathered, piece, piece))

    both = nt(weight[...], points[0])
    probs = head_softmax(both[:width])
    slot = lax.broadcasted_iota(jnp.int32, (1, slots), 1)
    keys = jnp.where(slot < counts[item, func], probs, 0.0).astype(bf16)
    values = both[width:].astype(bf16)
    keys_out[0] = keys
    values_out[0] = values
    extended = jnp.concatenate([values, jnp.ones_like(values)], axis=0)
    share = function_weight(presence, item, func, funcs, (1, width))
    mask = same_head(width, width, width)
    summed = nt(keys, extended)
    left = jnp.where(mask, summed[:, :width], 0.0) * share
    right = jnp.where(mask, summed[:, width:], 0.0)
    state[0, :, :width] = left.astype(bf16)
    state[0, :, width:] = (-right).astype(bf16)
    state_t[0, :width] = flip(left).astype(bf16)
    state_t[0, width:] = flip(right).astype(bf16)


def main_kernel(tokens, cotangent, coords, state_t, *refs, funcs, experts, shards, at):
    parts, outs, scratch = refs[:shards], refs[shards : 2 * shards + 9], refs[2 * shards + 9 :]
    (
        result,
        queries_out,
        cross_out,
        first_out,
        keys_out,
        values_out,
        grad_q_out,
        grad_second_out,
        grad_state_out,
    ) = outs[:9]
    grads_out = outs[9:]
    (
        params,
        grads_stage,
        first_keep,
        query_keep,
        state_sum,
        self_t,
        self_state,
        grad_state_sum,
        w_query,
        w_out_one,
        w_self,
        w_out_two_t,
        w_out_two,
        w_in_t,
        w_in,
        w_exit,
        w_exit_t,
        gain_one,
        bias_one,
        gain_two,
        bias_two,
        hidden_keep,
        inner_keep,
        sum_in,
        sum_exit,
        sum_out_two,
        sum_gain,
        sum_bias,
        sum_gate,
    ) = scratch
    item = pl.program_id(0)
    phase = pl.program_id(1)
    step = pl.program_id(2)
    steps = pl.num_programs(2)
    width = tokens.shape[1]
    rows = tokens.shape[0]
    piece = width // shards
    hidden = w_in.shape[1] // experts
    exit_piece = hidden // shards

    @pl.when((item == 0) & (phase == 0) & (step == 0))
    def _():
        assemble(parts, params)
        w_query[...] = flip(whole(params, at["query_first"], piece))
        w_out_one[...] = flip(whole(params, at["out_first"], piece))
        w_self[:width] = flip(whole(params, at["query_second"], piece))
        w_self[width : 2 * width] = flip(whole(params, at["key_second"], piece))
        w_self[2 * width :] = flip(whole(params, at["value_second"], piece))
        out_two = whole(params, at["out_second"], piece)
        w_out_two[...] = out_two
        w_out_two_t[...] = flip(out_two)
        for block in range(experts * hidden // width):
            part = whole(params, at["expert_in"] + block * piece, piece)
            w_in[:, block * width : (block + 1) * width] = part
            w_in_t[block * width : (block + 1) * width] = flip(part)
        for expert in range(experts):
            part = whole(params, at["expert_out"] + expert * exit_piece, exit_piece)
            w_exit[expert * hidden : (expert + 1) * hidden] = part
            w_exit_t[:, expert * hidden : (expert + 1) * hidden] = flip(part)
        found = columns(params, at["small"], 4)
        for vector, column in zip((gain_one, bias_one, gain_two, bias_two), found):
            vector[...] = jnp.broadcast_to(column, vector.shape)
        sum_in[...] = jnp.zeros_like(sum_in)
        sum_exit[...] = jnp.zeros_like(sum_exit)
        sum_out_two[...] = jnp.zeros_like(sum_out_two)
        sum_gain[...] = jnp.zeros_like(sum_gain)
        sum_bias[...] = jnp.zeros_like(sum_bias)
        sum_gate[...] = jnp.zeros_like(sum_gate)

    @pl.when(phase == 0)
    def _():
        rows_t = flip(tokens[...]).astype(f32)
        hat, _scale = standardize(rows_t)
        normed = (hat * gain_one[...] + bias_one[...]).astype(bf16)
        queries = head_softmax(nn(w_query[...], normed)).astype(bf16)
        queries_out[0] = queries
        mixed = jnp.zeros((width, rows), f32)
        for func in range(funcs):
            both = nn(state_t[func], queries)
            mixed = mixed + both[:width] * inverse(both[width:])
        cross = mixed.astype(bf16)
        cross_out[0] = cross
        first = rows_t + nn(w_out_one[...], cross)
        first_keep[step] = first
        first_low = first.astype(bf16)
        first_out[0] = first_low
        three = nn(w_self[...], first_low)
        query_keep[step] = head_softmax(three[:width]).astype(bf16)
        keys = head_softmax(three[width : 2 * width]).astype(bf16)
        values = three[2 * width :].astype(bf16)
        keys_out[0] = keys
        values_out[0] = values
        extended = jnp.concatenate([values, jnp.ones_like(values)], axis=0)
        found = nt(keys, extended)

        @pl.when(step == 0)
        def _():
            state_sum[...] = found

        @pl.when(step > 0)
        def _():
            state_sum[...] += found

        @pl.when(step == steps - 1)
        def _():
            mask = same_head(width, width, width)
            left = jnp.where(mask, state_sum[:, :width], 0.0)
            right = jnp.where(mask, state_sum[:, width:], 0.0)
            self_state[:, :width] = left.astype(bf16)
            self_state[:, width:] = (-right).astype(bf16)
            self_t[:width] = flip(left).astype(bf16)
            self_t[width:] = flip(right).astype(bf16)

    @pl.when(phase == 1)
    def _():
        queries = query_keep[step]
        both = nn(self_t[...], queries)
        undo = inverse(both[width:])
        own = both[:width] * undo
        own_low = own.astype(bf16)
        second = first_keep[step] + nn(w_out_two_t[...], own_low)
        hat, scale = standardize(second)
        normed = (hat * gain_two[...] + bias_two[...]).astype(bf16)
        grad = flip(cotangent[...])
        across, down = coords[0:1, :], coords[1:2, :]
        logits = []
        for expert in range(experts):
            pair = params[expert, at["small"] : at["small"] + 16, 0:1].astype(f32)
            logits.append(across * pair[8:9] + down * pair[9:10])
        peak = logits[0]
        for logit in logits[1:]:
            peak = jnp.maximum(peak, logit)
        raised = [jnp.exp(logit - peak) for logit in logits]
        total = raised[0]
        for other in raised[1:]:
            total = total + other
        gates = [other / total for other in raised]
        grad_gates = []
        for expert in range(experts):
            span = slice(expert * hidden, (expert + 1) * hidden)
            inner = nn(w_in_t[span], normed)
            back = nn(w_exit[span], grad)
            square = inner * inner
            tanh = jnp.tanh(inner * (0.7978845608028654 + 0.035677408136300125 * square))
            half = 0.5 + 0.5 * tanh
            active = inner * half
            grad_gates.append(jnp.sum(active * back, axis=0, keepdims=True))
            hidden_keep[span] = (active * gates[expert]).astype(bf16)
            slope = half + active * (1.0 - half) * (
                1.5957691216057308 + 0.21406444881780074 * square
            )
            inner_keep[span] = (slope * (back * gates[expert])).astype(bf16)
        total = second + nn(w_exit_t[...], hidden_keep[...])
        result[...] = flip(total.astype(bf16))
        grad_normed = nn(w_in[...], inner_keep[...])
        sum_exit[...] += nt(grad, hidden_keep[...])
        sum_in[...] += nt(normed, inner_keep[...])
        mean_gate = gates[0] * grad_gates[0]
        for expert in range(1, experts):
            mean_gate = mean_gate + gates[expert] * grad_gates[expert]
        for expert in range(experts):
            change = gates[expert] * (grad_gates[expert] - mean_gate)
            sum_gate[expert : expert + 1] += across * change
            sum_gate[experts + expert : experts + expert + 1] += down * change
        sum_gain[...] += lane_fold(grad_normed * hat)
        sum_bias[...] += lane_fold(grad_normed)
        grad_second = grad.astype(f32) + norm_back(grad_normed * gain_two[...], hat, scale)
        grad_second_out[0] = grad_second.astype(bf16)
        grad_own = grad_second.astype(bf16)
        sum_out_two[...] += nt(own_low, grad_own)
        share = nn(w_out_two[...], grad_own) * undo
        pair = jnp.concatenate([share.astype(bf16), (share * own).astype(bf16)], axis=0)
        grad_q = nn(self_state[...], pair)
        found = nt(queries, pair)

        @pl.when(step == 0)
        def _():
            grad_state_sum[...] = found

        @pl.when(step > 0)
        def _():
            grad_state_sum[...] += found

        grad_q_out[0] = softmax_back(queries, grad_q).astype(bf16)

        @pl.when(step == steps - 1)
        def _():
            grad_state_out[0] = grad_state_sum[...]

    @pl.when((item == pl.num_programs(0) - 1) & (phase == 1) & (step == steps - 1))
    def _():
        gain, bias = as_row(sum_gain[...]), as_row(sum_bias[...])
        gate = jnp.broadcast_to(jnp.sum(sum_gate[...], axis=1, keepdims=True), (8, width))
        row = lax.broadcasted_iota(jnp.int32, (8, width), 0)
        vectors = jnp.where(row == 0, gain[:8], bias[:8])
        small = jnp.concatenate([vectors, gate], axis=0).astype(bf16)
        start = 0
        for block in range(experts * hidden // width):
            part = sum_in[:, block * width : (block + 1) * width].astype(bf16)
            grads_stage[:, start : start + piece, :] = part.reshape(shards, piece, width)
            start += piece
        for expert in range(experts):
            part = flip(sum_exit[:, expert * hidden : (expert + 1) * hidden]).astype(bf16)
            grads_stage[:, start : start + exit_piece, :] = part.reshape(shards, exit_piece, width)
            start += exit_piece
        part = sum_out_two[...].astype(bf16)
        grads_stage[:, start : start + piece, :] = part.reshape(shards, piece, width)
        start += piece
        for shard in range(shards):
            grads_stage[shard, start : start + 16, :] = small
        scatter_blocks(grads_stage, grads_out)


def rest_kernel(
    presence,
    tokens,
    queries_in,
    cross_in,
    first_in,
    keys_in,
    values_in,
    grad_q_in,
    grad_second_in,
    grad_state_in,
    state_t,
    state,
    *refs,
    funcs,
    item,
    shards,
    at,
    first_call,
):
    parts, refs = refs[:shards], refs[shards:]
    if not first_call:
        carry, refs = refs[3], refs[4:]
    (
        grad_tokens,
        grad_cross_state_out,
        grad_totals_out,
        sums_out,
        params,
        w_self,
        w_out_one,
        w_query,
        gain_one,
        bias_one,
        grad_self_state,
        grad_totals,
        grad_state_sum,
        sums,
    ) = refs
    step = pl.program_id(0)
    steps = pl.num_programs(0)
    width = tokens.shape[1]
    piece = width // shards
    self_part = slice(0, 3 * width)
    out_part = slice(3 * width, 4 * width)
    query_part = slice(4 * width, 5 * width)
    gain_part = slice(5 * width, 6 * width)
    bias_part = slice(6 * width, 7 * width)

    @pl.when(step == 0)
    def _():
        assemble(parts, params)
        w_query[...] = whole(params, at["query_first"], piece)
        w_out_one[...] = whole(params, at["out_first"], piece)
        w_self[:, :width] = whole(params, at["query_second"], piece)
        w_self[:, width : 2 * width] = whole(params, at["key_second"], piece)
        w_self[:, 2 * width :] = whole(params, at["value_second"], piece)
        for vector, column in zip((gain_one, bias_one), columns(params, at["small"], 2)):
            vector[...] = jnp.broadcast_to(column, vector.shape)
        sums[...] = jnp.zeros_like(sums) if first_call else carry[...]
        mask = same_head(width, width, width)
        left = jnp.where(mask, grad_state_in[0, :, :width], 0.0)
        right = jnp.where(mask, grad_state_in[0, :, width:], 0.0)
        grad_self_state[0] = left.astype(bf16)
        grad_self_state[1] = flip(left).astype(bf16)
        grad_totals[...] = jnp.broadcast_to(
            -jnp.sum(right, axis=1, keepdims=True), grad_totals.shape
        )

    first_low = first_in[0]
    keys, values = keys_in[0], values_in[0]
    grad_k = softmax_back(keys, nn(grad_self_state[0], values) + grad_totals[...]).astype(bf16)
    grad_v = nn(grad_self_state[1], keys).astype(bf16)
    three = jnp.concatenate([grad_q_in[0], grad_k, grad_v], axis=0)
    sums[:, self_part] += nt(first_low, three)
    grad_first = grad_second_in[0].astype(f32) + nn(w_self[...], three)
    grad_cross = grad_first.astype(bf16)
    sums[:, out_part] += nt(cross_in[0], grad_cross)
    share = nn(w_out_one[...], grad_cross)
    queries = queries_in[0]
    pieces = []
    for func in range(funcs):
        both = nn(state_t[func], queries)
        undo = inverse(both[width:])
        part = share * undo
        pieces.append(part.astype(bf16))
        pieces.append((part * (both[:width] * undo)).astype(bf16))
    stack = jnp.concatenate(pieces, axis=0)
    found = nt(queries, stack)

    @pl.when(step == 0)
    def _():
        grad_state_sum[...] = found

    @pl.when(step > 0)
    def _():
        grad_state_sum[...] += found

    joined = jnp.concatenate([state[func] for func in range(funcs)], axis=1)
    grad_q = softmax_back(queries, nn(joined, stack)).astype(bf16)
    rows_t = flip(tokens[...]).astype(f32)
    hat, scale = standardize(rows_t)
    normed = (hat * gain_one[...] + bias_one[...]).astype(bf16)
    sums[:, query_part] += nt(normed, grad_q)
    grad_normed = nn(w_query[...], grad_q)
    sums[:, gain_part] += lane_fold(grad_normed * hat)
    sums[:, bias_part] += lane_fold(grad_normed)
    grad_rows = grad_first + norm_back(grad_normed * gain_one[...], hat, scale)
    grad_tokens[...] = flip(grad_rows)

    @pl.when(step == steps - 1)
    def _():
        mask = same_head(width, width, width)
        for func in range(funcs):
            weight = function_weight(presence, item, func, funcs, (1, width))
            start = 2 * func * width
            left = jnp.where(mask, grad_state_sum[:, start : start + width], 0.0) * weight
            right = jnp.where(mask, grad_state_sum[:, start + width : start + 2 * width], 0.0)
            grad_cross_state_out[func] = left.astype(bf16)
            grad_totals_out[func] = jnp.broadcast_to(
                -jnp.sum(right, axis=1, keepdims=True), (width, width)
            )
        sums_out[...] = sums[...]


def points_back(points, keys_in, values_in, grad_state, grad_totals, carry, *refs, shards):
    outs = refs[:shards]
    sums, stage = refs[shards:]
    step = pl.program_id(0)
    width = points.shape[2]
    piece = width // shards
    keys, values = keys_in[0], values_in[0]
    left = grad_state[0]
    grad_keys = nn(left, values) + grad_totals[0, :, 0:1]
    grad_k = softmax_back(keys, grad_keys).astype(bf16)
    grad_v = nn(flip(left), keys).astype(bf16)
    found = nn(jnp.concatenate([grad_k, grad_v], axis=0), points[0])

    @pl.when(step == 0)
    def _():
        sums[...] = found
        gain = as_row(carry[:, 5 * width : 6 * width])
        bias = as_row(carry[:, 6 * width : 7 * width])
        row = lax.broadcasted_iota(jnp.int32, (16, width), 0)
        small = jnp.where(row == 0, gain[:16], bias[:16]).astype(bf16)
        for place in range(5):
            part = carry[:, place * width : (place + 1) * width].astype(bf16)
            stage[:, place * piece : (place + 1) * piece, :] = part.reshape(shards, piece, width)
        for shard in range(shards):
            stage[shard, 5 * piece : 5 * piece + 16, :] = small

    @pl.when(step > 0)
    def _():
        sums[...] += found

    @pl.when(step == pl.num_programs(0) - 1)
    def _():
        for place in range(2):
            start = 5 * piece + 16 + place * piece
            part = flip(sums[place * width : (place + 1) * width]).astype(bf16)
            stage[:, start : start + piece, :] = part.reshape(shards, piece, width)
        scatter_blocks(stage, outs)


def join_kernel(*refs, counts, pieces, stride):
    outs, total = refs[-1 - pieces : -1], refs[-1]
    start = 0
    for count in counts:
        group, refs = refs[:count], refs[count:]
        value = group[0][...].astype(f32)
        for part in group[1:]:
            value = value + part[...].astype(f32)
        total[start : start + value.shape[0]] = value.astype(bf16)
        start += value.shape[0]
    if start < total.shape[0]:
        total[start:] = jnp.zeros_like(total[start:])
    scatter_digit(total, outs, pieces, stride)


def scatter_digit(total, outs, pieces, stride):
    size = total.shape[0] // pieces
    digit = lax.rem(lax.div(lax.axis_index("dp"), stride), pieces)
    for place, out in enumerate(outs):
        start = pl.multiple_of(lax.rem(digit + place, pieces) * size, 16)
        out[...] = total[pl.ds(start, size)]


def gather_digit(parts, whole_array, stride):
    pieces = len(parts)
    size = parts[0].shape[0]
    digit = lax.rem(lax.div(lax.axis_index("dp"), stride), pieces)
    for place, part in enumerate(parts):
        start = pl.multiple_of(lax.rem(digit + pieces - place, pieces) * size, 16)
        whole_array[pl.ds(start, size)] = part[...]


def place_kernel(*refs, stride):
    gather_digit(refs[:-1], refs[-1], stride)


def unpack_kernel(*refs, experts, piece, exit_piece, hidden, spots, stride):
    parts, outs, (small, joined) = refs[:-17], refs[-17:-2], refs[-2:]
    width = joined.shape[1]
    gather_digit(parts, joined, stride)
    (
        gain_one,
        bias_one,
        query_one,
        key_one,
        value_one,
        out_one,
        query_two,
        key_two,
        value_two,
        out_two,
        gain_two,
        bias_two,
        enter,
        leave,
        gate,
    ) = outs
    start = spots[0]
    for expert in range(experts):
        for half in range(hidden // width):
            block = joined[start : start + piece].astype(f32)
            enter[expert, :, half * width : (half + 1) * width] = block
            start += piece
    for expert in range(experts):
        leave[expert] = joined[start : start + exit_piece].astype(f32)
        start += exit_piece
    out_two[...] = joined[start : start + piece].astype(f32)
    start += piece
    small[:16] = joined[start : start + 16].astype(f32)
    start = spots[1]
    for out in (query_two, key_two, value_two, out_one, query_one):
        out[...] = joined[start : start + piece].astype(f32)
        start += piece
    small[16:] = joined[start : start + 16].astype(f32)
    start += 16
    for out in (key_one, value_one):
        out[...] = joined[start : start + piece].astype(f32)
        start += piece
    shard = lax.axis_index("fsdp")
    turned = pltpu.roll(small[...], lax.rem(width - shard * piece, width), 1)
    gain_two[...] = turned[0:1, :piece]
    bias_two[...] = turned[1:2, :piece]
    gain_one[...] = turned[16:17, :piece]
    bias_one[...] = turned[17:18, :piece]
    for row in range(2):
        gate[:, row : row + 1] = small[pl.ds(8 + row * experts + shard, 1), 0:1]


def whole_spec(shape):
    return pl.BlockSpec(shape, lambda *_: (0,) * len(shape))


def route(size, shift, digit, stride):
    def target(i):
        own = i // stride % digit
        return i + ((own + shift) % digit - own) * stride

    return [(i, target(i)) for i in range(size)]


def spread(value, axis, size, digit, stride):
    return [value] + [
        lax.ppermute(value, axis, route(size, shift, digit, stride)) for shift in range(1, digit)
    ]


def exchange(values, axis, size, stride):
    digit = len(values)
    return [values[0]] + [
        lax.ppermute(values[shift], axis, route(size, shift, digit, stride))
        for shift in range(1, digit)
    ]


def digits(size):
    found = []
    stride = 1
    while stride < size:
        rest = size // stride
        digit = 2 if stride == 1 and rest % 2 == 0 else 4 if rest % 4 == 0 else rest
        found.append((digit, stride))
        stride *= digit
    return found or [(1, 1)]


def padded(rows, pieces):
    unit = 16 * pieces
    return -(-rows // unit) * unit


def shards_fn(
    dp,
    shards,
    tokens,
    points,
    coords,
    presence,
    counts,
    cotangent,
    gain_first,
    bias_first,
    query_first,
    key_first,
    value_first,
    out_first,
    query_second,
    key_second,
    value_second,
    out_second,
    gain_second,
    bias_second,
    expert_in,
    expert_out,
    gate_weight,
):
    count, width = tokens.shape
    items, funcs, slots, _ = points.shape
    length = count // items
    experts, piece, hidden = expert_in.shape
    exit_piece = expert_out.shape[1]
    tile = min(TILE, length)
    steps = length // tile
    inner = experts * hidden
    enter_rows = experts * piece * (hidden // width)
    limit = pltpu.CompilerParams(vmem_limit_bytes=VMEM)

    at = {}
    place = 0
    for name, size in (
        ("query_first", piece),
        ("out_first", piece),
        ("query_second", piece),
        ("key_second", piece),
        ("value_second", piece),
        ("out_second", piece),
        ("expert_in", enter_rows),
        ("expert_out", experts * exit_piece),
        ("small", 16),
    ):
        at[name] = place
        place += size
    late_rows_count = place
    early_pack, late_pack = pl.pallas_call(
        pack_kernel,
        out_shape=[
            jax.ShapeDtypeStruct((2 * piece, width), bf16),
            jax.ShapeDtypeStruct((late_rows_count, width), bf16),
        ],
        name="pack",
    )(
        key_first,
        value_first,
        query_first,
        out_first,
        query_second,
        key_second,
        value_second,
        out_second,
        expert_in,
        expert_out,
        *(
            vector.reshape(1, piece)
            for vector in (gain_first, bias_first, gain_second, bias_second)
        ),
        gate_weight,
    )
    early_parts = spread(early_pack, "fsdp", shards, shards, 1)
    late_parts = spread(late_pack, "fsdp", shards, shards, 1)
    late_specs = [whole_spec((late_rows_count, width))] * shards
    gathered = pltpu.VMEM((shards, late_rows_count, width), bf16)

    smem = pl.BlockSpec(memory_space=pltpu.SMEM)
    units = items * funcs
    flat_points = points.reshape(units, slots, width)
    state_t, state, keys_one, values_one = pl.pallas_call(
        partial(points_forward, funcs=funcs, shards=shards),
        grid=(units,),
        in_specs=[smem, smem, pl.BlockSpec((1, slots, width), lambda u: (u, 0, 0))]
        + [whole_spec((2 * piece, width))] * shards,
        out_specs=[
            pl.BlockSpec((1, 2 * width, width), lambda u: (u, 0, 0)),
            pl.BlockSpec((1, width, 2 * width), lambda u: (u, 0, 0)),
            pl.BlockSpec((1, width, slots), lambda u: (u, 0, 0)),
            pl.BlockSpec((1, width, slots), lambda u: (u, 0, 0)),
        ],
        out_shape=[
            jax.ShapeDtypeStruct((units, 2 * width, width), bf16),
            jax.ShapeDtypeStruct((units, width, 2 * width), bf16),
            jax.ShapeDtypeStruct((units, width, slots), bf16),
            jax.ShapeDtypeStruct((units, width, slots), bf16),
        ],
        scratch_shapes=[
            pltpu.VMEM((shards, 2 * piece, width), bf16),
            pltpu.VMEM((2 * width, width), bf16),
        ],
        compiler_params=limit,
        cost_estimate=cost(8),
        name="points_forward",
    )(counts, presence, flat_points, *early_parts)

    kept = jax.ShapeDtypeStruct((items * steps, width, tile), bf16)
    main_rows = enter_rows + experts * exit_piece + piece + 16

    def early(i, p, j):
        return i * steps + jnp.where(p == 0, j, steps - 1)

    def late(i, p, j):
        return i * steps + jnp.where(p == 0, 0, j)

    early_keep = pl.BlockSpec((1, width, tile), lambda i, p, j: (early(i, p, j), 0, 0))
    late_keep = pl.BlockSpec((1, width, tile), lambda i, p, j: (late(i, p, j), 0, 0))
    late_rows = pl.BlockSpec((tile, width), lambda i, p, j: (late(i, p, j), 0))
    (
        result,
        queries_one,
        cross,
        first,
        keys_two,
        values_two,
        grad_q_two,
        grad_second,
        grad_state_two,
        *main_grads,
    ) = pl.pallas_call(
        partial(main_kernel, funcs=funcs, experts=experts, shards=shards, at=at),
        grid=(items, 2, steps),
        in_specs=[
            pl.BlockSpec((tile, width), lambda i, p, j: (early(i, p, j), 0)),
            late_rows,
            pl.BlockSpec((2, tile), lambda i, p, j: (0, late(i, p, j))),
            pl.BlockSpec((funcs, 2 * width, width), lambda i, p, j: (i, 0, 0)),
        ]
        + late_specs,
        out_specs=[
            late_rows,
            early_keep,
            early_keep,
            early_keep,
            early_keep,
            early_keep,
            late_keep,
            late_keep,
            pl.BlockSpec((1, width, 2 * width), lambda i, p, j: (i, 0, 0)),
        ]
        + [whole_spec((main_rows, width))] * shards,
        out_shape=[
            jax.ShapeDtypeStruct((count, width), bf16),
            kept,
            kept,
            kept,
            kept,
            kept,
            kept,
            kept,
            jax.ShapeDtypeStruct((items, width, 2 * width), f32),
        ]
        + [jax.ShapeDtypeStruct((main_rows, width), bf16)] * shards,
        scratch_shapes=[
            gathered,
            pltpu.VMEM((shards, main_rows, width), bf16),
            pltpu.VMEM((steps, width, tile), f32),
            pltpu.VMEM((steps, width, tile), bf16),
            pltpu.VMEM((width, 2 * width), f32),
            pltpu.VMEM((2 * width, width), bf16),
            pltpu.VMEM((width, 2 * width), bf16),
            pltpu.VMEM((width, 2 * width), f32),
            pltpu.VMEM((width, width), bf16),
            pltpu.VMEM((width, width), bf16),
            pltpu.VMEM((3 * width, width), bf16),
            pltpu.VMEM((width, width), bf16),
            pltpu.VMEM((width, width), bf16),
            pltpu.VMEM((inner, width), bf16),
            pltpu.VMEM((width, inner), bf16),
            pltpu.VMEM((inner, width), bf16),
            pltpu.VMEM((width, inner), bf16),
            pltpu.VMEM((width, tile), f32),
            pltpu.VMEM((width, tile), f32),
            pltpu.VMEM((width, tile), f32),
            pltpu.VMEM((width, tile), f32),
            pltpu.VMEM((inner, tile), bf16),
            pltpu.VMEM((inner, tile), bf16),
            pltpu.VMEM((width, inner), f32),
            pltpu.VMEM((width, inner), f32),
            pltpu.VMEM((width, width), f32),
            pltpu.VMEM((width, width), f32),
            pltpu.VMEM((width, width), f32),
            pltpu.VMEM((2 * experts, tile), f32),
        ],
        compiler_params=limit,
        cost_estimate=cost(80),
        name="main",
    )(tokens, cotangent, coords, state_t, *late_parts)

    rest_rows = 7 * piece + 16

    def rest_call(item, earlier):
        first_call = item == 0
        keep_spec = pl.BlockSpec((1, width, tile), lambda j: (item * steps + j, 0, 0))
        row_spec = pl.BlockSpec((tile, width), lambda j: (item * steps + j, 0))
        unit_spec = pl.BlockSpec((funcs, width, width), lambda j: (item, 0, 0))
        anywhere = pl.BlockSpec(memory_space=pl.ANY)
        in_specs = [
            smem,
            row_spec,
            keep_spec,
            keep_spec,
            keep_spec,
            keep_spec,
            keep_spec,
            keep_spec,
            keep_spec,
            pl.BlockSpec((1, width, 2 * width), lambda j: (item, 0, 0)),
            pl.BlockSpec((funcs, 2 * width, width), lambda j: (item, 0, 0)),
            pl.BlockSpec((funcs, width, 2 * width), lambda j: (item, 0, 0)),
        ] + late_specs
        operands = [
            presence,
            tokens,
            queries_one,
            cross,
            first,
            keys_two,
            values_two,
            grad_q_two,
            grad_second,
            grad_state_two,
            state_t,
            state,
            *late_parts,
        ]
        aliases = {}
        if not first_call:
            aliases = {len(operands) + k: k for k in range(3)}
            in_specs += [anywhere] * 3 + [whole_spec((width, 7 * width))]
            operands += earlier
        out_specs = [row_spec, unit_spec, unit_spec, whole_spec((width, 7 * width))]
        out_shape = [
            jax.ShapeDtypeStruct((count, width), f32),
            jax.ShapeDtypeStruct((units, width, width), bf16),
            jax.ShapeDtypeStruct((units, width, width), f32),
            jax.ShapeDtypeStruct((width, 7 * width), f32),
        ]
        return pl.pallas_call(
            partial(
                rest_kernel,
                funcs=funcs,
                item=item,
                shards=shards,
                at=at,
                first_call=first_call,
            ),
            grid=(steps,),
            in_specs=in_specs,
            out_specs=out_specs,
            out_shape=out_shape,
            input_output_aliases=aliases,
            scratch_shapes=[
                gathered,
                pltpu.VMEM((width, 3 * width), bf16),
                pltpu.VMEM((width, width), bf16),
                pltpu.VMEM((width, width), bf16),
                pltpu.VMEM((width, tile), f32),
                pltpu.VMEM((width, tile), f32),
                pltpu.VMEM((2, width, width), bf16),
                pltpu.VMEM((width, tile), f32),
                pltpu.VMEM((width, 2 * funcs * width), f32),
                pltpu.VMEM((width, 7 * width), f32),
            ],
            compiler_params=limit,
            cost_estimate=cost(18),
            name="rest",
        )(*operands)

    main_got = exchange(main_grads, "fsdp", shards, 1)
    found = None
    for item in range(items):
        found = rest_call(item, found)
    grad_tokens, grad_state_one, grad_totals_one, carry = found

    rest_grads = pl.pallas_call(
        partial(points_back, shards=shards),
        grid=(units,),
        in_specs=[
            pl.BlockSpec((1, slots, width), lambda u: (u, 0, 0)),
            pl.BlockSpec((1, width, slots), lambda u: (u, 0, 0)),
            pl.BlockSpec((1, width, slots), lambda u: (u, 0, 0)),
            pl.BlockSpec((1, width, width), lambda u: (u, 0, 0)),
            pl.BlockSpec((1, width, width), lambda u: (u, 0, 0)),
            whole_spec((width, 7 * width)),
        ],
        out_specs=[whole_spec((rest_rows, width))] * shards,
        out_shape=[jax.ShapeDtypeStruct((rest_rows, width), bf16)] * shards,
        scratch_shapes=[
            pltpu.VMEM((2 * width, width), f32),
            pltpu.VMEM((shards, rest_rows, width), bf16),
        ],
        compiler_params=limit,
        cost_estimate=cost(7),
        name="points_back",
    )(flat_points, keys_one, values_one, grad_state_one, grad_totals_one, carry)
    rest_got = exchange(rest_grads, "fsdp", shards, 1)

    spots = (0, main_rows)
    all_rows = padded(main_rows + rest_rows, dp)
    parts, counts = [*main_got, *rest_got], (shards, shards)
    rows_left = all_rows
    levels = digits(dp)
    for digit, stride in levels:
        pieces = pl.pallas_call(
            partial(join_kernel, counts=counts, pieces=digit, stride=stride),
            out_shape=[jax.ShapeDtypeStruct((rows_left // digit, width), bf16)] * digit,
            scratch_shapes=[pltpu.VMEM((rows_left, width), bf16)],
            name="join",
        )(*parts)
        parts = exchange(pieces, "dp", dp, stride)
        counts = (digit,)
        rows_left //= digit
    (own,) = pl.pallas_call(
        partial(join_kernel, counts=counts, pieces=1, stride=1),
        out_shape=[jax.ShapeDtypeStruct((rows_left, width), bf16)],
        scratch_shapes=[pltpu.VMEM((rows_left, width), bf16)],
        name="join",
    )(*parts)
    for level, (digit, stride) in reversed(list(enumerate(levels))):
        parts = spread(own, "dp", dp, digit, stride)
        rows_left *= digit
        if level:
            own = pl.pallas_call(
                partial(place_kernel, stride=stride),
                out_shape=jax.ShapeDtypeStruct((rows_left, width), bf16),
                name="place",
            )(*parts)

    matrix = jax.ShapeDtypeStruct((piece, width), f32)
    vector = jax.ShapeDtypeStruct((1, piece), f32)
    outs = pl.pallas_call(
        partial(
            unpack_kernel,
            experts=experts,
            piece=piece,
            exit_piece=exit_piece,
            hidden=hidden,
            spots=spots,
            stride=levels[0][1],
        ),
        out_shape=[vector] * 2
        + [matrix] * 8
        + [vector] * 2
        + [
            jax.ShapeDtypeStruct(expert_in.shape, f32),
            jax.ShapeDtypeStruct(expert_out.shape, f32),
            jax.ShapeDtypeStruct((1, 2), f32),
        ],
        scratch_shapes=[
            pltpu.VMEM((32, width), f32),
            pltpu.VMEM((all_rows, width), bf16),
        ],
        name="unpack",
    )(*parts)
    outs = [out.reshape(piece) if out.shape == (1, piece) else out for out in outs]
    return (result, grad_tokens, *outs[:-1], outs[-1].reshape(gate_weight.shape))


def solution(mesh):
    rows = P(("dp", "fsdp"), None)
    matrix = P("fsdp", None)
    vector = P("fsdp")
    expert = P(None, "fsdp", None)
    parameters = (
        (vector, vector)
        + (matrix,) * 8
        + (vector, vector, expert, expert, P(None, "fsdp"))
    )
    return jax.shard_map(
        partial(shards_fn, mesh.shape["dp"], mesh.shape["fsdp"]),
        mesh=mesh,
        in_specs=(
            rows,
            P(("dp", "fsdp"), None, None, None),
            P(None, ("dp", "fsdp")),
            rows,
            rows,
            rows,
        )
        + parameters,
        out_specs=(rows, rows) + parameters,
        check_vma=False,
    )
```

```python
from functools import partial

import jax
import jax.numpy as jnp
from jax import lax
from jax.experimental import pallas as pl
from jax.experimental.pallas import tpu as pltpu
from jax.sharding import PartitionSpec as P


HEADS = 8
eps = 1e-05
f32 = jnp.float32
bf16 = jnp.bfloat16
TILE = 1024
VMEM = 56 * 1024 * 1024


def cost(microseconds):
    return pl.CostEstimate(flops=microseconds * 10**9, bytes_accessed=10**6, transcendentals=0)


def nn(left, right):
    return jnp.dot(left, right, preferred_element_type=f32)


def nt(left, right):
    return lax.dot_general(left, right, (((1,), (1,)), ((), ())), preferred_element_type=f32)


def flip(value):
    return value.T


def inverse(value):
    return pl.reciprocal(value, approx=True)


def head_softmax(value):
    width, rows = value.shape
    split = value.reshape(HEADS, width // HEADS, rows)
    raised = jnp.exp(split - jnp.max(split, axis=1, keepdims=True))
    return (raised * inverse(jnp.sum(raised, axis=1, keepdims=True))).reshape(width, rows)


def softmax_back(probs, grad):
    width, rows = grad.shape
    probs = probs.astype(f32).reshape(HEADS, width // HEADS, rows)
    grad = grad.reshape(HEADS, width // HEADS, rows)
    inner = jnp.sum(probs * grad, axis=1, keepdims=True)
    return (probs * (grad - inner)).reshape(width, rows)


def standardize(value):
    centre = value - jnp.mean(value, axis=0, keepdims=True)
    scale = lax.rsqrt(jnp.mean(centre * centre, axis=0, keepdims=True) + eps)
    return centre * scale, scale


def norm_back(grad, hat, scale):
    return scale * (
        grad
        - jnp.mean(grad, axis=0, keepdims=True)
        - hat * jnp.mean(grad * hat, axis=0, keepdims=True)
    )


def same_head(rows, columns, width):
    head = width // HEADS
    row = lax.rem(lax.broadcasted_iota(jnp.int32, (rows, columns), 0), width)
    column = lax.rem(lax.broadcasted_iota(jnp.int32, (rows, columns), 1), width)
    return lax.div(row, head) == lax.div(column, head)


def assemble(parts, gathered):
    shards = len(parts)
    here = lax.axis_index("fsdp")
    for place, part in enumerate(parts):
        gathered[lax.rem(here + shards - place, shards)] = part[...]


def columns(gathered, start, count):
    shards, _, width = gathered.shape
    piece = width // shards
    small = [gathered[shard, start : start + 16, :].astype(f32) for shard in range(shards)]
    joined = jnp.concatenate([part[:, :piece] for part in small], axis=1)
    return [
        flip(jnp.broadcast_to(joined[place : place + 1], (width, width)))[:, 0:1]
        for place in range(count)
    ]


def lane_fold(value):
    width = value.shape[0]
    total = value[:, :width]
    for start in range(width, value.shape[1], width):
        total = total + value[:, start : start + width]
    return total


def as_row(value):
    width = value.shape[0]
    return flip(jnp.broadcast_to(jnp.sum(value, axis=1, keepdims=True), (width, width)))


def scatter_blocks(stage, outs):
    shards = len(outs)
    here = lax.axis_index("fsdp")
    for place, out in enumerate(outs):
        out[...] = stage[lax.rem(here + place, shards)]


def whole(gathered, start, rows):
    shards = gathered.shape[0]
    return gathered[:, start : start + rows, :].reshape(shards * rows, gathered.shape[2])


def function_weight(presence, item, func, funcs, shape):
    total = presence[item, 0]
    for other in range(1, funcs):
        total = total + presence[item, other]
    own = jnp.full(shape, presence[item, func], jnp.int32).astype(f32)
    return own / jnp.full(shape, total, jnp.int32).astype(f32)


def pack_kernel(*refs):
    weights, vectors, gate = refs[:10], refs[10:14], refs[14]
    early, late = refs[15:]
    keys, values, query, out, query_two, key_two, value_two, out_two, enter, leave = weights
    start = 0
    for weight in (keys, values):
        early[start : start + weight.shape[0]] = weight[...]
        start += weight.shape[0]
    start = 0
    for weight in (query, out, query_two, key_two, value_two, out_two):
        late[start : start + weight.shape[0]] = weight[...]
        start += weight.shape[0]
    experts, piece, hidden = enter.shape
    width = late.shape[1]
    for expert in range(experts):
        for half in range(hidden // width):
            late[start : start + piece] = enter[expert, :, half * width : (half + 1) * width]
            start += piece
    for expert in range(experts):
        late[start : start + leave.shape[1]] = leave[expert]
        start += leave.shape[1]
    rest = jnp.zeros((1, width - piece), f32)
    rows = [
        jnp.concatenate([vector[...].astype(f32), rest], axis=1) for vector in vectors
    ]
    rows.append(jnp.zeros((4, width), f32))
    for row in range(2):
        rows.append(jnp.broadcast_to(gate[row : row + 1, 0:1].astype(f32), (1, width)))
    rows.append(jnp.zeros((6, width), f32))
    late[start : start + 16] = jnp.concatenate(rows, axis=0).astype(bf16)


def points_forward(counts, presence, points, *refs, funcs, shards):
    parts = refs[:shards]
    state_t, state, keys_out, values_out, gathered, weight = refs[shards:]
    step = pl.program_id(0)
    item, func = lax.div(step, funcs), lax.rem(step, funcs)
    width = points.shape[2]
    slots = points.shape[1]
    piece = width // shards

    @pl.when(step == 0)
    def _():
        assemble(parts, gathered)
        weight[:width] = flip(whole(gathered, 0, piece))
        weight[width:] = flip(whole(gathered, piece, piece))

    both = nt(weight[...], points[0])
    probs = head_softmax(both[:width])
    slot = lax.broadcasted_iota(jnp.int32, (1, slots), 1)
    keys = jnp.where(slot < counts[item, func], probs, 0.0).astype(bf16)
    values = both[width:].astype(bf16)
    keys_out[0] = keys
    values_out[0] = values
    extended = jnp.concatenate([values, jnp.ones_like(values)], axis=0)
    share = function_weight(presence, item, func, funcs, (1, width))
    mask = same_head(width, width, width)
    summed = nt(keys, extended)
    left = jnp.where(mask, summed[:, :width], 0.0) * share
    right = jnp.where(mask, summed[:, width:], 0.0)
    state[0, :, :width] = left.astype(bf16)
    state[0, :, width:] = (-right).astype(bf16)
    state_t[0, :width] = flip(left).astype(bf16)
    state_t[0, width:] = flip(right).astype(bf16)


def main_kernel(tokens, cotangent, coords, state_t, *refs, funcs, experts, shards, at):
    parts, outs, scratch = refs[:shards], refs[shards : 2 * shards + 9], refs[2 * shards + 9 :]
    (
        result,
        queries_out,
        cross_out,
        first_out,
        keys_out,
        values_out,
        grad_q_out,
        grad_second_out,
        grad_state_out,
    ) = outs[:9]
    grads_out = outs[9:]
    (
        params,
        grads_stage,
        first_keep,
        query_keep,
        state_sum,
        self_t,
        self_state,
        grad_state_sum,
        w_query,
        w_out_one,
        w_self,
        w_out_two_t,
        w_out_two,
        w_in_t,
        w_in,
        w_exit,
        w_exit_t,
        gain_one,
        bias_one,
        gain_two,
        bias_two,
        hidden_keep,
        inner_keep,
        sum_in,
        sum_exit,
        sum_out_two,
        sum_gain,
        sum_bias,
        sum_gate,
    ) = scratch
    item = pl.program_id(0)
    phase = pl.program_id(1)
    step = pl.program_id(2)
    steps = pl.num_programs(2)
    width = tokens.shape[1]
    rows = tokens.shape[0]
    piece = width // shards
    hidden = w_in.shape[1] // experts
    exit_piece = hidden // shards

    @pl.when((item == 0) & (phase == 0) & (step == 0))
    def _():
        assemble(parts, params)
        w_query[...] = flip(whole(params, at["query_first"], piece))
        w_out_one[...] = flip(whole(params, at["out_first"], piece))
        w_self[:width] = flip(whole(params, at["query_second"], piece))
        w_self[width : 2 * width] = flip(whole(params, at["key_second"], piece))
        w_self[2 * width :] = flip(whole(params, at["value_second"], piece))
        out_two = whole(params, at["out_second"], piece)
        w_out_two[...] = out_two
        w_out_two_t[...] = flip(out_two)
        for block in range(experts * hidden // width):
            part = whole(params, at["expert_in"] + block * piece, piece)
            w_in[:, block * width : (block + 1) * width] = part
            w_in_t[block * width : (block + 1) * width] = flip(part)
        for expert in range(experts):
            part = whole(params, at["expert_out"] + expert * exit_piece, exit_piece)
            w_exit[expert * hidden : (expert + 1) * hidden] = part
            w_exit_t[:, expert * hidden : (expert + 1) * hidden] = flip(part)
        found = columns(params, at["small"], 4)
        for vector, column in zip((gain_one, bias_one, gain_two, bias_two), found):
            vector[...] = jnp.broadcast_to(column, vector.shape)
        sum_in[...] = jnp.zeros_like(sum_in)
        sum_exit[...] = jnp.zeros_like(sum_exit)
        sum_out_two[...] = jnp.zeros_like(sum_out_two)
        sum_gain[...] = jnp.zeros_like(sum_gain)
        sum_bias[...] = jnp.zeros_like(sum_bias)
        sum_gate[...] = jnp.zeros_like(sum_gate)

    @pl.when(phase == 0)
    def _():
        rows_t = flip(tokens[...]).astype(f32)
        hat, _scale = standardize(rows_t)
        normed = (hat * gain_one[...] + bias_one[...]).astype(bf16)
        queries = head_softmax(nn(w_query[...], normed)).astype(bf16)
        queries_out[0] = queries
        mixed = jnp.zeros((width, rows), f32)
        for func in range(funcs):
            both = nn(state_t[func], queries)
            mixed = mixed + both[:width] * inverse(both[width:])
        cross = mixed.astype(bf16)
        cross_out[0] = cross
        first = rows_t + nn(w_out_one[...], cross)
        first_keep[step] = first
        first_low = first.astype(bf16)
        first_out[0] = first_low
        three = nn(w_self[...], first_low)
        query_keep[step] = head_softmax(three[:width]).astype(bf16)
        keys = head_softmax(three[width : 2 * width]).astype(bf16)
        values = three[2 * width :].astype(bf16)
        keys_out[0] = keys
        values_out[0] = values
        extended = jnp.concatenate([values, jnp.ones_like(values)], axis=0)
        found = nt(keys, extended)

        @pl.when(step == 0)
        def _():
            state_sum[...] = found

        @pl.when(step > 0)
        def _():
            state_sum[...] += found

        @pl.when(step == steps - 1)
        def _():
            mask = same_head(width, width, width)
            left = jnp.where(mask, state_sum[:, :width], 0.0)
            right = jnp.where(mask, state_sum[:, width:], 0.0)
            self_state[:, :width] = left.astype(bf16)
            self_state[:, width:] = (-right).astype(bf16)
            self_t[:width] = flip(left).astype(bf16)
            self_t[width:] = flip(right).astype(bf16)

    @pl.when(phase == 1)
    def _():
        queries = query_keep[step]
        both = nn(self_t[...], queries)
        undo = inverse(both[width:])
        own = both[:width] * undo
        own_low = own.astype(bf16)
        second = first_keep[step] + nn(w_out_two_t[...], own_low)
        hat, scale = standardize(second)
        normed = (hat * gain_two[...] + bias_two[...]).astype(bf16)
        grad = flip(cotangent[...])
        across, down = coords[0:1, :], coords[1:2, :]
        logits = []
        for expert in range(experts):
            pair = params[expert, at["small"] : at["small"] + 16, 0:1].astype(f32)
            logits.append(across * pair[8:9] + down * pair[9:10])
        peak = logits[0]
        for logit in logits[1:]:
            peak = jnp.maximum(peak, logit)
        raised = [jnp.exp(logit - peak) for logit in logits]
        total = raised[0]
        for other in raised[1:]:
            total = total + other
        gates = [other / total for other in raised]
        grad_gates = []
        for expert in range(experts):
            span = slice(expert * hidden, (expert + 1) * hidden)
            inner = nn(w_in_t[span], normed)
            back = nn(w_exit[span], grad)
            square = inner * inner
            tanh = jnp.tanh(inner * (0.7978845608028654 + 0.035677408136300125 * square))
            half = 0.5 + 0.5 * tanh
            active = inner * half
            grad_gates.append(jnp.sum(active * back, axis=0, keepdims=True))
            hidden_keep[span] = (active * gates[expert]).astype(bf16)
            slope = half + active * (1.0 - half) * (
                1.5957691216057308 + 0.21406444881780074 * square
            )
            inner_keep[span] = (slope * (back * gates[expert])).astype(bf16)
        total = second + nn(w_exit_t[...], hidden_keep[...])
        result[...] = flip(total.astype(bf16))
        grad_normed = nn(w_in[...], inner_keep[...])
        sum_exit[...] += nt(grad, hidden_keep[...])
        sum_in[...] += nt(normed, inner_keep[...])
        mean_gate = gates[0] * grad_gates[0]
        for expert in range(1, experts):
            mean_gate = mean_gate + gates[expert] * grad_gates[expert]
        for expert in range(experts):
            change = gates[expert] * (grad_gates[expert] - mean_gate)
            sum_gate[expert : expert + 1] += across * change
            sum_gate[experts + expert : experts + expert + 1] += down * change
        sum_gain[...] += lane_fold(grad_normed * hat)
        sum_bias[...] += lane_fold(grad_normed)
        grad_second = grad.astype(f32) + norm_back(grad_normed * gain_two[...], hat, scale)
        grad_second_out[0] = grad_second.astype(bf16)
        grad_own = grad_second.astype(bf16)
        sum_out_two[...] += nt(own_low, grad_own)
        share = nn(w_out_two[...], grad_own) * undo
        pair = jnp.concatenate([share.astype(bf16), (share * own).astype(bf16)], axis=0)
        grad_q = nn(self_state[...], pair)
        found = nt(queries, pair)

        @pl.when(step == 0)
        def _():
            grad_state_sum[...] = found

        @pl.when(step > 0)
        def _():
            grad_state_sum[...] += found

        grad_q_out[0] = softmax_back(queries, grad_q).astype(bf16)

        @pl.when(step == steps - 1)
        def _():
            grad_state_out[0] = grad_state_sum[...]

    @pl.when((item == pl.num_programs(0) - 1) & (phase == 1) & (step == steps - 1))
    def _():
        gain, bias = as_row(sum_gain[...]), as_row(sum_bias[...])
        gate = jnp.broadcast_to(jnp.sum(sum_gate[...], axis=1, keepdims=True), (8, width))
        row = lax.broadcasted_iota(jnp.int32, (8, width), 0)
        vectors = jnp.where(row == 0, gain[:8], bias[:8])
        small = jnp.concatenate([vectors, gate], axis=0).astype(bf16)
        start = 0
        for block in range(experts * hidden // width):
            part = sum_in[:, block * width : (block + 1) * width].astype(bf16)
            grads_stage[:, start : start + piece, :] = part.reshape(shards, piece, width)
            start += piece
        for expert in range(experts):
            part = flip(sum_exit[:, expert * hidden : (expert + 1) * hidden]).astype(bf16)
            grads_stage[:, start : start + exit_piece, :] = part.reshape(shards, exit_piece, width)
            start += exit_piece
        part = sum_out_two[...].astype(bf16)
        grads_stage[:, start : start + piece, :] = part.reshape(shards, piece, width)
        start += piece
        for shard in range(shards):
            grads_stage[shard, start : start + 16, :] = small
        scatter_blocks(grads_stage, grads_out)


def rest_kernel(
    presence,
    tokens,
    queries_in,
    cross_in,
    first_in,
    keys_in,
    values_in,
    grad_q_in,
    grad_second_in,
    grad_state_in,
    state_t,
    state,
    *refs,
    funcs,
    item,
    shards,
    at,
    first_call,
):
    parts, refs = refs[:shards], refs[shards:]
    if not first_call:
        carry, refs = refs[3], refs[5:]
    (
        grad_tokens,
        grad_cross_state_out,
        grad_totals_out,
        sums_out,
        params,
        w_self,
        w_out_one,
        w_query,
        gain_one,
        bias_one,
        grad_self_state,
        grad_totals,
        grad_state_sum,
        sums,
    ) = refs
    step = pl.program_id(0)
    steps = pl.num_programs(0)
    width = tokens.shape[1]
    piece = width // shards
    self_part = slice(0, 3 * width)
    out_part = slice(3 * width, 4 * width)
    query_part = slice(4 * width, 5 * width)
    gain_part = slice(5 * width, 6 * width)
    bias_part = slice(6 * width, 7 * width)

    @pl.when(step == 0)
    def _():
        assemble(parts, params)
        w_query[...] = whole(params, at["query_first"], piece)
        w_out_one[...] = whole(params, at["out_first"], piece)
        w_self[:, :width] = whole(params, at["query_second"], piece)
        w_self[:, width : 2 * width] = whole(params, at["key_second"], piece)
        w_self[:, 2 * width :] = whole(params, at["value_second"], piece)
        for vector, column in zip((gain_one, bias_one), columns(params, at["small"], 2)):
            vector[...] = jnp.broadcast_to(column, vector.shape)
        sums[...] = jnp.zeros_like(sums) if first_call else carry[...]
        mask = same_head(width, width, width)
        left = jnp.where(mask, grad_state_in[0, :, :width], 0.0)
        right = jnp.where(mask, grad_state_in[0, :, width:], 0.0)
        grad_self_state[0] = left.astype(bf16)
        grad_self_state[1] = flip(left).astype(bf16)
        grad_totals[...] = jnp.broadcast_to(
            -jnp.sum(right, axis=1, keepdims=True), grad_totals.shape
        )

    first_low = first_in[0]
    keys, values = keys_in[0], values_in[0]
    grad_k = softmax_back(keys, nn(grad_self_state[0], values) + grad_totals[...]).astype(bf16)
    grad_v = nn(grad_self_state[1], keys).astype(bf16)
    three = jnp.concatenate([grad_q_in[0], grad_k, grad_v], axis=0)
    sums[:, self_part] += nt(first_low, three)
    grad_first = grad_second_in[0].astype(f32) + nn(w_self[...], three)
    grad_cross = grad_first.astype(bf16)
    sums[:, out_part] += nt(cross_in[0], grad_cross)
    share = nn(w_out_one[...], grad_cross)
    queries = queries_in[0]
    pieces = []
    for func in range(funcs):
        both = nn(state_t[func], queries)
        undo = inverse(both[width:])
        part = share * undo
        pieces.append(part.astype(bf16))
        pieces.append((part * (both[:width] * undo)).astype(bf16))
    stack = jnp.concatenate(pieces, axis=0)
    found = nt(queries, stack)

    @pl.when(step == 0)
    def _():
        grad_state_sum[...] = found

    @pl.when(step > 0)
    def _():
        grad_state_sum[...] += found

    joined = jnp.concatenate([state[func] for func in range(funcs)], axis=1)
    grad_q = softmax_back(queries, nn(joined, stack)).astype(bf16)
    rows_t = flip(tokens[...]).astype(f32)
    hat, scale = standardize(rows_t)
    normed = (hat * gain_one[...] + bias_one[...]).astype(bf16)
    sums[:, query_part] += nt(normed, grad_q)
    grad_normed = nn(w_query[...], grad_q)
    sums[:, gain_part] += lane_fold(grad_normed * hat)
    sums[:, bias_part] += lane_fold(grad_normed)
    grad_rows = grad_first + norm_back(grad_normed * gain_one[...], hat, scale)
    grad_tokens[...] = flip(grad_rows)

    @pl.when(step == steps - 1)
    def _():
        mask = same_head(width, width, width)
        for func in range(funcs):
            weight = function_weight(presence, item, func, funcs, (1, width))
            start = 2 * func * width
            left = jnp.where(mask, grad_state_sum[:, start : start + width], 0.0) * weight
            right = jnp.where(mask, grad_state_sum[:, start + width : start + 2 * width], 0.0)
            grad_cross_state_out[func] = left.astype(bf16)
            grad_totals_out[func] = jnp.broadcast_to(
                -jnp.sum(right, axis=1, keepdims=True), (width, width)
            )
        sums_out[...] = sums[...]


def points_back(points, keys_in, values_in, grad_state, grad_totals, carry, *refs, shards):
    outs = refs[:shards]
    sums, stage = refs[shards:]
    step = pl.program_id(0)
    width = points.shape[2]
    piece = width // shards
    keys, values = keys_in[0], values_in[0]
    left = grad_state[0]
    grad_keys = nn(left, values) + grad_totals[0, :, 0:1]
    grad_k = softmax_back(keys, grad_keys).astype(bf16)
    grad_v = nn(flip(left), keys).astype(bf16)
    found = nn(jnp.concatenate([grad_k, grad_v], axis=0), points[0])

    @pl.when(step == 0)
    def _():
        sums[...] = found
        gain = as_row(carry[:, 5 * width : 6 * width])
        bias = as_row(carry[:, 6 * width : 7 * width])
        row = lax.broadcasted_iota(jnp.int32, (16, width), 0)
        small = jnp.where(row == 0, gain[:16], bias[:16]).astype(bf16)
        for place in range(5):
            part = carry[:, place * width : (place + 1) * width].astype(bf16)
            stage[:, place * piece : (place + 1) * piece, :] = part.reshape(shards, piece, width)
        for shard in range(shards):
            stage[shard, 5 * piece : 5 * piece + 16, :] = small

    @pl.when(step > 0)
    def _():
        sums[...] += found

    @pl.when(step == pl.num_programs(0) - 1)
    def _():
        for place in range(2):
            start = 5 * piece + 16 + place * piece
            part = flip(sums[place * width : (place + 1) * width]).astype(bf16)
            stage[:, start : start + piece, :] = part.reshape(shards, piece, width)
        scatter_blocks(stage, outs)


def total_of(parts):
    value = parts[0][...].astype(f32)
    for part in parts[1:]:
        value = value + part[...].astype(f32)
    return value


def sum_kernel(*refs):
    refs[-1][...] = total_of(refs[:-1]).astype(bf16)


def unpack_kernel(main, *refs, experts, piece, exit_piece, hidden):
    parts, outs, (small, rest) = refs[:-17], refs[-17:-2], refs[-2:]
    width = main.shape[1]
    rest[...] = total_of(parts)
    (
        gain_one,
        bias_one,
        query_one,
        key_one,
        value_one,
        out_one,
        query_two,
        key_two,
        value_two,
        out_two,
        gain_two,
        bias_two,
        enter,
        leave,
        gate,
    ) = outs
    start = 0
    for expert in range(experts):
        for half in range(hidden // width):
            block = main[start : start + piece].astype(f32)
            enter[expert, :, half * width : (half + 1) * width] = block
            start += piece
    for expert in range(experts):
        leave[expert] = main[start : start + exit_piece].astype(f32)
        start += exit_piece
    out_two[...] = main[start : start + piece].astype(f32)
    start += piece
    small[:16] = main[start : start + 16].astype(f32)
    start = 0
    for out in (query_two, key_two, value_two, out_one, query_one):
        out[...] = rest[start : start + piece]
        start += piece
    small[16:] = rest[start : start + 16]
    start += 16
    for out in (key_one, value_one):
        out[...] = rest[start : start + piece]
        start += piece
    shard = lax.axis_index("fsdp")
    turned = pltpu.roll(small[...], lax.rem(width - shard * piece, width), 1)
    gain_two[...] = turned[0:1, :piece]
    bias_two[...] = turned[1:2, :piece]
    gain_one[...] = turned[16:17, :piece]
    bias_one[...] = turned[17:18, :piece]
    for row in range(2):
        gate[:, row : row + 1] = small[pl.ds(8 + row * experts + shard, 1), 0:1]


def whole_spec(shape):
    return pl.BlockSpec(shape, lambda *_: (0,) * len(shape))


def route(size, shift, digit, stride):
    def target(i):
        own = i // stride % digit
        return i + ((own + shift) % digit - own) * stride

    return [(i, target(i)) for i in range(size)]


def spread(value, axis, size, digit, stride):
    return [value] + [
        lax.ppermute(value, axis, route(size, shift, digit, stride)) for shift in range(1, digit)
    ]


def exchange(values, axis, size, stride):
    digit = len(values)
    return [values[0]] + [
        lax.ppermute(values[shift], axis, route(size, shift, digit, stride))
        for shift in range(1, digit)
    ]


def digits(size):
    found = []
    stride = 1
    while stride < size:
        rest = size // stride
        digit = 2 if stride == 1 and rest % 2 == 0 else 4 if rest % 4 == 0 else rest
        found.append((digit, stride))
        stride *= digit
    return found or [(1, 1)]


def sum_parts(parts, name):
    return pl.pallas_call(
        sum_kernel, out_shape=jax.ShapeDtypeStruct(parts[0].shape, bf16), name=name
    )(*parts)


def shards_fn(
    dp,
    shards,
    tokens,
    points,
    coords,
    presence,
    counts,
    cotangent,
    gain_first,
    bias_first,
    query_first,
    key_first,
    value_first,
    out_first,
    query_second,
    key_second,
    value_second,
    out_second,
    gain_second,
    bias_second,
    expert_in,
    expert_out,
    gate_weight,
):
    count, width = tokens.shape
    items, funcs, slots, _ = points.shape
    length = count // items
    experts, piece, hidden = expert_in.shape
    exit_piece = expert_out.shape[1]
    tile = min(TILE, length)
    steps = length // tile
    inner = experts * hidden
    enter_rows = experts * piece * (hidden // width)
    limit = pltpu.CompilerParams(vmem_limit_bytes=VMEM)

    at = {}
    place = 0
    for name, size in (
        ("query_first", piece),
        ("out_first", piece),
        ("query_second", piece),
        ("key_second", piece),
        ("value_second", piece),
        ("out_second", piece),
        ("expert_in", enter_rows),
        ("expert_out", experts * exit_piece),
        ("small", 16),
    ):
        at[name] = place
        place += size
    late_rows_count = place
    early_pack, late_pack = pl.pallas_call(
        pack_kernel,
        out_shape=[
            jax.ShapeDtypeStruct((2 * piece, width), bf16),
            jax.ShapeDtypeStruct((late_rows_count, width), bf16),
        ],
        name="pack",
    )(
        key_first,
        value_first,
        query_first,
        out_first,
        query_second,
        key_second,
        value_second,
        out_second,
        expert_in,
        expert_out,
        *(
            vector.reshape(1, piece)
            for vector in (gain_first, bias_first, gain_second, bias_second)
        ),
        gate_weight,
    )
    early_parts = spread(early_pack, "fsdp", shards, shards, 1)
    late_parts = spread(late_pack, "fsdp", shards, shards, 1)
    late_specs = [whole_spec((late_rows_count, width))] * shards
    gathered = pltpu.VMEM((shards, late_rows_count, width), bf16)

    smem = pl.BlockSpec(memory_space=pltpu.SMEM)
    units = items * funcs
    flat_points = points.reshape(units, slots, width)
    state_t, state, keys_one, values_one = pl.pallas_call(
        partial(points_forward, funcs=funcs, shards=shards),
        grid=(units,),
        in_specs=[smem, smem, pl.BlockSpec((1, slots, width), lambda u: (u, 0, 0))]
        + [whole_spec((2 * piece, width))] * shards,
        out_specs=[
            pl.BlockSpec((1, 2 * width, width), lambda u: (u, 0, 0)),
            pl.BlockSpec((1, width, 2 * width), lambda u: (u, 0, 0)),
            pl.BlockSpec((1, width, slots), lambda u: (u, 0, 0)),
            pl.BlockSpec((1, width, slots), lambda u: (u, 0, 0)),
        ],
        out_shape=[
            jax.ShapeDtypeStruct((units, 2 * width, width), bf16),
            jax.ShapeDtypeStruct((units, width, 2 * width), bf16),
            jax.ShapeDtypeStruct((units, width, slots), bf16),
            jax.ShapeDtypeStruct((units, width, slots), bf16),
        ],
        scratch_shapes=[
            pltpu.VMEM((shards, 2 * piece, width), bf16),
            pltpu.VMEM((2 * width, width), bf16),
        ],
        compiler_params=limit,
        cost_estimate=cost(8),
        name="points_forward",
    )(counts, presence, flat_points, *early_parts)

    kept = jax.ShapeDtypeStruct((items * steps, width, tile), bf16)
    main_rows = enter_rows + experts * exit_piece + piece + 16

    def early(i, p, j):
        return i * steps + jnp.where(p == 0, j, steps - 1)

    def late(i, p, j):
        return i * steps + jnp.where(p == 0, 0, j)

    early_keep = pl.BlockSpec((1, width, tile), lambda i, p, j: (early(i, p, j), 0, 0))
    late_keep = pl.BlockSpec((1, width, tile), lambda i, p, j: (late(i, p, j), 0, 0))
    late_rows = pl.BlockSpec((tile, width), lambda i, p, j: (late(i, p, j), 0))
    (
        result,
        queries_one,
        cross,
        first,
        keys_two,
        values_two,
        grad_q_two,
        grad_second,
        grad_state_two,
        *main_grads,
    ) = pl.pallas_call(
        partial(main_kernel, funcs=funcs, experts=experts, shards=shards, at=at),
        grid=(items, 2, steps),
        in_specs=[
            pl.BlockSpec((tile, width), lambda i, p, j: (early(i, p, j), 0)),
            late_rows,
            pl.BlockSpec((2, tile), lambda i, p, j: (0, late(i, p, j))),
            pl.BlockSpec((funcs, 2 * width, width), lambda i, p, j: (i, 0, 0)),
        ]
        + late_specs,
        out_specs=[
            late_rows,
            early_keep,
            early_keep,
            early_keep,
            early_keep,
            early_keep,
            late_keep,
            late_keep,
            pl.BlockSpec((1, width, 2 * width), lambda i, p, j: (i, 0, 0)),
        ]
        + [whole_spec((main_rows, width))] * shards,
        out_shape=[
            jax.ShapeDtypeStruct((count, width), bf16),
            kept,
            kept,
            kept,
            kept,
            kept,
            kept,
            kept,
            jax.ShapeDtypeStruct((items, width, 2 * width), f32),
        ]
        + [jax.ShapeDtypeStruct((main_rows, width), bf16)] * shards,
        scratch_shapes=[
            gathered,
            pltpu.VMEM((shards, main_rows, width), bf16),
            pltpu.VMEM((steps, width, tile), f32),
            pltpu.VMEM((steps, width, tile), bf16),
            pltpu.VMEM((width, 2 * width), f32),
            pltpu.VMEM((2 * width, width), bf16),
            pltpu.VMEM((width, 2 * width), bf16),
            pltpu.VMEM((width, 2 * width), f32),
            pltpu.VMEM((width, width), bf16),
            pltpu.VMEM((width, width), bf16),
            pltpu.VMEM((3 * width, width), bf16),
            pltpu.VMEM((width, width), bf16),
            pltpu.VMEM((width, width), bf16),
            pltpu.VMEM((inner, width), bf16),
            pltpu.VMEM((width, inner), bf16),
            pltpu.VMEM((inner, width), bf16),
            pltpu.VMEM((width, inner), bf16),
            pltpu.VMEM((width, tile), f32),
            pltpu.VMEM((width, tile), f32),
            pltpu.VMEM((width, tile), f32),
            pltpu.VMEM((width, tile), f32),
            pltpu.VMEM((inner, tile), bf16),
            pltpu.VMEM((inner, tile), bf16),
            pltpu.VMEM((width, inner), f32),
            pltpu.VMEM((width, inner), f32),
            pltpu.VMEM((width, width), f32),
            pltpu.VMEM((width, width), f32),
            pltpu.VMEM((width, width), f32),
            pltpu.VMEM((2 * experts, tile), f32),
        ],
        compiler_params=limit,
        cost_estimate=cost(80),
        name="main",
    )(tokens, cotangent, coords, state_t, *late_parts)

    rest_rows = 7 * piece + 16

    def rest_call(item, earlier, after):
        first_call = item == 0
        keep_spec = pl.BlockSpec((1, width, tile), lambda j: (item * steps + j, 0, 0))
        row_spec = pl.BlockSpec((tile, width), lambda j: (item * steps + j, 0))
        unit_spec = pl.BlockSpec((funcs, width, width), lambda j: (item, 0, 0))
        anywhere = pl.BlockSpec(memory_space=pl.ANY)
        in_specs = [
            smem,
            row_spec,
            keep_spec,
            keep_spec,
            keep_spec,
            keep_spec,
            keep_spec,
            keep_spec,
            keep_spec,
            pl.BlockSpec((1, width, 2 * width), lambda j: (item, 0, 0)),
            pl.BlockSpec((funcs, 2 * width, width), lambda j: (item, 0, 0)),
            pl.BlockSpec((funcs, width, 2 * width), lambda j: (item, 0, 0)),
        ] + late_specs
        operands = [
            presence,
            tokens,
            queries_one,
            cross,
            first,
            keys_two,
            values_two,
            grad_q_two,
            grad_second,
            grad_state_two,
            state_t,
            state,
            *late_parts,
        ]
        aliases = {}
        if not first_call:
            aliases = {len(operands) + k: k for k in range(3)}
            in_specs += [anywhere] * 3 + [whole_spec((width, 7 * width)), anywhere]
            operands += [*earlier, after]
        out_specs = [row_spec, unit_spec, unit_spec, whole_spec((width, 7 * width))]
        out_shape = [
            jax.ShapeDtypeStruct((count, width), f32),
            jax.ShapeDtypeStruct((units, width, width), bf16),
            jax.ShapeDtypeStruct((units, width, width), f32),
            jax.ShapeDtypeStruct((width, 7 * width), f32),
        ]
        return pl.pallas_call(
            partial(
                rest_kernel,
                funcs=funcs,
                item=item,
                shards=shards,
                at=at,
                first_call=first_call,
            ),
            grid=(steps,),
            in_specs=in_specs,
            out_specs=out_specs,
            out_shape=out_shape,
            input_output_aliases=aliases,
            scratch_shapes=[
                gathered,
                pltpu.VMEM((width, 3 * width), bf16),
                pltpu.VMEM((width, width), bf16),
                pltpu.VMEM((width, width), bf16),
                pltpu.VMEM((width, tile), f32),
                pltpu.VMEM((width, tile), f32),
                pltpu.VMEM((2, width, width), bf16),
                pltpu.VMEM((width, tile), f32),
                pltpu.VMEM((width, 2 * funcs * width), f32),
                pltpu.VMEM((width, 7 * width), f32),
            ],
            compiler_params=limit,
            cost_estimate=cost(18),
            name="rest",
        )(*operands)

    main_got = exchange(main_grads, "fsdp", shards, 1)
    found = rest_call(0, None, None)
    main_sum = sum_parts(main_got, "sum_main")
    main_total = lax.psum(main_sum, "dp")
    for item in range(1, items):
        found = rest_call(item, found, main_sum)
    grad_tokens, grad_state_one, grad_totals_one, carry = found

    rest_grads = pl.pallas_call(
        partial(points_back, shards=shards),
        grid=(units,),
        in_specs=[
            pl.BlockSpec((1, slots, width), lambda u: (u, 0, 0)),
            pl.BlockSpec((1, width, slots), lambda u: (u, 0, 0)),
            pl.BlockSpec((1, width, slots), lambda u: (u, 0, 0)),
            pl.BlockSpec((1, width, width), lambda u: (u, 0, 0)),
            pl.BlockSpec((1, width, width), lambda u: (u, 0, 0)),
            whole_spec((width, 7 * width)),
        ],
        out_specs=[whole_spec((rest_rows, width))] * shards,
        out_shape=[jax.ShapeDtypeStruct((rest_rows, width), bf16)] * shards,
        scratch_shapes=[
            pltpu.VMEM((2 * width, width), f32),
            pltpu.VMEM((shards, rest_rows, width), bf16),
        ],
        compiler_params=limit,
        cost_estimate=cost(7),
        name="points_back",
    )(flat_points, keys_one, values_one, grad_state_one, grad_totals_one, carry)
    rest_got = exchange(rest_grads, "fsdp", shards, 1)

    parts = rest_got
    for digit, stride in digits(dp):
        parts = spread(sum_parts(parts, "sum_rest"), "dp", dp, digit, stride)

    matrix = jax.ShapeDtypeStruct((piece, width), f32)
    vector = jax.ShapeDtypeStruct((1, piece), f32)
    outs = pl.pallas_call(
        partial(
            unpack_kernel,
            experts=experts,
            piece=piece,
            exit_piece=exit_piece,
            hidden=hidden,
        ),
        out_shape=[vector] * 2
        + [matrix] * 8
        + [vector] * 2
        + [
            jax.ShapeDtypeStruct(expert_in.shape, f32),
            jax.ShapeDtypeStruct(expert_out.shape, f32),
            jax.ShapeDtypeStruct((1, 2), f32),
        ],
        scratch_shapes=[
            pltpu.VMEM((32, width), f32),
            pltpu.VMEM((rest_rows, width), f32),
        ],
        name="unpack",
    )(main_total, *parts)
    outs = [out.reshape(piece) if out.shape == (1, piece) else out for out in outs]
    return (result, grad_tokens, *outs[:-1], outs[-1].reshape(gate_weight.shape))


def solution(mesh):
    rows = P(("dp", "fsdp"), None)
    matrix = P("fsdp", None)
    vector = P("fsdp")
    expert = P(None, "fsdp", None)
    parameters = (
        (vector, vector)
        + (matrix,) * 8
        + (vector, vector, expert, expert, P(None, "fsdp"))
    )
    return jax.shard_map(
        partial(shards_fn, mesh.shape["dp"], mesh.shape["fsdp"]),
        mesh=mesh,
        in_specs=(
            rows,
            P(("dp", "fsdp"), None, None, None),
            P(None, ("dp", "fsdp")),
            rows,
            rows,
            rows,
        )
        + parameters,
        out_specs=(rows, rows) + parameters,
        check_vma=False,
    )
```

```python
from functools import partial

import jax
import jax.numpy as jnp
from jax import lax
from jax.experimental import pallas as pl
from jax.experimental.pallas import tpu as pltpu
from jax.sharding import PartitionSpec as P


HEADS = 8
eps = 1e-05
f32 = jnp.float32
bf16 = jnp.bfloat16
TILE = 1024
CHUNK = 256
SLAB = 64
VMEM = 56 * 1024 * 1024


def cost(microseconds):
    return pl.CostEstimate(flops=microseconds * 10**9, bytes_accessed=10**6, transcendentals=0)


def nn(left, right):
    return jnp.dot(left, right, preferred_element_type=f32)


def nt(left, right):
    return lax.dot_general(left, right, (((1,), (1,)), ((), ())), preferred_element_type=f32)


def flip(value):
    return value.T


def inverse(value):
    return pl.reciprocal(value, approx=True)


def head_softmax(value):
    width, rows = value.shape
    split = value.reshape(HEADS, width // HEADS, rows)
    raised = jnp.exp(split - jnp.max(split, axis=1, keepdims=True))
    return (raised * inverse(jnp.sum(raised, axis=1, keepdims=True))).reshape(width, rows)


def softmax_back(probs, grad):
    width, rows = grad.shape
    probs = probs.astype(f32).reshape(HEADS, width // HEADS, rows)
    grad = grad.reshape(HEADS, width // HEADS, rows)
    inner = jnp.sum(probs * grad, axis=1, keepdims=True)
    return (probs * (grad - inner)).reshape(width, rows)


def standardize(value):
    centre = value - jnp.mean(value, axis=0, keepdims=True)
    scale = lax.rsqrt(jnp.mean(centre * centre, axis=0, keepdims=True) + eps)
    return centre * scale, scale


def norm_back(grad, hat, scale):
    return scale * (
        grad
        - jnp.mean(grad, axis=0, keepdims=True)
        - hat * jnp.mean(grad * hat, axis=0, keepdims=True)
    )


def same_head(rows, columns, width):
    head = width // HEADS
    row = lax.rem(lax.broadcasted_iota(jnp.int32, (rows, columns), 0), width)
    column = lax.rem(lax.broadcasted_iota(jnp.int32, (rows, columns), 1), width)
    return lax.div(row, head) == lax.div(column, head)


def assemble(parts, gathered):
    shards = len(parts)
    here = lax.axis_index("fsdp")
    for place, part in enumerate(parts):
        gathered[lax.rem(here + shards - place, shards)] = part[...]


def columns(gathered, start, count):
    shards, _, width = gathered.shape
    piece = width // shards
    small = [gathered[shard, start : start + 16, :].astype(f32) for shard in range(shards)]
    joined = jnp.concatenate([part[:, :piece] for part in small], axis=1)
    return [
        flip(jnp.broadcast_to(joined[place : place + 1], (width, width)))[:, 0:1]
        for place in range(count)
    ]


def lane_fold(value):
    width = value.shape[0]
    total = value[:, :width]
    for start in range(width, value.shape[1], width):
        total = total + value[:, start : start + width]
    return total


def as_row(value):
    width = value.shape[0]
    return flip(jnp.broadcast_to(jnp.sum(value, axis=1, keepdims=True), (width, width)))


def scatter_blocks(stage, outs):
    shards = len(outs)
    here = lax.axis_index("fsdp")
    for place, out in enumerate(outs):
        out[...] = stage[lax.rem(here + place, shards)]


def whole(gathered, start, rows):
    shards = gathered.shape[0]
    return gathered[:, start : start + rows, :].reshape(shards * rows, gathered.shape[2])


def function_weight(presence, item, func, funcs, shape):
    total = presence[item, 0]
    for other in range(1, funcs):
        total = total + presence[item, other]
    own = jnp.full(shape, presence[item, func], jnp.int32).astype(f32)
    return own / jnp.full(shape, total, jnp.int32).astype(f32)


def pack_kernel(*refs):
    weights, vectors, gate = refs[:10], refs[10:14], refs[14]
    early, late = refs[15:]
    keys, values, query, out, query_two, key_two, value_two, out_two, enter, leave = weights
    start = 0
    for weight in (keys, values):
        early[start : start + weight.shape[0]] = weight[...]
        start += weight.shape[0]
    start = 0
    for weight in (query, out, query_two, key_two, value_two, out_two):
        late[start : start + weight.shape[0]] = weight[...]
        start += weight.shape[0]
    experts, piece, hidden = enter.shape
    width = late.shape[1]
    for expert in range(experts):
        for half in range(hidden // width):
            late[start : start + piece] = enter[expert, :, half * width : (half + 1) * width]
            start += piece
    for expert in range(experts):
        late[start : start + leave.shape[1]] = leave[expert]
        start += leave.shape[1]
    rest = jnp.zeros((1, width - piece), f32)
    rows = [
        jnp.concatenate([vector[...].astype(f32), rest], axis=1) for vector in vectors
    ]
    rows.append(jnp.zeros((4, width), f32))
    for row in range(2):
        rows.append(jnp.broadcast_to(gate[row : row + 1, 0:1].astype(f32), (1, width)))
    rows.append(jnp.zeros((6, width), f32))
    late[start : start + 16] = jnp.concatenate(rows, axis=0).astype(bf16)


def points_forward(counts, presence, points, *refs, funcs, shards):
    parts = refs[:shards]
    state_t, state, keys_out, values_out, gathered, weight = refs[shards:]
    step = pl.program_id(0)
    item, func = lax.div(step, funcs), lax.rem(step, funcs)
    width = points.shape[2]
    slots = points.shape[1]
    piece = width // shards

    @pl.when(step == 0)
    def _():
        assemble(parts, gathered)
        weight[:width] = flip(whole(gathered, 0, piece))
        weight[width:] = flip(whole(gathered, piece, piece))

    both = nt(weight[...], points[0])
    probs = head_softmax(both[:width])
    slot = lax.broadcasted_iota(jnp.int32, (1, slots), 1)
    keys = jnp.where(slot < counts[item, func], probs, 0.0).astype(bf16)
    values = both[width:].astype(bf16)
    keys_out[0] = keys
    values_out[0] = values
    extended = jnp.concatenate([values, jnp.ones_like(values)], axis=0)
    share = function_weight(presence, item, func, funcs, (1, width))
    mask = same_head(width, width, width)
    summed = nt(keys, extended)
    left = jnp.where(mask, summed[:, :width], 0.0) * share
    right = jnp.where(mask, summed[:, width:], 0.0)
    state[0, :, :width] = left.astype(bf16)
    state[0, :, width:] = (-right).astype(bf16)
    state_t[0, :width] = flip(left).astype(bf16)
    state_t[0, width:] = flip(right).astype(bf16)


def main_kernel(tokens, cotangent, coords, state_t, *refs, funcs, experts, shards, at):
    parts, outs, scratch = refs[:shards], refs[shards : 2 * shards + 9], refs[2 * shards + 9 :]
    (
        result,
        queries_out,
        cross_out,
        first_out,
        keys_out,
        values_out,
        grad_q_out,
        grad_second_out,
        grad_state_out,
    ) = outs[:9]
    grads_out = outs[9:]
    (
        params,
        grads_stage,
        first_keep,
        query_keep,
        state_sum,
        self_t,
        self_state,
        grad_state_sum,
        w_query,
        w_out_one,
        w_self,
        w_out_two_t,
        w_out_two,
        w_in_t,
        w_in,
        w_exit,
        w_exit_t,
        gain_one,
        bias_one,
        gain_two,
        bias_two,
        hidden_keep,
        inner_keep,
        normed_keep,
        grad_keep,
        own_keep,
        pair_keep,
        sum_in,
        sum_exit,
        sum_out_two,
        sum_gain,
        sum_bias,
        sum_gate,
    ) = scratch
    item = pl.program_id(0)
    phase = pl.program_id(1)
    step = pl.program_id(2)
    steps = pl.num_programs(2)
    width = tokens.shape[1]
    rows = tokens.shape[0]
    piece = width // shards
    hidden = w_in.shape[1] // experts
    exit_piece = hidden // shards

    @pl.when((item == 0) & (phase == 0) & (step == 0))
    def _():
        assemble(parts, params)
        w_query[...] = flip(whole(params, at["query_first"], piece))
        w_out_one[...] = flip(whole(params, at["out_first"], piece))
        w_self[:width] = flip(whole(params, at["query_second"], piece))
        w_self[width : 2 * width] = flip(whole(params, at["key_second"], piece))
        w_self[2 * width :] = flip(whole(params, at["value_second"], piece))
        out_two = whole(params, at["out_second"], piece)
        w_out_two[...] = out_two
        w_out_two_t[...] = flip(out_two)
        for block in range(experts * hidden // width):
            part = whole(params, at["expert_in"] + block * piece, piece)
            w_in[:, block * width : (block + 1) * width] = part
            w_in_t[block * width : (block + 1) * width] = flip(part)
        for expert in range(experts):
            part = whole(params, at["expert_out"] + expert * exit_piece, exit_piece)
            w_exit[expert * hidden : (expert + 1) * hidden] = part
            w_exit_t[:, expert * hidden : (expert + 1) * hidden] = flip(part)
        found = columns(params, at["small"], 4)
        for vector, column in zip((gain_one, bias_one, gain_two, bias_two), found):
            vector[...] = jnp.broadcast_to(column, vector.shape)
        sum_in[...] = jnp.zeros_like(sum_in)
        sum_exit[...] = jnp.zeros_like(sum_exit)
        sum_out_two[...] = jnp.zeros_like(sum_out_two)
        sum_gain[...] = jnp.zeros_like(sum_gain)
        sum_bias[...] = jnp.zeros_like(sum_bias)
        sum_gate[...] = jnp.zeros_like(sum_gate)

    chunks = [slice(start, start + CHUNK) for start in range(0, rows, CHUNK)]

    @pl.when(phase == 0)
    def _():
        def enter(cols):
            rows_t = flip(tokens[cols, :]).astype(f32)
            hat, _scale = standardize(rows_t)
            normed = (hat * gain_one[...] + bias_one[...]).astype(bf16)
            return rows_t, head_softmax(nn(w_query[...], normed)).astype(bf16)

        def across(cols, queries):
            queries_out[0, :, cols] = queries
            mixed = None
            for func in range(funcs):
                both = nn(state_t[func], queries)
                part = both[:width] * inverse(both[width:])
                mixed = part if mixed is None else mixed + part
            cross = mixed.astype(bf16)
            cross_out[0, :, cols] = cross
            return cross

        def leave(cols, rows_t, cross):
            first = rows_t + nn(w_out_one[...], cross)
            first_keep[step, :, cols] = first
            first_low = first.astype(bf16)
            first_out[0, :, cols] = first_low
            return first_low

        def project(cols, first_low):
            three = nn(w_self[...], first_low)
            query_keep[step, :, cols] = head_softmax(three[:width]).astype(bf16)
            keys_out[0, :, cols] = head_softmax(three[width : 2 * width]).astype(bf16)
            values = three[2 * width :].astype(bf16)
            values_out[0, :, cols] = values
            pair_keep[:width, cols] = values
            pair_keep[width:, cols] = jnp.ones_like(values)

        entered = [enter(cols) for cols in chunks]
        crossed = [across(cols, queries) for cols, (_, queries) in zip(chunks, entered)]
        firsts = [
            leave(cols, rows_t, cross)
            for cols, (rows_t, _), cross in zip(chunks, entered, crossed)
        ]
        for cols, first_low in zip(chunks, firsts):
            project(cols, first_low)
        found = nt(keys_out[0], pair_keep[...])

        @pl.when(step == 0)
        def _():
            state_sum[...] = found

        @pl.when(step > 0)
        def _():
            state_sum[...] += found

        @pl.when(step == steps - 1)
        def _():
            mask = same_head(width, width, width)
            left = jnp.where(mask, state_sum[:, :width], 0.0)
            right = jnp.where(mask, state_sum[:, width:], 0.0)
            self_state[:, :width] = left.astype(bf16)
            self_state[:, width:] = (-right).astype(bf16)
            self_t[:width] = flip(left).astype(bf16)
            self_t[width:] = flip(right).astype(bf16)

    @pl.when(phase == 1)
    def _():
        def attend(cols):
            both = nn(self_t[...], query_keep[step, :, cols])
            undo = inverse(both[width:])
            own = both[:width] * undo
            own_keep[:, cols] = own.astype(bf16)
            grad_keep[:, cols] = flip(cotangent[cols, :])
            return undo, own

        def norm(cols):
            second = first_keep[step, :, cols] + nn(w_out_two_t[...], own_keep[:, cols])
            hat, scale = standardize(second)
            normed_keep[:, cols] = (hat * gain_two[...] + bias_two[...]).astype(bf16)
            return second, hat, scale

        def gate(cols):
            across, down = coords[0:1, cols], coords[1:2, cols]
            logits = []
            for expert in range(experts):
                pair = params[expert, at["small"] : at["small"] + 16, 0:1].astype(f32)
                logits.append(across * pair[8:9] + down * pair[9:10])
            peak = logits[0]
            for logit in logits[1:]:
                peak = jnp.maximum(peak, logit)
            raised = [jnp.exp(logit - peak) for logit in logits]
            total = raised[0]
            for other in raised[1:]:
                total = total + other
            return [other / total for other in raised]

        def expand(cols, gates):
            normed, grad = normed_keep[:, cols], grad_keep[:, cols]
            grad_gates = []
            for expert in range(experts):
                partial_sum = None
                for start in range(expert * hidden, (expert + 1) * hidden, SLAB):
                    span = slice(start, start + SLAB)
                    inner = nn(w_in_t[span], normed)
                    back = nn(w_exit[span], grad)
                    square = inner * inner
                    tanh = jnp.tanh(inner * (0.7978845608028654 + 0.035677408136300125 * square))
                    half = 0.5 + 0.5 * tanh
                    active = inner * half
                    folded = jnp.sum((active * back).reshape(SLAB // 8, 8, CHUNK), axis=0)
                    partial_sum = folded if partial_sum is None else partial_sum + folded
                    hidden_keep[span, cols] = (active * gates[expert]).astype(bf16)
                    slope = half + active * (1.0 - half) * (
                        1.5957691216057308 + 0.21406444881780074 * square
                    )
                    inner_keep[span, cols] = (slope * (back * gates[expert])).astype(bf16)
                grad_gates.append(jnp.sum(partial_sum, axis=0, keepdims=True))
            across, down = coords[0:1, cols], coords[1:2, cols]
            mean_gate = gates[0] * grad_gates[0]
            for expert in range(1, experts):
                mean_gate = mean_gate + gates[expert] * grad_gates[expert]
            for expert in range(experts):
                change = gates[expert] * (grad_gates[expert] - mean_gate)
                sum_gate[expert : expert + 1, cols] += across * change
                sum_gate[experts + expert : experts + expert + 1, cols] += down * change

        def contract(cols, second, hat, scale):
            total = second + nn(w_exit_t[...], hidden_keep[:, cols])
            result[cols, :] = flip(total.astype(bf16))
            grad_normed = nn(w_in[...], inner_keep[:, cols])
            sum_gain[...] += lane_fold(grad_normed * hat)
            sum_bias[...] += lane_fold(grad_normed)
            grad_second = grad_keep[:, cols].astype(f32) + norm_back(
                grad_normed * gain_two[...], hat, scale
            )
            grad_own = grad_second.astype(bf16)
            grad_second_out[0, :, cols] = grad_own
            return grad_own

        def attend_back(cols, grad_own, undo, own):
            share = nn(w_out_two[...], grad_own) * undo
            pair_keep[:width, cols] = share.astype(bf16)
            pair_keep[width:, cols] = (share * own).astype(bf16)

        def query_back(cols):
            grad_q = nn(self_state[...], pair_keep[:, cols])
            grad_q_out[0, :, cols] = softmax_back(query_keep[step, :, cols], grad_q).astype(bf16)

        attended = [attend(cols) for cols in chunks]
        normed = [norm(cols) for cols in chunks]
        gates = [gate(cols) for cols in chunks]
        for cols, own_gates in zip(chunks, gates):
            expand(cols, own_gates)
        grads = [contract(cols, *kept) for cols, kept in zip(chunks, normed)]
        for cols, grad_own, (undo, own) in zip(chunks, grads, attended):
            attend_back(cols, grad_own, undo, own)
        for cols in chunks:
            query_back(cols)
        sum_exit[...] += nt(grad_keep[...], hidden_keep[...])
        sum_in[...] += nt(normed_keep[...], inner_keep[...])
        sum_out_two[...] += nt(own_keep[...], grad_second_out[0])
        found = nt(query_keep[step], pair_keep[...])

        @pl.when(step == 0)
        def _():
            grad_state_sum[...] = found

        @pl.when(step > 0)
        def _():
            grad_state_sum[...] += found

        @pl.when(step == steps - 1)
        def _():
            grad_state_out[0] = grad_state_sum[...]

    @pl.when((item == pl.num_programs(0) - 1) & (phase == 1) & (step == steps - 1))
    def _():
        gain, bias = as_row(sum_gain[...]), as_row(sum_bias[...])
        gate = jnp.broadcast_to(jnp.sum(sum_gate[...], axis=1, keepdims=True), (8, width))
        row = lax.broadcasted_iota(jnp.int32, (8, width), 0)
        vectors = jnp.where(row == 0, gain[:8], bias[:8])
        small = jnp.concatenate([vectors, gate], axis=0).astype(bf16)
        start = 0
        for block in range(experts * hidden // width):
            part = sum_in[:, block * width : (block + 1) * width].astype(bf16)
            grads_stage[:, start : start + piece, :] = part.reshape(shards, piece, width)
            start += piece
        for expert in range(experts):
            part = flip(sum_exit[:, expert * hidden : (expert + 1) * hidden]).astype(bf16)
            grads_stage[:, start : start + exit_piece, :] = part.reshape(shards, exit_piece, width)
            start += exit_piece
        part = sum_out_two[...].astype(bf16)
        grads_stage[:, start : start + piece, :] = part.reshape(shards, piece, width)
        start += piece
        for shard in range(shards):
            grads_stage[shard, start : start + 16, :] = small
        scatter_blocks(grads_stage, grads_out)


def rest_kernel(
    presence,
    tokens,
    queries_in,
    cross_in,
    first_in,
    keys_in,
    values_in,
    grad_q_in,
    grad_second_in,
    grad_state_in,
    state_t,
    state,
    *refs,
    funcs,
    item,
    shards,
    at,
    first_call,
):
    parts, refs = refs[:shards], refs[shards:]
    if not first_call:
        carry, refs = refs[3], refs[5:]
    (
        grad_tokens,
        grad_cross_state_out,
        grad_totals_out,
        sums_out,
        params,
        w_self,
        w_out_one,
        w_query,
        gain_one,
        bias_one,
        grad_self_state,
        grad_totals,
        grad_state_sum,
        sums,
        three_keep,
        cross_keep,
        stack_keep,
        query_keep,
        normed_keep,
    ) = refs
    step = pl.program_id(0)
    steps = pl.num_programs(0)
    width = tokens.shape[1]
    piece = width // shards
    self_part = slice(0, 3 * width)
    out_part = slice(3 * width, 4 * width)
    query_part = slice(4 * width, 5 * width)
    gain_part = slice(5 * width, 6 * width)
    bias_part = slice(6 * width, 7 * width)

    @pl.when(step == 0)
    def _():
        assemble(parts, params)
        w_query[...] = whole(params, at["query_first"], piece)
        w_out_one[...] = whole(params, at["out_first"], piece)
        w_self[:, :width] = whole(params, at["query_second"], piece)
        w_self[:, width : 2 * width] = whole(params, at["key_second"], piece)
        w_self[:, 2 * width :] = whole(params, at["value_second"], piece)
        for vector, column in zip((gain_one, bias_one), columns(params, at["small"], 2)):
            vector[...] = jnp.broadcast_to(column, vector.shape)
        sums[...] = jnp.zeros_like(sums) if first_call else carry[...]
        mask = same_head(width, width, width)
        left = jnp.where(mask, grad_state_in[0, :, :width], 0.0)
        right = jnp.where(mask, grad_state_in[0, :, width:], 0.0)
        grad_self_state[0] = left.astype(bf16)
        grad_self_state[1] = flip(left).astype(bf16)
        grad_totals[...] = jnp.broadcast_to(
            -jnp.sum(right, axis=1, keepdims=True), grad_totals.shape
        )

    chunks = [slice(start, start + CHUNK) for start in range(0, tokens.shape[0], CHUNK)]

    def self_back(cols):
        keys, values = keys_in[0, :, cols], values_in[0, :, cols]
        grad_keys = nn(grad_self_state[0], values) + grad_totals[...]
        three_keep[:width, cols] = grad_q_in[0, :, cols]
        three_keep[width : 2 * width, cols] = softmax_back(keys, grad_keys).astype(bf16)
        three_keep[2 * width :, cols] = nn(grad_self_state[1], keys).astype(bf16)

    def join(cols):
        grad_first = grad_second_in[0, :, cols].astype(f32) + nn(w_self[...], three_keep[:, cols])
        cross_keep[:, cols] = grad_first.astype(bf16)
        return grad_first

    def cross_back(cols):
        share = nn(w_out_one[...], cross_keep[:, cols])
        for func in range(funcs):
            both = nn(state_t[func], queries_in[0, :, cols])
            undo = inverse(both[width:])
            part = share * undo
            start = 2 * func * width
            stack_keep[start : start + width, cols] = part.astype(bf16)
            stack_keep[start + width : start + 2 * width, cols] = (
                part * (both[:width] * undo)
            ).astype(bf16)

    def query_back(cols):
        joined = jnp.concatenate([state[func] for func in range(funcs)], axis=1)
        grad_q = softmax_back(queries_in[0, :, cols], nn(joined, stack_keep[:, cols]))
        query_keep[:, cols] = grad_q.astype(bf16)

    def finish(cols, grad_first):
        hat, scale = standardize(flip(tokens[cols, :]).astype(f32))
        normed_keep[:, cols] = (hat * gain_one[...] + bias_one[...]).astype(bf16)
        grad_normed = nn(w_query[...], query_keep[:, cols])
        sums[:, gain_part] += lane_fold(grad_normed * hat)
        sums[:, bias_part] += lane_fold(grad_normed)
        grad_rows = grad_first + norm_back(grad_normed * gain_one[...], hat, scale)
        grad_tokens[cols, :] = flip(grad_rows)

    for cols in chunks:
        self_back(cols)
    grad_firsts = [join(cols) for cols in chunks]
    for cols in chunks:
        cross_back(cols)
    for cols in chunks:
        query_back(cols)
    for cols, grad_first in zip(chunks, grad_firsts):
        finish(cols, grad_first)
    sums[:, self_part] += nt(first_in[0], three_keep[...])
    sums[:, out_part] += nt(cross_in[0], cross_keep[...])
    sums[:, query_part] += nt(normed_keep[...], query_keep[...])
    found = nt(queries_in[0], stack_keep[...])

    @pl.when(step == 0)
    def _():
        grad_state_sum[...] = found

    @pl.when(step > 0)
    def _():
        grad_state_sum[...] += found

    @pl.when(step == steps - 1)
    def _():
        mask = same_head(width, width, width)
        for func in range(funcs):
            weight = function_weight(presence, item, func, funcs, (1, width))
            start = 2 * func * width
            left = jnp.where(mask, grad_state_sum[:, start : start + width], 0.0) * weight
            right = jnp.where(mask, grad_state_sum[:, start + width : start + 2 * width], 0.0)
            grad_cross_state_out[func] = left.astype(bf16)
            grad_totals_out[func] = jnp.broadcast_to(
                -jnp.sum(right, axis=1, keepdims=True), (width, width)
            )
        sums_out[...] = sums[...]


def points_back(points, keys_in, values_in, grad_state, grad_totals, carry, _after, *refs, shards):
    outs = refs[:shards]
    sums, stage = refs[shards:]
    step = pl.program_id(0)
    width = points.shape[2]
    piece = width // shards
    keys, values = keys_in[0], values_in[0]
    left = grad_state[0]
    grad_keys = nn(left, values) + grad_totals[0, :, 0:1]
    grad_k = softmax_back(keys, grad_keys).astype(bf16)
    grad_v = nn(flip(left), keys).astype(bf16)
    found = nn(jnp.concatenate([grad_k, grad_v], axis=0), points[0])

    @pl.when(step == 0)
    def _():
        sums[...] = found
        gain = as_row(carry[:, 5 * width : 6 * width])
        bias = as_row(carry[:, 6 * width : 7 * width])
        row = lax.broadcasted_iota(jnp.int32, (16, width), 0)
        small = jnp.where(row == 0, gain[:16], bias[:16]).astype(bf16)
        for place in range(5):
            part = carry[:, place * width : (place + 1) * width].astype(bf16)
            stage[:, place * piece : (place + 1) * piece, :] = part.reshape(shards, piece, width)
        for shard in range(shards):
            stage[shard, 5 * piece : 5 * piece + 16, :] = small

    @pl.when(step > 0)
    def _():
        sums[...] += found

    @pl.when(step == pl.num_programs(0) - 1)
    def _():
        for place in range(2):
            start = 5 * piece + 16 + place * piece
            part = flip(sums[place * width : (place + 1) * width]).astype(bf16)
            stage[:, start : start + piece, :] = part.reshape(shards, piece, width)
        scatter_blocks(stage, outs)


def total_of(parts):
    value = parts[0][...].astype(f32)
    for part in parts[1:]:
        value = value + part[...].astype(f32)
    return value


def unpack_kernel(*refs, count, experts, piece, exit_piece, hidden):
    main_parts, parts = refs[:count], refs[count : 2 * count]
    outs, (small, main, rest) = refs[2 * count : 2 * count + 15], refs[2 * count + 15 :]
    width = main.shape[1]
    main[...] = total_of(main_parts)
    rest[...] = total_of(parts)
    (
        gain_one,
        bias_one,
        query_one,
        key_one,
        value_one,
        out_one,
        query_two,
        key_two,
        value_two,
        out_two,
        gain_two,
        bias_two,
        enter,
        leave,
        gate,
    ) = outs
    start = 0
    for expert in range(experts):
        for half in range(hidden // width):
            block = main[start : start + piece]
            enter[expert, :, half * width : (half + 1) * width] = block
            start += piece
    for expert in range(experts):
        leave[expert] = main[start : start + exit_piece]
        start += exit_piece
    out_two[...] = main[start : start + piece]
    start += piece
    small[:16] = main[start : start + 16]
    start = 0
    for out in (query_two, key_two, value_two, out_one, query_one):
        out[...] = rest[start : start + piece]
        start += piece
    small[16:] = rest[start : start + 16]
    start += 16
    for out in (key_one, value_one):
        out[...] = rest[start : start + piece]
        start += piece
    shard = lax.axis_index("fsdp")
    turned = pltpu.roll(small[...], lax.rem(width - shard * piece, width), 1)
    gain_two[...] = turned[0:1, :piece]
    bias_two[...] = turned[1:2, :piece]
    gain_one[...] = turned[16:17, :piece]
    bias_one[...] = turned[17:18, :piece]
    for row in range(2):
        gate[:, row : row + 1] = small[pl.ds(8 + row * experts + shard, 1), 0:1]


def whole_spec(shape):
    return pl.BlockSpec(shape, lambda *_: (0,) * len(shape))


def route(size, shift, digit, stride):
    def target(i):
        own = i // stride % digit
        return i + ((own + shift) % digit - own) * stride

    return [(i, target(i)) for i in range(size)]


def spread(value, axis, size, digit, stride):
    return [value] + [
        lax.ppermute(value, axis, route(size, shift, digit, stride)) for shift in range(1, digit)
    ]


def exchange(values, axis, size, stride):
    digit = len(values)
    return [values[0]] + [
        lax.ppermute(values[shift], axis, route(size, shift, digit, stride))
        for shift in range(1, digit)
    ]


def digits(size):
    found = []
    stride = 1
    while stride < size:
        rest = size // stride
        digit = 2 if stride == 1 and rest % 2 == 0 else 4 if rest % 4 == 0 else rest
        found.append((digit, stride))
        stride *= digit
    return found or [(1, 1)]


def sum_parts(parts):
    return total_of([part.astype(f32) for part in parts]).astype(bf16)


def shards_fn(
    dp,
    shards,
    tokens,
    points,
    coords,
    presence,
    counts,
    cotangent,
    gain_first,
    bias_first,
    query_first,
    key_first,
    value_first,
    out_first,
    query_second,
    key_second,
    value_second,
    out_second,
    gain_second,
    bias_second,
    expert_in,
    expert_out,
    gate_weight,
):
    count, width = tokens.shape
    items, funcs, slots, _ = points.shape
    length = count // items
    experts, piece, hidden = expert_in.shape
    exit_piece = expert_out.shape[1]
    tile = min(TILE, length)
    steps = length // tile
    inner = experts * hidden
    enter_rows = experts * piece * (hidden // width)
    limit = pltpu.CompilerParams(vmem_limit_bytes=VMEM)

    at = {}
    place = 0
    for name, size in (
        ("query_first", piece),
        ("out_first", piece),
        ("query_second", piece),
        ("key_second", piece),
        ("value_second", piece),
        ("out_second", piece),
        ("expert_in", enter_rows),
        ("expert_out", experts * exit_piece),
        ("small", 16),
    ):
        at[name] = place
        place += size
    late_rows_count = place
    early_pack, late_pack = pl.pallas_call(
        pack_kernel,
        out_shape=[
            jax.ShapeDtypeStruct((2 * piece, width), bf16),
            jax.ShapeDtypeStruct((late_rows_count, width), bf16),
        ],
        name="pack",
    )(
        key_first,
        value_first,
        query_first,
        out_first,
        query_second,
        key_second,
        value_second,
        out_second,
        expert_in,
        expert_out,
        *(
            vector.reshape(1, piece)
            for vector in (gain_first, bias_first, gain_second, bias_second)
        ),
        gate_weight,
    )
    early_parts = spread(early_pack, "fsdp", shards, shards, 1)
    late_parts = spread(late_pack, "fsdp", shards, shards, 1)
    late_specs = [whole_spec((late_rows_count, width))] * shards
    gathered = pltpu.VMEM((shards, late_rows_count, width), bf16)

    smem = pl.BlockSpec(memory_space=pltpu.SMEM)
    units = items * funcs
    flat_points = points.reshape(units, slots, width)
    state_t, state, keys_one, values_one = pl.pallas_call(
        partial(points_forward, funcs=funcs, shards=shards),
        grid=(units,),
        in_specs=[smem, smem, pl.BlockSpec((1, slots, width), lambda u: (u, 0, 0))]
        + [whole_spec((2 * piece, width))] * shards,
        out_specs=[
            pl.BlockSpec((1, 2 * width, width), lambda u: (u, 0, 0)),
            pl.BlockSpec((1, width, 2 * width), lambda u: (u, 0, 0)),
            pl.BlockSpec((1, width, slots), lambda u: (u, 0, 0)),
            pl.BlockSpec((1, width, slots), lambda u: (u, 0, 0)),
        ],
        out_shape=[
            jax.ShapeDtypeStruct((units, 2 * width, width), bf16),
            jax.ShapeDtypeStruct((units, width, 2 * width), bf16),
            jax.ShapeDtypeStruct((units, width, slots), bf16),
            jax.ShapeDtypeStruct((units, width, slots), bf16),
        ],
        scratch_shapes=[
            pltpu.VMEM((shards, 2 * piece, width), bf16),
            pltpu.VMEM((2 * width, width), bf16),
        ],
        compiler_params=limit,
        cost_estimate=cost(8),
        name="points_forward",
    )(counts, presence, flat_points, *early_parts)

    kept = jax.ShapeDtypeStruct((items * steps, width, tile), bf16)
    main_rows = enter_rows + experts * exit_piece + piece + 16

    def early(i, p, j):
        return i * steps + jnp.where(p == 0, j, steps - 1)

    def late(i, p, j):
        return i * steps + jnp.where(p == 0, 0, j)

    early_keep = pl.BlockSpec((1, width, tile), lambda i, p, j: (early(i, p, j), 0, 0))
    late_keep = pl.BlockSpec((1, width, tile), lambda i, p, j: (late(i, p, j), 0, 0))
    late_rows = pl.BlockSpec((tile, width), lambda i, p, j: (late(i, p, j), 0))
    (
        result,
        queries_one,
        cross,
        first,
        keys_two,
        values_two,
        grad_q_two,
        grad_second,
        grad_state_two,
        *main_grads,
    ) = pl.pallas_call(
        partial(main_kernel, funcs=funcs, experts=experts, shards=shards, at=at),
        grid=(items, 2, steps),
        in_specs=[
            pl.BlockSpec((tile, width), lambda i, p, j: (early(i, p, j), 0)),
            late_rows,
            pl.BlockSpec((2, tile), lambda i, p, j: (0, late(i, p, j))),
            pl.BlockSpec((funcs, 2 * width, width), lambda i, p, j: (i, 0, 0)),
        ]
        + late_specs,
        out_specs=[
            late_rows,
            early_keep,
            early_keep,
            early_keep,
            early_keep,
            early_keep,
            late_keep,
            late_keep,
            pl.BlockSpec((1, width, 2 * width), lambda i, p, j: (i, 0, 0)),
        ]
        + [whole_spec((main_rows, width))] * shards,
        out_shape=[
            jax.ShapeDtypeStruct((count, width), bf16),
            kept,
            kept,
            kept,
            kept,
            kept,
            kept,
            kept,
            jax.ShapeDtypeStruct((items, width, 2 * width), f32),
        ]
        + [jax.ShapeDtypeStruct((main_rows, width), bf16)] * shards,
        scratch_shapes=[
            gathered,
            pltpu.VMEM((shards, main_rows, width), bf16),
            pltpu.VMEM((steps, width, tile), f32),
            pltpu.VMEM((steps, width, tile), bf16),
            pltpu.VMEM((width, 2 * width), f32),
            pltpu.VMEM((2 * width, width), bf16),
            pltpu.VMEM((width, 2 * width), bf16),
            pltpu.VMEM((width, 2 * width), f32),
            pltpu.VMEM((width, width), bf16),
            pltpu.VMEM((width, width), bf16),
            pltpu.VMEM((3 * width, width), bf16),
            pltpu.VMEM((width, width), bf16),
            pltpu.VMEM((width, width), bf16),
            pltpu.VMEM((inner, width), bf16),
            pltpu.VMEM((width, inner), bf16),
            pltpu.VMEM((inner, width), bf16),
            pltpu.VMEM((width, inner), bf16),
            pltpu.VMEM((width, CHUNK), f32),
            pltpu.VMEM((width, CHUNK), f32),
            pltpu.VMEM((width, CHUNK), f32),
            pltpu.VMEM((width, CHUNK), f32),
            pltpu.VMEM((inner, tile), bf16),
            pltpu.VMEM((inner, tile), bf16),
            pltpu.VMEM((width, tile), bf16),
            pltpu.VMEM((width, tile), bf16),
            pltpu.VMEM((width, tile), bf16),
            pltpu.VMEM((2 * width, tile), bf16),
            pltpu.VMEM((width, inner), f32),
            pltpu.VMEM((width, inner), f32),
            pltpu.VMEM((width, width), f32),
            pltpu.VMEM((width, width), f32),
            pltpu.VMEM((width, width), f32),
            pltpu.VMEM((2 * experts, tile), f32),
        ],
        compiler_params=limit,
        cost_estimate=cost(80),
        name="main",
    )(tokens, cotangent, coords, state_t, *late_parts)

    rest_rows = 7 * piece + 16

    def rest_call(item, earlier, after):
        first_call = item == 0
        keep_spec = pl.BlockSpec((1, width, tile), lambda j: (item * steps + j, 0, 0))
        row_spec = pl.BlockSpec((tile, width), lambda j: (item * steps + j, 0))
        unit_spec = pl.BlockSpec((funcs, width, width), lambda j: (item, 0, 0))
        anywhere = pl.BlockSpec(memory_space=pl.ANY)
        in_specs = [
            smem,
            row_spec,
            keep_spec,
            keep_spec,
            keep_spec,
            keep_spec,
            keep_spec,
            keep_spec,
            keep_spec,
            pl.BlockSpec((1, width, 2 * width), lambda j: (item, 0, 0)),
            pl.BlockSpec((funcs, 2 * width, width), lambda j: (item, 0, 0)),
            pl.BlockSpec((funcs, width, 2 * width), lambda j: (item, 0, 0)),
        ] + late_specs
        operands = [
            presence,
            tokens,
            queries_one,
            cross,
            first,
            keys_two,
            values_two,
            grad_q_two,
            grad_second,
            grad_state_two,
            state_t,
            state,
            *late_parts,
        ]
        aliases = {}
        if not first_call:
            aliases = {len(operands) + k: k for k in range(3)}
            in_specs += [anywhere] * 3 + [whole_spec((width, 7 * width)), anywhere]
            operands += [*earlier, after]
        out_specs = [row_spec, unit_spec, unit_spec, whole_spec((width, 7 * width))]
        out_shape = [
            jax.ShapeDtypeStruct((count, width), f32),
            jax.ShapeDtypeStruct((units, width, width), bf16),
            jax.ShapeDtypeStruct((units, width, width), f32),
            jax.ShapeDtypeStruct((width, 7 * width), f32),
        ]
        return pl.pallas_call(
            partial(
                rest_kernel,
                funcs=funcs,
                item=item,
                shards=shards,
                at=at,
                first_call=first_call,
            ),
            grid=(steps,),
            in_specs=in_specs,
            out_specs=out_specs,
            out_shape=out_shape,
            input_output_aliases=aliases,
            scratch_shapes=[
                gathered,
                pltpu.VMEM((width, 3 * width), bf16),
                pltpu.VMEM((width, width), bf16),
                pltpu.VMEM((width, width), bf16),
                pltpu.VMEM((width, CHUNK), f32),
                pltpu.VMEM((width, CHUNK), f32),
                pltpu.VMEM((2, width, width), bf16),
                pltpu.VMEM((width, CHUNK), f32),
                pltpu.VMEM((width, 2 * funcs * width), f32),
                pltpu.VMEM((width, 7 * width), f32),
                pltpu.VMEM((3 * width, tile), bf16),
                pltpu.VMEM((width, tile), bf16),
                pltpu.VMEM((2 * funcs * width, tile), bf16),
                pltpu.VMEM((width, tile), bf16),
                pltpu.VMEM((width, tile), bf16),
            ],
            compiler_params=limit,
            cost_estimate=cost(18),
            name="rest",
        )(*operands)

    levels = digits(dp)
    main_parts = exchange(main_grads, "fsdp", shards, 1)
    level = 0
    found = None
    for item in range(items):
        found = rest_call(item, found, main_sum if item else None)
        if item < len(levels):
            main_sum = sum_parts(main_parts)
            main_parts = spread(main_sum, "dp", dp, *levels[item])
            level = item + 1
    grad_tokens, grad_state_one, grad_totals_one, carry = found

    rest_grads = pl.pallas_call(
        partial(points_back, shards=shards),
        grid=(units,),
        in_specs=[
            pl.BlockSpec((1, slots, width), lambda u: (u, 0, 0)),
            pl.BlockSpec((1, width, slots), lambda u: (u, 0, 0)),
            pl.BlockSpec((1, width, slots), lambda u: (u, 0, 0)),
            pl.BlockSpec((1, width, width), lambda u: (u, 0, 0)),
            pl.BlockSpec((1, width, width), lambda u: (u, 0, 0)),
            whole_spec((width, 7 * width)),
            pl.BlockSpec(memory_space=pl.ANY),
        ],
        out_specs=[whole_spec((rest_rows, width))] * shards,
        out_shape=[jax.ShapeDtypeStruct((rest_rows, width), bf16)] * shards,
        scratch_shapes=[
            pltpu.VMEM((2 * width, width), f32),
            pltpu.VMEM((shards, rest_rows, width), bf16),
        ],
        compiler_params=limit,
        cost_estimate=cost(7),
        name="points_back",
    )(flat_points, keys_one, values_one, grad_state_one, grad_totals_one, carry, main_sum)
    rest_got = exchange(rest_grads, "fsdp", shards, 1)

    parts = rest_got
    for digit, stride in levels[level:]:
        main_parts = spread(sum_parts(main_parts), "dp", dp, digit, stride)
    for digit, stride in levels:
        parts = spread(sum_parts(parts), "dp", dp, digit, stride)

    matrix = jax.ShapeDtypeStruct((piece, width), f32)
    vector = jax.ShapeDtypeStruct((1, piece), f32)
    outs = pl.pallas_call(
        partial(
            unpack_kernel,
            count=levels[-1][0],
            experts=experts,
            piece=piece,
            exit_piece=exit_piece,
            hidden=hidden,
        ),
        out_shape=[vector] * 2
        + [matrix] * 8
        + [vector] * 2
        + [
            jax.ShapeDtypeStruct(expert_in.shape, f32),
            jax.ShapeDtypeStruct(expert_out.shape, f32),
            jax.ShapeDtypeStruct((1, 2), f32),
        ],
        scratch_shapes=[
            pltpu.VMEM((32, width), f32),
            pltpu.VMEM((main_rows, width), f32),
            pltpu.VMEM((rest_rows, width), f32),
        ],
        name="unpack",
    )(*main_parts, *parts)
    outs = [out.reshape(piece) if out.shape == (1, piece) else out for out in outs]
    return (result, grad_tokens, *outs[:-1], outs[-1].reshape(gate_weight.shape))


def solution(mesh):
    rows = P(("dp", "fsdp"), None)
    matrix = P("fsdp", None)
    vector = P("fsdp")
    expert = P(None, "fsdp", None)
    parameters = (
        (vector, vector)
        + (matrix,) * 8
        + (vector, vector, expert, expert, P(None, "fsdp"))
    )
    return jax.shard_map(
        partial(shards_fn, mesh.shape["dp"], mesh.shape["fsdp"]),
        mesh=mesh,
        in_specs=(
            rows,
            P(("dp", "fsdp"), None, None, None),
            P(None, ("dp", "fsdp")),
            rows,
            rows,
            rows,
        )
        + parameters,
        out_specs=(rows, rows) + parameters,
        check_vma=False,
    )
```

```python
from functools import partial

import jax
import jax.numpy as jnp
from jax import lax
from jax.experimental import pallas as pl
from jax.experimental.pallas import tpu as pltpu
from jax.sharding import PartitionSpec as P


HEADS = 8
eps = 1e-05
f32 = jnp.float32
bf16 = jnp.bfloat16
TILE = 1024
CHUNK = 256
SLAB = 64
VMEM = 56 * 1024 * 1024


def cost(microseconds):
    return pl.CostEstimate(flops=microseconds * 10**9, bytes_accessed=10**6, transcendentals=0)


def nn(left, right):
    return jnp.dot(left, right, preferred_element_type=f32)


def nt(left, right):
    return lax.dot_general(left, right, (((1,), (1,)), ((), ())), preferred_element_type=f32)


def flip(value):
    return value.T


def inverse(value):
    return pl.reciprocal(value, approx=True)


def head_softmax(value):
    width, rows = value.shape
    split = value.reshape(HEADS, width // HEADS, rows)
    raised = jnp.exp(split - jnp.max(split, axis=1, keepdims=True))
    return (raised * inverse(jnp.sum(raised, axis=1, keepdims=True))).reshape(width, rows)


def softmax_back(probs, grad):
    width, rows = grad.shape
    probs = probs.astype(f32).reshape(HEADS, width // HEADS, rows)
    grad = grad.reshape(HEADS, width // HEADS, rows)
    inner = jnp.sum(probs * grad, axis=1, keepdims=True)
    return (probs * (grad - inner)).reshape(width, rows)


def standardize(value):
    centre = value - jnp.mean(value, axis=0, keepdims=True)
    scale = lax.rsqrt(jnp.mean(centre * centre, axis=0, keepdims=True) + eps)
    return centre * scale, scale


def norm_back(grad, hat, scale):
    return scale * (
        grad
        - jnp.mean(grad, axis=0, keepdims=True)
        - hat * jnp.mean(grad * hat, axis=0, keepdims=True)
    )


def same_head(rows, columns, width):
    head = width // HEADS
    row = lax.rem(lax.broadcasted_iota(jnp.int32, (rows, columns), 0), width)
    column = lax.rem(lax.broadcasted_iota(jnp.int32, (rows, columns), 1), width)
    return lax.div(row, head) == lax.div(column, head)


def assemble(parts, gathered):
    shards = len(parts)
    here = lax.axis_index("fsdp")
    for place, part in enumerate(parts):
        gathered[lax.rem(here + shards - place, shards)] = part[...]


def columns(gathered, start, count):
    shards, _, width = gathered.shape
    piece = width // shards
    small = [gathered[shard, start : start + 16, :].astype(f32) for shard in range(shards)]
    joined = jnp.concatenate([part[:, :piece] for part in small], axis=1)
    return [
        flip(jnp.broadcast_to(joined[place : place + 1], (width, width)))[:, 0:1]
        for place in range(count)
    ]


def lane_fold(value):
    width = value.shape[0]
    total = value[:, :width]
    for start in range(width, value.shape[1], width):
        total = total + value[:, start : start + width]
    return total


def as_row(value):
    width = value.shape[0]
    return flip(jnp.broadcast_to(jnp.sum(value, axis=1, keepdims=True), (width, width)))


def scatter_blocks(stage, outs):
    shards = len(outs)
    here = lax.axis_index("fsdp")
    for place, out in enumerate(outs):
        out[...] = stage[lax.rem(here + place, shards)]


def whole(gathered, start, rows):
    shards = gathered.shape[0]
    return gathered[:, start : start + rows, :].reshape(shards * rows, gathered.shape[2])


def function_weight(presence, item, func, funcs, shape):
    total = presence[item, 0]
    for other in range(1, funcs):
        total = total + presence[item, other]
    own = jnp.full(shape, presence[item, func], jnp.int32).astype(f32)
    return own / jnp.full(shape, total, jnp.int32).astype(f32)


def pack_kernel(*refs):
    weights, vectors, gate = refs[:10], refs[10:14], refs[14]
    early, late = refs[15:]
    keys, values, query, out, query_two, key_two, value_two, out_two, enter, leave = weights
    start = 0
    for weight in (keys, values):
        early[start : start + weight.shape[0]] = weight[...]
        start += weight.shape[0]
    start = 0
    for weight in (query, out, query_two, key_two, value_two, out_two):
        late[start : start + weight.shape[0]] = weight[...]
        start += weight.shape[0]
    experts, piece, hidden = enter.shape
    width = late.shape[1]
    for expert in range(experts):
        for half in range(hidden // width):
            late[start : start + piece] = enter[expert, :, half * width : (half + 1) * width]
            start += piece
    for expert in range(experts):
        late[start : start + leave.shape[1]] = leave[expert]
        start += leave.shape[1]
    rest = jnp.zeros((1, width - piece), f32)
    rows = [
        jnp.concatenate([vector[...].astype(f32), rest], axis=1) for vector in vectors
    ]
    rows.append(jnp.zeros((4, width), f32))
    for row in range(2):
        rows.append(jnp.broadcast_to(gate[row : row + 1, 0:1].astype(f32), (1, width)))
    rows.append(jnp.zeros((6, width), f32))
    late[start : start + 16] = jnp.concatenate(rows, axis=0).astype(bf16)


def points_forward(counts, presence, points, *refs, funcs, shards):
    parts = refs[:shards]
    state_t, state, keys_out, values_out, gathered, weight = refs[shards:]
    item = pl.program_id(0)
    width = points.shape[2]
    slots = points.shape[1]
    piece = width // shards

    @pl.when(item == 0)
    def _():
        assemble(parts, gathered)
        weight[:width] = flip(whole(gathered, 0, piece))
        weight[width:] = flip(whole(gathered, piece, piece))

    def project(func):
        both = nt(weight[...], points[func])
        slot = lax.broadcasted_iota(jnp.int32, (1, slots), 1)
        probs = head_softmax(both[:width])
        keys_out[func] = jnp.where(slot < counts[item, func], probs, 0.0).astype(bf16)
        values_out[func] = both[width:].astype(bf16)

    def summarize(func):
        values = values_out[func]
        extended = jnp.concatenate([values, jnp.ones_like(values)], axis=0)
        share = function_weight(presence, item, func, funcs, (1, width))
        mask = same_head(width, width, width)
        summed = nt(keys_out[func], extended)
        left = jnp.where(mask, summed[:, :width], 0.0) * share
        right = jnp.where(mask, summed[:, width:], 0.0)
        state[func, :, :width] = left.astype(bf16)
        state[func, :, width:] = (-right).astype(bf16)
        state_t[func, :width] = flip(left).astype(bf16)
        state_t[func, width:] = flip(right).astype(bf16)

    for func in range(funcs):
        project(func)
    for func in range(funcs):
        summarize(func)


def main_kernel(tokens, cotangent, coords, state_t, *refs, funcs, experts, shards, at):
    parts, outs, scratch = refs[:shards], refs[shards : 2 * shards + 9], refs[2 * shards + 9 :]
    (
        result,
        queries_out,
        cross_out,
        first_out,
        keys_out,
        values_out,
        grad_q_out,
        grad_second_out,
        grad_state_out,
    ) = outs[:9]
    grads_out = outs[9:]
    (
        params,
        grads_stage,
        first_keep,
        query_keep,
        state_sum,
        self_t,
        self_state,
        grad_state_sum,
        w_query,
        w_out_one,
        w_self,
        w_out_two_t,
        w_out_two,
        w_in_t,
        w_in,
        w_exit,
        w_exit_t,
        gain_one,
        bias_one,
        gain_two,
        bias_two,
        hidden_keep,
        inner_keep,
        normed_keep,
        grad_keep,
        own_keep,
        pair_keep,
        sum_in,
        sum_exit,
        sum_out_two,
        sum_gain,
        sum_bias,
        sum_gate,
    ) = scratch
    item = pl.program_id(0)
    phase = pl.program_id(1)
    step = pl.program_id(2)
    steps = pl.num_programs(2)
    width = tokens.shape[1]
    rows = tokens.shape[0]
    piece = width // shards
    hidden = w_in.shape[1] // experts
    exit_piece = hidden // shards

    @pl.when((item == 0) & (phase == 0) & (step == 0))
    def _():
        assemble(parts, params)
        w_query[...] = flip(whole(params, at["query_first"], piece))
        w_out_one[...] = flip(whole(params, at["out_first"], piece))
        w_self[:width] = flip(whole(params, at["query_second"], piece))
        w_self[width : 2 * width] = flip(whole(params, at["key_second"], piece))
        w_self[2 * width :] = flip(whole(params, at["value_second"], piece))
        out_two = whole(params, at["out_second"], piece)
        w_out_two[...] = out_two
        w_out_two_t[...] = flip(out_two)
        for block in range(experts * hidden // width):
            part = whole(params, at["expert_in"] + block * piece, piece)
            w_in[:, block * width : (block + 1) * width] = part
            w_in_t[block * width : (block + 1) * width] = flip(part)
        for expert in range(experts):
            part = whole(params, at["expert_out"] + expert * exit_piece, exit_piece)
            w_exit[expert * hidden : (expert + 1) * hidden] = part
            w_exit_t[:, expert * hidden : (expert + 1) * hidden] = flip(part)
        found = columns(params, at["small"], 4)
        for vector, column in zip((gain_one, bias_one, gain_two, bias_two), found):
            vector[...] = jnp.broadcast_to(column, vector.shape)
        sum_in[...] = jnp.zeros_like(sum_in)
        sum_exit[...] = jnp.zeros_like(sum_exit)
        sum_out_two[...] = jnp.zeros_like(sum_out_two)
        sum_gain[...] = jnp.zeros_like(sum_gain)
        sum_bias[...] = jnp.zeros_like(sum_bias)
        sum_gate[...] = jnp.zeros_like(sum_gate)

    chunks = [slice(start, start + CHUNK) for start in range(0, rows, CHUNK)]

    @pl.when(phase == 0)
    def _():
        def enter(cols):
            rows_t = flip(tokens[cols, :]).astype(f32)
            hat, _scale = standardize(rows_t)
            normed = (hat * gain_one[...] + bias_one[...]).astype(bf16)
            return rows_t, head_softmax(nn(w_query[...], normed)).astype(bf16)

        def across(cols, queries):
            queries_out[0, :, cols] = queries
            mixed = None
            for func in range(funcs):
                both = nn(state_t[func], queries)
                part = both[:width] * inverse(both[width:])
                mixed = part if mixed is None else mixed + part
            cross = mixed.astype(bf16)
            cross_out[0, :, cols] = cross
            return cross

        def leave(cols, rows_t, cross):
            first = rows_t + nn(w_out_one[...], cross)
            first_keep[step, :, cols] = first
            first_low = first.astype(bf16)
            first_out[0, :, cols] = first_low
            return first_low

        def project(cols, first_low):
            three = nn(w_self[...], first_low)
            query_keep[step, :, cols] = head_softmax(three[:width]).astype(bf16)
            keys_out[0, :, cols] = head_softmax(three[width : 2 * width]).astype(bf16)
            values = three[2 * width :].astype(bf16)
            values_out[0, :, cols] = values
            pair_keep[:width, cols] = values
            pair_keep[width:, cols] = jnp.ones_like(values)

        entered = [enter(cols) for cols in chunks]
        crossed = [across(cols, queries) for cols, (_, queries) in zip(chunks, entered)]
        firsts = [
            leave(cols, rows_t, cross)
            for cols, (rows_t, _), cross in zip(chunks, entered, crossed)
        ]
        for cols, first_low in zip(chunks, firsts):
            project(cols, first_low)
        found = nt(keys_out[0], pair_keep[...])

        @pl.when(step == 0)
        def _():
            state_sum[...] = found

        @pl.when(step > 0)
        def _():
            state_sum[...] += found

        @pl.when(step == steps - 1)
        def _():
            mask = same_head(width, width, width)
            left = jnp.where(mask, state_sum[:, :width], 0.0)
            right = jnp.where(mask, state_sum[:, width:], 0.0)
            self_state[:, :width] = left.astype(bf16)
            self_state[:, width:] = (-right).astype(bf16)
            self_t[:width] = flip(left).astype(bf16)
            self_t[width:] = flip(right).astype(bf16)

    @pl.when(phase == 1)
    def _():
        def attend(cols):
            both = nn(self_t[...], query_keep[step, :, cols])
            undo = inverse(both[width:])
            own = both[:width] * undo
            own_keep[:, cols] = own.astype(bf16)
            grad_keep[:, cols] = flip(cotangent[cols, :])
            return undo, own

        def norm(cols):
            second = first_keep[step, :, cols] + nn(w_out_two_t[...], own_keep[:, cols])
            hat, scale = standardize(second)
            normed_keep[:, cols] = (hat * gain_two[...] + bias_two[...]).astype(bf16)
            return second, hat, scale

        def gate(cols):
            across, down = coords[0:1, cols], coords[1:2, cols]
            logits = []
            for expert in range(experts):
                pair = params[expert, at["small"] : at["small"] + 16, 0:1].astype(f32)
                logits.append(across * pair[8:9] + down * pair[9:10])
            peak = logits[0]
            for logit in logits[1:]:
                peak = jnp.maximum(peak, logit)
            raised = [jnp.exp(logit - peak) for logit in logits]
            total = raised[0]
            for other in raised[1:]:
                total = total + other
            return [other / total for other in raised]

        def expand(cols, gates):
            normed, grad = normed_keep[:, cols], grad_keep[:, cols]
            grad_gates = []
            for expert in range(experts):
                partial_sum = None
                for start in range(expert * hidden, (expert + 1) * hidden, SLAB):
                    span = slice(start, start + SLAB)
                    inner = nn(w_in_t[span], normed)
                    back = nn(w_exit[span], grad)
                    square = inner * inner
                    tanh = jnp.tanh(inner * (0.7978845608028654 + 0.035677408136300125 * square))
                    half = 0.5 + 0.5 * tanh
                    active = inner * half
                    folded = jnp.sum((active * back).reshape(SLAB // 8, 8, CHUNK), axis=0)
                    partial_sum = folded if partial_sum is None else partial_sum + folded
                    hidden_keep[span, cols] = (active * gates[expert]).astype(bf16)
                    slope = half + active * (1.0 - half) * (
                        1.5957691216057308 + 0.21406444881780074 * square
                    )
                    inner_keep[span, cols] = (slope * (back * gates[expert])).astype(bf16)
                grad_gates.append(jnp.sum(partial_sum, axis=0, keepdims=True))
            across, down = coords[0:1, cols], coords[1:2, cols]
            mean_gate = gates[0] * grad_gates[0]
            for expert in range(1, experts):
                mean_gate = mean_gate + gates[expert] * grad_gates[expert]
            for expert in range(experts):
                change = gates[expert] * (grad_gates[expert] - mean_gate)
                sum_gate[expert : expert + 1, cols] += across * change
                sum_gate[experts + expert : experts + expert + 1, cols] += down * change

        def contract(cols, second, hat, scale):
            total = second + nn(w_exit_t[...], hidden_keep[:, cols])
            result[cols, :] = flip(total.astype(bf16))
            grad_normed = nn(w_in[...], inner_keep[:, cols])
            sum_gain[...] += lane_fold(grad_normed * hat)
            sum_bias[...] += lane_fold(grad_normed)
            grad_second = grad_keep[:, cols].astype(f32) + norm_back(
                grad_normed * gain_two[...], hat, scale
            )
            grad_own = grad_second.astype(bf16)
            grad_second_out[0, :, cols] = grad_own
            return grad_own

        def attend_back(cols, grad_own, undo, own):
            share = nn(w_out_two[...], grad_own) * undo
            pair_keep[:width, cols] = share.astype(bf16)
            pair_keep[width:, cols] = (share * own).astype(bf16)

        def query_back(cols):
            grad_q = nn(self_state[...], pair_keep[:, cols])
            grad_q_out[0, :, cols] = softmax_back(query_keep[step, :, cols], grad_q).astype(bf16)

        attended = [attend(cols) for cols in chunks]
        normed = [norm(cols) for cols in chunks]
        gates = [gate(cols) for cols in chunks]
        for cols, own_gates in zip(chunks, gates):
            expand(cols, own_gates)
        grads = [contract(cols, *kept) for cols, kept in zip(chunks, normed)]
        for cols, grad_own, (undo, own) in zip(chunks, grads, attended):
            attend_back(cols, grad_own, undo, own)
        for cols in chunks:
            query_back(cols)
        sum_exit[...] += nn(hidden_keep[...], cotangent[...])
        sum_in[...] += nt(inner_keep[...], normed_keep[...])
        sum_out_two[...] += nt(own_keep[...], grad_second_out[0])
        found = nt(query_keep[step], pair_keep[...])

        @pl.when(step == 0)
        def _():
            grad_state_sum[...] = found

        @pl.when(step > 0)
        def _():
            grad_state_sum[...] += found

        @pl.when(step == steps - 1)
        def _():
            grad_state_out[0] = grad_state_sum[...]

    @pl.when((item == pl.num_programs(0) - 1) & (phase == 1) & (step == steps - 1))
    def _():
        gain, bias = as_row(sum_gain[...]), as_row(sum_bias[...])
        gate = jnp.broadcast_to(jnp.sum(sum_gate[...], axis=1, keepdims=True), (8, width))
        row = lax.broadcasted_iota(jnp.int32, (8, width), 0)
        vectors = jnp.where(row == 0, gain[:8], bias[:8])
        small = jnp.concatenate([vectors, gate], axis=0).astype(bf16)
        start = 0
        for block in range(experts * hidden // width):
            part = flip(sum_in[block * width : (block + 1) * width]).astype(bf16)
            grads_stage[:, start : start + piece, :] = part.reshape(shards, piece, width)
            start += piece
        for expert in range(experts):
            part = sum_exit[expert * hidden : (expert + 1) * hidden].astype(bf16)
            grads_stage[:, start : start + exit_piece, :] = part.reshape(shards, exit_piece, width)
            start += exit_piece
        part = sum_out_two[...].astype(bf16)
        grads_stage[:, start : start + piece, :] = part.reshape(shards, piece, width)
        start += piece
        for shard in range(shards):
            grads_stage[shard, start : start + 16, :] = small
        scatter_blocks(grads_stage, grads_out)


def rest_kernel(
    presence,
    tokens,
    queries_in,
    cross_in,
    first_in,
    keys_in,
    values_in,
    grad_q_in,
    grad_second_in,
    grad_state_in,
    state_t,
    state,
    *refs,
    funcs,
    item,
    shards,
    at,
    first_call,
):
    parts, refs = refs[:shards], refs[shards:]
    if not first_call:
        carry, refs = refs[3], refs[5:]
    (
        grad_tokens,
        grad_cross_state_out,
        grad_totals_out,
        sums_out,
        params,
        w_self,
        w_out_one,
        w_query,
        gain_one,
        bias_one,
        grad_self_state,
        grad_totals,
        grad_state_sum,
        sums,
        three_keep,
        cross_keep,
        stack_keep,
        query_keep,
        normed_keep,
    ) = refs
    step = pl.program_id(0)
    steps = pl.num_programs(0)
    width = tokens.shape[1]
    piece = width // shards
    self_part = slice(0, 3 * width)
    out_part = slice(3 * width, 4 * width)
    query_part = slice(4 * width, 5 * width)
    gain_part = slice(5 * width, 6 * width)
    bias_part = slice(6 * width, 7 * width)

    @pl.when(step == 0)
    def _():
        assemble(parts, params)
        w_query[...] = whole(params, at["query_first"], piece)
        w_out_one[...] = whole(params, at["out_first"], piece)
        w_self[:, :width] = whole(params, at["query_second"], piece)
        w_self[:, width : 2 * width] = whole(params, at["key_second"], piece)
        w_self[:, 2 * width :] = whole(params, at["value_second"], piece)
        for vector, column in zip((gain_one, bias_one), columns(params, at["small"], 2)):
            vector[...] = jnp.broadcast_to(column, vector.shape)
        sums[...] = jnp.zeros_like(sums) if first_call else carry[...]
        mask = same_head(width, width, width)
        left = jnp.where(mask, grad_state_in[0, :, :width], 0.0)
        right = jnp.where(mask, grad_state_in[0, :, width:], 0.0)
        grad_self_state[0] = left.astype(bf16)
        grad_self_state[1] = flip(left).astype(bf16)
        grad_totals[...] = jnp.broadcast_to(
            -jnp.sum(right, axis=1, keepdims=True), grad_totals.shape
        )

    chunks = [slice(start, start + CHUNK) for start in range(0, tokens.shape[0], CHUNK)]

    def self_back(cols):
        keys, values = keys_in[0, :, cols], values_in[0, :, cols]
        grad_keys = nn(grad_self_state[0], values) + grad_totals[...]
        three_keep[:width, cols] = grad_q_in[0, :, cols]
        three_keep[width : 2 * width, cols] = softmax_back(keys, grad_keys).astype(bf16)
        three_keep[2 * width :, cols] = nn(grad_self_state[1], keys).astype(bf16)

    def join(cols):
        grad_first = grad_second_in[0, :, cols].astype(f32) + nn(w_self[...], three_keep[:, cols])
        cross_keep[:, cols] = grad_first.astype(bf16)
        return grad_first

    def cross_back(cols):
        share = nn(w_out_one[...], cross_keep[:, cols])
        for func in range(funcs):
            both = nn(state_t[func], queries_in[0, :, cols])
            undo = inverse(both[width:])
            part = share * undo
            start = 2 * func * width
            stack_keep[start : start + width, cols] = part.astype(bf16)
            stack_keep[start + width : start + 2 * width, cols] = (
                part * (both[:width] * undo)
            ).astype(bf16)

    def query_back(cols):
        joined = jnp.concatenate([state[func] for func in range(funcs)], axis=1)
        grad_q = softmax_back(queries_in[0, :, cols], nn(joined, stack_keep[:, cols]))
        query_keep[:, cols] = grad_q.astype(bf16)

    def finish(cols, grad_first):
        hat, scale = standardize(flip(tokens[cols, :]).astype(f32))
        normed_keep[:, cols] = (hat * gain_one[...] + bias_one[...]).astype(bf16)
        grad_normed = nn(w_query[...], query_keep[:, cols])
        sums[:, gain_part] += lane_fold(grad_normed * hat)
        sums[:, bias_part] += lane_fold(grad_normed)
        grad_rows = grad_first + norm_back(grad_normed * gain_one[...], hat, scale)
        grad_tokens[cols, :] = flip(grad_rows)

    for cols in chunks:
        self_back(cols)
    grad_firsts = [join(cols) for cols in chunks]
    for cols in chunks:
        cross_back(cols)
    for cols in chunks:
        query_back(cols)
    for cols, grad_first in zip(chunks, grad_firsts):
        finish(cols, grad_first)
    sums[:, self_part] += nt(first_in[0], three_keep[...])
    sums[:, out_part] += nt(cross_in[0], cross_keep[...])
    sums[:, query_part] += nt(normed_keep[...], query_keep[...])
    found = nt(queries_in[0], stack_keep[...])

    @pl.when(step == 0)
    def _():
        grad_state_sum[...] = found

    @pl.when(step > 0)
    def _():
        grad_state_sum[...] += found

    @pl.when(step == steps - 1)
    def _():
        mask = same_head(width, width, width)
        for func in range(funcs):
            weight = function_weight(presence, item, func, funcs, (1, width))
            start = 2 * func * width
            left = jnp.where(mask, grad_state_sum[:, start : start + width], 0.0) * weight
            right = jnp.where(mask, grad_state_sum[:, start + width : start + 2 * width], 0.0)
            grad_cross_state_out[func] = left.astype(bf16)
            grad_totals_out[func] = jnp.broadcast_to(
                -jnp.sum(right, axis=1, keepdims=True), (width, width)
            )
        sums_out[...] = sums[...]


def points_back(points, keys_in, values_in, grad_state, grad_totals, carry, _after, *refs, shards):
    outs = refs[:shards]
    sums, stage = refs[shards:]
    step = pl.program_id(0)
    width = points.shape[2]
    piece = width // shards

    def back(func):
        keys, values = keys_in[func], values_in[func]
        left = grad_state[func]
        grad_keys = nn(left, values) + grad_totals[func, :, 0:1]
        grad_k = softmax_back(keys, grad_keys).astype(bf16)
        grad_v = nn(flip(left), keys).astype(bf16)
        return jnp.concatenate([grad_k, grad_v], axis=0)

    grads = [back(func) for func in range(points.shape[0])]
    found = nn(grads[0], points[0])
    for func in range(1, points.shape[0]):
        found = found + nn(grads[func], points[func])

    @pl.when(step == 0)
    def _():
        sums[...] = found
        gain = as_row(carry[:, 5 * width : 6 * width])
        bias = as_row(carry[:, 6 * width : 7 * width])
        row = lax.broadcasted_iota(jnp.int32, (16, width), 0)
        small = jnp.where(row == 0, gain[:16], bias[:16]).astype(bf16)
        for place in range(5):
            part = carry[:, place * width : (place + 1) * width].astype(bf16)
            stage[:, place * piece : (place + 1) * piece, :] = part.reshape(shards, piece, width)
        for shard in range(shards):
            stage[shard, 5 * piece : 5 * piece + 16, :] = small

    @pl.when(step > 0)
    def _():
        sums[...] += found

    @pl.when(step == pl.num_programs(0) - 1)
    def _():
        for place in range(2):
            start = 5 * piece + 16 + place * piece
            part = flip(sums[place * width : (place + 1) * width]).astype(bf16)
            stage[:, start : start + piece, :] = part.reshape(shards, piece, width)
        scatter_blocks(stage, outs)


def total_of(parts):
    value = parts[0][...].astype(f32)
    for part in parts[1:]:
        value = value + part[...].astype(f32)
    return value


def unpack_kernel(*refs, counts, experts, piece, exit_piece, hidden):
    main_parts, parts = refs[: counts[0]], refs[counts[0] : sum(counts)]
    outs, (small, main, rest) = refs[-18:-3], refs[-3:]
    width = main.shape[1]
    main[...] = total_of(main_parts)
    rest[...] = total_of(parts)
    (
        gain_one,
        bias_one,
        query_one,
        key_one,
        value_one,
        out_one,
        query_two,
        key_two,
        value_two,
        out_two,
        gain_two,
        bias_two,
        enter,
        leave,
        gate,
    ) = outs
    start = 0
    for expert in range(experts):
        for half in range(hidden // width):
            block = main[start : start + piece]
            enter[expert, :, half * width : (half + 1) * width] = block
            start += piece
    for expert in range(experts):
        leave[expert] = main[start : start + exit_piece]
        start += exit_piece
    out_two[...] = main[start : start + piece]
    start += piece
    small[:16] = main[start : start + 16]
    start = 0
    for out in (query_two, key_two, value_two, out_one, query_one):
        out[...] = rest[start : start + piece]
        start += piece
    small[16:] = rest[start : start + 16]
    start += 16
    for out in (key_one, value_one):
        out[...] = rest[start : start + piece]
        start += piece
    shard = lax.axis_index("fsdp")
    turned = pltpu.roll(small[...], lax.rem(width - shard * piece, width), 1)
    gain_two[...] = turned[0:1, :piece]
    bias_two[...] = turned[1:2, :piece]
    gain_one[...] = turned[16:17, :piece]
    bias_one[...] = turned[17:18, :piece]
    for row in range(2):
        gate[:, row : row + 1] = small[pl.ds(8 + row * experts + shard, 1), 0:1]


def whole_spec(shape):
    return pl.BlockSpec(shape, lambda *_: (0,) * len(shape))


def route(size, shift, digit, stride):
    def target(i):
        own = i // stride % digit
        return i + ((own + shift) % digit - own) * stride

    return [(i, target(i)) for i in range(size)]


def spread(value, axis, size, digit, stride):
    return [value] + [
        lax.ppermute(value, axis, route(size, shift, digit, stride)) for shift in range(1, digit)
    ]


def exchange(values, axis, size, stride):
    digit = len(values)
    return [values[0]] + [
        lax.ppermute(values[shift], axis, route(size, shift, digit, stride))
        for shift in range(1, digit)
    ]


def digits(size):
    found = []
    stride = 1
    while stride < size:
        rest = size // stride
        digit = 2 if stride == 1 and rest % 2 == 0 else 4 if rest % 4 == 0 else rest
        found.append((digit, stride))
        stride *= digit
    return found or [(1, 1)]


def sum_parts(parts):
    return total_of([part.astype(f32) for part in parts]).astype(bf16)


def shards_fn(
    dp,
    shards,
    tokens,
    points,
    coords,
    presence,
    counts,
    cotangent,
    gain_first,
    bias_first,
    query_first,
    key_first,
    value_first,
    out_first,
    query_second,
    key_second,
    value_second,
    out_second,
    gain_second,
    bias_second,
    expert_in,
    expert_out,
    gate_weight,
):
    count, width = tokens.shape
    items, funcs, slots, _ = points.shape
    length = count // items
    experts, piece, hidden = expert_in.shape
    exit_piece = expert_out.shape[1]
    tile = min(TILE, length)
    steps = length // tile
    inner = experts * hidden
    enter_rows = experts * piece * (hidden // width)
    limit = pltpu.CompilerParams(vmem_limit_bytes=VMEM)

    at = {}
    place = 0
    for name, size in (
        ("query_first", piece),
        ("out_first", piece),
        ("query_second", piece),
        ("key_second", piece),
        ("value_second", piece),
        ("out_second", piece),
        ("expert_in", enter_rows),
        ("expert_out", experts * exit_piece),
        ("small", 16),
    ):
        at[name] = place
        place += size
    late_rows_count = place
    early_pack, late_pack = pl.pallas_call(
        pack_kernel,
        out_shape=[
            jax.ShapeDtypeStruct((2 * piece, width), bf16),
            jax.ShapeDtypeStruct((late_rows_count, width), bf16),
        ],
        name="pack",
    )(
        key_first,
        value_first,
        query_first,
        out_first,
        query_second,
        key_second,
        value_second,
        out_second,
        expert_in,
        expert_out,
        *(
            vector.reshape(1, piece)
            for vector in (gain_first, bias_first, gain_second, bias_second)
        ),
        gate_weight,
    )
    early_parts = spread(early_pack, "fsdp", shards, shards, 1)
    late_parts = spread(late_pack, "fsdp", shards, shards, 1)
    late_specs = [whole_spec((late_rows_count, width))] * shards
    gathered = pltpu.VMEM((shards, late_rows_count, width), bf16)

    smem = pl.BlockSpec(memory_space=pltpu.SMEM)
    units = items * funcs
    flat_points = points.reshape(units, slots, width)
    state_t, state, keys_one, values_one = pl.pallas_call(
        partial(points_forward, funcs=funcs, shards=shards),
        grid=(items,),
        in_specs=[smem, smem, pl.BlockSpec((funcs, slots, width), lambda u: (u, 0, 0))]
        + [whole_spec((2 * piece, width))] * shards,
        out_specs=[
            pl.BlockSpec((funcs, 2 * width, width), lambda u: (u, 0, 0)),
            pl.BlockSpec((funcs, width, 2 * width), lambda u: (u, 0, 0)),
            pl.BlockSpec((funcs, width, slots), lambda u: (u, 0, 0)),
            pl.BlockSpec((funcs, width, slots), lambda u: (u, 0, 0)),
        ],
        out_shape=[
            jax.ShapeDtypeStruct((units, 2 * width, width), bf16),
            jax.ShapeDtypeStruct((units, width, 2 * width), bf16),
            jax.ShapeDtypeStruct((units, width, slots), bf16),
            jax.ShapeDtypeStruct((units, width, slots), bf16),
        ],
        scratch_shapes=[
            pltpu.VMEM((shards, 2 * piece, width), bf16),
            pltpu.VMEM((2 * width, width), bf16),
        ],
        compiler_params=limit,
        cost_estimate=cost(8),
        name="points_forward",
    )(counts, presence, flat_points, *early_parts)

    kept = jax.ShapeDtypeStruct((items * steps, width, tile), bf16)
    main_rows = enter_rows + experts * exit_piece + piece + 16

    def early(i, p, j):
        return i * steps + jnp.where(p == 0, j, steps - 1)

    def late(i, p, j):
        return i * steps + jnp.where(p == 0, 0, j)

    early_keep = pl.BlockSpec((1, width, tile), lambda i, p, j: (early(i, p, j), 0, 0))
    late_keep = pl.BlockSpec((1, width, tile), lambda i, p, j: (late(i, p, j), 0, 0))
    late_rows = pl.BlockSpec((tile, width), lambda i, p, j: (late(i, p, j), 0))
    (
        result,
        queries_one,
        cross,
        first,
        keys_two,
        values_two,
        grad_q_two,
        grad_second,
        grad_state_two,
        *main_grads,
    ) = pl.pallas_call(
        partial(main_kernel, funcs=funcs, experts=experts, shards=shards, at=at),
        grid=(items, 2, steps),
        in_specs=[
            pl.BlockSpec((tile, width), lambda i, p, j: (early(i, p, j), 0)),
            late_rows,
            pl.BlockSpec((2, tile), lambda i, p, j: (0, late(i, p, j))),
            pl.BlockSpec((funcs, 2 * width, width), lambda i, p, j: (i, 0, 0)),
        ]
        + late_specs,
        out_specs=[
            late_rows,
            early_keep,
            early_keep,
            early_keep,
            early_keep,
            early_keep,
            late_keep,
            late_keep,
            pl.BlockSpec((1, width, 2 * width), lambda i, p, j: (i, 0, 0)),
        ]
        + [whole_spec((main_rows, width))] * shards,
        out_shape=[
            jax.ShapeDtypeStruct((count, width), bf16),
            kept,
            kept,
            kept,
            kept,
            kept,
            kept,
            kept,
            jax.ShapeDtypeStruct((items, width, 2 * width), f32),
        ]
        + [jax.ShapeDtypeStruct((main_rows, width), bf16)] * shards,
        scratch_shapes=[
            gathered,
            pltpu.VMEM((shards, main_rows, width), bf16),
            pltpu.VMEM((steps, width, tile), f32),
            pltpu.VMEM((steps, width, tile), bf16),
            pltpu.VMEM((width, 2 * width), f32),
            pltpu.VMEM((2 * width, width), bf16),
            pltpu.VMEM((width, 2 * width), bf16),
            pltpu.VMEM((width, 2 * width), f32),
            pltpu.VMEM((width, width), bf16),
            pltpu.VMEM((width, width), bf16),
            pltpu.VMEM((3 * width, width), bf16),
            pltpu.VMEM((width, width), bf16),
            pltpu.VMEM((width, width), bf16),
            pltpu.VMEM((inner, width), bf16),
            pltpu.VMEM((width, inner), bf16),
            pltpu.VMEM((inner, width), bf16),
            pltpu.VMEM((width, inner), bf16),
            pltpu.VMEM((width, CHUNK), f32),
            pltpu.VMEM((width, CHUNK), f32),
            pltpu.VMEM((width, CHUNK), f32),
            pltpu.VMEM((width, CHUNK), f32),
            pltpu.VMEM((inner, tile), bf16),
            pltpu.VMEM((inner, tile), bf16),
            pltpu.VMEM((width, tile), bf16),
            pltpu.VMEM((width, tile), bf16),
            pltpu.VMEM((width, tile), bf16),
            pltpu.VMEM((2 * width, tile), bf16),
            pltpu.VMEM((inner, width), f32),
            pltpu.VMEM((inner, width), f32),
            pltpu.VMEM((width, width), f32),
            pltpu.VMEM((width, width), f32),
            pltpu.VMEM((width, width), f32),
            pltpu.VMEM((2 * experts, tile), f32),
        ],
        compiler_params=limit,
        cost_estimate=cost(80),
        name="main",
    )(tokens, cotangent, coords, state_t, *late_parts)

    rest_rows = 7 * piece + 16

    def rest_call(item, earlier, after):
        first_call = item == 0
        keep_spec = pl.BlockSpec((1, width, tile), lambda j: (item * steps + j, 0, 0))
        row_spec = pl.BlockSpec((tile, width), lambda j: (item * steps + j, 0))
        unit_spec = pl.BlockSpec((funcs, width, width), lambda j: (item, 0, 0))
        anywhere = pl.BlockSpec(memory_space=pl.ANY)
        in_specs = [
            smem,
            row_spec,
            keep_spec,
            keep_spec,
            keep_spec,
            keep_spec,
            keep_spec,
            keep_spec,
            keep_spec,
            pl.BlockSpec((1, width, 2 * width), lambda j: (item, 0, 0)),
            pl.BlockSpec((funcs, 2 * width, width), lambda j: (item, 0, 0)),
            pl.BlockSpec((funcs, width, 2 * width), lambda j: (item, 0, 0)),
        ] + late_specs
        operands = [
            presence,
            tokens,
            queries_one,
            cross,
            first,
            keys_two,
            values_two,
            grad_q_two,
            grad_second,
            grad_state_two,
            state_t,
            state,
            *late_parts,
        ]
        aliases = {}
        if not first_call:
            aliases = {len(operands) + k: k for k in range(3)}
            in_specs += [anywhere] * 3 + [whole_spec((width, 7 * width)), anywhere]
            operands += [*earlier, after]
        out_specs = [row_spec, unit_spec, unit_spec, whole_spec((width, 7 * width))]
        out_shape = [
            jax.ShapeDtypeStruct((count, width), f32),
            jax.ShapeDtypeStruct((units, width, width), bf16),
            jax.ShapeDtypeStruct((units, width, width), f32),
            jax.ShapeDtypeStruct((width, 7 * width), f32),
        ]
        return pl.pallas_call(
            partial(
                rest_kernel,
                funcs=funcs,
                item=item,
                shards=shards,
                at=at,
                first_call=first_call,
            ),
            grid=(steps,),
            in_specs=in_specs,
            out_specs=out_specs,
            out_shape=out_shape,
            input_output_aliases=aliases,
            scratch_shapes=[
                gathered,
                pltpu.VMEM((width, 3 * width), bf16),
                pltpu.VMEM((width, width), bf16),
                pltpu.VMEM((width, width), bf16),
                pltpu.VMEM((width, CHUNK), f32),
                pltpu.VMEM((width, CHUNK), f32),
                pltpu.VMEM((2, width, width), bf16),
                pltpu.VMEM((width, CHUNK), f32),
                pltpu.VMEM((width, 2 * funcs * width), f32),
                pltpu.VMEM((width, 7 * width), f32),
                pltpu.VMEM((3 * width, tile), bf16),
                pltpu.VMEM((width, tile), bf16),
                pltpu.VMEM((2 * funcs * width, tile), bf16),
                pltpu.VMEM((width, tile), bf16),
                pltpu.VMEM((width, tile), bf16),
            ],
            compiler_params=limit,
            cost_estimate=cost(18),
            name="rest",
        )(*operands)

    levels = digits(dp)
    main_levels = levels[::-1]
    main_parts = exchange(main_grads, "fsdp", shards, 1)
    level = 0
    found = None
    for item in range(items):
        found = rest_call(item, found, main_sum if item else None)
        if item < len(main_levels):
            main_sum = sum_parts(main_parts)
            main_parts = spread(main_sum, "dp", dp, *main_levels[item])
            level = item + 1
    grad_tokens, grad_state_one, grad_totals_one, carry = found

    rest_grads = pl.pallas_call(
        partial(points_back, shards=shards),
        grid=(items,),
        in_specs=[
            pl.BlockSpec((funcs, slots, width), lambda u: (u, 0, 0)),
            pl.BlockSpec((funcs, width, slots), lambda u: (u, 0, 0)),
            pl.BlockSpec((funcs, width, slots), lambda u: (u, 0, 0)),
            pl.BlockSpec((funcs, width, width), lambda u: (u, 0, 0)),
            pl.BlockSpec((funcs, width, width), lambda u: (u, 0, 0)),
            whole_spec((width, 7 * width)),
            pl.BlockSpec(memory_space=pl.ANY),
        ],
        out_specs=[whole_spec((rest_rows, width))] * shards,
        out_shape=[jax.ShapeDtypeStruct((rest_rows, width), bf16)] * shards,
        scratch_shapes=[
            pltpu.VMEM((2 * width, width), f32),
            pltpu.VMEM((shards, rest_rows, width), bf16),
        ],
        compiler_params=limit,
        cost_estimate=cost(7),
        name="points_back",
    )(flat_points, keys_one, values_one, grad_state_one, grad_totals_one, carry, main_sum)
    rest_got = exchange(rest_grads, "fsdp", shards, 1)

    parts = rest_got
    for digit, stride in main_levels[level:]:
        main_parts = spread(sum_parts(main_parts), "dp", dp, digit, stride)
    for digit, stride in levels:
        parts = spread(sum_parts(parts), "dp", dp, digit, stride)

    matrix = jax.ShapeDtypeStruct((piece, width), f32)
    vector = jax.ShapeDtypeStruct((1, piece), f32)
    outs = pl.pallas_call(
        partial(
            unpack_kernel,
            counts=(len(main_parts), len(parts)),
            experts=experts,
            piece=piece,
            exit_piece=exit_piece,
            hidden=hidden,
        ),
        out_shape=[vector] * 2
        + [matrix] * 8
        + [vector] * 2
        + [
            jax.ShapeDtypeStruct(expert_in.shape, f32),
            jax.ShapeDtypeStruct(expert_out.shape, f32),
            jax.ShapeDtypeStruct((1, 2), f32),
        ],
        scratch_shapes=[
            pltpu.VMEM((32, width), f32),
            pltpu.VMEM((main_rows, width), f32),
            pltpu.VMEM((rest_rows, width), f32),
        ],
        name="unpack",
    )(*main_parts, *parts)
    outs = [out.reshape(piece) if out.shape == (1, piece) else out for out in outs]
    return (result, grad_tokens, *outs[:-1], outs[-1].reshape(gate_weight.shape))


def solution(mesh):
    rows = P(("dp", "fsdp"), None)
    matrix = P("fsdp", None)
    vector = P("fsdp")
    expert = P(None, "fsdp", None)
    parameters = (
        (vector, vector)
        + (matrix,) * 8
        + (vector, vector, expert, expert, P(None, "fsdp"))
    )
    return jax.shard_map(
        partial(shards_fn, mesh.shape["dp"], mesh.shape["fsdp"]),
        mesh=mesh,
        in_specs=(
            rows,
            P(("dp", "fsdp"), None, None, None),
            P(None, ("dp", "fsdp")),
            rows,
            rows,
            rows,
        )
        + parameters,
        out_specs=(rows, rows) + parameters,
        check_vma=False,
    )
```

```python
from functools import partial

import jax
import jax.numpy as jnp
from jax import lax
from jax.experimental import pallas as pl
from jax.experimental.pallas import tpu as pltpu
from jax.sharding import PartitionSpec as P


HEADS = 8
eps = 1e-05
f32 = jnp.float32
bf16 = jnp.bfloat16
TILE = 1024
CHUNK = 256
SLAB = 64
VMEM = 56 * 1024 * 1024


def cost(microseconds):
    return pl.CostEstimate(flops=microseconds * 10**9, bytes_accessed=10**6, transcendentals=0)


def nn(left, right):
    return jnp.dot(left, right, preferred_element_type=f32)


def nt(left, right):
    return lax.dot_general(left, right, (((1,), (1,)), ((), ())), preferred_element_type=f32)


def flip(value):
    return value.T


def inverse(value):
    return pl.reciprocal(value, approx=True)


def head_softmax(value):
    width, rows = value.shape
    split = value.reshape(HEADS, width // HEADS, rows)
    raised = jnp.exp(split - jnp.max(split, axis=1, keepdims=True))
    return (raised * inverse(jnp.sum(raised, axis=1, keepdims=True))).reshape(width, rows)


def softmax_back(probs, grad):
    width, rows = grad.shape
    probs = probs.astype(f32).reshape(HEADS, width // HEADS, rows)
    grad = grad.reshape(HEADS, width // HEADS, rows)
    inner = jnp.sum(probs * grad, axis=1, keepdims=True)
    return (probs * (grad - inner)).reshape(width, rows)


def standardize(value):
    centre = value - jnp.mean(value, axis=0, keepdims=True)
    scale = lax.rsqrt(jnp.mean(centre * centre, axis=0, keepdims=True) + eps)
    return centre * scale, scale


def norm_back(grad, hat, scale):
    return scale * (
        grad
        - jnp.mean(grad, axis=0, keepdims=True)
        - hat * jnp.mean(grad * hat, axis=0, keepdims=True)
    )


def same_head(rows, columns, width):
    head = width // HEADS
    row = lax.rem(lax.broadcasted_iota(jnp.int32, (rows, columns), 0), width)
    column = lax.rem(lax.broadcasted_iota(jnp.int32, (rows, columns), 1), width)
    return lax.div(row, head) == lax.div(column, head)


def assemble(parts, gathered):
    shards = len(parts)
    here = lax.axis_index("fsdp")
    for place, part in enumerate(parts):
        gathered[lax.rem(here + shards - place, shards)] = part[...]


def columns(gathered, start, count):
    shards, _, width = gathered.shape
    piece = width // shards
    small = [gathered[shard, start : start + 16, :].astype(f32) for shard in range(shards)]
    joined = jnp.concatenate([part[:, :piece] for part in small], axis=1)
    return [
        flip(jnp.broadcast_to(joined[place : place + 1], (width, width)))[:, 0:1]
        for place in range(count)
    ]


def lane_fold(value):
    width = value.shape[0]
    total = value[:, :width]
    for start in range(width, value.shape[1], width):
        total = total + value[:, start : start + width]
    return total


def as_row(value):
    width = value.shape[0]
    return flip(jnp.broadcast_to(jnp.sum(value, axis=1, keepdims=True), (width, width)))


def scatter_blocks(stage, outs):
    shards = len(outs)
    here = lax.axis_index("fsdp")
    for place, out in enumerate(outs):
        out[...] = stage[lax.rem(here + place, shards)]


def whole(gathered, start, rows):
    shards = gathered.shape[0]
    return gathered[:, start : start + rows, :].reshape(shards * rows, gathered.shape[2])


def function_weight(presence, item, func, funcs, shape):
    total = presence[item, 0]
    for other in range(1, funcs):
        total = total + presence[item, other]
    own = jnp.full(shape, presence[item, func], jnp.int32).astype(f32)
    return own / jnp.full(shape, total, jnp.int32).astype(f32)


def pack_kernel(*refs):
    weights, vectors, gate = refs[:10], refs[10:14], refs[14]
    early, late = refs[15:]
    keys, values, query, out, query_two, key_two, value_two, out_two, enter, leave = weights
    start = 0
    for weight in (keys, values):
        early[start : start + weight.shape[0]] = weight[...]
        start += weight.shape[0]
    start = 0
    for weight in (query, out, query_two, key_two, value_two, out_two):
        late[start : start + weight.shape[0]] = weight[...]
        start += weight.shape[0]
    experts, piece, hidden = enter.shape
    width = late.shape[1]
    for expert in range(experts):
        for half in range(hidden // width):
            late[start : start + piece] = enter[expert, :, half * width : (half + 1) * width]
            start += piece
    for expert in range(experts):
        late[start : start + leave.shape[1]] = leave[expert]
        start += leave.shape[1]
    rest = jnp.zeros((1, width - piece), f32)
    rows = [
        jnp.concatenate([vector[...].astype(f32), rest], axis=1) for vector in vectors
    ]
    rows.append(jnp.zeros((4, width), f32))
    for row in range(2):
        rows.append(jnp.broadcast_to(gate[row : row + 1, 0:1].astype(f32), (1, width)))
    rows.append(jnp.zeros((6, width), f32))
    late[start : start + 16] = jnp.concatenate(rows, axis=0).astype(bf16)


def points_forward(counts, presence, points, *refs, funcs, shards):
    parts = refs[:shards]
    state_t, state, keys_out, values_out, gathered, weight = refs[shards:]
    item = pl.program_id(0)
    width = points.shape[2]
    slots = points.shape[1]
    piece = width // shards

    @pl.when(item == 0)
    def _():
        assemble(parts, gathered)
        weight[:width] = flip(whole(gathered, 0, piece))
        weight[width:] = flip(whole(gathered, piece, piece))

    def project(func):
        both = nt(weight[...], points[func])
        slot = lax.broadcasted_iota(jnp.int32, (1, slots), 1)
        probs = head_softmax(both[:width])
        keys_out[func] = jnp.where(slot < counts[item, func], probs, 0.0).astype(bf16)
        values_out[func] = both[width:].astype(bf16)

    def summarize(func):
        values = values_out[func]
        extended = jnp.concatenate([values, jnp.ones_like(values)], axis=0)
        share = function_weight(presence, item, func, funcs, (1, width))
        mask = same_head(width, width, width)
        summed = nt(keys_out[func], extended)
        left = jnp.where(mask, summed[:, :width], 0.0) * share
        right = jnp.where(mask, summed[:, width:], 0.0)
        state[func, :, :width] = left.astype(bf16)
        state[func, :, width:] = (-right).astype(bf16)
        state_t[func, :width] = flip(left).astype(bf16)
        state_t[func, width:] = flip(right).astype(bf16)

    for func in range(funcs):
        project(func)
    for func in range(funcs):
        summarize(func)


def main_kernel(tokens, cotangent, coords, state_t, *refs, funcs, experts, shards, at):
    parts, outs, scratch = refs[:shards], refs[shards : 2 * shards + 9], refs[2 * shards + 9 :]
    (
        result,
        queries_out,
        cross_out,
        first_out,
        keys_out,
        values_out,
        grad_q_out,
        grad_second_out,
        grad_state_out,
    ) = outs[:9]
    grads_out = outs[9:]
    (
        params,
        grads_stage,
        first_keep,
        query_keep,
        state_sum,
        self_t,
        self_state,
        grad_state_sum,
        w_query,
        w_out_one,
        w_self,
        w_out_two_t,
        w_out_two,
        w_in_t,
        w_in,
        w_exit,
        w_exit_t,
        gain_one,
        bias_one,
        gain_two,
        bias_two,
        hidden_keep,
        inner_keep,
        normed_keep,
        grad_keep,
        own_keep,
        pair_keep,
        sum_in,
        sum_exit,
        sum_out_two,
        sum_gain,
        sum_bias,
        sum_gate,
    ) = scratch
    item = pl.program_id(0)
    phase = pl.program_id(1)
    step = pl.program_id(2)
    steps = pl.num_programs(2)
    width = tokens.shape[1]
    rows = tokens.shape[0]
    piece = width // shards
    hidden = w_in.shape[1] // experts
    exit_piece = hidden // shards

    @pl.when((item == 0) & (phase == 0) & (step == 0))
    def _():
        assemble(parts, params)
        w_query[...] = flip(whole(params, at["query_first"], piece))
        w_out_one[...] = flip(whole(params, at["out_first"], piece))
        w_self[:width] = flip(whole(params, at["query_second"], piece))
        w_self[width : 2 * width] = flip(whole(params, at["key_second"], piece))
        w_self[2 * width :] = flip(whole(params, at["value_second"], piece))
        out_two = whole(params, at["out_second"], piece)
        w_out_two[...] = out_two
        w_out_two_t[...] = flip(out_two)
        for block in range(experts * hidden // width):
            part = whole(params, at["expert_in"] + block * piece, piece)
            w_in[:, block * width : (block + 1) * width] = part
            w_in_t[block * width : (block + 1) * width] = flip(part)
        for expert in range(experts):
            part = whole(params, at["expert_out"] + expert * exit_piece, exit_piece)
            w_exit[expert * hidden : (expert + 1) * hidden] = part
            w_exit_t[:, expert * hidden : (expert + 1) * hidden] = flip(part)
        found = columns(params, at["small"], 4)
        for vector, column in zip((gain_one, bias_one, gain_two, bias_two), found):
            vector[...] = jnp.broadcast_to(column, vector.shape)
        sum_in[...] = jnp.zeros_like(sum_in)
        sum_exit[...] = jnp.zeros_like(sum_exit)
        sum_out_two[...] = jnp.zeros_like(sum_out_two)
        sum_gain[...] = jnp.zeros_like(sum_gain)
        sum_bias[...] = jnp.zeros_like(sum_bias)
        sum_gate[...] = jnp.zeros_like(sum_gate)

    chunks = [slice(start, start + CHUNK) for start in range(0, rows, CHUNK)]

    @pl.when(phase == 0)
    def _():
        def enter(cols):
            rows_t = flip(tokens[cols, :]).astype(f32)
            hat, _scale = standardize(rows_t)
            normed = (hat * gain_one[...] + bias_one[...]).astype(bf16)
            return rows_t, head_softmax(nn(w_query[...], normed)).astype(bf16)

        def across(cols, queries):
            queries_out[0, :, cols] = queries
            mixed = None
            for func in range(funcs):
                both = nn(state_t[func], queries)
                part = both[:width] * inverse(both[width:])
                mixed = part if mixed is None else mixed + part
            cross = mixed.astype(bf16)
            cross_out[0, :, cols] = cross
            return cross

        def leave(cols, rows_t, cross):
            first = rows_t + nn(w_out_one[...], cross)
            first_keep[step, :, cols] = first
            first_low = first.astype(bf16)
            first_out[0, :, cols] = first_low
            return first_low

        def project(cols, first_low):
            three = nn(w_self[...], first_low)
            query_keep[step, :, cols] = head_softmax(three[:width]).astype(bf16)
            keys_out[0, :, cols] = head_softmax(three[width : 2 * width]).astype(bf16)
            values = three[2 * width :].astype(bf16)
            values_out[0, :, cols] = values
            pair_keep[:width, cols] = values
            pair_keep[width:, cols] = jnp.ones_like(values)

        entered = [enter(cols) for cols in chunks]
        crossed = [across(cols, queries) for cols, (_, queries) in zip(chunks, entered)]
        firsts = [
            leave(cols, rows_t, cross)
            for cols, (rows_t, _), cross in zip(chunks, entered, crossed)
        ]
        for cols, first_low in zip(chunks, firsts):
            project(cols, first_low)
        found = nt(keys_out[0], pair_keep[...])

        @pl.when(step == 0)
        def _():
            state_sum[...] = found

        @pl.when(step > 0)
        def _():
            state_sum[...] += found

        @pl.when(step == steps - 1)
        def _():
            mask = same_head(width, width, width)
            left = jnp.where(mask, state_sum[:, :width], 0.0)
            right = jnp.where(mask, state_sum[:, width:], 0.0)
            self_state[:, :width] = left.astype(bf16)
            self_state[:, width:] = (-right).astype(bf16)
            self_t[:width] = flip(left).astype(bf16)
            self_t[width:] = flip(right).astype(bf16)

    @pl.when(phase == 1)
    def _():
        def attend(cols):
            both = nn(self_t[...], query_keep[step, :, cols])
            undo = inverse(both[width:])
            own = both[:width] * undo
            own_keep[:, cols] = own.astype(bf16)
            grad_keep[:, cols] = flip(cotangent[cols, :])
            return undo, own

        def norm(cols):
            second = first_keep[step, :, cols] + nn(w_out_two_t[...], own_keep[:, cols])
            hat, scale = standardize(second)
            normed_keep[:, cols] = (hat * gain_two[...] + bias_two[...]).astype(bf16)
            return second, hat, scale

        def gate(cols):
            across, down = coords[0:1, cols], coords[1:2, cols]
            logits = []
            for expert in range(experts):
                pair = params[expert, at["small"] : at["small"] + 16, 0:1].astype(f32)
                logits.append(across * pair[8:9] + down * pair[9:10])
            peak = logits[0]
            for logit in logits[1:]:
                peak = jnp.maximum(peak, logit)
            raised = [jnp.exp(logit - peak) for logit in logits]
            total = raised[0]
            for other in raised[1:]:
                total = total + other
            return [other / total for other in raised]

        def expand(cols, gates):
            normed, grad = normed_keep[:, cols], grad_keep[:, cols]
            gates_low = [gate.astype(bf16) for gate in gates]
            grad_gates = []
            for expert in range(experts):
                partial_sum = None
                for start in range(expert * hidden, (expert + 1) * hidden, SLAB):
                    span = slice(start, start + SLAB)
                    inner = nn(w_in_t[span], normed).astype(bf16)
                    back = nn(w_exit[span], grad).astype(bf16)
                    square = inner * inner
                    tanh = jnp.tanh(inner * (0.7978845608028654 + 0.035677408136300125 * square))
                    half = 0.5 + 0.5 * tanh
                    active = inner * half
                    product = active * back
                    folded = product[:16]
                    for row in range(16, SLAB, 16):
                        folded = folded + product[row : row + 16]
                    folded = folded.astype(f32)
                    partial_sum = folded if partial_sum is None else partial_sum + folded
                    hidden_keep[span, cols] = active * gates_low[expert]
                    slope = half + active * (1.0 - half) * (
                        1.5957691216057308 + 0.21406444881780074 * square
                    )
                    inner_keep[span, cols] = slope * (back * gates_low[expert])
                grad_gates.append(jnp.sum(partial_sum, axis=0, keepdims=True))
            across, down = coords[0:1, cols], coords[1:2, cols]
            mean_gate = gates[0] * grad_gates[0]
            for expert in range(1, experts):
                mean_gate = mean_gate + gates[expert] * grad_gates[expert]
            for expert in range(experts):
                change = gates[expert] * (grad_gates[expert] - mean_gate)
                sum_gate[expert : expert + 1, cols] += across * change
                sum_gate[experts + expert : experts + expert + 1, cols] += down * change

        def contract(cols, second, hat, scale):
            total = second + nn(w_exit_t[...], hidden_keep[:, cols])
            result[cols, :] = flip(total.astype(bf16))
            grad_normed = nn(w_in[...], inner_keep[:, cols])
            sum_gain[...] += lane_fold(grad_normed * hat)
            sum_bias[...] += lane_fold(grad_normed)
            grad_second = grad_keep[:, cols].astype(f32) + norm_back(
                grad_normed * gain_two[...], hat, scale
            )
            grad_own = grad_second.astype(bf16)
            grad_second_out[0, :, cols] = grad_own
            return grad_own

        def attend_back(cols, grad_own, undo, own):
            share = nn(w_out_two[...], grad_own) * undo
            pair_keep[:width, cols] = share.astype(bf16)
            pair_keep[width:, cols] = (share * own).astype(bf16)

        def query_back(cols):
            grad_q = nn(self_state[...], pair_keep[:, cols])
            grad_q_out[0, :, cols] = softmax_back(query_keep[step, :, cols], grad_q).astype(bf16)

        attended = [attend(cols) for cols in chunks]
        normed = [norm(cols) for cols in chunks]
        gates = [gate(cols) for cols in chunks]
        for cols, own_gates in zip(chunks, gates):
            expand(cols, own_gates)
        grads = [contract(cols, *kept) for cols, kept in zip(chunks, normed)]
        for cols, grad_own, (undo, own) in zip(chunks, grads, attended):
            attend_back(cols, grad_own, undo, own)
        for cols in chunks:
            query_back(cols)
        sum_exit[...] += nn(hidden_keep[...], cotangent[...])
        sum_in[...] += nt(inner_keep[...], normed_keep[...])
        sum_out_two[...] += nt(own_keep[...], grad_second_out[0])
        found = nt(query_keep[step], pair_keep[...])

        @pl.when(step == 0)
        def _():
            grad_state_sum[...] = found

        @pl.when(step > 0)
        def _():
            grad_state_sum[...] += found

        @pl.when(step == steps - 1)
        def _():
            grad_state_out[0] = grad_state_sum[...]

    @pl.when((item == pl.num_programs(0) - 1) & (phase == 1) & (step == steps - 1))
    def _():
        gain, bias = as_row(sum_gain[...]), as_row(sum_bias[...])
        gate = jnp.broadcast_to(jnp.sum(sum_gate[...], axis=1, keepdims=True), (8, width))
        row = lax.broadcasted_iota(jnp.int32, (8, width), 0)
        vectors = jnp.where(row == 0, gain[:8], bias[:8])
        small = jnp.concatenate([vectors, gate], axis=0).astype(bf16)
        start = 0
        for block in range(experts * hidden // width):
            part = flip(sum_in[block * width : (block + 1) * width]).astype(bf16)
            grads_stage[:, start : start + piece, :] = part.reshape(shards, piece, width)
            start += piece
        for expert in range(experts):
            part = sum_exit[expert * hidden : (expert + 1) * hidden].astype(bf16)
            grads_stage[:, start : start + exit_piece, :] = part.reshape(shards, exit_piece, width)
            start += exit_piece
        part = sum_out_two[...].astype(bf16)
        grads_stage[:, start : start + piece, :] = part.reshape(shards, piece, width)
        start += piece
        for shard in range(shards):
            grads_stage[shard, start : start + 16, :] = small
        scatter_blocks(grads_stage, grads_out)


def rest_kernel(
    presence,
    tokens,
    queries_in,
    cross_in,
    first_in,
    keys_in,
    values_in,
    grad_q_in,
    grad_second_in,
    grad_state_in,
    state_t,
    state,
    *refs,
    funcs,
    item,
    shards,
    at,
    first_call,
):
    parts, refs = refs[:shards], refs[shards:]
    if not first_call:
        carry, refs = refs[3], refs[5:]
    (
        grad_tokens,
        grad_cross_state_out,
        grad_totals_out,
        sums_out,
        params,
        w_self,
        w_out_one,
        w_query,
        gain_one,
        bias_one,
        grad_self_state,
        grad_totals,
        grad_state_sum,
        sums,
        three_keep,
        cross_keep,
        stack_keep,
        query_keep,
        normed_keep,
    ) = refs
    step = pl.program_id(0)
    steps = pl.num_programs(0)
    width = tokens.shape[1]
    piece = width // shards
    self_part = slice(0, 3 * width)
    out_part = slice(3 * width, 4 * width)
    query_part = slice(4 * width, 5 * width)
    gain_part = slice(5 * width, 6 * width)
    bias_part = slice(6 * width, 7 * width)

    @pl.when(step == 0)
    def _():
        assemble(parts, params)
        w_query[...] = whole(params, at["query_first"], piece)
        w_out_one[...] = whole(params, at["out_first"], piece)
        w_self[:, :width] = whole(params, at["query_second"], piece)
        w_self[:, width : 2 * width] = whole(params, at["key_second"], piece)
        w_self[:, 2 * width :] = whole(params, at["value_second"], piece)
        for vector, column in zip((gain_one, bias_one), columns(params, at["small"], 2)):
            vector[...] = jnp.broadcast_to(column, vector.shape)
        sums[...] = jnp.zeros_like(sums) if first_call else carry[...]
        mask = same_head(width, width, width)
        left = jnp.where(mask, grad_state_in[0, :, :width], 0.0)
        right = jnp.where(mask, grad_state_in[0, :, width:], 0.0)
        grad_self_state[0] = left.astype(bf16)
        grad_self_state[1] = flip(left).astype(bf16)
        grad_totals[...] = jnp.broadcast_to(
            -jnp.sum(right, axis=1, keepdims=True), grad_totals.shape
        )

    chunks = [slice(start, start + CHUNK) for start in range(0, tokens.shape[0], CHUNK)]

    def self_back(cols):
        keys, values = keys_in[0, :, cols], values_in[0, :, cols]
        grad_keys = nn(grad_self_state[0], values) + grad_totals[...]
        three_keep[:width, cols] = grad_q_in[0, :, cols]
        three_keep[width : 2 * width, cols] = softmax_back(keys, grad_keys).astype(bf16)
        three_keep[2 * width :, cols] = nn(grad_self_state[1], keys).astype(bf16)

    def join(cols):
        grad_first = grad_second_in[0, :, cols].astype(f32) + nn(w_self[...], three_keep[:, cols])
        cross_keep[:, cols] = grad_first.astype(bf16)
        return grad_first

    def cross_back(cols):
        share = nn(w_out_one[...], cross_keep[:, cols])
        for func in range(funcs):
            both = nn(state_t[func], queries_in[0, :, cols])
            undo = inverse(both[width:])
            part = share * undo
            start = 2 * func * width
            stack_keep[start : start + width, cols] = part.astype(bf16)
            stack_keep[start + width : start + 2 * width, cols] = (
                part * (both[:width] * undo)
            ).astype(bf16)

    def query_back(cols):
        joined = jnp.concatenate([state[func] for func in range(funcs)], axis=1)
        grad_q = softmax_back(queries_in[0, :, cols], nn(joined, stack_keep[:, cols]))
        query_keep[:, cols] = grad_q.astype(bf16)

    def finish(cols, grad_first):
        hat, scale = standardize(flip(tokens[cols, :]).astype(f32))
        normed_keep[:, cols] = (hat * gain_one[...] + bias_one[...]).astype(bf16)
        grad_normed = nn(w_query[...], query_keep[:, cols])
        sums[:, gain_part] += lane_fold(grad_normed * hat)
        sums[:, bias_part] += lane_fold(grad_normed)
        grad_rows = grad_first + norm_back(grad_normed * gain_one[...], hat, scale)
        grad_tokens[cols, :] = flip(grad_rows)

    for cols in chunks:
        self_back(cols)
    grad_firsts = [join(cols) for cols in chunks]
    for cols in chunks:
        cross_back(cols)
    for cols in chunks:
        query_back(cols)
    for cols, grad_first in zip(chunks, grad_firsts):
        finish(cols, grad_first)
    sums[:, self_part] += nt(first_in[0], three_keep[...])
    sums[:, out_part] += nt(cross_in[0], cross_keep[...])
    sums[:, query_part] += nt(normed_keep[...], query_keep[...])
    found = nt(queries_in[0], stack_keep[...])

    @pl.when(step == 0)
    def _():
        grad_state_sum[...] = found

    @pl.when(step > 0)
    def _():
        grad_state_sum[...] += found

    @pl.when(step == steps - 1)
    def _():
        mask = same_head(width, width, width)
        for func in range(funcs):
            weight = function_weight(presence, item, func, funcs, (1, width))
            start = 2 * func * width
            left = jnp.where(mask, grad_state_sum[:, start : start + width], 0.0) * weight
            right = jnp.where(mask, grad_state_sum[:, start + width : start + 2 * width], 0.0)
            grad_cross_state_out[func] = left.astype(bf16)
            grad_totals_out[func] = jnp.broadcast_to(
                -jnp.sum(right, axis=1, keepdims=True), (width, width)
            )
        sums_out[...] = sums[...]


def points_back(points, keys_in, values_in, grad_state, grad_totals, carry, _after, *refs, shards):
    outs = refs[:shards]
    sums, stage = refs[shards:]
    step = pl.program_id(0)
    width = points.shape[2]
    piece = width // shards

    def back(func):
        keys, values = keys_in[func], values_in[func]
        left = grad_state[func]
        grad_keys = nn(left, values) + grad_totals[func, :, 0:1]
        grad_k = softmax_back(keys, grad_keys).astype(bf16)
        grad_v = nn(flip(left), keys).astype(bf16)
        return jnp.concatenate([grad_k, grad_v], axis=0)

    grads = [back(func) for func in range(points.shape[0])]
    found = nn(grads[0], points[0])
    for func in range(1, points.shape[0]):
        found = found + nn(grads[func], points[func])

    @pl.when(step == 0)
    def _():
        sums[...] = found
        gain = as_row(carry[:, 5 * width : 6 * width])
        bias = as_row(carry[:, 6 * width : 7 * width])
        row = lax.broadcasted_iota(jnp.int32, (16, width), 0)
        small = jnp.where(row == 0, gain[:16], bias[:16]).astype(bf16)
        for place in range(5):
            part = carry[:, place * width : (place + 1) * width].astype(bf16)
            stage[:, place * piece : (place + 1) * piece, :] = part.reshape(shards, piece, width)
        for shard in range(shards):
            stage[shard, 5 * piece : 5 * piece + 16, :] = small

    @pl.when(step > 0)
    def _():
        sums[...] += found

    @pl.when(step == pl.num_programs(0) - 1)
    def _():
        for place in range(2):
            start = 5 * piece + 16 + place * piece
            part = flip(sums[place * width : (place + 1) * width]).astype(bf16)
            stage[:, start : start + piece, :] = part.reshape(shards, piece, width)
        scatter_blocks(stage, outs)


def total_of(parts):
    value = parts[0][...].astype(f32)
    for part in parts[1:]:
        value = value + part[...].astype(f32)
    return value


def unpack_kernel(*refs, counts, experts, piece, exit_piece, hidden):
    main_parts, parts = refs[: counts[0]], refs[counts[0] : sum(counts)]
    outs, (small, main, rest) = refs[-18:-3], refs[-3:]
    width = main.shape[1]
    main[...] = total_of(main_parts)
    rest[...] = total_of(parts)
    (
        gain_one,
        bias_one,
        query_one,
        key_one,
        value_one,
        out_one,
        query_two,
        key_two,
        value_two,
        out_two,
        gain_two,
        bias_two,
        enter,
        leave,
        gate,
    ) = outs
    start = 0
    for expert in range(experts):
        for half in range(hidden // width):
            block = main[start : start + piece]
            enter[expert, :, half * width : (half + 1) * width] = block
            start += piece
    for expert in range(experts):
        leave[expert] = main[start : start + exit_piece]
        start += exit_piece
    out_two[...] = main[start : start + piece]
    start += piece
    small[:16] = main[start : start + 16]
    start = 0
    for out in (query_two, key_two, value_two, out_one, query_one):
        out[...] = rest[start : start + piece]
        start += piece
    small[16:] = rest[start : start + 16]
    start += 16
    for out in (key_one, value_one):
        out[...] = rest[start : start + piece]
        start += piece
    shard = lax.axis_index("fsdp")
    turned = pltpu.roll(small[...], lax.rem(width - shard * piece, width), 1)
    gain_two[...] = turned[0:1, :piece]
    bias_two[...] = turned[1:2, :piece]
    gain_one[...] = turned[16:17, :piece]
    bias_one[...] = turned[17:18, :piece]
    for row in range(2):
        gate[:, row : row + 1] = small[pl.ds(8 + row * experts + shard, 1), 0:1]


def whole_spec(shape):
    return pl.BlockSpec(shape, lambda *_: (0,) * len(shape))


def route(size, shift, digit, stride):
    def target(i):
        own = i // stride % digit
        return i + ((own + shift) % digit - own) * stride

    return [(i, target(i)) for i in range(size)]


def spread(value, axis, size, digit, stride):
    return [value] + [
        lax.ppermute(value, axis, route(size, shift, digit, stride)) for shift in range(1, digit)
    ]


def exchange(values, axis, size, stride):
    digit = len(values)
    return [values[0]] + [
        lax.ppermute(values[shift], axis, route(size, shift, digit, stride))
        for shift in range(1, digit)
    ]


def digits(size):
    found = []
    stride = 1
    while stride < size:
        rest = size // stride
        digit = 2 if stride == 1 and rest % 2 == 0 else 4 if rest % 4 == 0 else rest
        found.append((digit, stride))
        stride *= digit
    return found or [(1, 1)]


def sum_parts(parts):
    return total_of([part.astype(f32) for part in parts]).astype(bf16)


def shards_fn(
    dp,
    shards,
    tokens,
    points,
    coords,
    presence,
    counts,
    cotangent,
    gain_first,
    bias_first,
    query_first,
    key_first,
    value_first,
    out_first,
    query_second,
    key_second,
    value_second,
    out_second,
    gain_second,
    bias_second,
    expert_in,
    expert_out,
    gate_weight,
):
    count, width = tokens.shape
    items, funcs, slots, _ = points.shape
    length = count // items
    experts, piece, hidden = expert_in.shape
    exit_piece = expert_out.shape[1]
    tile = min(TILE, length)
    steps = length // tile
    inner = experts * hidden
    enter_rows = experts * piece * (hidden // width)
    limit = pltpu.CompilerParams(vmem_limit_bytes=VMEM)

    at = {}
    place = 0
    for name, size in (
        ("query_first", piece),
        ("out_first", piece),
        ("query_second", piece),
        ("key_second", piece),
        ("value_second", piece),
        ("out_second", piece),
        ("expert_in", enter_rows),
        ("expert_out", experts * exit_piece),
        ("small", 16),
    ):
        at[name] = place
        place += size
    late_rows_count = place
    early_pack, late_pack = pl.pallas_call(
        pack_kernel,
        out_shape=[
            jax.ShapeDtypeStruct((2 * piece, width), bf16),
            jax.ShapeDtypeStruct((late_rows_count, width), bf16),
        ],
        name="pack",
    )(
        key_first,
        value_first,
        query_first,
        out_first,
        query_second,
        key_second,
        value_second,
        out_second,
        expert_in,
        expert_out,
        *(
            vector.reshape(1, piece)
            for vector in (gain_first, bias_first, gain_second, bias_second)
        ),
        gate_weight,
    )
    early_parts = spread(early_pack, "fsdp", shards, shards, 1)
    late_parts = spread(late_pack, "fsdp", shards, shards, 1)
    late_specs = [whole_spec((late_rows_count, width))] * shards
    gathered = pltpu.VMEM((shards, late_rows_count, width), bf16)

    smem = pl.BlockSpec(memory_space=pltpu.SMEM)
    units = items * funcs
    flat_points = points.reshape(units, slots, width)
    state_t, state, keys_one, values_one = pl.pallas_call(
        partial(points_forward, funcs=funcs, shards=shards),
        grid=(items,),
        in_specs=[smem, smem, pl.BlockSpec((funcs, slots, width), lambda u: (u, 0, 0))]
        + [whole_spec((2 * piece, width))] * shards,
        out_specs=[
            pl.BlockSpec((funcs, 2 * width, width), lambda u: (u, 0, 0)),
            pl.BlockSpec((funcs, width, 2 * width), lambda u: (u, 0, 0)),
            pl.BlockSpec((funcs, width, slots), lambda u: (u, 0, 0)),
            pl.BlockSpec((funcs, width, slots), lambda u: (u, 0, 0)),
        ],
        out_shape=[
            jax.ShapeDtypeStruct((units, 2 * width, width), bf16),
            jax.ShapeDtypeStruct((units, width, 2 * width), bf16),
            jax.ShapeDtypeStruct((units, width, slots), bf16),
            jax.ShapeDtypeStruct((units, width, slots), bf16),
        ],
        scratch_shapes=[
            pltpu.VMEM((shards, 2 * piece, width), bf16),
            pltpu.VMEM((2 * width, width), bf16),
        ],
        compiler_params=limit,
        cost_estimate=cost(8),
        name="points_forward",
    )(counts, presence, flat_points, *early_parts)

    kept = jax.ShapeDtypeStruct((items * steps, width, tile), bf16)
    main_rows = enter_rows + experts * exit_piece + piece + 16

    def early(i, p, j):
        return i * steps + jnp.where(p == 0, j, steps - 1)

    def late(i, p, j):
        return i * steps + jnp.where(p == 0, 0, j)

    early_keep = pl.BlockSpec((1, width, tile), lambda i, p, j: (early(i, p, j), 0, 0))
    late_keep = pl.BlockSpec((1, width, tile), lambda i, p, j: (late(i, p, j), 0, 0))
    late_rows = pl.BlockSpec((tile, width), lambda i, p, j: (late(i, p, j), 0))
    (
        result,
        queries_one,
        cross,
        first,
        keys_two,
        values_two,
        grad_q_two,
        grad_second,
        grad_state_two,
        *main_grads,
    ) = pl.pallas_call(
        partial(main_kernel, funcs=funcs, experts=experts, shards=shards, at=at),
        grid=(items, 2, steps),
        in_specs=[
            pl.BlockSpec((tile, width), lambda i, p, j: (early(i, p, j), 0)),
            late_rows,
            pl.BlockSpec((2, tile), lambda i, p, j: (0, late(i, p, j))),
            pl.BlockSpec((funcs, 2 * width, width), lambda i, p, j: (i, 0, 0)),
        ]
        + late_specs,
        out_specs=[
            late_rows,
            early_keep,
            early_keep,
            early_keep,
            early_keep,
            early_keep,
            late_keep,
            late_keep,
            pl.BlockSpec((1, width, 2 * width), lambda i, p, j: (i, 0, 0)),
        ]
        + [whole_spec((main_rows, width))] * shards,
        out_shape=[
            jax.ShapeDtypeStruct((count, width), bf16),
            kept,
            kept,
            kept,
            kept,
            kept,
            kept,
            kept,
            jax.ShapeDtypeStruct((items, width, 2 * width), f32),
        ]
        + [jax.ShapeDtypeStruct((main_rows, width), bf16)] * shards,
        scratch_shapes=[
            gathered,
            pltpu.VMEM((shards, main_rows, width), bf16),
            pltpu.VMEM((steps, width, tile), f32),
            pltpu.VMEM((steps, width, tile), bf16),
            pltpu.VMEM((width, 2 * width), f32),
            pltpu.VMEM((2 * width, width), bf16),
            pltpu.VMEM((width, 2 * width), bf16),
            pltpu.VMEM((width, 2 * width), f32),
            pltpu.VMEM((width, width), bf16),
            pltpu.VMEM((width, width), bf16),
            pltpu.VMEM((3 * width, width), bf16),
            pltpu.VMEM((width, width), bf16),
            pltpu.VMEM((width, width), bf16),
            pltpu.VMEM((inner, width), bf16),
            pltpu.VMEM((width, inner), bf16),
            pltpu.VMEM((inner, width), bf16),
            pltpu.VMEM((width, inner), bf16),
            pltpu.VMEM((width, CHUNK), f32),
            pltpu.VMEM((width, CHUNK), f32),
            pltpu.VMEM((width, CHUNK), f32),
            pltpu.VMEM((width, CHUNK), f32),
            pltpu.VMEM((inner, tile), bf16),
            pltpu.VMEM((inner, tile), bf16),
            pltpu.VMEM((width, tile), bf16),
            pltpu.VMEM((width, tile), bf16),
            pltpu.VMEM((width, tile), bf16),
            pltpu.VMEM((2 * width, tile), bf16),
            pltpu.VMEM((inner, width), f32),
            pltpu.VMEM((inner, width), f32),
            pltpu.VMEM((width, width), f32),
            pltpu.VMEM((width, width), f32),
            pltpu.VMEM((width, width), f32),
            pltpu.VMEM((2 * experts, tile), f32),
        ],
        compiler_params=limit,
        cost_estimate=cost(80),
        name="main",
    )(tokens, cotangent, coords, state_t, *late_parts)

    rest_rows = 7 * piece + 16

    def rest_call(item, earlier, after):
        first_call = item == 0
        keep_spec = pl.BlockSpec((1, width, tile), lambda j: (item * steps + j, 0, 0))
        row_spec = pl.BlockSpec((tile, width), lambda j: (item * steps + j, 0))
        unit_spec = pl.BlockSpec((funcs, width, width), lambda j: (item, 0, 0))
        anywhere = pl.BlockSpec(memory_space=pl.ANY)
        in_specs = [
            smem,
            row_spec,
            keep_spec,
            keep_spec,
            keep_spec,
            keep_spec,
            keep_spec,
            keep_spec,
            keep_spec,
            pl.BlockSpec((1, width, 2 * width), lambda j: (item, 0, 0)),
            pl.BlockSpec((funcs, 2 * width, width), lambda j: (item, 0, 0)),
            pl.BlockSpec((funcs, width, 2 * width), lambda j: (item, 0, 0)),
        ] + late_specs
        operands = [
            presence,
            tokens,
            queries_one,
            cross,
            first,
            keys_two,
            values_two,
            grad_q_two,
            grad_second,
            grad_state_two,
            state_t,
            state,
            *late_parts,
        ]
        aliases = {}
        if not first_call:
            aliases = {len(operands) + k: k for k in range(3)}
            in_specs += [anywhere] * 3 + [whole_spec((width, 7 * width)), anywhere]
            operands += [*earlier, after]
        out_specs = [row_spec, unit_spec, unit_spec, whole_spec((width, 7 * width))]
        out_shape = [
            jax.ShapeDtypeStruct((count, width), f32),
            jax.ShapeDtypeStruct((units, width, width), bf16),
            jax.ShapeDtypeStruct((units, width, width), f32),
            jax.ShapeDtypeStruct((width, 7 * width), f32),
        ]
        return pl.pallas_call(
            partial(
                rest_kernel,
                funcs=funcs,
                item=item,
                shards=shards,
                at=at,
                first_call=first_call,
            ),
            grid=(steps,),
            in_specs=in_specs,
            out_specs=out_specs,
            out_shape=out_shape,
            input_output_aliases=aliases,
            scratch_shapes=[
                gathered,
                pltpu.VMEM((width, 3 * width), bf16),
                pltpu.VMEM((width, width), bf16),
                pltpu.VMEM((width, width), bf16),
                pltpu.VMEM((width, CHUNK), f32),
                pltpu.VMEM((width, CHUNK), f32),
                pltpu.VMEM((2, width, width), bf16),
                pltpu.VMEM((width, CHUNK), f32),
                pltpu.VMEM((width, 2 * funcs * width), f32),
                pltpu.VMEM((width, 7 * width), f32),
                pltpu.VMEM((3 * width, tile), bf16),
                pltpu.VMEM((width, tile), bf16),
                pltpu.VMEM((2 * funcs * width, tile), bf16),
                pltpu.VMEM((width, tile), bf16),
                pltpu.VMEM((width, tile), bf16),
            ],
            compiler_params=limit,
            cost_estimate=cost(18),
            name="rest",
        )(*operands)

    levels = digits(dp)
    main_levels = levels[::-1]
    main_parts = exchange(main_grads, "fsdp", shards, 1)
    level = 0
    found = None
    for item in range(items):
        found = rest_call(item, found, main_sum if item else None)
        if item < len(main_levels):
            main_sum = sum_parts(main_parts)
            main_parts = spread(main_sum, "dp", dp, *main_levels[item])
            level = item + 1
    grad_tokens, grad_state_one, grad_totals_one, carry = found

    rest_grads = pl.pallas_call(
        partial(points_back, shards=shards),
        grid=(items,),
        in_specs=[
            pl.BlockSpec((funcs, slots, width), lambda u: (u, 0, 0)),
            pl.BlockSpec((funcs, width, slots), lambda u: (u, 0, 0)),
            pl.BlockSpec((funcs, width, slots), lambda u: (u, 0, 0)),
            pl.BlockSpec((funcs, width, width), lambda u: (u, 0, 0)),
            pl.BlockSpec((funcs, width, width), lambda u: (u, 0, 0)),
            whole_spec((width, 7 * width)),
            pl.BlockSpec(memory_space=pl.ANY),
        ],
        out_specs=[whole_spec((rest_rows, width))] * shards,
        out_shape=[jax.ShapeDtypeStruct((rest_rows, width), bf16)] * shards,
        scratch_shapes=[
            pltpu.VMEM((2 * width, width), f32),
            pltpu.VMEM((shards, rest_rows, width), bf16),
        ],
        compiler_params=limit,
        cost_estimate=cost(7),
        name="points_back",
    )(flat_points, keys_one, values_one, grad_state_one, grad_totals_one, carry, main_sum)
    rest_got = exchange(rest_grads, "fsdp", shards, 1)

    parts = rest_got
    for digit, stride in main_levels[level:]:
        main_parts = spread(sum_parts(main_parts), "dp", dp, digit, stride)
    for digit, stride in levels:
        parts = spread(sum_parts(parts), "dp", dp, digit, stride)

    matrix = jax.ShapeDtypeStruct((piece, width), f32)
    vector = jax.ShapeDtypeStruct((1, piece), f32)
    outs = pl.pallas_call(
        partial(
            unpack_kernel,
            counts=(len(main_parts), len(parts)),
            experts=experts,
            piece=piece,
            exit_piece=exit_piece,
            hidden=hidden,
        ),
        out_shape=[vector] * 2
        + [matrix] * 8
        + [vector] * 2
        + [
            jax.ShapeDtypeStruct(expert_in.shape, f32),
            jax.ShapeDtypeStruct(expert_out.shape, f32),
            jax.ShapeDtypeStruct((1, 2), f32),
        ],
        scratch_shapes=[
            pltpu.VMEM((32, width), f32),
            pltpu.VMEM((main_rows, width), f32),
            pltpu.VMEM((rest_rows, width), f32),
        ],
        name="unpack",
    )(*main_parts, *parts)
    outs = [out.reshape(piece) if out.shape == (1, piece) else out for out in outs]
    return (result, grad_tokens, *outs[:-1], outs[-1].reshape(gate_weight.shape))


def solution(mesh):
    rows = P(("dp", "fsdp"), None)
    matrix = P("fsdp", None)
    vector = P("fsdp")
    expert = P(None, "fsdp", None)
    parameters = (
        (vector, vector)
        + (matrix,) * 8
        + (vector, vector, expert, expert, P(None, "fsdp"))
    )
    return jax.shard_map(
        partial(shards_fn, mesh.shape["dp"], mesh.shape["fsdp"]),
        mesh=mesh,
        in_specs=(
            rows,
            P(("dp", "fsdp"), None, None, None),
            P(None, ("dp", "fsdp")),
            rows,
            rows,
            rows,
        )
        + parameters,
        out_specs=(rows, rows) + parameters,
        check_vma=False,
    )
```

```python
from functools import partial

import jax
import jax.numpy as jnp
from jax import lax
from jax.experimental import pallas as pl
from jax.experimental.pallas import tpu as pltpu
from jax.sharding import PartitionSpec as P


HEADS = 8
eps = 1e-05
f32 = jnp.float32
bf16 = jnp.bfloat16
TILE = 1024
CHUNK = 256
SLAB = 64
PAD = 16
VMEM = 56 * 1024 * 1024


def cost(microseconds):
    return pl.CostEstimate(flops=microseconds * 10**9, bytes_accessed=10**6, transcendentals=0)


def nn(left, right):
    return jnp.dot(left, right, preferred_element_type=f32)


def nt(left, right):
    return lax.dot_general(left, right, (((1,), (1,)), ((), ())), preferred_element_type=f32)


def flip(value):
    return value.T


def inverse(value):
    return pl.reciprocal(value, approx=True)


def head_softmax(value):
    width, rows = value.shape
    split = value.reshape(HEADS, width // HEADS, rows)
    raised = jnp.exp(split - jnp.max(split, axis=1, keepdims=True))
    return (raised * inverse(jnp.sum(raised, axis=1, keepdims=True))).reshape(width, rows)


def softmax_back(probs, grad):
    width, rows = grad.shape
    probs = probs.astype(f32).reshape(HEADS, width // HEADS, rows)
    grad = grad.reshape(HEADS, width // HEADS, rows)
    inner = jnp.sum(probs * grad, axis=1, keepdims=True)
    return (probs * (grad - inner)).reshape(width, rows)


def standardize(value):
    centre = value - jnp.mean(value, axis=0, keepdims=True)
    scale = lax.rsqrt(jnp.mean(centre * centre, axis=0, keepdims=True) + eps)
    return centre * scale, scale


def norm_back(grad, hat, scale):
    return scale * (
        grad
        - jnp.mean(grad, axis=0, keepdims=True)
        - hat * jnp.mean(grad * hat, axis=0, keepdims=True)
    )


def same_head(width):
    shape, head = (width, width), width // HEADS
    row = lax.broadcasted_iota(jnp.int32, shape, 0)
    column = lax.broadcasted_iota(jnp.int32, shape, 1)
    return lax.div(row, head) == lax.div(column, head)


def own_head(width):
    shape, head = (HEADS, width), width // HEADS
    row = lax.broadcasted_iota(jnp.int32, shape, 0)
    return row == lax.div(lax.broadcasted_iota(jnp.int32, shape, 1), head)


def by_head(value, scales):
    width, rows = value.shape
    split = value.reshape(HEADS, width // HEADS, rows)
    return (split * scales.reshape(HEADS, 1, rows)).reshape(width, rows)


def head_sums(value):
    width, rows = value.shape
    return jnp.sum(value.reshape(HEADS, width // HEADS, rows), axis=1)


def totals_column(rows, width):
    row = jnp.sum(jnp.where(own_head(width), rows, 0.0), axis=0, keepdims=True)
    return flip(jnp.broadcast_to(-row, (width, width)))


def pack_states(lefts, totals, state_t, state, width):
    count = len(lefts)
    rights = [jnp.where(own_head(width), total, 0.0) for total in totals]
    rest = jnp.zeros((width - count * HEADS, width), f32)
    right = jnp.concatenate(rights + [rest], axis=0)
    for place, left in enumerate(lefts):
        span = slice(place * width, (place + 1) * width)
        state_t[span] = left.astype(bf16)
        state[:, span] = flip(left).astype(bf16)
    start = count * width
    used = state_t.shape[0] - start
    state_t[start:] = right[:used].astype(bf16)
    state[:, start : start + width] = -flip(right).astype(bf16)


def assemble(parts, gathered):
    shards = len(parts)
    here = lax.axis_index("fsdp")
    for place, part in enumerate(parts):
        gathered[lax.rem(here + shards - place, shards)] = part[...]


def columns(gathered, start, count):
    shards, _, width = gathered.shape
    piece = width // shards
    small = [gathered[shard, start : start + 16, :].astype(f32) for shard in range(shards)]
    joined = jnp.concatenate([part[:, :piece] for part in small], axis=1)
    return [
        flip(jnp.broadcast_to(joined[place : place + 1], (width, width)))[:, 0:1]
        for place in range(count)
    ]


def lane_fold(value):
    width = value.shape[0]
    total = value[:, :width]
    for start in range(width, value.shape[1], width):
        total = total + value[:, start : start + width]
    return total


def as_row(value):
    width = value.shape[0]
    return flip(jnp.broadcast_to(jnp.sum(value, axis=1, keepdims=True), (width, width)))


def scatter_blocks(stage, outs):
    shards = len(outs)
    here = lax.axis_index("fsdp")
    for place, out in enumerate(outs):
        out[...] = stage[lax.rem(here + place, shards)]


def whole(gathered, start, rows):
    shards = gathered.shape[0]
    return gathered[:, start : start + rows, :].reshape(shards * rows, gathered.shape[2])


def function_weight(presence, item, func, funcs, shape):
    total = presence[item, 0]
    for other in range(1, funcs):
        total = total + presence[item, other]
    own = jnp.full(shape, presence[item, func], jnp.int32).astype(f32)
    return own / jnp.full(shape, total, jnp.int32).astype(f32)


def pack_kernel(*refs):
    weights, vectors, gate = refs[:10], refs[10:14], refs[14]
    early, late = refs[15:]
    keys, values, query, out, query_two, key_two, value_two, out_two, enter, leave = weights
    start = 0
    for weight in (keys, values):
        early[start : start + weight.shape[0]] = weight[...]
        start += weight.shape[0]
    start = 0
    for weight in (query, out, query_two, key_two, value_two, out_two):
        late[start : start + weight.shape[0]] = weight[...]
        start += weight.shape[0]
    experts, piece, hidden = enter.shape
    width = late.shape[1]
    for expert in range(experts):
        for half in range(hidden // width):
            late[start : start + piece] = enter[expert, :, half * width : (half + 1) * width]
            start += piece
    for expert in range(experts):
        late[start : start + leave.shape[1]] = leave[expert]
        start += leave.shape[1]
    rest = jnp.zeros((1, width - piece), f32)
    rows = [
        jnp.concatenate([vector[...].astype(f32), rest], axis=1) for vector in vectors
    ]
    rows.append(jnp.zeros((4, width), f32))
    for row in range(2):
        rows.append(jnp.broadcast_to(gate[row : row + 1, 0:1].astype(f32), (1, width)))
    rows.append(jnp.zeros((6, width), f32))
    late[start : start + 16] = jnp.concatenate(rows, axis=0).astype(bf16)


def points_forward(counts, presence, points, *refs, funcs, shards):
    parts = refs[:shards]
    state_t, state, keys_out, values_out, gathered, weight = refs[shards:]
    item = pl.program_id(0)
    width = points.shape[2]
    slots = points.shape[1]
    piece = width // shards

    @pl.when(item == 0)
    def _():
        assemble(parts, gathered)
        weight[:width] = flip(whole(gathered, 0, piece))
        weight[width:] = flip(whole(gathered, piece, piece))

    def project(func):
        both = nt(weight[...], points[func])
        slot = lax.broadcasted_iota(jnp.int32, (1, slots), 1)
        probs = head_softmax(both[:width])
        keys_out[func] = jnp.where(slot < counts[item, func], probs, 0.0).astype(bf16)
        values_out[func] = both[width:].astype(bf16)

    def summarize(func):
        values = values_out[func]
        extended = jnp.concatenate([values, jnp.ones((PAD, slots), bf16)], axis=0)
        share = function_weight(presence, item, func, funcs, (1, width))
        summed = nt(extended, keys_out[func])
        left = jnp.where(same_head(width), summed[:width], 0.0) * share
        return left, summed[width : width + 1]

    for func in range(funcs):
        project(func)
    lefts, totals = zip(*(summarize(func) for func in range(funcs)))
    pack_states(lefts, totals, state_t.at[0], state.at[0], width)


def main_kernel(tokens, cotangent, coords, state_t, *refs, funcs, experts, shards, at):
    parts, outs, scratch = refs[:shards], refs[shards : 2 * shards + 9], refs[2 * shards + 9 :]
    (
        result,
        queries_out,
        cross_out,
        first_out,
        keys_out,
        values_out,
        grad_q_out,
        grad_second_out,
        grad_state_out,
    ) = outs[:9]
    grads_out = outs[9:]
    (
        params,
        grads_stage,
        first_keep,
        query_keep,
        state_sum,
        self_t,
        self_state,
        grad_state_sum,
        w_query,
        w_out_one,
        w_self,
        w_out_two_t,
        w_out_two,
        w_in_t,
        w_in,
        w_exit,
        w_exit_t,
        gain_one,
        bias_one,
        gain_two,
        bias_two,
        hidden_keep,
        inner_keep,
        normed_keep,
        grad_keep,
        own_keep,
        pair_keep,
        sum_in,
        sum_exit,
        sum_out_two,
        sum_gain,
        sum_bias,
        sum_gate,
    ) = scratch
    item = pl.program_id(0)
    phase = pl.program_id(1)
    step = pl.program_id(2)
    steps = pl.num_programs(2)
    width = tokens.shape[1]
    rows = tokens.shape[0]
    piece = width // shards
    hidden = w_in.shape[1] // experts
    exit_piece = hidden // shards

    @pl.when((item == 0) & (phase == 0) & (step == 0))
    def _():
        assemble(parts, params)
        w_query[...] = flip(whole(params, at["query_first"], piece))
        w_out_one[...] = flip(whole(params, at["out_first"], piece))
        w_self[:width] = flip(whole(params, at["query_second"], piece))
        w_self[width : 2 * width] = flip(whole(params, at["key_second"], piece))
        w_self[2 * width :] = flip(whole(params, at["value_second"], piece))
        out_two = whole(params, at["out_second"], piece)
        w_out_two[...] = out_two
        w_out_two_t[...] = flip(out_two)
        for block in range(experts * hidden // width):
            part = whole(params, at["expert_in"] + block * piece, piece)
            w_in[:, block * width : (block + 1) * width] = part
            w_in_t[block * width : (block + 1) * width] = flip(part)
        for expert in range(experts):
            part = whole(params, at["expert_out"] + expert * exit_piece, exit_piece)
            w_exit[expert * hidden : (expert + 1) * hidden] = part
            w_exit_t[:, expert * hidden : (expert + 1) * hidden] = flip(part)
        found = columns(params, at["small"], 4)
        for vector, column in zip((gain_one, bias_one, gain_two, bias_two), found):
            vector[...] = jnp.broadcast_to(column, vector.shape)
        sum_in[...] = jnp.zeros_like(sum_in)
        sum_exit[...] = jnp.zeros_like(sum_exit)
        sum_out_two[...] = jnp.zeros_like(sum_out_two)
        sum_gain[...] = jnp.zeros_like(sum_gain)
        sum_bias[...] = jnp.zeros_like(sum_bias)
        sum_gate[...] = jnp.zeros_like(sum_gate)

    chunks = [slice(start, start + CHUNK) for start in range(0, rows, CHUNK)]

    @pl.when(phase == 0)
    def _():
        def enter(cols):
            rows_t = flip(tokens[cols, :]).astype(f32)
            hat, _scale = standardize(rows_t)
            normed = (hat * gain_one[...] + bias_one[...]).astype(bf16)
            return rows_t, head_softmax(nn(w_query[...], normed)).astype(bf16)

        def across(cols, queries):
            queries_out[0, :, cols] = queries
            both = nn(state_t[0], queries)
            undo = inverse(both[funcs * width :])
            mixed = None
            for func in range(funcs):
                part = by_head(
                    both[func * width : (func + 1) * width],
                    undo[func * HEADS : (func + 1) * HEADS],
                )
                mixed = part if mixed is None else mixed + part
            cross = mixed.astype(bf16)
            cross_out[0, :, cols] = cross
            return cross

        def leave(cols, rows_t, cross):
            first = rows_t + nn(w_out_one[...], cross)
            first_keep[step, :, cols] = first
            first_low = first.astype(bf16)
            first_out[0, :, cols] = first_low
            return first_low

        def project(cols, first_low):
            three = nn(w_self[...], first_low)
            query_keep[step, :, cols] = head_softmax(three[:width]).astype(bf16)
            keys_out[0, :, cols] = head_softmax(three[width : 2 * width]).astype(bf16)
            values = three[2 * width :].astype(bf16)
            values_out[0, :, cols] = values
            pair_keep[:width, cols] = values
            pair_keep[width:, cols] = jnp.ones((PAD, CHUNK), bf16)

        entered = [enter(cols) for cols in chunks]
        crossed = [across(cols, queries) for cols, (_, queries) in zip(chunks, entered)]
        firsts = [
            leave(cols, rows_t, cross)
            for cols, (rows_t, _), cross in zip(chunks, entered, crossed)
        ]
        for cols, first_low in zip(chunks, firsts):
            project(cols, first_low)
        found = nt(pair_keep[...], keys_out[0])

        @pl.when(step == 0)
        def _():
            state_sum[...] = found

        @pl.when(step > 0)
        def _():
            state_sum[...] += found

        @pl.when(step == steps - 1)
        def _():
            left = jnp.where(same_head(width), state_sum[:width], 0.0)
            pack_states([left], [state_sum[width : width + 1]], self_t, self_state, width)

    @pl.when(phase == 1)
    def _():
        def attend(cols):
            both = nn(self_t[...], query_keep[step, :, cols])
            undo = inverse(both[width : width + HEADS])
            own = by_head(both[:width], undo)
            own_keep[:, cols] = own.astype(bf16)
            grad_keep[:, cols] = flip(cotangent[cols, :])
            return undo, own

        def norm(cols):
            second = first_keep[step, :, cols] + nn(w_out_two_t[...], own_keep[:, cols])
            hat, scale = standardize(second)
            normed_keep[:, cols] = (hat * gain_two[...] + bias_two[...]).astype(bf16)
            return second, hat, scale

        def gate(cols):
            across, down = coords[0:1, cols], coords[1:2, cols]
            logits = []
            for expert in range(experts):
                pair = params[expert, at["small"] : at["small"] + 16, 0:1].astype(f32)
                logits.append(across * pair[8:9] + down * pair[9:10])
            peak = logits[0]
            for logit in logits[1:]:
                peak = jnp.maximum(peak, logit)
            raised = [jnp.exp(logit - peak) for logit in logits]
            total = raised[0]
            for other in raised[1:]:
                total = total + other
            return [other / total for other in raised]

        def expand(cols, gates):
            normed, grad = normed_keep[:, cols], grad_keep[:, cols]
            gates_low = [gate.astype(bf16) for gate in gates]
            grad_gates = []
            for expert in range(experts):
                partial_sum = None
                span = slice(expert * hidden, (expert + 1) * hidden)
                inners = nn(w_in_t[span], normed).astype(bf16)
                backs = nn(w_exit[span], grad).astype(bf16)
                for start in range(0, hidden, SLAB):
                    inner, back = inners[start : start + SLAB], backs[start : start + SLAB]
                    span = slice(expert * hidden + start, expert * hidden + start + SLAB)
                    square = inner * inner
                    tanh = jnp.tanh(inner * (0.7978845608028654 + 0.035677408136300125 * square))
                    half = 0.5 + 0.5 * tanh
                    active = inner * half
                    product = active * back
                    folded = product[:16]
                    for row in range(16, SLAB, 16):
                        folded = folded + product[row : row + 16]
                    folded = folded.astype(f32)
                    partial_sum = folded if partial_sum is None else partial_sum + folded
                    hidden_keep[span, cols] = active * gates_low[expert]
                    slope = half + active * (1.0 - half) * (
                        1.5957691216057308 + 0.21406444881780074 * square
                    )
                    inner_keep[span, cols] = slope * (back * gates_low[expert])
                grad_gates.append(jnp.sum(partial_sum, axis=0, keepdims=True))
            across, down = coords[0:1, cols], coords[1:2, cols]
            mean_gate = gates[0] * grad_gates[0]
            for expert in range(1, experts):
                mean_gate = mean_gate + gates[expert] * grad_gates[expert]
            for expert in range(experts):
                change = gates[expert] * (grad_gates[expert] - mean_gate)
                sum_gate[expert : expert + 1, cols] += across * change
                sum_gate[experts + expert : experts + expert + 1, cols] += down * change

        def contract(cols, second, hat, scale):
            total = second + nn(w_exit_t[...], hidden_keep[:, cols])
            result[cols, :] = flip(total.astype(bf16))
            grad_normed = nn(w_in[...], inner_keep[:, cols])
            sum_gain[...] += lane_fold(grad_normed * hat)
            sum_bias[...] += lane_fold(grad_normed)
            grad_second = grad_keep[:, cols].astype(f32) + norm_back(
                grad_normed * gain_two[...], hat, scale
            )
            grad_own = grad_second.astype(bf16)
            grad_second_out[0, :, cols] = grad_own
            return grad_own

        def attend_back(cols, grad_own, undo, own):
            share = by_head(nn(w_out_two[...], grad_own), undo)
            pair_keep[:width, cols] = share.astype(bf16)
            sums = head_sums(share * own)
            pair_keep[width:, cols] = jnp.concatenate(
                [sums, jnp.zeros((PAD - HEADS, CHUNK), f32)], axis=0
            ).astype(bf16)

        def query_back(cols):
            grad_q = nn(self_state[:, : width + PAD], pair_keep[:, cols])
            grad_q_out[0, :, cols] = softmax_back(query_keep[step, :, cols], grad_q).astype(bf16)

        attended = [attend(cols) for cols in chunks]
        normed = [norm(cols) for cols in chunks]
        gates = [gate(cols) for cols in chunks]
        for cols, own_gates in zip(chunks, gates):
            expand(cols, own_gates)
        grads = [contract(cols, *kept) for cols, kept in zip(chunks, normed)]
        for cols, grad_own, (undo, own) in zip(chunks, grads, attended):
            attend_back(cols, grad_own, undo, own)
        for cols in chunks:
            query_back(cols)
        sum_exit[...] += nn(hidden_keep[...], cotangent[...])
        sum_in[...] += nt(inner_keep[...], normed_keep[...])
        sum_out_two[...] += nt(own_keep[...], grad_second_out[0])
        found = nt(pair_keep[...], query_keep[step])

        @pl.when(step == 0)
        def _():
            grad_state_sum[...] = found

        @pl.when(step > 0)
        def _():
            grad_state_sum[...] += found

        @pl.when(step == steps - 1)
        def _():
            grad_state_out[0] = grad_state_sum[...]

    @pl.when((item == pl.num_programs(0) - 1) & (phase == 1) & (step == steps - 1))
    def _():
        gain, bias = as_row(sum_gain[...]), as_row(sum_bias[...])
        gate = jnp.broadcast_to(jnp.sum(sum_gate[...], axis=1, keepdims=True), (8, width))
        row = lax.broadcasted_iota(jnp.int32, (8, width), 0)
        vectors = jnp.where(row == 0, gain[:8], bias[:8])
        small = jnp.concatenate([vectors, gate], axis=0).astype(bf16)
        start = 0
        for block in range(experts * hidden // width):
            part = flip(sum_in[block * width : (block + 1) * width]).astype(bf16)
            grads_stage[:, start : start + piece, :] = part.reshape(shards, piece, width)
            start += piece
        for expert in range(experts):
            part = sum_exit[expert * hidden : (expert + 1) * hidden].astype(bf16)
            grads_stage[:, start : start + exit_piece, :] = part.reshape(shards, exit_piece, width)
            start += exit_piece
        part = sum_out_two[...].astype(bf16)
        grads_stage[:, start : start + piece, :] = part.reshape(shards, piece, width)
        start += piece
        for shard in range(shards):
            grads_stage[shard, start : start + 16, :] = small
        scatter_blocks(grads_stage, grads_out)


def rest_kernel(
    presence,
    tokens,
    queries_in,
    cross_in,
    first_in,
    keys_in,
    values_in,
    grad_q_in,
    grad_second_in,
    grad_state_in,
    state_t,
    state,
    *refs,
    funcs,
    item,
    shards,
    at,
    first_call,
):
    parts, refs = refs[:shards], refs[shards:]
    if not first_call:
        carry, refs = refs[3], refs[5:]
    (
        grad_tokens,
        grad_cross_state_out,
        grad_totals_out,
        sums_out,
        params,
        w_self,
        w_out_one,
        w_query,
        gain_one,
        bias_one,
        grad_self_state,
        grad_totals,
        grad_state_sum,
        sums,
        three_keep,
        cross_keep,
        stack_keep,
        query_keep,
        normed_keep,
    ) = refs
    step = pl.program_id(0)
    steps = pl.num_programs(0)
    width = tokens.shape[1]
    piece = width // shards
    self_part = slice(0, 3 * width)
    out_part = slice(3 * width, 4 * width)
    query_part = slice(4 * width, 5 * width)
    gain_part = slice(5 * width, 6 * width)
    bias_part = slice(6 * width, 7 * width)

    @pl.when(step == 0)
    def _():
        assemble(parts, params)
        w_query[...] = whole(params, at["query_first"], piece)
        w_out_one[...] = whole(params, at["out_first"], piece)
        w_self[:, :width] = whole(params, at["query_second"], piece)
        w_self[:, width : 2 * width] = whole(params, at["key_second"], piece)
        w_self[:, 2 * width :] = whole(params, at["value_second"], piece)
        for vector, column in zip((gain_one, bias_one), columns(params, at["small"], 2)):
            vector[...] = jnp.broadcast_to(column, vector.shape)
        sums[...] = jnp.zeros_like(sums) if first_call else carry[...]
        left = jnp.where(same_head(width), grad_state_in[0, :width], 0.0)
        grad_self_state[0] = flip(left).astype(bf16)
        grad_self_state[1] = left.astype(bf16)
        column = totals_column(grad_state_in[0, width : width + HEADS], width)
        grad_totals[...] = jnp.broadcast_to(column[:, 0:1], grad_totals.shape)

    chunks = [slice(start, start + CHUNK) for start in range(0, tokens.shape[0], CHUNK)]

    def self_back(cols):
        keys, values = keys_in[0, :, cols], values_in[0, :, cols]
        grad_keys = nn(grad_self_state[0], values) + grad_totals[...]
        three_keep[:width, cols] = grad_q_in[0, :, cols]
        three_keep[width : 2 * width, cols] = softmax_back(keys, grad_keys).astype(bf16)
        three_keep[2 * width :, cols] = nn(grad_self_state[1], keys).astype(bf16)

    def join(cols):
        grad_first = grad_second_in[0, :, cols].astype(f32) + nn(w_self[...], three_keep[:, cols])
        cross_keep[:, cols] = grad_first.astype(bf16)
        return grad_first

    def cross_back(cols):
        share = nn(w_out_one[...], cross_keep[:, cols])
        both = nn(state_t[0], queries_in[0, :, cols])
        undo = inverse(both[funcs * width :])
        sums_by_head = []
        for func in range(funcs):
            span = slice(func * width, (func + 1) * width)
            scales = undo[func * HEADS : (func + 1) * HEADS]
            part = by_head(share, scales)
            stack_keep[span, cols] = part.astype(bf16)
            sums_by_head.append(head_sums(part * by_head(both[span], scales)))
        spare = stack_keep.shape[0] - funcs * (width + HEADS)
        if spare:
            sums_by_head.append(jnp.zeros((spare, CHUNK), f32))
        stack_keep[funcs * width :, cols] = jnp.concatenate(sums_by_head, axis=0).astype(bf16)

    def query_back(cols):
        joined = state[0, :, : stack_keep.shape[0]]
        grad_q = softmax_back(queries_in[0, :, cols], nn(joined, stack_keep[:, cols]))
        query_keep[:, cols] = grad_q.astype(bf16)

    def finish(cols, grad_first):
        hat, scale = standardize(flip(tokens[cols, :]).astype(f32))
        normed_keep[:, cols] = (hat * gain_one[...] + bias_one[...]).astype(bf16)
        grad_normed = nn(w_query[...], query_keep[:, cols])
        sums[gain_part] += lane_fold(grad_normed * hat)
        sums[bias_part] += lane_fold(grad_normed)
        grad_rows = grad_first + norm_back(grad_normed * gain_one[...], hat, scale)
        grad_tokens[cols, :] = flip(grad_rows)

    for cols in chunks:
        self_back(cols)
    grad_firsts = [join(cols) for cols in chunks]
    for cols in chunks:
        cross_back(cols)
    for cols in chunks:
        query_back(cols)
    for cols, grad_first in zip(chunks, grad_firsts):
        finish(cols, grad_first)
    sums[self_part] += nt(three_keep[...], first_in[0])
    sums[out_part] += nt(cross_in[0], cross_keep[...])
    sums[query_part] += nt(normed_keep[...], query_keep[...])
    found = nt(stack_keep[...], queries_in[0])

    @pl.when(step == 0)
    def _():
        grad_state_sum[...] = found

    @pl.when(step > 0)
    def _():
        grad_state_sum[...] += found

    @pl.when(step == steps - 1)
    def _():
        mask = same_head(width)
        for func in range(funcs):
            weight = function_weight(presence, item, func, funcs, (1, width))
            left = jnp.where(mask, grad_state_sum[func * width : (func + 1) * width], 0.0)
            grad_cross_state_out[func] = (left * weight).astype(bf16)
            start = funcs * width + func * HEADS
            grad_totals_out[func] = totals_column(grad_state_sum[start : start + HEADS], width)
        sums_out[...] = sums[...]


def points_back(points, keys_in, values_in, grad_state, grad_totals, carry, _after, *refs, shards):
    outs = refs[:shards]
    sums, stage = refs[shards:]
    step = pl.program_id(0)
    width = points.shape[2]
    piece = width // shards

    def back(func):
        keys, values = keys_in[func], values_in[func]
        left = grad_state[func]
        grad_keys = nn(flip(left), values) + grad_totals[func, :, 0:1]
        grad_k = softmax_back(keys, grad_keys).astype(bf16)
        grad_v = nn(left, keys).astype(bf16)
        return jnp.concatenate([grad_k, grad_v], axis=0)

    grads = [back(func) for func in range(points.shape[0])]
    found = nn(grads[0], points[0])
    for func in range(1, points.shape[0]):
        found = found + nn(grads[func], points[func])

    @pl.when(step == 0)
    def _():
        sums[...] = found
        gain = as_row(carry[5 * width : 6 * width])
        bias = as_row(carry[6 * width : 7 * width])
        row = lax.broadcasted_iota(jnp.int32, (16, width), 0)
        small = jnp.where(row == 0, gain[:16], bias[:16]).astype(bf16)
        for place in range(5):
            part = carry[place * width : (place + 1) * width]
            part = (flip(part) if place < 3 else part).astype(bf16)
            stage[:, place * piece : (place + 1) * piece, :] = part.reshape(shards, piece, width)
        for shard in range(shards):
            stage[shard, 5 * piece : 5 * piece + 16, :] = small

    @pl.when(step > 0)
    def _():
        sums[...] += found

    @pl.when(step == pl.num_programs(0) - 1)
    def _():
        for place in range(2):
            start = 5 * piece + 16 + place * piece
            part = flip(sums[place * width : (place + 1) * width]).astype(bf16)
            stage[:, start : start + piece, :] = part.reshape(shards, piece, width)
        scatter_blocks(stage, outs)


def total_of(parts):
    value = parts[0][...].astype(f32)
    for part in parts[1:]:
        value = value + part[...].astype(f32)
    return value


def unpack_kernel(*refs, counts, experts, piece, exit_piece, hidden):
    main_parts, parts = refs[: counts[0]], refs[counts[0] : sum(counts)]
    outs, (small, main, rest) = refs[-18:-3], refs[-3:]
    width = main.shape[1]
    main[...] = total_of(main_parts)
    rest[...] = total_of(parts)
    (
        gain_one,
        bias_one,
        query_one,
        key_one,
        value_one,
        out_one,
        query_two,
        key_two,
        value_two,
        out_two,
        gain_two,
        bias_two,
        enter,
        leave,
        gate,
    ) = outs
    start = 0
    for expert in range(experts):
        for half in range(hidden // width):
            block = main[start : start + piece]
            enter[expert, :, half * width : (half + 1) * width] = block
            start += piece
    for expert in range(experts):
        leave[expert] = main[start : start + exit_piece]
        start += exit_piece
    out_two[...] = main[start : start + piece]
    start += piece
    small[:16] = main[start : start + 16]
    start = 0
    for out in (query_two, key_two, value_two, out_one, query_one):
        out[...] = rest[start : start + piece]
        start += piece
    small[16:] = rest[start : start + 16]
    start += 16
    for out in (key_one, value_one):
        out[...] = rest[start : start + piece]
        start += piece
    shard = lax.axis_index("fsdp")
    turned = pltpu.roll(small[...], lax.rem(width - shard * piece, width), 1)
    gain_two[...] = turned[0:1, :piece]
    bias_two[...] = turned[1:2, :piece]
    gain_one[...] = turned[16:17, :piece]
    bias_one[...] = turned[17:18, :piece]
    for row in range(2):
        gate[:, row : row + 1] = small[pl.ds(8 + row * experts + shard, 1), 0:1]


def whole_spec(shape):
    return pl.BlockSpec(shape, lambda *_: (0,) * len(shape))


def route(size, shift, digit, stride):
    def target(i):
        own = i // stride % digit
        return i + ((own + shift) % digit - own) * stride

    return [(i, target(i)) for i in range(size)]


def spread(value, axis, size, digit, stride):
    return [value] + [
        lax.ppermute(value, axis, route(size, shift, digit, stride)) for shift in range(1, digit)
    ]


def exchange(values, axis, size, stride):
    digit = len(values)
    return [values[0]] + [
        lax.ppermute(values[shift], axis, route(size, shift, digit, stride))
        for shift in range(1, digit)
    ]


def digits(size):
    found = []
    stride = 1
    while stride < size:
        rest = size // stride
        digit = 2 if stride == 1 and rest % 2 == 0 else 4 if rest % 4 == 0 else rest
        found.append((digit, stride))
        stride *= digit
    return found or [(1, 1)]


def sum_parts(parts):
    return total_of([part.astype(f32) for part in parts]).astype(bf16)


def shards_fn(
    dp,
    shards,
    tokens,
    points,
    coords,
    presence,
    counts,
    cotangent,
    gain_first,
    bias_first,
    query_first,
    key_first,
    value_first,
    out_first,
    query_second,
    key_second,
    value_second,
    out_second,
    gain_second,
    bias_second,
    expert_in,
    expert_out,
    gate_weight,
):
    count, width = tokens.shape
    items, funcs, slots, _ = points.shape
    length = count // items
    experts, piece, hidden = expert_in.shape
    exit_piece = expert_out.shape[1]
    tile = min(TILE, length)
    steps = length // tile
    inner = experts * hidden
    enter_rows = experts * piece * (hidden // width)
    limit = pltpu.CompilerParams(vmem_limit_bytes=VMEM)

    at = {}
    place = 0
    for name, size in (
        ("query_first", piece),
        ("out_first", piece),
        ("query_second", piece),
        ("key_second", piece),
        ("value_second", piece),
        ("out_second", piece),
        ("expert_in", enter_rows),
        ("expert_out", experts * exit_piece),
        ("small", 16),
    ):
        at[name] = place
        place += size
    late_rows_count = place
    early_pack, late_pack = pl.pallas_call(
        pack_kernel,
        out_shape=[
            jax.ShapeDtypeStruct((2 * piece, width), bf16),
            jax.ShapeDtypeStruct((late_rows_count, width), bf16),
        ],
        name="pack",
    )(
        key_first,
        value_first,
        query_first,
        out_first,
        query_second,
        key_second,
        value_second,
        out_second,
        expert_in,
        expert_out,
        *(
            vector.reshape(1, piece)
            for vector in (gain_first, bias_first, gain_second, bias_second)
        ),
        gate_weight,
    )
    early_parts = spread(early_pack, "fsdp", shards, shards, 1)
    late_parts = spread(late_pack, "fsdp", shards, shards, 1)
    late_specs = [whole_spec((late_rows_count, width))] * shards
    gathered = pltpu.VMEM((shards, late_rows_count, width), bf16)

    smem = pl.BlockSpec(memory_space=pltpu.SMEM)
    units = items * funcs
    state_rows = funcs * width + -(-funcs * HEADS // PAD) * PAD
    flat_points = points.reshape(units, slots, width)
    state_t, state, keys_one, values_one = pl.pallas_call(
        partial(points_forward, funcs=funcs, shards=shards),
        grid=(items,),
        in_specs=[smem, smem, pl.BlockSpec((funcs, slots, width), lambda u: (u, 0, 0))]
        + [whole_spec((2 * piece, width))] * shards,
        out_specs=[
            pl.BlockSpec((1, state_rows, width), lambda u: (u, 0, 0)),
            pl.BlockSpec((1, width, (funcs + 1) * width), lambda u: (u, 0, 0)),
            pl.BlockSpec((funcs, width, slots), lambda u: (u, 0, 0)),
            pl.BlockSpec((funcs, width, slots), lambda u: (u, 0, 0)),
        ],
        out_shape=[
            jax.ShapeDtypeStruct((items, state_rows, width), bf16),
            jax.ShapeDtypeStruct((items, width, (funcs + 1) * width), bf16),
            jax.ShapeDtypeStruct((units, width, slots), bf16),
            jax.ShapeDtypeStruct((units, width, slots), bf16),
        ],
        scratch_shapes=[
            pltpu.VMEM((shards, 2 * piece, width), bf16),
            pltpu.VMEM((2 * width, width), bf16),
        ],
        compiler_params=limit,
        cost_estimate=cost(8),
        name="points_forward",
    )(counts, presence, flat_points, *early_parts)

    kept = jax.ShapeDtypeStruct((items * steps, width, tile), bf16)
    main_rows = enter_rows + experts * exit_piece + piece + 16

    def early(i, p, j):
        return i * steps + jnp.where(p == 0, j, steps - 1)

    def late(i, p, j):
        return i * steps + jnp.where(p == 0, 0, j)

    early_keep = pl.BlockSpec((1, width, tile), lambda i, p, j: (early(i, p, j), 0, 0))
    late_keep = pl.BlockSpec((1, width, tile), lambda i, p, j: (late(i, p, j), 0, 0))
    late_rows = pl.BlockSpec((tile, width), lambda i, p, j: (late(i, p, j), 0))
    (
        result,
        queries_one,
        cross,
        first,
        keys_two,
        values_two,
        grad_q_two,
        grad_second,
        grad_state_two,
        *main_grads,
    ) = pl.pallas_call(
        partial(main_kernel, funcs=funcs, experts=experts, shards=shards, at=at),
        grid=(items, 2, steps),
        in_specs=[
            pl.BlockSpec((tile, width), lambda i, p, j: (early(i, p, j), 0)),
            late_rows,
            pl.BlockSpec((2, tile), lambda i, p, j: (0, late(i, p, j))),
            pl.BlockSpec((1, state_rows, width), lambda i, p, j: (i, 0, 0)),
        ]
        + late_specs,
        out_specs=[
            late_rows,
            early_keep,
            early_keep,
            early_keep,
            early_keep,
            early_keep,
            late_keep,
            late_keep,
            pl.BlockSpec((1, width + PAD, width), lambda i, p, j: (i, 0, 0)),
        ]
        + [whole_spec((main_rows, width))] * shards,
        out_shape=[
            jax.ShapeDtypeStruct((count, width), bf16),
            kept,
            kept,
            kept,
            kept,
            kept,
            kept,
            kept,
            jax.ShapeDtypeStruct((items, width + PAD, width), f32),
        ]
        + [jax.ShapeDtypeStruct((main_rows, width), bf16)] * shards,
        scratch_shapes=[
            gathered,
            pltpu.VMEM((shards, main_rows, width), bf16),
            pltpu.VMEM((steps, width, tile), f32),
            pltpu.VMEM((steps, width, tile), bf16),
            pltpu.VMEM((width + PAD, width), f32),
            pltpu.VMEM((width + PAD, width), bf16),
            pltpu.VMEM((width, 2 * width), bf16),
            pltpu.VMEM((width + PAD, width), f32),
            pltpu.VMEM((width, width), bf16),
            pltpu.VMEM((width, width), bf16),
            pltpu.VMEM((3 * width, width), bf16),
            pltpu.VMEM((width, width), bf16),
            pltpu.VMEM((width, width), bf16),
            pltpu.VMEM((inner, width), bf16),
            pltpu.VMEM((width, inner), bf16),
            pltpu.VMEM((inner, width), bf16),
            pltpu.VMEM((width, inner), bf16),
            pltpu.VMEM((width, CHUNK), f32),
            pltpu.VMEM((width, CHUNK), f32),
            pltpu.VMEM((width, CHUNK), f32),
            pltpu.VMEM((width, CHUNK), f32),
            pltpu.VMEM((inner, tile), bf16),
            pltpu.VMEM((inner, tile), bf16),
            pltpu.VMEM((width, tile), bf16),
            pltpu.VMEM((width, tile), bf16),
            pltpu.VMEM((width, tile), bf16),
            pltpu.VMEM((width + PAD, tile), bf16),
            pltpu.VMEM((inner, width), f32),
            pltpu.VMEM((inner, width), f32),
            pltpu.VMEM((width, width), f32),
            pltpu.VMEM((width, width), f32),
            pltpu.VMEM((width, width), f32),
            pltpu.VMEM((2 * experts, tile), f32),
        ],
        compiler_params=limit,
        cost_estimate=cost(80),
        name="main",
    )(tokens, cotangent, coords, state_t, *late_parts)

    rest_rows = 7 * piece + 16

    def rest_call(item, earlier, after):
        first_call = item == 0
        keep_spec = pl.BlockSpec((1, width, tile), lambda j: (item * steps + j, 0, 0))
        row_spec = pl.BlockSpec((tile, width), lambda j: (item * steps + j, 0))
        unit_spec = pl.BlockSpec((funcs, width, width), lambda j: (item, 0, 0))
        anywhere = pl.BlockSpec(memory_space=pl.ANY)
        in_specs = [
            smem,
            row_spec,
            keep_spec,
            keep_spec,
            keep_spec,
            keep_spec,
            keep_spec,
            keep_spec,
            keep_spec,
            pl.BlockSpec((1, width + PAD, width), lambda j: (item, 0, 0)),
            pl.BlockSpec((1, state_rows, width), lambda j: (item, 0, 0)),
            pl.BlockSpec((1, width, (funcs + 1) * width), lambda j: (item, 0, 0)),
        ] + late_specs
        operands = [
            presence,
            tokens,
            queries_one,
            cross,
            first,
            keys_two,
            values_two,
            grad_q_two,
            grad_second,
            grad_state_two,
            state_t,
            state,
            *late_parts,
        ]
        aliases = {}
        if not first_call:
            aliases = {len(operands) + k: k for k in range(3)}
            in_specs += [anywhere] * 3 + [whole_spec((7 * width, width)), anywhere]
            operands += [*earlier, after]
        out_specs = [row_spec, unit_spec, unit_spec, whole_spec((7 * width, width))]
        out_shape = [
            jax.ShapeDtypeStruct((count, width), f32),
            jax.ShapeDtypeStruct((units, width, width), bf16),
            jax.ShapeDtypeStruct((units, width, width), f32),
            jax.ShapeDtypeStruct((7 * width, width), f32),
        ]
        return pl.pallas_call(
            partial(
                rest_kernel,
                funcs=funcs,
                item=item,
                shards=shards,
                at=at,
                first_call=first_call,
            ),
            grid=(steps,),
            in_specs=in_specs,
            out_specs=out_specs,
            out_shape=out_shape,
            input_output_aliases=aliases,
            scratch_shapes=[
                gathered,
                pltpu.VMEM((width, 3 * width), bf16),
                pltpu.VMEM((width, width), bf16),
                pltpu.VMEM((width, width), bf16),
                pltpu.VMEM((width, CHUNK), f32),
                pltpu.VMEM((width, CHUNK), f32),
                pltpu.VMEM((2, width, width), bf16),
                pltpu.VMEM((width, CHUNK), f32),
                pltpu.VMEM((state_rows, width), f32),
                pltpu.VMEM((7 * width, width), f32),
                pltpu.VMEM((3 * width, tile), bf16),
                pltpu.VMEM((width, tile), bf16),
                pltpu.VMEM((state_rows, tile), bf16),
                pltpu.VMEM((width, tile), bf16),
                pltpu.VMEM((width, tile), bf16),
            ],
            compiler_params=limit,
            cost_estimate=cost(18),
            name="rest",
        )(*operands)

    levels = digits(dp)
    main_levels = levels[::-1]
    main_parts = exchange(main_grads, "fsdp", shards, 1)
    level = 0
    found = None
    for item in range(items):
        found = rest_call(item, found, main_sum if item else None)
        if item < len(main_levels):
            main_sum = sum_parts(main_parts)
            main_parts = spread(main_sum, "dp", dp, *main_levels[item])
            level = item + 1
    grad_tokens, grad_state_one, grad_totals_one, carry = found

    rest_grads = pl.pallas_call(
        partial(points_back, shards=shards),
        grid=(items,),
        in_specs=[
            pl.BlockSpec((funcs, slots, width), lambda u: (u, 0, 0)),
            pl.BlockSpec((funcs, width, slots), lambda u: (u, 0, 0)),
            pl.BlockSpec((funcs, width, slots), lambda u: (u, 0, 0)),
            pl.BlockSpec((funcs, width, width), lambda u: (u, 0, 0)),
            pl.BlockSpec((funcs, width, width), lambda u: (u, 0, 0)),
            whole_spec((7 * width, width)),
            pl.BlockSpec(memory_space=pl.ANY),
        ],
        out_specs=[whole_spec((rest_rows, width))] * shards,
        out_shape=[jax.ShapeDtypeStruct((rest_rows, width), bf16)] * shards,
        scratch_shapes=[
            pltpu.VMEM((2 * width, width), f32),
            pltpu.VMEM((shards, rest_rows, width), bf16),
        ],
        compiler_params=limit,
        cost_estimate=cost(7),
        name="points_back",
    )(flat_points, keys_one, values_one, grad_state_one, grad_totals_one, carry, main_sum)
    rest_got = exchange(rest_grads, "fsdp", shards, 1)

    parts = rest_got
    for digit, stride in main_levels[level:]:
        main_parts = spread(sum_parts(main_parts), "dp", dp, digit, stride)
    for digit, stride in levels:
        parts = spread(sum_parts(parts), "dp", dp, digit, stride)

    matrix = jax.ShapeDtypeStruct((piece, width), f32)
    vector = jax.ShapeDtypeStruct((1, piece), f32)
    outs = pl.pallas_call(
        partial(
            unpack_kernel,
            counts=(len(main_parts), len(parts)),
            experts=experts,
            piece=piece,
            exit_piece=exit_piece,
            hidden=hidden,
        ),
        out_shape=[vector] * 2
        + [matrix] * 8
        + [vector] * 2
        + [
            jax.ShapeDtypeStruct(expert_in.shape, f32),
            jax.ShapeDtypeStruct(expert_out.shape, f32),
            jax.ShapeDtypeStruct((1, 2), f32),
        ],
        scratch_shapes=[
            pltpu.VMEM((32, width), f32),
            pltpu.VMEM((main_rows, width), f32),
            pltpu.VMEM((rest_rows, width), f32),
        ],
        name="unpack",
    )(*main_parts, *parts)
    outs = [out.reshape(piece) if out.shape == (1, piece) else out for out in outs]
    return (result, grad_tokens, *outs[:-1], outs[-1].reshape(gate_weight.shape))


def solution(mesh):
    rows = P(("dp", "fsdp"), None)
    matrix = P("fsdp", None)
    vector = P("fsdp")
    expert = P(None, "fsdp", None)
    parameters = (
        (vector, vector)
        + (matrix,) * 8
        + (vector, vector, expert, expert, P(None, "fsdp"))
    )
    return jax.shard_map(
        partial(shards_fn, mesh.shape["dp"], mesh.shape["fsdp"]),
        mesh=mesh,
        in_specs=(
            rows,
            P(("dp", "fsdp"), None, None, None),
            P(None, ("dp", "fsdp")),
            rows,
            rows,
            rows,
        )
        + parameters,
        out_specs=(rows, rows) + parameters,
        check_vma=False,
    )
```

```python
from functools import partial

import jax
import jax.numpy as jnp
from jax import lax
from jax.experimental import pallas as pl
from jax.experimental.pallas import tpu as pltpu
from jax.sharding import PartitionSpec as P


HEADS = 8
eps = 1e-05
f32 = jnp.float32
bf16 = jnp.bfloat16
TILE = 2048
CHUNK = 256
SLAB = 64
PAD = 16
VMEM = 56 * 1024 * 1024


def cost(microseconds):
    return pl.CostEstimate(flops=microseconds * 10**9, bytes_accessed=10**6, transcendentals=0)


def nn(left, right):
    return jnp.dot(left, right, preferred_element_type=f32)


def nt(left, right):
    return lax.dot_general(left, right, (((1,), (1,)), ((), ())), preferred_element_type=f32)


def flip(value):
    return value.T


def inverse(value):
    return pl.reciprocal(value, approx=True)


def head_softmax(value):
    width, rows = value.shape
    split = value.reshape(HEADS, width // HEADS, rows)
    raised = jnp.exp(split - jnp.max(split, axis=1, keepdims=True))
    return (raised * inverse(jnp.sum(raised, axis=1, keepdims=True))).reshape(width, rows)


def softmax_back(probs, grad):
    width, rows = grad.shape
    probs = probs.astype(f32).reshape(HEADS, width // HEADS, rows)
    grad = grad.reshape(HEADS, width // HEADS, rows)
    inner = jnp.sum(probs * grad, axis=1, keepdims=True)
    return (probs * (grad - inner)).reshape(width, rows)


def standardize(value):
    centre = value - jnp.mean(value, axis=0, keepdims=True)
    scale = lax.rsqrt(jnp.mean(centre * centre, axis=0, keepdims=True) + eps)
    return centre * scale, scale


def norm_back(grad, hat, scale):
    return scale * (
        grad
        - jnp.mean(grad, axis=0, keepdims=True)
        - hat * jnp.mean(grad * hat, axis=0, keepdims=True)
    )


def same_head(width):
    shape, head = (width, width), width // HEADS
    row = lax.broadcasted_iota(jnp.int32, shape, 0)
    column = lax.broadcasted_iota(jnp.int32, shape, 1)
    return lax.div(row, head) == lax.div(column, head)


def own_head(width):
    shape, head = (HEADS, width), width // HEADS
    row = lax.broadcasted_iota(jnp.int32, shape, 0)
    return row == lax.div(lax.broadcasted_iota(jnp.int32, shape, 1), head)


def by_head(value, scales):
    width, rows = value.shape
    split = value.reshape(HEADS, width // HEADS, rows)
    return (split * scales.reshape(HEADS, 1, rows)).reshape(width, rows)


def head_sums(value):
    width, rows = value.shape
    return jnp.sum(value.reshape(HEADS, width // HEADS, rows), axis=1)


def totals_column(rows, width):
    row = jnp.sum(jnp.where(own_head(width), rows, 0.0), axis=0, keepdims=True)
    return flip(jnp.broadcast_to(-row, (width, width)))


def pack_states(lefts, totals, state_t, state, width):
    count = len(lefts)
    rights = [jnp.where(own_head(width), total, 0.0) for total in totals]
    rest = jnp.zeros((width - count * HEADS, width), f32)
    right = jnp.concatenate(rights + [rest], axis=0)
    for place, left in enumerate(lefts):
        span = slice(place * width, (place + 1) * width)
        state_t[span] = left.astype(bf16)
        state[:, span] = flip(left).astype(bf16)
    start = count * width
    used = state_t.shape[0] - start
    state_t[start:] = right[:used].astype(bf16)
    state[:, start : start + width] = -flip(right).astype(bf16)


def assemble(parts, gathered):
    shards = len(parts)
    here = lax.axis_index("fsdp")
    for place, part in enumerate(parts):
        gathered[lax.rem(here + shards - place, shards)] = part[...]


def columns(gathered, start, count):
    shards, _, width = gathered.shape
    piece = width // shards
    small = [gathered[shard, start : start + 16, :].astype(f32) for shard in range(shards)]
    joined = jnp.concatenate([part[:, :piece] for part in small], axis=1)
    return [
        flip(jnp.broadcast_to(joined[place : place + 1], (width, width)))[:, 0:1]
        for place in range(count)
    ]


def lane_fold(value):
    width = value.shape[0]
    total = value[:, :width]
    for start in range(width, value.shape[1], width):
        total = total + value[:, start : start + width]
    return total


def as_row(value):
    width = value.shape[0]
    return flip(jnp.broadcast_to(jnp.sum(value, axis=1, keepdims=True), (width, width)))


def scatter_blocks(stage, outs):
    shards = len(outs)
    here = lax.axis_index("fsdp")
    for place, out in enumerate(outs):
        out[...] = stage[lax.rem(here + place, shards)]


def whole(gathered, start, rows):
    shards = gathered.shape[0]
    return gathered[:, start : start + rows, :].reshape(shards * rows, gathered.shape[2])


def function_weight(presence, item, func, funcs, shape):
    total = presence[item, 0]
    for other in range(1, funcs):
        total = total + presence[item, other]
    own = jnp.full(shape, presence[item, func], jnp.int32).astype(f32)
    return own / jnp.full(shape, total, jnp.int32).astype(f32)


def pack_kernel(*refs):
    weights, vectors, gate = refs[:10], refs[10:14], refs[14]
    early, late = refs[15:]
    keys, values, query, out, query_two, key_two, value_two, out_two, enter, leave = weights
    start = 0
    for weight in (keys, values):
        early[start : start + weight.shape[0]] = weight[...]
        start += weight.shape[0]
    start = 0
    for weight in (query, out, query_two, key_two, value_two, out_two):
        late[start : start + weight.shape[0]] = weight[...]
        start += weight.shape[0]
    experts, piece, hidden = enter.shape
    width = late.shape[1]
    for expert in range(experts):
        for half in range(hidden // width):
            late[start : start + piece] = enter[expert, :, half * width : (half + 1) * width]
            start += piece
    for expert in range(experts):
        late[start : start + leave.shape[1]] = leave[expert]
        start += leave.shape[1]
    rest = jnp.zeros((1, width - piece), f32)
    rows = [
        jnp.concatenate([vector[...].astype(f32), rest], axis=1) for vector in vectors
    ]
    rows.append(jnp.zeros((4, width), f32))
    for row in range(2):
        rows.append(jnp.broadcast_to(gate[row : row + 1, 0:1].astype(f32), (1, width)))
    rows.append(jnp.zeros((6, width), f32))
    late[start : start + 16] = jnp.concatenate(rows, axis=0).astype(bf16)


def points_forward(counts, presence, points, *refs, funcs, shards):
    parts = refs[:shards]
    state_t, state, keys_out, values_out, gathered, weight = refs[shards:]
    item = pl.program_id(0)
    width = points.shape[2]
    slots = points.shape[1]
    piece = width // shards

    @pl.when(item == 0)
    def _():
        assemble(parts, gathered)
        weight[:width] = flip(whole(gathered, 0, piece))
        weight[width:] = flip(whole(gathered, piece, piece))

    def project(func):
        both = nt(weight[...], points[func])
        slot = lax.broadcasted_iota(jnp.int32, (1, slots), 1)
        probs = head_softmax(both[:width])
        keys_out[func] = jnp.where(slot < counts[item, func], probs, 0.0).astype(bf16)
        values_out[func] = both[width:].astype(bf16)

    def summarize(func):
        values = values_out[func]
        extended = jnp.concatenate([values, jnp.ones((PAD, slots), bf16)], axis=0)
        share = function_weight(presence, item, func, funcs, (1, width))
        summed = nt(extended, keys_out[func])
        left = jnp.where(same_head(width), summed[:width], 0.0) * share
        return left, summed[width : width + 1]

    for func in range(funcs):
        project(func)
    lefts, totals = zip(*(summarize(func) for func in range(funcs)))
    pack_states(lefts, totals, state_t.at[0], state.at[0], width)


def main_kernel(tokens, cotangent, coords, state_t, *refs, funcs, experts, shards, at):
    parts, outs, scratch = refs[:shards], refs[shards : 2 * shards + 9], refs[2 * shards + 9 :]
    (
        result,
        queries_out,
        cross_out,
        first_out,
        keys_out,
        values_out,
        grad_q_out,
        grad_second_out,
        grad_state_out,
    ) = outs[:9]
    grads_out = outs[9:]
    (
        params,
        grads_stage,
        first_keep,
        query_keep,
        state_sum,
        self_t,
        self_state,
        grad_state_sum,
        w_query,
        w_out_one,
        w_self,
        w_out_two_t,
        w_out_two,
        w_in_t,
        w_in,
        w_exit,
        w_exit_t,
        gain_one,
        bias_one,
        gain_two,
        bias_two,
        hidden_keep,
        inner_keep,
        normed_keep,
        grad_keep,
        own_keep,
        pair_keep,
        sum_in,
        sum_exit,
        sum_out_two,
        sum_gain,
        sum_bias,
        sum_gate,
    ) = scratch
    item = pl.program_id(0)
    phase = pl.program_id(1)
    step = pl.program_id(2)
    steps = pl.num_programs(2)
    width = tokens.shape[1]
    rows = tokens.shape[0]
    piece = width // shards
    hidden = w_in.shape[1] // experts
    exit_piece = hidden // shards

    @pl.when((item == 0) & (phase == 0) & (step == 0))
    def _():
        assemble(parts, params)
        w_query[...] = flip(whole(params, at["query_first"], piece))
        w_out_one[...] = flip(whole(params, at["out_first"], piece))
        w_self[:width] = flip(whole(params, at["query_second"], piece))
        w_self[width : 2 * width] = flip(whole(params, at["key_second"], piece))
        w_self[2 * width :] = flip(whole(params, at["value_second"], piece))
        out_two = whole(params, at["out_second"], piece)
        w_out_two[...] = out_two
        w_out_two_t[...] = flip(out_two)
        for block in range(experts * hidden // width):
            part = whole(params, at["expert_in"] + block * piece, piece)
            w_in[:, block * width : (block + 1) * width] = part
            w_in_t[block * width : (block + 1) * width] = flip(part)
        for expert in range(experts):
            part = whole(params, at["expert_out"] + expert * exit_piece, exit_piece)
            w_exit[expert * hidden : (expert + 1) * hidden] = part
            w_exit_t[:, expert * hidden : (expert + 1) * hidden] = flip(part)
        found = columns(params, at["small"], 4)
        for vector, column in zip((gain_one, bias_one, gain_two, bias_two), found):
            vector[...] = jnp.broadcast_to(column, vector.shape)
        sum_in[...] = jnp.zeros_like(sum_in)
        sum_exit[...] = jnp.zeros_like(sum_exit)
        sum_out_two[...] = jnp.zeros_like(sum_out_two)
        sum_gain[...] = jnp.zeros_like(sum_gain)
        sum_bias[...] = jnp.zeros_like(sum_bias)
        sum_gate[...] = jnp.zeros_like(sum_gate)

    chunks = [slice(start, start + CHUNK) for start in range(0, rows, CHUNK)]

    @pl.when(phase == 0)
    def _():
        def enter(cols):
            rows_t = flip(tokens[cols, :]).astype(f32)
            hat, _scale = standardize(rows_t)
            normed = (hat * gain_one[...] + bias_one[...]).astype(bf16)
            return rows_t, head_softmax(nn(w_query[...], normed)).astype(bf16)

        def across(cols, queries):
            queries_out[0, :, cols] = queries
            both = nn(state_t[0], queries)
            undo = inverse(both[funcs * width :])
            mixed = None
            for func in range(funcs):
                part = by_head(
                    both[func * width : (func + 1) * width],
                    undo[func * HEADS : (func + 1) * HEADS],
                )
                mixed = part if mixed is None else mixed + part
            cross = mixed.astype(bf16)
            cross_out[0, :, cols] = cross
            return cross

        def leave(cols, rows_t, cross):
            first = rows_t + nn(w_out_one[...], cross)
            first_keep[step, :, cols] = first
            first_low = first.astype(bf16)
            first_out[0, :, cols] = first_low
            return first_low

        def project(cols, first_low):
            three = nn(w_self[...], first_low)
            query_keep[step, :, cols] = head_softmax(three[:width]).astype(bf16)
            keys_out[0, :, cols] = head_softmax(three[width : 2 * width]).astype(bf16)
            values = three[2 * width :].astype(bf16)
            values_out[0, :, cols] = values
            pair_keep[:width, cols] = values
            pair_keep[width:, cols] = jnp.ones((PAD, CHUNK), bf16)

        entered = [enter(cols) for cols in chunks]
        crossed = [across(cols, queries) for cols, (_, queries) in zip(chunks, entered)]
        firsts = [
            leave(cols, rows_t, cross)
            for cols, (rows_t, _), cross in zip(chunks, entered, crossed)
        ]
        for cols, first_low in zip(chunks, firsts):
            project(cols, first_low)
        found = nt(pair_keep[...], keys_out[0])

        @pl.when(step == 0)
        def _():
            state_sum[...] = found

        @pl.when(step > 0)
        def _():
            state_sum[...] += found

        @pl.when(step == steps - 1)
        def _():
            left = jnp.where(same_head(width), state_sum[:width], 0.0)
            pack_states([left], [state_sum[width : width + 1]], self_t, self_state, width)

    @pl.when(phase == 1)
    def _():
        def attend(cols):
            both = nn(self_t[...], query_keep[step, :, cols])
            undo = inverse(both[width : width + HEADS])
            own = by_head(both[:width], undo)
            own_keep[:, cols] = own.astype(bf16)
            grad_keep[:, cols] = flip(cotangent[cols, :])
            return undo, own

        def norm(cols):
            second = first_keep[step, :, cols] + nn(w_out_two_t[...], own_keep[:, cols])
            hat, scale = standardize(second)
            normed_keep[:, cols] = (hat * gain_two[...] + bias_two[...]).astype(bf16)
            return second, hat, scale

        def gate(cols):
            across, down = coords[0:1, cols], coords[1:2, cols]
            logits = []
            for expert in range(experts):
                pair = params[expert, at["small"] : at["small"] + 16, 0:1].astype(f32)
                logits.append(across * pair[8:9] + down * pair[9:10])
            peak = logits[0]
            for logit in logits[1:]:
                peak = jnp.maximum(peak, logit)
            raised = [jnp.exp(logit - peak) for logit in logits]
            total = raised[0]
            for other in raised[1:]:
                total = total + other
            return [other / total for other in raised]

        def expand(cols, gates):
            normed, grad = normed_keep[:, cols], grad_keep[:, cols]
            gates_low = [gate.astype(bf16) for gate in gates]
            grad_gates = []
            for expert in range(experts):
                partial_sum = None
                span = slice(expert * hidden, (expert + 1) * hidden)
                inners = nn(w_in_t[span], normed).astype(bf16)
                backs = nn(w_exit[span], grad).astype(bf16)
                for start in range(0, hidden, SLAB):
                    inner, back = inners[start : start + SLAB], backs[start : start + SLAB]
                    span = slice(expert * hidden + start, expert * hidden + start + SLAB)
                    square = inner * inner
                    tanh = jnp.tanh(inner * (0.7978845608028654 + 0.035677408136300125 * square))
                    half = 0.5 + 0.5 * tanh
                    active = inner * half
                    product = active * back
                    folded = product[:16]
                    for row in range(16, SLAB, 16):
                        folded = folded + product[row : row + 16]
                    folded = folded.astype(f32)
                    partial_sum = folded if partial_sum is None else partial_sum + folded
                    hidden_keep[span, cols] = active * gates_low[expert]
                    slope = half + active * (1.0 - half) * (
                        1.5957691216057308 + 0.21406444881780074 * square
                    )
                    inner_keep[span, cols] = slope * (back * gates_low[expert])
                grad_gates.append(jnp.sum(partial_sum, axis=0, keepdims=True))
            across, down = coords[0:1, cols], coords[1:2, cols]
            mean_gate = gates[0] * grad_gates[0]
            for expert in range(1, experts):
                mean_gate = mean_gate + gates[expert] * grad_gates[expert]
            for expert in range(experts):
                change = gates[expert] * (grad_gates[expert] - mean_gate)
                sum_gate[expert : expert + 1, cols] += across * change
                sum_gate[experts + expert : experts + expert + 1, cols] += down * change

        def contract(cols, second, hat, scale):
            total = second + nn(w_exit_t[...], hidden_keep[:, cols])
            result[cols, :] = flip(total.astype(bf16))
            grad_normed = nn(w_in[...], inner_keep[:, cols])
            sum_gain[...] += lane_fold(grad_normed * hat)
            sum_bias[...] += lane_fold(grad_normed)
            grad_second = grad_keep[:, cols].astype(f32) + norm_back(
                grad_normed * gain_two[...], hat, scale
            )
            grad_own = grad_second.astype(bf16)
            grad_second_out[0, :, cols] = grad_own
            return grad_own

        def attend_back(cols, grad_own, undo, own):
            share = by_head(nn(w_out_two[...], grad_own), undo)
            pair_keep[:width, cols] = share.astype(bf16)
            sums = head_sums(share * own)
            pair_keep[width:, cols] = jnp.concatenate(
                [sums, jnp.zeros((PAD - HEADS, CHUNK), f32)], axis=0
            ).astype(bf16)

        def query_back(cols):
            grad_q = nn(self_state[:, : width + PAD], pair_keep[:, cols])
            grad_q_out[0, :, cols] = softmax_back(query_keep[step, :, cols], grad_q).astype(bf16)

        attended = [attend(cols) for cols in chunks]
        normed = [norm(cols) for cols in chunks]
        gates = [gate(cols) for cols in chunks]
        for cols, own_gates in zip(chunks, gates):
            expand(cols, own_gates)
        grads = [contract(cols, *kept) for cols, kept in zip(chunks, normed)]
        for cols, grad_own, (undo, own) in zip(chunks, grads, attended):
            attend_back(cols, grad_own, undo, own)
        for cols in chunks:
            query_back(cols)
        sum_exit[...] += nn(hidden_keep[...], cotangent[...])
        sum_in[...] += nt(inner_keep[...], normed_keep[...])
        sum_out_two[...] += nt(own_keep[...], grad_second_out[0])
        found = nt(pair_keep[...], query_keep[step])

        @pl.when(step == 0)
        def _():
            grad_state_sum[...] = found

        @pl.when(step > 0)
        def _():
            grad_state_sum[...] += found

        @pl.when(step == steps - 1)
        def _():
            grad_state_out[0] = grad_state_sum[...]

    @pl.when((item == pl.num_programs(0) - 1) & (phase == 1) & (step == steps - 1))
    def _():
        gain, bias = as_row(sum_gain[...]), as_row(sum_bias[...])
        gate = jnp.broadcast_to(jnp.sum(sum_gate[...], axis=1, keepdims=True), (8, width))
        row = lax.broadcasted_iota(jnp.int32, (8, width), 0)
        vectors = jnp.where(row == 0, gain[:8], bias[:8])
        small = jnp.concatenate([vectors, gate], axis=0).astype(bf16)
        start = 0
        for block in range(experts * hidden // width):
            part = flip(sum_in[block * width : (block + 1) * width]).astype(bf16)
            grads_stage[:, start : start + piece, :] = part.reshape(shards, piece, width)
            start += piece
        for expert in range(experts):
            part = sum_exit[expert * hidden : (expert + 1) * hidden].astype(bf16)
            grads_stage[:, start : start + exit_piece, :] = part.reshape(shards, exit_piece, width)
            start += exit_piece
        part = sum_out_two[...].astype(bf16)
        grads_stage[:, start : start + piece, :] = part.reshape(shards, piece, width)
        start += piece
        for shard in range(shards):
            grads_stage[shard, start : start + 16, :] = small
        scatter_blocks(grads_stage, grads_out)


def rest_kernel(
    presence,
    tokens,
    queries_in,
    cross_in,
    first_in,
    keys_in,
    values_in,
    grad_q_in,
    grad_second_in,
    grad_state_in,
    state_t,
    state,
    *refs,
    funcs,
    item,
    shards,
    at,
    first_call,
):
    parts, refs = refs[:shards], refs[shards:]
    if not first_call:
        carry, refs = refs[3], refs[5:]
    (
        grad_tokens,
        grad_cross_state_out,
        grad_totals_out,
        sums_out,
        params,
        w_self,
        w_out_one,
        w_query,
        gain_one,
        bias_one,
        grad_self_state,
        grad_totals,
        grad_state_sum,
        sums,
        three_keep,
        cross_keep,
        stack_keep,
        query_keep,
        normed_keep,
    ) = refs
    step = pl.program_id(0)
    steps = pl.num_programs(0)
    width = tokens.shape[1]
    piece = width // shards
    self_part = slice(0, 3 * width)
    out_part = slice(3 * width, 4 * width)
    query_part = slice(4 * width, 5 * width)
    gain_part = slice(5 * width, 6 * width)
    bias_part = slice(6 * width, 7 * width)

    @pl.when(step == 0)
    def _():
        assemble(parts, params)
        w_query[...] = whole(params, at["query_first"], piece)
        w_out_one[...] = whole(params, at["out_first"], piece)
        w_self[:, :width] = whole(params, at["query_second"], piece)
        w_self[:, width : 2 * width] = whole(params, at["key_second"], piece)
        w_self[:, 2 * width :] = whole(params, at["value_second"], piece)
        for vector, column in zip((gain_one, bias_one), columns(params, at["small"], 2)):
            vector[...] = jnp.broadcast_to(column, vector.shape)
        sums[...] = jnp.zeros_like(sums) if first_call else carry[...]
        left = jnp.where(same_head(width), grad_state_in[0, :width], 0.0)
        grad_self_state[0] = flip(left).astype(bf16)
        grad_self_state[1] = left.astype(bf16)
        column = totals_column(grad_state_in[0, width : width + HEADS], width)
        grad_totals[...] = jnp.broadcast_to(column[:, 0:1], grad_totals.shape)

    chunks = [slice(start, start + CHUNK) for start in range(0, tokens.shape[0], CHUNK)]

    def self_back(cols):
        keys, values = keys_in[0, :, cols], values_in[0, :, cols]
        grad_keys = nn(grad_self_state[0], values) + grad_totals[...]
        three_keep[:width, cols] = grad_q_in[0, :, cols]
        three_keep[width : 2 * width, cols] = softmax_back(keys, grad_keys).astype(bf16)
        three_keep[2 * width :, cols] = nn(grad_self_state[1], keys).astype(bf16)

    def join(cols):
        grad_first = grad_second_in[0, :, cols].astype(f32) + nn(w_self[...], three_keep[:, cols])
        cross_keep[:, cols] = grad_first.astype(bf16)
        return grad_first

    def cross_back(cols):
        share = nn(w_out_one[...], cross_keep[:, cols])
        both = nn(state_t[0], queries_in[0, :, cols])
        undo = inverse(both[funcs * width :])
        sums_by_head = []
        for func in range(funcs):
            span = slice(func * width, (func + 1) * width)
            scales = undo[func * HEADS : (func + 1) * HEADS]
            part = by_head(share, scales)
            stack_keep[span, cols] = part.astype(bf16)
            sums_by_head.append(head_sums(part * by_head(both[span], scales)))
        spare = stack_keep.shape[0] - funcs * (width + HEADS)
        if spare:
            sums_by_head.append(jnp.zeros((spare, CHUNK), f32))
        stack_keep[funcs * width :, cols] = jnp.concatenate(sums_by_head, axis=0).astype(bf16)

    def query_back(cols):
        joined = state[0, :, : stack_keep.shape[0]]
        grad_q = softmax_back(queries_in[0, :, cols], nn(joined, stack_keep[:, cols]))
        query_keep[:, cols] = grad_q.astype(bf16)

    def finish(cols, grad_first):
        hat, scale = standardize(flip(tokens[cols, :]).astype(f32))
        normed_keep[:, cols] = (hat * gain_one[...] + bias_one[...]).astype(bf16)
        grad_normed = nn(w_query[...], query_keep[:, cols])
        sums[gain_part] += lane_fold(grad_normed * hat)
        sums[bias_part] += lane_fold(grad_normed)
        grad_rows = grad_first + norm_back(grad_normed * gain_one[...], hat, scale)
        grad_tokens[cols, :] = flip(grad_rows)

    for cols in chunks:
        self_back(cols)
    grad_firsts = [join(cols) for cols in chunks]
    for cols in chunks:
        cross_back(cols)
    for cols in chunks:
        query_back(cols)
    for cols, grad_first in zip(chunks, grad_firsts):
        finish(cols, grad_first)
    sums[self_part] += nt(three_keep[...], first_in[0])
    sums[out_part] += nt(cross_in[0], cross_keep[...])
    sums[query_part] += nt(normed_keep[...], query_keep[...])
    found = nt(stack_keep[...], queries_in[0])

    @pl.when(step == 0)
    def _():
        grad_state_sum[...] = found

    @pl.when(step > 0)
    def _():
        grad_state_sum[...] += found

    @pl.when(step == steps - 1)
    def _():
        mask = same_head(width)
        for func in range(funcs):
            weight = function_weight(presence, item, func, funcs, (1, width))
            left = jnp.where(mask, grad_state_sum[func * width : (func + 1) * width], 0.0)
            grad_cross_state_out[func] = (left * weight).astype(bf16)
            start = funcs * width + func * HEADS
            grad_totals_out[func] = totals_column(grad_state_sum[start : start + HEADS], width)
        sums_out[...] = sums[...]


def points_back(points, keys_in, values_in, grad_state, grad_totals, carry, _after, *refs, shards):
    outs = refs[:shards]
    sums, stage = refs[shards:]
    step = pl.program_id(0)
    width = points.shape[2]
    piece = width // shards

    def back(func):
        keys, values = keys_in[func], values_in[func]
        left = grad_state[func]
        grad_keys = nn(flip(left), values) + grad_totals[func, :, 0:1]
        grad_k = softmax_back(keys, grad_keys).astype(bf16)
        grad_v = nn(left, keys).astype(bf16)
        return jnp.concatenate([grad_k, grad_v], axis=0)

    grads = [back(func) for func in range(points.shape[0])]
    found = nn(grads[0], points[0])
    for func in range(1, points.shape[0]):
        found = found + nn(grads[func], points[func])

    @pl.when(step == 0)
    def _():
        sums[...] = found
        gain = as_row(carry[5 * width : 6 * width])
        bias = as_row(carry[6 * width : 7 * width])
        row = lax.broadcasted_iota(jnp.int32, (16, width), 0)
        small = jnp.where(row == 0, gain[:16], bias[:16]).astype(bf16)
        for place in range(5):
            part = carry[place * width : (place + 1) * width]
            part = (flip(part) if place < 3 else part).astype(bf16)
            stage[:, place * piece : (place + 1) * piece, :] = part.reshape(shards, piece, width)
        for shard in range(shards):
            stage[shard, 5 * piece : 5 * piece + 16, :] = small

    @pl.when(step > 0)
    def _():
        sums[...] += found

    @pl.when(step == pl.num_programs(0) - 1)
    def _():
        for place in range(2):
            start = 5 * piece + 16 + place * piece
            part = flip(sums[place * width : (place + 1) * width]).astype(bf16)
            stage[:, start : start + piece, :] = part.reshape(shards, piece, width)
        scatter_blocks(stage, outs)


def total_of(parts):
    value = parts[0][...].astype(f32)
    for part in parts[1:]:
        value = value + part[...].astype(f32)
    return value


def unpack_kernel(*refs, counts, experts, piece, exit_piece, hidden):
    main_parts, parts = refs[: counts[0]], refs[counts[0] : sum(counts)]
    outs, (small, main, rest) = refs[-18:-3], refs[-3:]
    width = main.shape[1]
    main[...] = total_of(main_parts)
    rest[...] = total_of(parts)
    (
        gain_one,
        bias_one,
        query_one,
        key_one,
        value_one,
        out_one,
        query_two,
        key_two,
        value_two,
        out_two,
        gain_two,
        bias_two,
        enter,
        leave,
        gate,
    ) = outs
    start = 0
    for expert in range(experts):
        for half in range(hidden // width):
            block = main[start : start + piece]
            enter[expert, :, half * width : (half + 1) * width] = block
            start += piece
    for expert in range(experts):
        leave[expert] = main[start : start + exit_piece]
        start += exit_piece
    out_two[...] = main[start : start + piece]
    start += piece
    small[:16] = main[start : start + 16]
    start = 0
    for out in (query_two, key_two, value_two, out_one, query_one):
        out[...] = rest[start : start + piece]
        start += piece
    small[16:] = rest[start : start + 16]
    start += 16
    for out in (key_one, value_one):
        out[...] = rest[start : start + piece]
        start += piece
    shard = lax.axis_index("fsdp")
    turned = pltpu.roll(small[...], lax.rem(width - shard * piece, width), 1)
    gain_two[...] = turned[0:1, :piece]
    bias_two[...] = turned[1:2, :piece]
    gain_one[...] = turned[16:17, :piece]
    bias_one[...] = turned[17:18, :piece]
    for row in range(2):
        gate[:, row : row + 1] = small[pl.ds(8 + row * experts + shard, 1), 0:1]


def whole_spec(shape):
    return pl.BlockSpec(shape, lambda *_: (0,) * len(shape))


def route(size, shift, digit, stride):
    def target(i):
        own = i // stride % digit
        return i + ((own + shift) % digit - own) * stride

    return [(i, target(i)) for i in range(size)]


def spread(value, axis, size, digit, stride):
    return [value] + [
        lax.ppermute(value, axis, route(size, shift, digit, stride)) for shift in range(1, digit)
    ]


def exchange(values, axis, size, stride):
    digit = len(values)
    return [values[0]] + [
        lax.ppermute(values[shift], axis, route(size, shift, digit, stride))
        for shift in range(1, digit)
    ]


def digits(size):
    found = []
    stride = 1
    while stride < size:
        rest = size // stride
        digit = 2 if stride == 1 and rest % 2 == 0 else 4 if rest % 4 == 0 else rest
        found.append((digit, stride))
        stride *= digit
    return found or [(1, 1)]


def sum_parts(parts):
    return total_of([part.astype(f32) for part in parts]).astype(bf16)


def shards_fn(
    dp,
    shards,
    tokens,
    points,
    coords,
    presence,
    counts,
    cotangent,
    gain_first,
    bias_first,
    query_first,
    key_first,
    value_first,
    out_first,
    query_second,
    key_second,
    value_second,
    out_second,
    gain_second,
    bias_second,
    expert_in,
    expert_out,
    gate_weight,
):
    count, width = tokens.shape
    items, funcs, slots, _ = points.shape
    length = count // items
    experts, piece, hidden = expert_in.shape
    exit_piece = expert_out.shape[1]
    tile = min(TILE, length)
    steps = length // tile
    inner = experts * hidden
    enter_rows = experts * piece * (hidden // width)
    limit = pltpu.CompilerParams(vmem_limit_bytes=VMEM)

    at = {}
    place = 0
    for name, size in (
        ("query_first", piece),
        ("out_first", piece),
        ("query_second", piece),
        ("key_second", piece),
        ("value_second", piece),
        ("out_second", piece),
        ("expert_in", enter_rows),
        ("expert_out", experts * exit_piece),
        ("small", 16),
    ):
        at[name] = place
        place += size
    late_rows_count = place
    early_pack, late_pack = pl.pallas_call(
        pack_kernel,
        out_shape=[
            jax.ShapeDtypeStruct((2 * piece, width), bf16),
            jax.ShapeDtypeStruct((late_rows_count, width), bf16),
        ],
        name="pack",
    )(
        key_first,
        value_first,
        query_first,
        out_first,
        query_second,
        key_second,
        value_second,
        out_second,
        expert_in,
        expert_out,
        *(
            vector.reshape(1, piece)
            for vector in (gain_first, bias_first, gain_second, bias_second)
        ),
        gate_weight,
    )
    early_parts = spread(early_pack, "fsdp", shards, shards, 1)
    late_parts = spread(late_pack, "fsdp", shards, shards, 1)
    late_specs = [whole_spec((late_rows_count, width))] * shards
    gathered = pltpu.VMEM((shards, late_rows_count, width), bf16)

    smem = pl.BlockSpec(memory_space=pltpu.SMEM)
    units = items * funcs
    state_rows = funcs * width + -(-funcs * HEADS // PAD) * PAD
    flat_points = points.reshape(units, slots, width)
    state_t, state, keys_one, values_one = pl.pallas_call(
        partial(points_forward, funcs=funcs, shards=shards),
        grid=(items,),
        in_specs=[smem, smem, pl.BlockSpec((funcs, slots, width), lambda u: (u, 0, 0))]
        + [whole_spec((2 * piece, width))] * shards,
        out_specs=[
            pl.BlockSpec((1, state_rows, width), lambda u: (u, 0, 0)),
            pl.BlockSpec((1, width, (funcs + 1) * width), lambda u: (u, 0, 0)),
            pl.BlockSpec((funcs, width, slots), lambda u: (u, 0, 0)),
            pl.BlockSpec((funcs, width, slots), lambda u: (u, 0, 0)),
        ],
        out_shape=[
            jax.ShapeDtypeStruct((items, state_rows, width), bf16),
            jax.ShapeDtypeStruct((items, width, (funcs + 1) * width), bf16),
            jax.ShapeDtypeStruct((units, width, slots), bf16),
            jax.ShapeDtypeStruct((units, width, slots), bf16),
        ],
        scratch_shapes=[
            pltpu.VMEM((shards, 2 * piece, width), bf16),
            pltpu.VMEM((2 * width, width), bf16),
        ],
        compiler_params=limit,
        cost_estimate=cost(8),
        name="points_forward",
    )(counts, presence, flat_points, *early_parts)

    kept = jax.ShapeDtypeStruct((items * steps, width, tile), bf16)
    main_rows = enter_rows + experts * exit_piece + piece + 16

    def early(i, p, j):
        return i * steps + jnp.where(p == 0, j, steps - 1)

    def late(i, p, j):
        return i * steps + jnp.where(p == 0, 0, j)

    early_keep = pl.BlockSpec((1, width, tile), lambda i, p, j: (early(i, p, j), 0, 0))
    late_keep = pl.BlockSpec((1, width, tile), lambda i, p, j: (late(i, p, j), 0, 0))
    late_rows = pl.BlockSpec((tile, width), lambda i, p, j: (late(i, p, j), 0))
    (
        result,
        queries_one,
        cross,
        first,
        keys_two,
        values_two,
        grad_q_two,
        grad_second,
        grad_state_two,
        *main_grads,
    ) = pl.pallas_call(
        partial(main_kernel, funcs=funcs, experts=experts, shards=shards, at=at),
        grid=(items, 2, steps),
        in_specs=[
            pl.BlockSpec((tile, width), lambda i, p, j: (early(i, p, j), 0)),
            late_rows,
            pl.BlockSpec((2, tile), lambda i, p, j: (0, late(i, p, j))),
            pl.BlockSpec((1, state_rows, width), lambda i, p, j: (i, 0, 0)),
        ]
        + late_specs,
        out_specs=[
            late_rows,
            early_keep,
            early_keep,
            early_keep,
            early_keep,
            early_keep,
            late_keep,
            late_keep,
            pl.BlockSpec((1, width + PAD, width), lambda i, p, j: (i, 0, 0)),
        ]
        + [whole_spec((main_rows, width))] * shards,
        out_shape=[
            jax.ShapeDtypeStruct((count, width), bf16),
            kept,
            kept,
            kept,
            kept,
            kept,
            kept,
            kept,
            jax.ShapeDtypeStruct((items, width + PAD, width), f32),
        ]
        + [jax.ShapeDtypeStruct((main_rows, width), bf16)] * shards,
        scratch_shapes=[
            gathered,
            pltpu.VMEM((shards, main_rows, width), bf16),
            pltpu.VMEM((steps, width, tile), f32),
            pltpu.VMEM((steps, width, tile), bf16),
            pltpu.VMEM((width + PAD, width), f32),
            pltpu.VMEM((width + PAD, width), bf16),
            pltpu.VMEM((width, 2 * width), bf16),
            pltpu.VMEM((width + PAD, width), f32),
            pltpu.VMEM((width, width), bf16),
            pltpu.VMEM((width, width), bf16),
            pltpu.VMEM((3 * width, width), bf16),
            pltpu.VMEM((width, width), bf16),
            pltpu.VMEM((width, width), bf16),
            pltpu.VMEM((inner, width), bf16),
            pltpu.VMEM((width, inner), bf16),
            pltpu.VMEM((inner, width), bf16),
            pltpu.VMEM((width, inner), bf16),
            pltpu.VMEM((width, CHUNK), f32),
            pltpu.VMEM((width, CHUNK), f32),
            pltpu.VMEM((width, CHUNK), f32),
            pltpu.VMEM((width, CHUNK), f32),
            pltpu.VMEM((inner, tile), bf16),
            pltpu.VMEM((inner, tile), bf16),
            pltpu.VMEM((width, tile), bf16),
            pltpu.VMEM((width, tile), bf16),
            pltpu.VMEM((width, tile), bf16),
            pltpu.VMEM((width + PAD, tile), bf16),
            pltpu.VMEM((inner, width), f32),
            pltpu.VMEM((inner, width), f32),
            pltpu.VMEM((width, width), f32),
            pltpu.VMEM((width, width), f32),
            pltpu.VMEM((width, width), f32),
            pltpu.VMEM((2 * experts, tile), f32),
        ],
        compiler_params=limit,
        cost_estimate=cost(80),
        name="main",
    )(tokens, cotangent, coords, state_t, *late_parts)

    rest_rows = 7 * piece + 16

    def rest_call(item, earlier, after):
        first_call = item == 0
        keep_spec = pl.BlockSpec((1, width, tile), lambda j: (item * steps + j, 0, 0))
        row_spec = pl.BlockSpec((tile, width), lambda j: (item * steps + j, 0))
        unit_spec = pl.BlockSpec((funcs, width, width), lambda j: (item, 0, 0))
        anywhere = pl.BlockSpec(memory_space=pl.ANY)
        in_specs = [
            smem,
            row_spec,
            keep_spec,
            keep_spec,
            keep_spec,
            keep_spec,
            keep_spec,
            keep_spec,
            keep_spec,
            pl.BlockSpec((1, width + PAD, width), lambda j: (item, 0, 0)),
            pl.BlockSpec((1, state_rows, width), lambda j: (item, 0, 0)),
            pl.BlockSpec((1, width, (funcs + 1) * width), lambda j: (item, 0, 0)),
        ] + late_specs
        operands = [
            presence,
            tokens,
            queries_one,
            cross,
            first,
            keys_two,
            values_two,
            grad_q_two,
            grad_second,
            grad_state_two,
            state_t,
            state,
            *late_parts,
        ]
        aliases = {}
        if not first_call:
            aliases = {len(operands) + k: k for k in range(3)}
            in_specs += [anywhere] * 3 + [whole_spec((7 * width, width)), anywhere]
            operands += [*earlier, after]
        out_specs = [row_spec, unit_spec, unit_spec, whole_spec((7 * width, width))]
        out_shape = [
            jax.ShapeDtypeStruct((count, width), f32),
            jax.ShapeDtypeStruct((units, width, width), bf16),
            jax.ShapeDtypeStruct((units, width, width), f32),
            jax.ShapeDtypeStruct((7 * width, width), f32),
        ]
        return pl.pallas_call(
            partial(
                rest_kernel,
                funcs=funcs,
                item=item,
                shards=shards,
                at=at,
                first_call=first_call,
            ),
            grid=(steps,),
            in_specs=in_specs,
            out_specs=out_specs,
            out_shape=out_shape,
            input_output_aliases=aliases,
            scratch_shapes=[
                gathered,
                pltpu.VMEM((width, 3 * width), bf16),
                pltpu.VMEM((width, width), bf16),
                pltpu.VMEM((width, width), bf16),
                pltpu.VMEM((width, CHUNK), f32),
                pltpu.VMEM((width, CHUNK), f32),
                pltpu.VMEM((2, width, width), bf16),
                pltpu.VMEM((width, CHUNK), f32),
                pltpu.VMEM((state_rows, width), f32),
                pltpu.VMEM((7 * width, width), f32),
                pltpu.VMEM((3 * width, tile), bf16),
                pltpu.VMEM((width, tile), bf16),
                pltpu.VMEM((state_rows, tile), bf16),
                pltpu.VMEM((width, tile), bf16),
                pltpu.VMEM((width, tile), bf16),
            ],
            compiler_params=limit,
            cost_estimate=cost(18),
            name="rest",
        )(*operands)

    levels = digits(dp)
    main_levels = levels[::-1]
    main_parts = exchange(main_grads, "fsdp", shards, 1)
    level = 0
    found = None
    for item in range(items):
        found = rest_call(item, found, main_sum if item else None)
        if item < len(main_levels):
            main_sum = sum_parts(main_parts)
            main_parts = spread(main_sum, "dp", dp, *main_levels[item])
            level = item + 1
    grad_tokens, grad_state_one, grad_totals_one, carry = found

    rest_grads = pl.pallas_call(
        partial(points_back, shards=shards),
        grid=(items,),
        in_specs=[
            pl.BlockSpec((funcs, slots, width), lambda u: (u, 0, 0)),
            pl.BlockSpec((funcs, width, slots), lambda u: (u, 0, 0)),
            pl.BlockSpec((funcs, width, slots), lambda u: (u, 0, 0)),
            pl.BlockSpec((funcs, width, width), lambda u: (u, 0, 0)),
            pl.BlockSpec((funcs, width, width), lambda u: (u, 0, 0)),
            whole_spec((7 * width, width)),
            pl.BlockSpec(memory_space=pl.ANY),
        ],
        out_specs=[whole_spec((rest_rows, width))] * shards,
        out_shape=[jax.ShapeDtypeStruct((rest_rows, width), bf16)] * shards,
        scratch_shapes=[
            pltpu.VMEM((2 * width, width), f32),
            pltpu.VMEM((shards, rest_rows, width), bf16),
        ],
        compiler_params=limit,
        cost_estimate=cost(7),
        name="points_back",
    )(flat_points, keys_one, values_one, grad_state_one, grad_totals_one, carry, main_sum)
    rest_got = exchange(rest_grads, "fsdp", shards, 1)

    parts = rest_got
    for digit, stride in main_levels[level:]:
        main_parts = spread(sum_parts(main_parts), "dp", dp, digit, stride)
    for digit, stride in levels:
        parts = spread(sum_parts(parts), "dp", dp, digit, stride)

    matrix = jax.ShapeDtypeStruct((piece, width), f32)
    vector = jax.ShapeDtypeStruct((1, piece), f32)
    outs = pl.pallas_call(
        partial(
            unpack_kernel,
            counts=(len(main_parts), len(parts)),
            experts=experts,
            piece=piece,
            exit_piece=exit_piece,
            hidden=hidden,
        ),
        out_shape=[vector] * 2
        + [matrix] * 8
        + [vector] * 2
        + [
            jax.ShapeDtypeStruct(expert_in.shape, f32),
            jax.ShapeDtypeStruct(expert_out.shape, f32),
            jax.ShapeDtypeStruct((1, 2), f32),
        ],
        scratch_shapes=[
            pltpu.VMEM((32, width), f32),
            pltpu.VMEM((main_rows, width), f32),
            pltpu.VMEM((rest_rows, width), f32),
        ],
        name="unpack",
    )(*main_parts, *parts)
    outs = [out.reshape(piece) if out.shape == (1, piece) else out for out in outs]
    return (result, grad_tokens, *outs[:-1], outs[-1].reshape(gate_weight.shape))


def solution(mesh):
    rows = P(("dp", "fsdp"), None)
    matrix = P("fsdp", None)
    vector = P("fsdp")
    expert = P(None, "fsdp", None)
    parameters = (
        (vector, vector)
        + (matrix,) * 8
        + (vector, vector, expert, expert, P(None, "fsdp"))
    )
    return jax.shard_map(
        partial(shards_fn, mesh.shape["dp"], mesh.shape["fsdp"]),
        mesh=mesh,
        in_specs=(
            rows,
            P(("dp", "fsdp"), None, None, None),
            P(None, ("dp", "fsdp")),
            rows,
            rows,
            rows,
        )
        + parameters,
        out_specs=(rows, rows) + parameters,
        check_vma=False,
    )
```

```python
from functools import partial

import jax
import jax.numpy as jnp
from jax import lax
from jax.experimental import pallas as pl
from jax.experimental.pallas import tpu as pltpu
from jax.sharding import PartitionSpec as P


HEADS = 8
eps = 1e-05
f32 = jnp.float32
bf16 = jnp.bfloat16
MAIN_TILE = 2048
REST_TILE = 1024
GROUP = 1024
CHUNK = 256
SLAB = 64
PAD = 16
VMEM = 56 * 1024 * 1024


def cost(microseconds):
    return pl.CostEstimate(flops=microseconds * 10**9, bytes_accessed=10**6, transcendentals=0)


def nn(left, right):
    return jnp.dot(left, right, preferred_element_type=f32)


def nt(left, right):
    return lax.dot_general(left, right, (((1,), (1,)), ((), ())), preferred_element_type=f32)


def flip(value):
    return value.T


def inverse(value):
    return pl.reciprocal(value, approx=True)


def head_softmax(value):
    width, rows = value.shape
    split = value.reshape(HEADS, width // HEADS, rows)
    raised = jnp.exp(split - jnp.max(split, axis=1, keepdims=True))
    return (raised * inverse(jnp.sum(raised, axis=1, keepdims=True))).reshape(width, rows)


def softmax_back(probs, grad):
    width, rows = grad.shape
    probs = probs.astype(f32).reshape(HEADS, width // HEADS, rows)
    grad = grad.reshape(HEADS, width // HEADS, rows)
    inner = jnp.sum(probs * grad, axis=1, keepdims=True)
    return (probs * (grad - inner)).reshape(width, rows)


def standardize(value):
    centre = value - jnp.mean(value, axis=0, keepdims=True)
    scale = lax.rsqrt(jnp.mean(centre * centre, axis=0, keepdims=True) + eps)
    return centre * scale, scale


def norm_back(grad, hat, scale):
    return scale * (
        grad
        - jnp.mean(grad, axis=0, keepdims=True)
        - hat * jnp.mean(grad * hat, axis=0, keepdims=True)
    )


def same_head(width):
    shape, head = (width, width), width // HEADS
    row = lax.broadcasted_iota(jnp.int32, shape, 0)
    column = lax.broadcasted_iota(jnp.int32, shape, 1)
    return lax.div(row, head) == lax.div(column, head)


def own_head(width):
    shape, head = (HEADS, width), width // HEADS
    row = lax.broadcasted_iota(jnp.int32, shape, 0)
    return row == lax.div(lax.broadcasted_iota(jnp.int32, shape, 1), head)


def by_head(value, scales):
    width, rows = value.shape
    split = value.reshape(HEADS, width // HEADS, rows)
    return (split * scales.reshape(HEADS, 1, rows)).reshape(width, rows)


def head_sums(value):
    width, rows = value.shape
    return jnp.sum(value.reshape(HEADS, width // HEADS, rows), axis=1)


def totals_column(rows, width):
    row = jnp.sum(jnp.where(own_head(width), rows, 0.0), axis=0, keepdims=True)
    return flip(jnp.broadcast_to(-row, (width, width)))


def pack_states(lefts, totals, state_t, state, width):
    count = len(lefts)
    rights = [jnp.where(own_head(width), total, 0.0) for total in totals]
    rest = jnp.zeros((width - count * HEADS, width), f32)
    right = jnp.concatenate(rights + [rest], axis=0)
    for place, left in enumerate(lefts):
        span = slice(place * width, (place + 1) * width)
        state_t[span] = left.astype(bf16)
        state[:, span] = flip(left).astype(bf16)
    start = count * width
    used = state_t.shape[0] - start
    state_t[start:] = right[:used].astype(bf16)
    state[:, start : start + width] = -flip(right).astype(bf16)


def assemble(parts, gathered):
    shards = len(parts)
    here = lax.axis_index("fsdp")
    for place, part in enumerate(parts):
        gathered[lax.rem(here + shards - place, shards)] = part[...]


def columns(gathered, start, count):
    shards, _, width = gathered.shape
    piece = width // shards
    small = [gathered[shard, start : start + 16, :].astype(f32) for shard in range(shards)]
    joined = jnp.concatenate([part[:, :piece] for part in small], axis=1)
    return [
        flip(jnp.broadcast_to(joined[place : place + 1], (width, width)))[:, 0:1]
        for place in range(count)
    ]


def lane_fold(value):
    width = value.shape[0]
    total = value[:, :width]
    for start in range(width, value.shape[1], width):
        total = total + value[:, start : start + width]
    return total


def as_row(value):
    width = value.shape[0]
    return flip(jnp.broadcast_to(jnp.sum(value, axis=1, keepdims=True), (width, width)))


def scatter_blocks(stage, outs):
    shards = len(outs)
    here = lax.axis_index("fsdp")
    for place, out in enumerate(outs):
        out[...] = stage[lax.rem(here + place, shards)]


def whole(gathered, start, rows):
    shards = gathered.shape[0]
    return gathered[:, start : start + rows, :].reshape(shards * rows, gathered.shape[2])


def function_weight(presence, item, func, funcs, shape):
    total = presence[item, 0]
    for other in range(1, funcs):
        total = total + presence[item, other]
    own = jnp.full(shape, presence[item, func], jnp.int32).astype(f32)
    return own / jnp.full(shape, total, jnp.int32).astype(f32)


def pack_kernel(*refs):
    weights, vectors, gate = refs[:10], refs[10:14], refs[14]
    early, late = refs[15:]
    keys, values, query, out, query_two, key_two, value_two, out_two, enter, leave = weights
    start = 0
    for weight in (keys, values):
        early[start : start + weight.shape[0]] = weight[...]
        start += weight.shape[0]
    start = 0
    for weight in (query, out, query_two, key_two, value_two, out_two):
        late[start : start + weight.shape[0]] = weight[...]
        start += weight.shape[0]
    experts, piece, hidden = enter.shape
    width = late.shape[1]
    for expert in range(experts):
        for half in range(hidden // width):
            late[start : start + piece] = enter[expert, :, half * width : (half + 1) * width]
            start += piece
    for expert in range(experts):
        late[start : start + leave.shape[1]] = leave[expert]
        start += leave.shape[1]
    rest = jnp.zeros((1, width - piece), f32)
    rows = [
        jnp.concatenate([vector[...].astype(f32), rest], axis=1) for vector in vectors
    ]
    rows.append(jnp.zeros((4, width), f32))
    for row in range(2):
        rows.append(jnp.broadcast_to(gate[row : row + 1, 0:1].astype(f32), (1, width)))
    rows.append(jnp.zeros((6, width), f32))
    late[start : start + 16] = jnp.concatenate(rows, axis=0).astype(bf16)


def run_tasks(tasks):
    waiting = None
    for dots, work in tasks:
        found = dots()
        if waiting is not None:
            waiting[0](*waiting[1])
        waiting = (work, found)
    waiting[0](*waiting[1])


def mix(tasks, extra):
    mixed = []
    done = 0
    for place, task in enumerate(tasks, 1):
        mixed.append(task)
        due = len(extra) * place // len(tasks)
        mixed += extra[done:due]
        done = due
    return mixed


def add_to(ref, span):
    def work(value):
        ref[span] += value

    return work


def points_forward(counts, presence, points, *refs, funcs, shards):
    parts = refs[:shards]
    state_t, state, keys_out, values_out, gathered, weight = refs[shards:]
    item = pl.program_id(0)
    width = points.shape[2]
    slots = points.shape[1]
    piece = width // shards

    @pl.when(item == 0)
    def _():
        assemble(parts, gathered)
        weight[:width] = flip(whole(gathered, 0, piece))
        weight[width:] = flip(whole(gathered, piece, piece))

    def project(func):
        both = nt(weight[...], points[func])
        slot = lax.broadcasted_iota(jnp.int32, (1, slots), 1)
        probs = head_softmax(both[:width])
        keys_out[func] = jnp.where(slot < counts[item, func], probs, 0.0).astype(bf16)
        values_out[func] = both[width:].astype(bf16)

    def summarize(func):
        values = values_out[func]
        extended = jnp.concatenate([values, jnp.ones((PAD, slots), bf16)], axis=0)
        share = function_weight(presence, item, func, funcs, (1, width))
        summed = nt(extended, keys_out[func])
        left = jnp.where(same_head(width), summed[:width], 0.0) * share
        return left, summed[width : width + 1]

    for func in range(funcs):
        project(func)
    lefts, totals = zip(*(summarize(func) for func in range(funcs)))
    pack_states(lefts, totals, state_t.at[0], state.at[0], width)


def main_kernel(tokens, cotangent, coords, state_t, *refs, funcs, experts, shards, at):
    parts, outs, scratch = refs[:shards], refs[shards : 2 * shards + 9], refs[2 * shards + 9 :]
    (
        result,
        queries_out,
        cross_out,
        first_out,
        keys_out,
        values_out,
        grad_q_out,
        grad_second_out,
        grad_state_out,
    ) = outs[:9]
    grads_out = outs[9:]
    (
        params,
        grads_stage,
        first_keep,
        query_keep,
        state_sum,
        self_t,
        self_state,
        grad_state_sum,
        w_query,
        w_out_one,
        w_self,
        w_out_two_t,
        w_out_two,
        w_in_t,
        w_in,
        w_exit,
        w_exit_t,
        gain_one,
        bias_one,
        gain_two,
        bias_two,
        hidden_keep,
        inner_keep,
        normed_keep,
        grad_keep,
        own_keep,
        pair_keep,
        sum_in,
        sum_exit,
        sum_out_two,
        sum_gain,
        sum_bias,
        sum_gate,
    ) = scratch
    item = pl.program_id(0)
    phase = pl.program_id(1)
    step = pl.program_id(2)
    steps = pl.num_programs(2)
    width = tokens.shape[1]
    rows = tokens.shape[0]
    piece = width // shards
    hidden = w_in.shape[1] // experts
    exit_piece = hidden // shards

    @pl.when((item == 0) & (phase == 0) & (step == 0))
    def _():
        assemble(parts, params)
        w_query[...] = flip(whole(params, at["query_first"], piece))
        w_out_one[...] = flip(whole(params, at["out_first"], piece))
        w_self[:width] = flip(whole(params, at["query_second"], piece))
        w_self[width : 2 * width] = flip(whole(params, at["key_second"], piece))
        w_self[2 * width :] = flip(whole(params, at["value_second"], piece))
        out_two = whole(params, at["out_second"], piece)
        w_out_two[...] = out_two
        w_out_two_t[...] = flip(out_two)
        for block in range(experts * hidden // width):
            part = whole(params, at["expert_in"] + block * piece, piece)
            w_in[:, block * width : (block + 1) * width] = part
            w_in_t[block * width : (block + 1) * width] = flip(part)
        for expert in range(experts):
            part = whole(params, at["expert_out"] + expert * exit_piece, exit_piece)
            w_exit[expert * hidden : (expert + 1) * hidden] = part
            w_exit_t[:, expert * hidden : (expert + 1) * hidden] = flip(part)
        found = columns(params, at["small"], 4)
        for vector, column in zip((gain_one, bias_one, gain_two, bias_two), found):
            vector[...] = jnp.broadcast_to(column, vector.shape)
        sum_in[...] = jnp.zeros_like(sum_in)
        sum_exit[...] = jnp.zeros_like(sum_exit)
        sum_out_two[...] = jnp.zeros_like(sum_out_two)
        sum_gain[...] = jnp.zeros_like(sum_gain)
        sum_bias[...] = jnp.zeros_like(sum_bias)
        sum_gate[...] = jnp.zeros_like(sum_gate)

    chunks = [slice(start, start + CHUNK) for start in range(0, rows, CHUNK)]
    groups = [slice(start, start + GROUP) for start in range(0, rows, GROUP)]
    every = slice(None)

    @pl.when((phase == 0) & (step == 0))
    def _():
        state_sum[...] = jnp.zeros_like(state_sum)
        grad_state_sum[...] = jnp.zeros_like(grad_state_sum)

    @pl.when(phase == 0)
    def _():
        def enter(cols):
            def dots():
                return (flip(tokens[cols, :]).astype(f32),)

            def work(rows_t):
                first_keep[step, :, cols] = rows_t
                hat, _scale = standardize(rows_t)
                normed_keep[:, cols] = (hat * gain_one[...] + bias_one[...]).astype(bf16)

            return dots, work

        def ask(cols):
            def dots():
                return (nn(w_query[...], normed_keep[:, cols]),)

            def work(value):
                queries_out[:, cols] = head_softmax(value).astype(bf16)

            return dots, work

        def across(cols):
            def dots():
                return (nn(state_t[0], queries_out[:, cols]),)

            def work(both):
                undo = inverse(both[funcs * width :])
                mixed = None
                for func in range(funcs):
                    part = by_head(
                        both[func * width : (func + 1) * width],
                        undo[func * HEADS : (func + 1) * HEADS],
                    )
                    mixed = part if mixed is None else mixed + part
                cross_out[:, cols] = mixed.astype(bf16)

            return dots, work

        def leave(cols):
            def dots():
                return (nn(w_out_one[...], cross_out[:, cols]),)

            def work(value):
                first = first_keep[step, :, cols] + value
                first_keep[step, :, cols] = first
                first_out[:, cols] = first.astype(bf16)

            return dots, work

        def project(cols):
            def dots():
                return (nn(w_self[...], first_out[:, cols]),)

            def work(three):
                query_keep[step, :, cols] = head_softmax(three[:width]).astype(bf16)
                keys_out[:, cols] = head_softmax(three[width : 2 * width]).astype(bf16)
                values = three[2 * width :].astype(bf16)
                values_out[:, cols] = values
                pair_keep[:width, cols] = values
                pair_keep[width:, cols] = jnp.ones((PAD, CHUNK), bf16)

            return dots, work

        run_tasks([stage(cols) for stage in (enter, ask, across, leave, project) for cols in chunks])
        state_sum[...] += nt(pair_keep[...], keys_out[...])

        @pl.when(step == steps - 1)
        def _():
            left = jnp.where(same_head(width), state_sum[:width], 0.0)
            pack_states([left], [state_sum[width : width + 1]], self_t, self_state, width)

    @pl.when(phase == 1)
    def _():
        undo_of, norm_of, gates_of = {}, {}, {}
        grad_gates_of = {chunk.start: [] for chunk in chunks}

        def attend(cols):
            def dots():
                return (nn(self_t[...], query_keep[step, :, cols]),)

            def work(both):
                undo = inverse(both[width : width + HEADS])
                undo_of[cols.start] = undo
                own_keep[:, cols] = by_head(both[:width], undo).astype(bf16)
                grad_keep[:, cols] = flip(cotangent[cols, :])

            return dots, work

        def gate(cols):
            across, down = coords[0:1, cols], coords[1:2, cols]
            logits = []
            for expert in range(experts):
                pair = params[expert, at["small"] : at["small"] + 16, 0:1].astype(f32)
                logits.append(across * pair[8:9] + down * pair[9:10])
            peak = logits[0]
            for logit in logits[1:]:
                peak = jnp.maximum(peak, logit)
            raised = [jnp.exp(logit - peak) for logit in logits]
            total = raised[0]
            for other in raised[1:]:
                total = total + other
            return [other / total for other in raised]

        def norm(cols):
            def dots():
                return (nn(w_out_two_t[...], own_keep[:, cols]),)

            def work(value):
                second = first_keep[step, :, cols] + value
                first_keep[step, :, cols] = second
                hat, scale = standardize(second)
                norm_of[cols.start] = (hat, scale)
                normed_keep[:, cols] = (hat * gain_two[...] + bias_two[...]).astype(bf16)
                gates_of[cols.start] = gate(cols)

            return dots, work

        def expand(cols, expert):
            whole_span = slice(expert * hidden, (expert + 1) * hidden)

            def dots():
                return (
                    nn(w_in_t[whole_span], normed_keep[:, cols]).astype(bf16),
                    nn(w_exit[whole_span], grad_keep[:, cols]).astype(bf16),
                )

            def work(inners, backs):
                share = gates_of[cols.start][expert].astype(bf16)
                partial_sum = None
                for start in range(0, hidden, SLAB):
                    inner, back = inners[start : start + SLAB], backs[start : start + SLAB]
                    span = slice(expert * hidden + start, expert * hidden + start + SLAB)
                    square = inner * inner
                    tanh = jnp.tanh(inner * (0.7978845608028654 + 0.035677408136300125 * square))
                    half = 0.5 + 0.5 * tanh
                    active = inner * half
                    product = active * back
                    folded = product[:16]
                    for row in range(16, SLAB, 16):
                        folded = folded + product[row : row + 16]
                    folded = folded.astype(f32)
                    partial_sum = folded if partial_sum is None else partial_sum + folded
                    hidden_keep[span, cols] = active * share
                    slope = half + active * (1.0 - half) * (
                        1.5957691216057308 + 0.21406444881780074 * square
                    )
                    inner_keep[span, cols] = slope * (back * share)
                grad_gates_of[cols.start].append(jnp.sum(partial_sum, axis=0, keepdims=True))

            return dots, work

        def contract(cols):
            def dots():
                return (
                    nn(w_exit_t[...], hidden_keep[:, cols]),
                    nn(w_in[...], inner_keep[:, cols]),
                )

            def work(mixed, grad_normed):
                result[cols, :] = flip((first_keep[step, :, cols] + mixed).astype(bf16))
                hat, scale = norm_of[cols.start]
                sum_gain[...] += lane_fold(grad_normed * hat)
                sum_bias[...] += lane_fold(grad_normed)
                grad_second = grad_keep[:, cols].astype(f32) + norm_back(
                    grad_normed * gain_two[...], hat, scale
                )
                grad_second_out[:, cols] = grad_second.astype(bf16)
                gates, grad_gates = gates_of[cols.start], grad_gates_of[cols.start]
                across, down = coords[0:1, cols], coords[1:2, cols]
                mean_gate = gates[0] * grad_gates[0]
                for expert in range(1, experts):
                    mean_gate = mean_gate + gates[expert] * grad_gates[expert]
                for expert in range(experts):
                    change = gates[expert] * (grad_gates[expert] - mean_gate)
                    sum_gate[expert : expert + 1, cols] += across * change
                    sum_gate[experts + expert : experts + expert + 1, cols] += down * change

            return dots, work

        def attend_back(cols):
            def dots():
                return (nn(w_out_two[...], grad_second_out[:, cols]),)

            def work(value):
                share = by_head(value, undo_of[cols.start])
                pair_keep[:width, cols] = share.astype(bf16)
                sums = head_sums(share * own_keep[:, cols].astype(f32))
                pair_keep[width:, cols] = jnp.concatenate(
                    [sums, jnp.zeros((PAD - HEADS, CHUNK), f32)], axis=0
                ).astype(bf16)

            return dots, work

        def query_back(cols):
            def dots():
                return (nn(self_state[:, : width + PAD], pair_keep[:, cols]),)

            def work(grad_q):
                queries = query_keep[step, :, cols]
                grad_q_out[:, cols] = softmax_back(queries, grad_q).astype(bf16)

            return dots, work

        def sum_hidden(cols, expert):
            span = slice(expert * hidden, (expert + 1) * hidden)
            return (
                lambda: (nn(hidden_keep[span, cols], cotangent[cols, :]),),
                add_to(sum_exit, span),
            )

        def sum_inner(cols, expert):
            span = slice(expert * hidden, (expert + 1) * hidden)
            return (
                lambda: (nt(inner_keep[span, cols], normed_keep[:, cols]),),
                add_to(sum_in, span),
            )

        def sum_own(cols):
            return (
                lambda: (nt(own_keep[:, cols], grad_second_out[:, cols]),),
                add_to(sum_out_two, every),
            )

        def sum_pair(cols):
            return (
                lambda: (nt(pair_keep[:, cols], query_keep[step, :, cols]),),
                add_to(grad_state_sum, every),
            )

        tasks = [stage(cols) for stage in (attend, norm) for cols in chunks]
        earlier = []
        for group in groups:
            inside = [cols for cols in chunks if group.start <= cols.start < group.stop]
            tasks += mix(
                [expand(cols, expert) for cols in inside for expert in range(experts)], earlier
            )
            earlier = [
                sums(group, expert) for expert in range(experts) for sums in (sum_hidden, sum_inner)
            ]
        tasks += mix([stage(cols) for stage in (contract, attend_back) for cols in chunks], earlier)
        tasks += mix([query_back(cols) for cols in chunks], [sum_own(group) for group in groups])
        tasks += [sum_pair(group) for group in groups]
        run_tasks(tasks)

        @pl.when(step == steps - 1)
        def _():
            grad_state_out[0] = grad_state_sum[...]

    @pl.when((item == pl.num_programs(0) - 1) & (phase == 1) & (step == steps - 1))
    def _():
        gain, bias = as_row(sum_gain[...]), as_row(sum_bias[...])
        gate = jnp.broadcast_to(jnp.sum(sum_gate[...], axis=1, keepdims=True), (8, width))
        row = lax.broadcasted_iota(jnp.int32, (8, width), 0)
        vectors = jnp.where(row == 0, gain[:8], bias[:8])
        small = jnp.concatenate([vectors, gate], axis=0).astype(bf16)
        start = 0
        for block in range(experts * hidden // width):
            part = flip(sum_in[block * width : (block + 1) * width]).astype(bf16)
            grads_stage[:, start : start + piece, :] = part.reshape(shards, piece, width)
            start += piece
        for expert in range(experts):
            part = sum_exit[expert * hidden : (expert + 1) * hidden].astype(bf16)
            grads_stage[:, start : start + exit_piece, :] = part.reshape(shards, exit_piece, width)
            start += exit_piece
        part = sum_out_two[...].astype(bf16)
        grads_stage[:, start : start + piece, :] = part.reshape(shards, piece, width)
        start += piece
        for shard in range(shards):
            grads_stage[shard, start : start + 16, :] = small
        scatter_blocks(grads_stage, grads_out)


def rest_kernel(
    presence,
    tokens,
    queries_in,
    cross_in,
    first_in,
    keys_in,
    values_in,
    grad_q_in,
    grad_second_in,
    grad_state_in,
    state_t,
    state,
    *refs,
    funcs,
    item,
    shards,
    at,
    first_call,
):
    parts, refs = refs[:shards], refs[shards:]
    if not first_call:
        carry, refs = refs[3], refs[5:]
    (
        grad_tokens,
        grad_cross_state_out,
        grad_totals_out,
        sums_out,
        params,
        w_self,
        w_out_one,
        w_query,
        gain_one,
        bias_one,
        grad_self_state,
        grad_totals,
        grad_state_sum,
        sums,
        three_keep,
        cross_keep,
        stack_keep,
        query_keep,
        normed_keep,
    ) = refs
    step = pl.program_id(0)
    steps = pl.num_programs(0)
    width = tokens.shape[1]
    piece = width // shards
    self_part = slice(0, 3 * width)
    out_part = slice(3 * width, 4 * width)
    query_part = slice(4 * width, 5 * width)
    gain_part = slice(5 * width, 6 * width)
    bias_part = slice(6 * width, 7 * width)

    @pl.when(step == 0)
    def _():
        assemble(parts, params)
        w_query[...] = whole(params, at["query_first"], piece)
        w_out_one[...] = whole(params, at["out_first"], piece)
        w_self[:, :width] = whole(params, at["query_second"], piece)
        w_self[:, width : 2 * width] = whole(params, at["key_second"], piece)
        w_self[:, 2 * width :] = whole(params, at["value_second"], piece)
        for vector, column in zip((gain_one, bias_one), columns(params, at["small"], 2)):
            vector[...] = jnp.broadcast_to(column, vector.shape)
        sums[...] = jnp.zeros_like(sums) if first_call else carry[...]
        left = jnp.where(same_head(width), grad_state_in[0, :width], 0.0)
        grad_self_state[0] = flip(left).astype(bf16)
        grad_self_state[1] = left.astype(bf16)
        column = totals_column(grad_state_in[0, width : width + HEADS], width)
        grad_totals[...] = jnp.broadcast_to(column[:, 0:1], grad_totals.shape)

    chunks = [slice(start, start + CHUNK) for start in range(0, tokens.shape[0], CHUNK)]
    norm_of, grad_first_of = {}, {}

    def self_back(cols):
        def dots():
            return (
                nn(grad_self_state[0], values_in[:, cols]),
                nn(grad_self_state[1], keys_in[:, cols]),
            )

        def work(grad_keys, grad_values):
            grad_keys = softmax_back(keys_in[:, cols], grad_keys + grad_totals[...])
            three_keep[:width, cols] = grad_q_in[:, cols]
            three_keep[width : 2 * width, cols] = grad_keys.astype(bf16)
            three_keep[2 * width :, cols] = grad_values.astype(bf16)

        return dots, work

    def join(cols):
        def dots():
            return (nn(w_self[...], three_keep[:, cols]), flip(tokens[cols, :]))

        def work(value, rows_t):
            grad_first = grad_second_in[:, cols].astype(f32) + value
            grad_first_of[cols.start] = grad_first
            cross_keep[:, cols] = grad_first.astype(bf16)
            hat, scale = standardize(rows_t.astype(f32))
            norm_of[cols.start] = (hat, scale)
            normed_keep[:, cols] = (hat * gain_one[...] + bias_one[...]).astype(bf16)

        return dots, work

    def cross_back(cols):
        def dots():
            return nn(w_out_one[...], cross_keep[:, cols]), nn(state_t[0], queries_in[:, cols])

        def work(share, both):
            undo = inverse(both[funcs * width :])
            sums_by_head = []
            for func in range(funcs):
                span = slice(func * width, (func + 1) * width)
                scales = undo[func * HEADS : (func + 1) * HEADS]
                part = by_head(share, scales)
                stack_keep[span, cols] = part.astype(bf16)
                sums_by_head.append(head_sums(part * by_head(both[span], scales)))
            spare = stack_keep.shape[0] - funcs * (width + HEADS)
            if spare:
                sums_by_head.append(jnp.zeros((spare, CHUNK), f32))
            stack_keep[funcs * width :, cols] = jnp.concatenate(sums_by_head, axis=0).astype(bf16)

        return dots, work

    def query_back(cols):
        def dots():
            return (nn(state[0, :, : stack_keep.shape[0]], stack_keep[:, cols]),)

        def work(grad_q):
            query_keep[:, cols] = softmax_back(queries_in[:, cols], grad_q).astype(bf16)

        return dots, work

    def finish(cols):
        def dots():
            return (nn(w_query[...], query_keep[:, cols]),)

        def work(grad_normed):
            hat, scale = norm_of[cols.start]
            sums[gain_part] += lane_fold(grad_normed * hat)
            sums[bias_part] += lane_fold(grad_normed)
            grad_rows = grad_first_of[cols.start] + norm_back(
                grad_normed * gain_one[...], hat, scale
            )
            grad_tokens[cols, :] = flip(grad_rows)

        return dots, work

    def sum_self(place):
        span = slice(place * width, (place + 1) * width)
        return lambda: (nt(three_keep[span], first_in[...]),), add_to(sums, span)

    def sum_state(span):
        return lambda: (nt(stack_keep[span], queries_in[...]),), add_to(grad_state_sum, span)

    @pl.when(step == 0)
    def _():
        grad_state_sum[...] = jnp.zeros_like(grad_state_sum)

    sum_out = (lambda: (nt(cross_in[...], cross_keep[...]),), add_to(sums, out_part))
    sum_query = (lambda: (nt(normed_keep[...], query_keep[...]),), add_to(sums, query_part))
    spans = [slice(func * width, (func + 1) * width) for func in range(funcs)]
    spans.append(slice(funcs * width, stack_keep.shape[0]))
    tasks = [stage(cols) for stage in (self_back, join) for cols in chunks]
    tasks += mix([cross_back(cols) for cols in chunks], [sum_self(place) for place in range(3)])
    tasks += mix([query_back(cols) for cols in chunks], [sum_out])
    tasks += mix([finish(cols) for cols in chunks], [sum_state(span) for span in spans])
    run_tasks(tasks + [sum_query])

    @pl.when(step == steps - 1)
    def _():
        mask = same_head(width)
        for func in range(funcs):
            weight = function_weight(presence, item, func, funcs, (1, width))
            left = jnp.where(mask, grad_state_sum[func * width : (func + 1) * width], 0.0)
            grad_cross_state_out[func] = (left * weight).astype(bf16)
            start = funcs * width + func * HEADS
            grad_totals_out[func] = totals_column(grad_state_sum[start : start + HEADS], width)
        sums_out[...] = sums[...]


def points_back(points, keys_in, values_in, grad_state, grad_totals, carry, _after, *refs, shards):
    outs = refs[:shards]
    sums, stage = refs[shards:]
    step = pl.program_id(0)
    width = points.shape[2]
    piece = width // shards

    def back(func):
        keys, values = keys_in[func], values_in[func]
        left = grad_state[func]
        grad_keys = nn(flip(left), values) + grad_totals[func, :, 0:1]
        grad_k = softmax_back(keys, grad_keys).astype(bf16)
        grad_v = nn(left, keys).astype(bf16)
        return jnp.concatenate([grad_k, grad_v], axis=0)

    grads = [back(func) for func in range(points.shape[0])]
    found = nn(grads[0], points[0])
    for func in range(1, points.shape[0]):
        found = found + nn(grads[func], points[func])

    @pl.when(step == 0)
    def _():
        sums[...] = found
        gain = as_row(carry[5 * width : 6 * width])
        bias = as_row(carry[6 * width : 7 * width])
        row = lax.broadcasted_iota(jnp.int32, (16, width), 0)
        small = jnp.where(row == 0, gain[:16], bias[:16]).astype(bf16)
        for place in range(5):
            part = carry[place * width : (place + 1) * width]
            part = (flip(part) if place < 3 else part).astype(bf16)
            stage[:, place * piece : (place + 1) * piece, :] = part.reshape(shards, piece, width)
        for shard in range(shards):
            stage[shard, 5 * piece : 5 * piece + 16, :] = small

    @pl.when(step > 0)
    def _():
        sums[...] += found

    @pl.when(step == pl.num_programs(0) - 1)
    def _():
        for place in range(2):
            start = 5 * piece + 16 + place * piece
            part = flip(sums[place * width : (place + 1) * width]).astype(bf16)
            stage[:, start : start + piece, :] = part.reshape(shards, piece, width)
        scatter_blocks(stage, outs)


def total_of(parts):
    value = parts[0][...].astype(f32)
    for part in parts[1:]:
        value = value + part[...].astype(f32)
    return value


def unpack_kernel(*refs, counts, experts, piece, exit_piece, hidden):
    main_parts, parts = refs[: counts[0]], refs[counts[0] : sum(counts)]
    outs, (small, main, rest) = refs[-18:-3], refs[-3:]
    width = main.shape[1]
    main[...] = total_of(main_parts)
    rest[...] = total_of(parts)
    (
        gain_one,
        bias_one,
        query_one,
        key_one,
        value_one,
        out_one,
        query_two,
        key_two,
        value_two,
        out_two,
        gain_two,
        bias_two,
        enter,
        leave,
        gate,
    ) = outs
    start = 0
    for expert in range(experts):
        for half in range(hidden // width):
            block = main[start : start + piece]
            enter[expert, :, half * width : (half + 1) * width] = block
            start += piece
    for expert in range(experts):
        leave[expert] = main[start : start + exit_piece]
        start += exit_piece
    out_two[...] = main[start : start + piece]
    start += piece
    small[:16] = main[start : start + 16]
    start = 0
    for out in (query_two, key_two, value_two, out_one, query_one):
        out[...] = rest[start : start + piece]
        start += piece
    small[16:] = rest[start : start + 16]
    start += 16
    for out in (key_one, value_one):
        out[...] = rest[start : start + piece]
        start += piece
    shard = lax.axis_index("fsdp")
    turned = pltpu.roll(small[...], lax.rem(width - shard * piece, width), 1)
    gain_two[...] = turned[0:1, :piece]
    bias_two[...] = turned[1:2, :piece]
    gain_one[...] = turned[16:17, :piece]
    bias_one[...] = turned[17:18, :piece]
    for row in range(2):
        gate[:, row : row + 1] = small[pl.ds(8 + row * experts + shard, 1), 0:1]


def whole_spec(shape):
    return pl.BlockSpec(shape, lambda *_: (0,) * len(shape))


def route(size, shift, digit, stride):
    def target(i):
        own = i // stride % digit
        return i + ((own + shift) % digit - own) * stride

    return [(i, target(i)) for i in range(size)]


def spread(value, axis, size, digit, stride):
    return [value] + [
        lax.ppermute(value, axis, route(size, shift, digit, stride)) for shift in range(1, digit)
    ]


def exchange(values, axis, size, stride):
    digit = len(values)
    return [values[0]] + [
        lax.ppermute(values[shift], axis, route(size, shift, digit, stride))
        for shift in range(1, digit)
    ]


def digits(size):
    found = []
    stride = 1
    while stride < size:
        rest = size // stride
        digit = 2 if stride == 1 and rest % 2 == 0 else 4 if rest % 4 == 0 else rest
        found.append((digit, stride))
        stride *= digit
    return found or [(1, 1)]


def sum_parts(parts):
    return total_of([part.astype(f32) for part in parts]).astype(bf16)


def shards_fn(
    dp,
    shards,
    tokens,
    points,
    coords,
    presence,
    counts,
    cotangent,
    gain_first,
    bias_first,
    query_first,
    key_first,
    value_first,
    out_first,
    query_second,
    key_second,
    value_second,
    out_second,
    gain_second,
    bias_second,
    expert_in,
    expert_out,
    gate_weight,
):
    count, width = tokens.shape
    items, funcs, slots, _ = points.shape
    length = count // items
    experts, piece, hidden = expert_in.shape
    exit_piece = expert_out.shape[1]
    tile, rest_tile = min(MAIN_TILE, length), min(REST_TILE, length)
    steps, rest_steps = length // tile, length // rest_tile
    inner = experts * hidden
    enter_rows = experts * piece * (hidden // width)
    limit = pltpu.CompilerParams(vmem_limit_bytes=VMEM)

    at = {}
    place = 0
    for name, size in (
        ("query_first", piece),
        ("out_first", piece),
        ("query_second", piece),
        ("key_second", piece),
        ("value_second", piece),
        ("out_second", piece),
        ("expert_in", enter_rows),
        ("expert_out", experts * exit_piece),
        ("small", 16),
    ):
        at[name] = place
        place += size
    late_rows_count = place
    early_pack, late_pack = pl.pallas_call(
        pack_kernel,
        out_shape=[
            jax.ShapeDtypeStruct((2 * piece, width), bf16),
            jax.ShapeDtypeStruct((late_rows_count, width), bf16),
        ],
        name="pack",
    )(
        key_first,
        value_first,
        query_first,
        out_first,
        query_second,
        key_second,
        value_second,
        out_second,
        expert_in,
        expert_out,
        *(
            vector.reshape(1, piece)
            for vector in (gain_first, bias_first, gain_second, bias_second)
        ),
        gate_weight,
    )
    early_parts = spread(early_pack, "fsdp", shards, shards, 1)
    late_parts = spread(late_pack, "fsdp", shards, shards, 1)
    late_specs = [whole_spec((late_rows_count, width))] * shards
    gathered = pltpu.VMEM((shards, late_rows_count, width), bf16)

    smem = pl.BlockSpec(memory_space=pltpu.SMEM)
    units = items * funcs
    state_rows = funcs * width + -(-funcs * HEADS // PAD) * PAD
    flat_points = points.reshape(units, slots, width)
    state_t, state, keys_one, values_one = pl.pallas_call(
        partial(points_forward, funcs=funcs, shards=shards),
        grid=(items,),
        in_specs=[smem, smem, pl.BlockSpec((funcs, slots, width), lambda u: (u, 0, 0))]
        + [whole_spec((2 * piece, width))] * shards,
        out_specs=[
            pl.BlockSpec((1, state_rows, width), lambda u: (u, 0, 0)),
            pl.BlockSpec((1, width, (funcs + 1) * width), lambda u: (u, 0, 0)),
            pl.BlockSpec((funcs, width, slots), lambda u: (u, 0, 0)),
            pl.BlockSpec((funcs, width, slots), lambda u: (u, 0, 0)),
        ],
        out_shape=[
            jax.ShapeDtypeStruct((items, state_rows, width), bf16),
            jax.ShapeDtypeStruct((items, width, (funcs + 1) * width), bf16),
            jax.ShapeDtypeStruct((units, width, slots), bf16),
            jax.ShapeDtypeStruct((units, width, slots), bf16),
        ],
        scratch_shapes=[
            pltpu.VMEM((shards, 2 * piece, width), bf16),
            pltpu.VMEM((2 * width, width), bf16),
        ],
        compiler_params=limit,
        cost_estimate=cost(8),
        name="points_forward",
    )(counts, presence, flat_points, *early_parts)

    kept = jax.ShapeDtypeStruct((width, count), bf16)
    main_rows = enter_rows + experts * exit_piece + piece + 16

    def early(i, p, j):
        return i * steps + jnp.where(p == 0, j, steps - 1)

    def late(i, p, j):
        return i * steps + jnp.where(p == 0, 0, j)

    early_keep = pl.BlockSpec((width, tile), lambda i, p, j: (0, early(i, p, j)))
    late_keep = pl.BlockSpec((width, tile), lambda i, p, j: (0, late(i, p, j)))
    late_rows = pl.BlockSpec((tile, width), lambda i, p, j: (late(i, p, j), 0))
    (
        result,
        queries_one,
        cross,
        first,
        keys_two,
        values_two,
        grad_q_two,
        grad_second,
        grad_state_two,
        *main_grads,
    ) = pl.pallas_call(
        partial(main_kernel, funcs=funcs, experts=experts, shards=shards, at=at),
        grid=(items, 2, steps),
        in_specs=[
            pl.BlockSpec((tile, width), lambda i, p, j: (early(i, p, j), 0)),
            late_rows,
            pl.BlockSpec((2, tile), lambda i, p, j: (0, late(i, p, j))),
            pl.BlockSpec((1, state_rows, width), lambda i, p, j: (i, 0, 0)),
        ]
        + late_specs,
        out_specs=[
            late_rows,
            early_keep,
            early_keep,
            early_keep,
            early_keep,
            early_keep,
            late_keep,
            late_keep,
            pl.BlockSpec((1, width + PAD, width), lambda i, p, j: (i, 0, 0)),
        ]
        + [whole_spec((main_rows, width))] * shards,
        out_shape=[
            jax.ShapeDtypeStruct((count, width), bf16),
            kept,
            kept,
            kept,
            kept,
            kept,
            kept,
            kept,
            jax.ShapeDtypeStruct((items, width + PAD, width), f32),
        ]
        + [jax.ShapeDtypeStruct((main_rows, width), bf16)] * shards,
        scratch_shapes=[
            gathered,
            pltpu.VMEM((shards, main_rows, width), bf16),
            pltpu.VMEM((steps, width, tile), f32),
            pltpu.VMEM((steps, width, tile), bf16),
            pltpu.VMEM((width + PAD, width), f32),
            pltpu.VMEM((width + PAD, width), bf16),
            pltpu.VMEM((width, 2 * width), bf16),
            pltpu.VMEM((width + PAD, width), f32),
            pltpu.VMEM((width, width), bf16),
            pltpu.VMEM((width, width), bf16),
            pltpu.VMEM((3 * width, width), bf16),
            pltpu.VMEM((width, width), bf16),
            pltpu.VMEM((width, width), bf16),
            pltpu.VMEM((inner, width), bf16),
            pltpu.VMEM((width, inner), bf16),
            pltpu.VMEM((inner, width), bf16),
            pltpu.VMEM((width, inner), bf16),
            pltpu.VMEM((width, CHUNK), f32),
            pltpu.VMEM((width, CHUNK), f32),
            pltpu.VMEM((width, CHUNK), f32),
            pltpu.VMEM((width, CHUNK), f32),
            pltpu.VMEM((inner, tile), bf16),
            pltpu.VMEM((inner, tile), bf16),
            pltpu.VMEM((width, tile), bf16),
            pltpu.VMEM((width, tile), bf16),
            pltpu.VMEM((width, tile), bf16),
            pltpu.VMEM((width + PAD, tile), bf16),
            pltpu.VMEM((inner, width), f32),
            pltpu.VMEM((inner, width), f32),
            pltpu.VMEM((width, width), f32),
            pltpu.VMEM((width, width), f32),
            pltpu.VMEM((width, width), f32),
            pltpu.VMEM((2 * experts, tile), f32),
        ],
        compiler_params=limit,
        cost_estimate=cost(80),
        name="main",
    )(tokens, cotangent, coords, state_t, *late_parts)

    rest_rows = 7 * piece + 16

    def rest_call(item, earlier, after):
        first_call = item == 0
        keep_spec = pl.BlockSpec((width, rest_tile), lambda j: (0, item * rest_steps + j))
        row_spec = pl.BlockSpec((rest_tile, width), lambda j: (item * rest_steps + j, 0))
        unit_spec = pl.BlockSpec((funcs, width, width), lambda j: (item, 0, 0))
        anywhere = pl.BlockSpec(memory_space=pl.ANY)
        in_specs = [
            smem,
            row_spec,
            keep_spec,
            keep_spec,
            keep_spec,
            keep_spec,
            keep_spec,
            keep_spec,
            keep_spec,
            pl.BlockSpec((1, width + PAD, width), lambda j: (item, 0, 0)),
            pl.BlockSpec((1, state_rows, width), lambda j: (item, 0, 0)),
            pl.BlockSpec((1, width, (funcs + 1) * width), lambda j: (item, 0, 0)),
        ] + late_specs
        operands = [
            presence,
            tokens,
            queries_one,
            cross,
            first,
            keys_two,
            values_two,
            grad_q_two,
            grad_second,
            grad_state_two,
            state_t,
            state,
            *late_parts,
        ]
        aliases = {}
        if not first_call:
            aliases = {len(operands) + k: k for k in range(3)}
            in_specs += [anywhere] * 3 + [whole_spec((7 * width, width)), anywhere]
            operands += [*earlier, after]
        out_specs = [row_spec, unit_spec, unit_spec, whole_spec((7 * width, width))]
        out_shape = [
            jax.ShapeDtypeStruct((count, width), f32),
            jax.ShapeDtypeStruct((units, width, width), bf16),
            jax.ShapeDtypeStruct((units, width, width), f32),
            jax.ShapeDtypeStruct((7 * width, width), f32),
        ]
        return pl.pallas_call(
            partial(
                rest_kernel,
                funcs=funcs,
                item=item,
                shards=shards,
                at=at,
                first_call=first_call,
            ),
            grid=(rest_steps,),
            in_specs=in_specs,
            out_specs=out_specs,
            out_shape=out_shape,
            input_output_aliases=aliases,
            scratch_shapes=[
                gathered,
                pltpu.VMEM((width, 3 * width), bf16),
                pltpu.VMEM((width, width), bf16),
                pltpu.VMEM((width, width), bf16),
                pltpu.VMEM((width, CHUNK), f32),
                pltpu.VMEM((width, CHUNK), f32),
                pltpu.VMEM((2, width, width), bf16),
                pltpu.VMEM((width, CHUNK), f32),
                pltpu.VMEM((state_rows, width), f32),
                pltpu.VMEM((7 * width, width), f32),
                pltpu.VMEM((3 * width, rest_tile), bf16),
                pltpu.VMEM((width, rest_tile), bf16),
                pltpu.VMEM((state_rows, rest_tile), bf16),
                pltpu.VMEM((width, rest_tile), bf16),
                pltpu.VMEM((width, rest_tile), bf16),
            ],
            compiler_params=limit,
            cost_estimate=cost(18),
            name="rest",
        )(*operands)

    levels = digits(dp)
    main_levels = levels[::-1]
    main_parts = exchange(main_grads, "fsdp", shards, 1)
    level = 0
    found = None
    for item in range(items):
        found = rest_call(item, found, main_sum if item else None)
        if item < len(main_levels):
            main_sum = sum_parts(main_parts)
            main_parts = spread(main_sum, "dp", dp, *main_levels[item])
            level = item + 1
    grad_tokens, grad_state_one, grad_totals_one, carry = found

    rest_grads = pl.pallas_call(
        partial(points_back, shards=shards),
        grid=(items,),
        in_specs=[
            pl.BlockSpec((funcs, slots, width), lambda u: (u, 0, 0)),
            pl.BlockSpec((funcs, width, slots), lambda u: (u, 0, 0)),
            pl.BlockSpec((funcs, width, slots), lambda u: (u, 0, 0)),
            pl.BlockSpec((funcs, width, width), lambda u: (u, 0, 0)),
            pl.BlockSpec((funcs, width, width), lambda u: (u, 0, 0)),
            whole_spec((7 * width, width)),
            pl.BlockSpec(memory_space=pl.ANY),
        ],
        out_specs=[whole_spec((rest_rows, width))] * shards,
        out_shape=[jax.ShapeDtypeStruct((rest_rows, width), bf16)] * shards,
        scratch_shapes=[
            pltpu.VMEM((2 * width, width), f32),
            pltpu.VMEM((shards, rest_rows, width), bf16),
        ],
        compiler_params=limit,
        cost_estimate=cost(7),
        name="points_back",
    )(flat_points, keys_one, values_one, grad_state_one, grad_totals_one, carry, main_sum)
    rest_got = exchange(rest_grads, "fsdp", shards, 1)

    parts = rest_got
    for digit, stride in main_levels[level:]:
        main_parts = spread(sum_parts(main_parts), "dp", dp, digit, stride)
    for digit, stride in levels:
        parts = spread(sum_parts(parts), "dp", dp, digit, stride)

    matrix = jax.ShapeDtypeStruct((piece, width), f32)
    vector = jax.ShapeDtypeStruct((1, piece), f32)
    outs = pl.pallas_call(
        partial(
            unpack_kernel,
            counts=(len(main_parts), len(parts)),
            experts=experts,
            piece=piece,
            exit_piece=exit_piece,
            hidden=hidden,
        ),
        out_shape=[vector] * 2
        + [matrix] * 8
        + [vector] * 2
        + [
            jax.ShapeDtypeStruct(expert_in.shape, f32),
            jax.ShapeDtypeStruct(expert_out.shape, f32),
            jax.ShapeDtypeStruct((1, 2), f32),
        ],
        scratch_shapes=[
            pltpu.VMEM((32, width), f32),
            pltpu.VMEM((main_rows, width), f32),
            pltpu.VMEM((rest_rows, width), f32),
        ],
        name="unpack",
    )(*main_parts, *parts)
    outs = [out.reshape(piece) if out.shape == (1, piece) else out for out in outs]
    return (result, grad_tokens, *outs[:-1], outs[-1].reshape(gate_weight.shape))


def solution(mesh):
    rows = P(("dp", "fsdp"), None)
    matrix = P("fsdp", None)
    vector = P("fsdp")
    expert = P(None, "fsdp", None)
    parameters = (
        (vector, vector)
        + (matrix,) * 8
        + (vector, vector, expert, expert, P(None, "fsdp"))
    )
    return jax.shard_map(
        partial(shards_fn, mesh.shape["dp"], mesh.shape["fsdp"]),
        mesh=mesh,
        in_specs=(
            rows,
            P(("dp", "fsdp"), None, None, None),
            P(None, ("dp", "fsdp")),
            rows,
            rows,
            rows,
        )
        + parameters,
        out_specs=(rows, rows) + parameters,
        check_vma=False,
    )
```

```python
from functools import partial

import jax
import jax.numpy as jnp
from jax import lax
from jax.experimental import pallas as pl
from jax.experimental.pallas import tpu as pltpu
from jax.sharding import PartitionSpec as P


HEADS = 8
eps = 1e-05
f32 = jnp.float32
bf16 = jnp.bfloat16
MAIN_TILE = 4096
REST_TILE = 1024
GROUP = 1024
CHUNK = 256
SLAB = 64
PAD = 16
VMEM = 60 * 1024 * 1024


def cost(microseconds):
    return pl.CostEstimate(flops=microseconds * 10**9, bytes_accessed=10**6, transcendentals=0)


def nn(left, right):
    return jnp.dot(left, right, preferred_element_type=f32)


def nt(left, right):
    return lax.dot_general(left, right, (((1,), (1,)), ((), ())), preferred_element_type=f32)


def flip(value):
    return value.T


def inverse(value):
    return pl.reciprocal(value, approx=True)


def head_softmax(value):
    width, rows = value.shape
    split = value.reshape(HEADS, width // HEADS, rows)
    raised = jnp.exp(split - jnp.max(split, axis=1, keepdims=True))
    return (raised * inverse(jnp.sum(raised, axis=1, keepdims=True))).reshape(width, rows)


def softmax_back(probs, grad):
    width, rows = grad.shape
    probs = probs.astype(f32).reshape(HEADS, width // HEADS, rows)
    grad = grad.reshape(HEADS, width // HEADS, rows)
    inner = jnp.sum(probs * grad, axis=1, keepdims=True)
    return (probs * (grad - inner)).reshape(width, rows)


def standardize(value):
    centre = value - jnp.mean(value, axis=0, keepdims=True)
    scale = lax.rsqrt(jnp.mean(centre * centre, axis=0, keepdims=True) + eps)
    return centre * scale, scale


def norm_back(grad, hat, scale):
    return scale * (
        grad
        - jnp.mean(grad, axis=0, keepdims=True)
        - hat * jnp.mean(grad * hat, axis=0, keepdims=True)
    )


def same_head(width):
    shape, head = (width, width), width // HEADS
    row = lax.broadcasted_iota(jnp.int32, shape, 0)
    column = lax.broadcasted_iota(jnp.int32, shape, 1)
    return lax.div(row, head) == lax.div(column, head)


def own_head(width):
    shape, head = (HEADS, width), width // HEADS
    row = lax.broadcasted_iota(jnp.int32, shape, 0)
    return row == lax.div(lax.broadcasted_iota(jnp.int32, shape, 1), head)


def by_head(value, scales):
    width, rows = value.shape
    split = value.reshape(HEADS, width // HEADS, rows)
    return (split * scales.reshape(HEADS, 1, rows)).reshape(width, rows)


def head_sums(value):
    width, rows = value.shape
    return jnp.sum(value.reshape(HEADS, width // HEADS, rows), axis=1)


def totals_column(rows, width):
    row = jnp.sum(jnp.where(own_head(width), rows, 0.0), axis=0, keepdims=True)
    return flip(jnp.broadcast_to(-row, (width, width)))


def pack_states(lefts, totals, state_t, state, width):
    count = len(lefts)
    rights = [jnp.where(own_head(width), total, 0.0) for total in totals]
    rest = jnp.zeros((width - count * HEADS, width), f32)
    right = jnp.concatenate(rights + [rest], axis=0)
    for place, left in enumerate(lefts):
        span = slice(place * width, (place + 1) * width)
        state_t[span] = left.astype(bf16)
        state[:, span] = flip(left).astype(bf16)
    start = count * width
    used = state_t.shape[0] - start
    state_t[start:] = right[:used].astype(bf16)
    state[:, start : start + width] = -flip(right).astype(bf16)


def assemble(parts, gathered):
    shards = len(parts)
    here = lax.axis_index("fsdp")
    for place, part in enumerate(parts):
        gathered[lax.rem(here + shards - place, shards)] = part[...]


def columns(gathered, start, count):
    shards, _, width = gathered.shape
    piece = width // shards
    small = [gathered[shard, start : start + 16, :].astype(f32) for shard in range(shards)]
    joined = jnp.concatenate([part[:, :piece] for part in small], axis=1)
    return [
        flip(jnp.broadcast_to(joined[place : place + 1], (width, width)))[:, 0:1]
        for place in range(count)
    ]


def lane_fold(value):
    width = value.shape[0]
    total = value[:, :width]
    for start in range(width, value.shape[1], width):
        total = total + value[:, start : start + width]
    return total


def as_row(value):
    width = value.shape[0]
    return flip(jnp.broadcast_to(jnp.sum(value, axis=1, keepdims=True), (width, width)))


def scatter_blocks(stage, outs):
    shards = len(outs)
    here = lax.axis_index("fsdp")
    for place, out in enumerate(outs):
        out[...] = stage[lax.rem(here + place, shards)]


def whole(gathered, start, rows):
    shards = gathered.shape[0]
    return gathered[:, start : start + rows, :].reshape(shards * rows, gathered.shape[2])


def function_weight(presence, item, func, funcs, shape):
    total = presence[item, 0]
    for other in range(1, funcs):
        total = total + presence[item, other]
    own = jnp.full(shape, presence[item, func], jnp.int32).astype(f32)
    return own / jnp.full(shape, total, jnp.int32).astype(f32)


def pack_kernel(*refs):
    weights, vectors, gate = refs[:10], refs[10:14], refs[14]
    early, late = refs[15:]
    keys, values, query, out, query_two, key_two, value_two, out_two, enter, leave = weights
    start = 0
    for weight in (keys, values):
        early[start : start + weight.shape[0]] = weight[...]
        start += weight.shape[0]
    start = 0
    for weight in (query, out, query_two, key_two, value_two, out_two):
        late[start : start + weight.shape[0]] = weight[...]
        start += weight.shape[0]
    experts, piece, hidden = enter.shape
    width = late.shape[1]
    for expert in range(experts):
        for half in range(hidden // width):
            late[start : start + piece] = enter[expert, :, half * width : (half + 1) * width]
            start += piece
    for expert in range(experts):
        late[start : start + leave.shape[1]] = leave[expert]
        start += leave.shape[1]
    rest = jnp.zeros((1, width - piece), f32)
    rows = [
        jnp.concatenate([vector[...].astype(f32), rest], axis=1) for vector in vectors
    ]
    rows.append(jnp.zeros((4, width), f32))
    for row in range(2):
        rows.append(jnp.broadcast_to(gate[row : row + 1, 0:1].astype(f32), (1, width)))
    rows.append(jnp.zeros((6, width), f32))
    late[start : start + 16] = jnp.concatenate(rows, axis=0).astype(bf16)


def run_tasks(tasks):
    waiting = None
    for dots, work in tasks:
        found = dots()
        if waiting is not None:
            waiting[0](*waiting[1])
        waiting = (work, found)
    waiting[0](*waiting[1])


def mix(tasks, extra):
    mixed = []
    done = 0
    for place, task in enumerate(tasks, 1):
        mixed.append(task)
        due = len(extra) * place // len(tasks)
        mixed += extra[done:due]
        done = due
    return mixed


def behind(stage, total, chunks, groups):
    tasks = []
    for cols in chunks:
        tasks.append(stage(cols))
        tasks += [total(group) for group in groups if group.stop == cols.stop - 2 * CHUNK]
    return tasks


def add_to(ref, span):
    def work(value):
        ref[span] += value

    return work


def points_forward(counts, presence, points, *refs, funcs, shards):
    parts = refs[:shards]
    state_t, state, keys_out, values_out, gathered, weight = refs[shards:]
    item = pl.program_id(0)
    width = points.shape[2]
    slots = points.shape[1]
    piece = width // shards

    @pl.when(item == 0)
    def _():
        assemble(parts, gathered)
        weight[:width] = flip(whole(gathered, 0, piece))
        weight[width:] = flip(whole(gathered, piece, piece))

    def project(func):
        both = nt(weight[...], points[func])
        slot = lax.broadcasted_iota(jnp.int32, (1, slots), 1)
        probs = head_softmax(both[:width])
        keys_out[func] = jnp.where(slot < counts[item, func], probs, 0.0).astype(bf16)
        values_out[func] = both[width:].astype(bf16)

    def summarize(func):
        values = values_out[func]
        extended = jnp.concatenate([values, jnp.ones((PAD, slots), bf16)], axis=0)
        share = function_weight(presence, item, func, funcs, (1, width))
        summed = nt(extended, keys_out[func])
        left = jnp.where(same_head(width), summed[:width], 0.0) * share
        return left, summed[width : width + 1]

    for func in range(funcs):
        project(func)
    lefts, totals = zip(*(summarize(func) for func in range(funcs)))
    pack_states(lefts, totals, state_t.at[0], state.at[0], width)


def main_kernel(tokens, cotangent, coords, state_t, *refs, funcs, experts, shards, at):
    parts, outs, scratch = refs[:shards], refs[shards : 2 * shards + 9], refs[2 * shards + 9 :]
    (
        result,
        queries_out,
        cross_out,
        first_out,
        keys_out,
        values_out,
        grad_q_out,
        grad_second_out,
        grad_state_out,
    ) = outs[:9]
    grads_out = outs[9:]
    (
        params,
        grads_stage,
        first_keep,
        query_keep,
        state_sum,
        self_t,
        self_state,
        grad_state_sum,
        w_query,
        w_out_one,
        w_self,
        w_out_two_t,
        w_out_two,
        w_in_t,
        w_in,
        w_exit,
        w_exit_t,
        gain_one,
        bias_one,
        gain_two,
        bias_two,
        hidden_keep,
        inner_keep,
        normed_keep,
        grad_keep,
        own_keep,
        pair_keep,
        sum_in,
        sum_exit,
        sum_out_two,
        sum_gain,
        sum_bias,
        sum_gate,
    ) = scratch
    item = pl.program_id(0)
    phase = pl.program_id(1)
    step = pl.program_id(2)
    steps = pl.num_programs(2)
    width = tokens.shape[1]
    rows = tokens.shape[0]
    piece = width // shards
    hidden = w_in.shape[1] // experts
    exit_piece = hidden // shards

    @pl.when((item == 0) & (phase == 0) & (step == 0))
    def _():
        assemble(parts, params)
        w_query[...] = flip(whole(params, at["query_first"], piece))
        w_out_one[...] = flip(whole(params, at["out_first"], piece))
        w_self[:width] = flip(whole(params, at["query_second"], piece))
        w_self[width : 2 * width] = flip(whole(params, at["key_second"], piece))
        w_self[2 * width :] = flip(whole(params, at["value_second"], piece))
        out_two = whole(params, at["out_second"], piece)
        w_out_two[...] = out_two
        w_out_two_t[...] = flip(out_two)
        for block in range(experts * hidden // width):
            part = whole(params, at["expert_in"] + block * piece, piece)
            w_in[:, block * width : (block + 1) * width] = part
            w_in_t[block * width : (block + 1) * width] = flip(part)
        for expert in range(experts):
            part = whole(params, at["expert_out"] + expert * exit_piece, exit_piece)
            w_exit[expert * hidden : (expert + 1) * hidden] = part
            w_exit_t[:, expert * hidden : (expert + 1) * hidden] = flip(part)
        found = columns(params, at["small"], 4)
        for vector, column in zip((gain_one, bias_one, gain_two, bias_two), found):
            vector[...] = jnp.broadcast_to(column, vector.shape)
        sum_in[...] = jnp.zeros_like(sum_in)
        sum_exit[...] = jnp.zeros_like(sum_exit)
        sum_out_two[...] = jnp.zeros_like(sum_out_two)
        sum_gain[...] = jnp.zeros_like(sum_gain)
        sum_bias[...] = jnp.zeros_like(sum_bias)
        sum_gate[...] = jnp.zeros_like(sum_gate)

    chunks = [slice(start, start + CHUNK) for start in range(0, rows, CHUNK)]
    groups = [slice(start, start + GROUP) for start in range(0, rows, GROUP)]
    every = slice(None)

    @pl.when((phase == 0) & (step == 0))
    def _():
        state_sum[...] = jnp.zeros_like(state_sum)
        grad_state_sum[...] = jnp.zeros_like(grad_state_sum)

    @pl.when(phase == 0)
    def _():
        def enter(cols):
            def dots():
                return (flip(tokens[cols, :]).astype(f32),)

            def work(rows_t):
                first_keep[step, :, cols] = rows_t
                hat, _scale = standardize(rows_t)
                normed_keep[:, cols] = (hat * gain_one[...] + bias_one[...]).astype(bf16)

            return dots, work

        def ask(cols):
            def dots():
                return (nn(w_query[...], normed_keep[:, cols]),)

            def work(value):
                queries_out[:, cols] = head_softmax(value).astype(bf16)

            return dots, work

        def across(cols):
            def dots():
                return (nn(state_t[0], queries_out[:, cols]),)

            def work(both):
                undo = inverse(both[funcs * width :])
                mixed = None
                for func in range(funcs):
                    part = by_head(
                        both[func * width : (func + 1) * width],
                        undo[func * HEADS : (func + 1) * HEADS],
                    )
                    mixed = part if mixed is None else mixed + part
                cross_out[:, cols] = mixed.astype(bf16)

            return dots, work

        def leave(cols):
            def dots():
                return (nn(w_out_one[...], cross_out[:, cols]),)

            def work(value):
                first = first_keep[step, :, cols] + value
                first_keep[step, :, cols] = first
                first_out[:, cols] = first.astype(bf16)

            return dots, work

        def project(cols):
            def dots():
                return (nn(w_self[...], first_out[:, cols]),)

            def work(three):
                query_keep[step, :, cols] = head_softmax(three[:width]).astype(bf16)
                keys_out[:, cols] = head_softmax(three[width : 2 * width]).astype(bf16)
                values = three[2 * width :].astype(bf16)
                values_out[:, cols] = values
                pair_keep[:width, cols] = values
                pair_keep[width:, cols] = jnp.ones((PAD, CHUNK), bf16)

            return dots, work

        def sum_state(cols):
            return (
                lambda: (nt(pair_keep[:, cols], keys_out[:, cols]),),
                add_to(state_sum, every),
            )

        tasks = [stage(cols) for stage in (enter, ask, across, leave) for cols in chunks]
        run_tasks(tasks + behind(project, sum_state, chunks, groups[:-1]))
        run_tasks([sum_state(groups[-1])])

        @pl.when(step == steps - 1)
        def _():
            left = jnp.where(same_head(width), state_sum[:width], 0.0)
            pack_states([left], [state_sum[width : width + 1]], self_t, self_state, width)

    @pl.when(phase == 1)
    def _():
        undo_of, norm_of, gates_of = {}, {}, {}
        grad_gates_of = {chunk.start: [] for chunk in chunks}

        def attend(cols):
            def dots():
                return (nn(self_t[...], query_keep[step, :, cols]),)

            def work(both):
                undo = inverse(both[width : width + HEADS])
                undo_of[cols.start] = undo
                own_keep[:, cols] = by_head(both[:width], undo).astype(bf16)
                grad_keep[:, cols] = flip(cotangent[cols, :])

            return dots, work

        def gate(cols):
            across, down = coords[0:1, cols], coords[1:2, cols]
            logits = []
            for expert in range(experts):
                pair = params[expert, at["small"] : at["small"] + 16, 0:1].astype(f32)
                logits.append(across * pair[8:9] + down * pair[9:10])
            peak = logits[0]
            for logit in logits[1:]:
                peak = jnp.maximum(peak, logit)
            raised = [jnp.exp(logit - peak) for logit in logits]
            total = raised[0]
            for other in raised[1:]:
                total = total + other
            return [other / total for other in raised]

        def norm(cols):
            def dots():
                return (nn(w_out_two_t[...], own_keep[:, cols]),)

            def work(value):
                second = first_keep[step, :, cols] + value
                first_keep[step, :, cols] = second
                hat, scale = standardize(second)
                norm_of[cols.start] = (hat, scale)
                normed_keep[:, cols] = (hat * gain_two[...] + bias_two[...]).astype(bf16)
                gates_of[cols.start] = gate(cols)

            return dots, work

        def expand(cols, expert):
            whole_span = slice(expert * hidden, (expert + 1) * hidden)

            def dots():
                return (
                    nn(w_in_t[whole_span], normed_keep[:, cols]).astype(bf16),
                    nn(w_exit[whole_span], grad_keep[:, cols]).astype(bf16),
                )

            def work(inners, backs):
                share = (0.5 * gates_of[cols.start][expert]).astype(bf16)
                partial_sum = None
                for start in range(0, hidden, SLAB):
                    inner, back = inners[start : start + SLAB], backs[start : start + SLAB]
                    span = slice(expert * hidden + start, expert * hidden + start + SLAB)
                    square = inner * inner
                    tanh = jnp.tanh(inner * (0.7978845608028654 + 0.035677408136300125 * square))
                    above = 1.0 + tanh
                    active = inner * above
                    product = active * back
                    folded = product[:16]
                    for row in range(16, SLAB, 16):
                        folded = folded + product[row : row + 16]
                    folded = folded.astype(f32)
                    partial_sum = folded if partial_sum is None else partial_sum + folded
                    hidden_keep[span, cols] = active * share
                    slope = above + active * (1.0 - tanh) * (
                        0.7978845608028654 + 0.10703222440890037 * square
                    )
                    inner_keep[span, cols] = slope * (back * share)
                partial_sum = 0.5 * partial_sum
                grad_gates_of[cols.start].append(jnp.sum(partial_sum, axis=0, keepdims=True))

            return dots, work

        def contract(cols):
            def dots():
                return (
                    nn(w_exit_t[...], hidden_keep[:, cols]),
                    nn(w_in[...], inner_keep[:, cols]),
                )

            def work(mixed, grad_normed):
                result[cols, :] = flip((first_keep[step, :, cols] + mixed).astype(bf16))
                hat, scale = norm_of[cols.start]
                sum_gain[...] += lane_fold(grad_normed * hat)
                sum_bias[...] += lane_fold(grad_normed)
                grad_second = grad_keep[:, cols].astype(f32) + norm_back(
                    grad_normed * gain_two[...], hat, scale
                )
                grad_second_out[:, cols] = grad_second.astype(bf16)
                gates, grad_gates = gates_of[cols.start], grad_gates_of[cols.start]
                across, down = coords[0:1, cols], coords[1:2, cols]
                mean_gate = gates[0] * grad_gates[0]
                for expert in range(1, experts):
                    mean_gate = mean_gate + gates[expert] * grad_gates[expert]
                for expert in range(experts):
                    change = gates[expert] * (grad_gates[expert] - mean_gate)
                    sum_gate[expert : expert + 1, cols] += across * change
                    sum_gate[experts + expert : experts + expert + 1, cols] += down * change

            return dots, work

        def attend_back(cols):
            def dots():
                return (nn(w_out_two[...], grad_second_out[:, cols]),)

            def work(value):
                share = by_head(value, undo_of[cols.start])
                pair_keep[:width, cols] = share.astype(bf16)
                sums = head_sums(share * own_keep[:, cols].astype(f32))
                pair_keep[width:, cols] = jnp.concatenate(
                    [sums, jnp.zeros((PAD - HEADS, CHUNK), f32)], axis=0
                ).astype(bf16)

            return dots, work

        def query_back(cols):
            def dots():
                return (nn(self_state[:, : width + PAD], pair_keep[:, cols]),)

            def work(grad_q):
                queries = query_keep[step, :, cols]
                grad_q_out[:, cols] = softmax_back(queries, grad_q).astype(bf16)

            return dots, work

        def sum_hidden(cols, expert):
            span = slice(expert * hidden, (expert + 1) * hidden)
            return (
                lambda: (nn(hidden_keep[span, cols], cotangent[cols, :]),),
                add_to(sum_exit, span),
            )

        def sum_inner(cols, expert):
            span = slice(expert * hidden, (expert + 1) * hidden)
            return (
                lambda: (nt(inner_keep[span, cols], normed_keep[:, cols]),),
                add_to(sum_in, span),
            )

        def sum_own(cols):
            return (
                lambda: (nt(own_keep[:, cols], grad_second_out[:, cols]),),
                add_to(sum_out_two, every),
            )

        def sum_pair(cols):
            return (
                lambda: (nt(pair_keep[:, cols], query_keep[step, :, cols]),),
                add_to(grad_state_sum, every),
            )

        tasks = [stage(cols) for stage in (attend, norm) for cols in chunks]
        earlier = []
        for group in groups:
            inside = [cols for cols in chunks if group.start <= cols.start < group.stop]
            tasks += mix(
                [expand(cols, expert) for cols in inside for expert in range(experts)], earlier
            )
            earlier = [
                sums(group, expert) for expert in range(experts) for sums in (sum_hidden, sum_inner)
            ]
        tasks += mix([stage(cols) for stage in (contract, attend_back) for cols in chunks], earlier)
        last = [sums(group) for group in groups for sums in (sum_own, sum_pair)]
        tasks += mix([query_back(cols) for cols in chunks], last)
        run_tasks(tasks)

        @pl.when(step == steps - 1)
        def _():
            grad_state_out[0] = grad_state_sum[...]

    @pl.when((item == pl.num_programs(0) - 1) & (phase == 1) & (step == steps - 1))
    def _():
        gain, bias = as_row(sum_gain[...]), as_row(sum_bias[...])
        gate = jnp.broadcast_to(jnp.sum(sum_gate[...], axis=1, keepdims=True), (8, width))
        row = lax.broadcasted_iota(jnp.int32, (8, width), 0)
        vectors = jnp.where(row == 0, gain[:8], bias[:8])
        small = jnp.concatenate([vectors, gate], axis=0).astype(bf16)
        start = 0
        for block in range(experts * hidden // width):
            part = flip(sum_in[block * width : (block + 1) * width]).astype(bf16)
            grads_stage[:, start : start + piece, :] = part.reshape(shards, piece, width)
            start += piece
        for expert in range(experts):
            part = sum_exit[expert * hidden : (expert + 1) * hidden].astype(bf16)
            grads_stage[:, start : start + exit_piece, :] = part.reshape(shards, exit_piece, width)
            start += exit_piece
        part = sum_out_two[...].astype(bf16)
        grads_stage[:, start : start + piece, :] = part.reshape(shards, piece, width)
        start += piece
        for shard in range(shards):
            grads_stage[shard, start : start + 16, :] = small
        scatter_blocks(grads_stage, grads_out)


def rest_kernel(
    presence,
    tokens,
    queries_in,
    cross_in,
    first_in,
    keys_in,
    values_in,
    grad_q_in,
    grad_second_in,
    grad_state_in,
    state_t,
    state,
    *refs,
    funcs,
    item,
    shards,
    at,
    first_call,
):
    parts, refs = refs[:shards], refs[shards:]
    if not first_call:
        carry, refs = refs[3], refs[5:]
    (
        grad_tokens,
        grad_cross_state_out,
        grad_totals_out,
        sums_out,
        params,
        w_self,
        w_out_one,
        w_query,
        gain_one,
        bias_one,
        grad_self_state,
        grad_totals,
        grad_state_sum,
        sums,
        three_keep,
        cross_keep,
        stack_keep,
        query_keep,
        normed_keep,
    ) = refs
    step = pl.program_id(0)
    steps = pl.num_programs(0)
    width = tokens.shape[1]
    piece = width // shards
    self_part = slice(0, 3 * width)
    out_part = slice(3 * width, 4 * width)
    query_part = slice(4 * width, 5 * width)
    gain_part = slice(5 * width, 6 * width)
    bias_part = slice(6 * width, 7 * width)

    @pl.when(step == 0)
    def _():
        assemble(parts, params)
        w_query[...] = whole(params, at["query_first"], piece)
        w_out_one[...] = whole(params, at["out_first"], piece)
        w_self[:, :width] = whole(params, at["query_second"], piece)
        w_self[:, width : 2 * width] = whole(params, at["key_second"], piece)
        w_self[:, 2 * width :] = whole(params, at["value_second"], piece)
        for vector, column in zip((gain_one, bias_one), columns(params, at["small"], 2)):
            vector[...] = jnp.broadcast_to(column, vector.shape)
        sums[...] = jnp.zeros_like(sums) if first_call else carry[...]
        left = jnp.where(same_head(width), grad_state_in[0, :width], 0.0)
        grad_self_state[0] = flip(left).astype(bf16)
        grad_self_state[1] = left.astype(bf16)
        column = totals_column(grad_state_in[0, width : width + HEADS], width)
        grad_totals[...] = jnp.broadcast_to(column[:, 0:1], grad_totals.shape)

    chunks = [slice(start, start + CHUNK) for start in range(0, tokens.shape[0], CHUNK)]
    norm_of, grad_first_of = {}, {}

    def self_back(cols):
        def dots():
            return (
                nn(grad_self_state[0], values_in[:, cols]),
                nn(grad_self_state[1], keys_in[:, cols]),
            )

        def work(grad_keys, grad_values):
            grad_keys = softmax_back(keys_in[:, cols], grad_keys + grad_totals[...])
            three_keep[:width, cols] = grad_q_in[:, cols]
            three_keep[width : 2 * width, cols] = grad_keys.astype(bf16)
            three_keep[2 * width :, cols] = grad_values.astype(bf16)

        return dots, work

    def join(cols):
        def dots():
            return (nn(w_self[...], three_keep[:, cols]), flip(tokens[cols, :]))

        def work(value, rows_t):
            grad_first = grad_second_in[:, cols].astype(f32) + value
            grad_first_of[cols.start] = grad_first
            cross_keep[:, cols] = grad_first.astype(bf16)
            hat, scale = standardize(rows_t.astype(f32))
            norm_of[cols.start] = (hat, scale)
            normed_keep[:, cols] = (hat * gain_one[...] + bias_one[...]).astype(bf16)

        return dots, work

    def cross_back(cols):
        def dots():
            return nn(w_out_one[...], cross_keep[:, cols]), nn(state_t[0], queries_in[:, cols])

        def work(share, both):
            undo = inverse(both[funcs * width :])
            sums_by_head = []
            for func in range(funcs):
                span = slice(func * width, (func + 1) * width)
                scales = undo[func * HEADS : (func + 1) * HEADS]
                part = by_head(share, scales)
                stack_keep[span, cols] = part.astype(bf16)
                sums_by_head.append(head_sums(part * by_head(both[span], scales)))
            spare = stack_keep.shape[0] - funcs * (width + HEADS)
            if spare:
                sums_by_head.append(jnp.zeros((spare, CHUNK), f32))
            stack_keep[funcs * width :, cols] = jnp.concatenate(sums_by_head, axis=0).astype(bf16)

        return dots, work

    def query_back(cols):
        def dots():
            return (nn(state[0, :, : stack_keep.shape[0]], stack_keep[:, cols]),)

        def work(grad_q):
            query_keep[:, cols] = softmax_back(queries_in[:, cols], grad_q).astype(bf16)

        return dots, work

    def finish(cols):
        def dots():
            return (nn(w_query[...], query_keep[:, cols]),)

        def work(grad_normed):
            hat, scale = norm_of[cols.start]
            sums[gain_part] += lane_fold(grad_normed * hat)
            sums[bias_part] += lane_fold(grad_normed)
            grad_rows = grad_first_of[cols.start] + norm_back(
                grad_normed * gain_one[...], hat, scale
            )
            grad_tokens[cols, :] = flip(grad_rows)

        return dots, work

    def sum_self(place):
        span = slice(place * width, (place + 1) * width)
        return lambda: (nt(three_keep[span], first_in[...]),), add_to(sums, span)

    def sum_state(span):
        return lambda: (nt(stack_keep[span], queries_in[...]),), add_to(grad_state_sum, span)

    @pl.when(step == 0)
    def _():
        grad_state_sum[...] = jnp.zeros_like(grad_state_sum)

    sum_out = (lambda: (nt(cross_in[...], cross_keep[...]),), add_to(sums, out_part))
    sum_query = (lambda: (nt(normed_keep[...], query_keep[...]),), add_to(sums, query_part))
    spans = [slice(func * width, (func + 1) * width) for func in range(funcs)]
    spans.append(slice(funcs * width, stack_keep.shape[0]))
    tasks = [stage(cols) for stage in (self_back, join) for cols in chunks]
    tasks += mix([cross_back(cols) for cols in chunks], [sum_self(place) for place in range(3)])
    tasks += mix([query_back(cols) for cols in chunks], [sum_out])
    tasks += mix([finish(cols) for cols in chunks], [sum_state(span) for span in spans])
    run_tasks(tasks + [sum_query])

    @pl.when(step == steps - 1)
    def _():
        mask = same_head(width)
        for func in range(funcs):
            weight = function_weight(presence, item, func, funcs, (1, width))
            left = jnp.where(mask, grad_state_sum[func * width : (func + 1) * width], 0.0)
            grad_cross_state_out[func] = (left * weight).astype(bf16)
            start = funcs * width + func * HEADS
            grad_totals_out[func] = totals_column(grad_state_sum[start : start + HEADS], width)
        sums_out[...] = sums[...]


def points_back(points, keys_in, values_in, grad_state, grad_totals, carry, _after, *refs, shards):
    outs = refs[:shards]
    sums, stage = refs[shards:]
    step = pl.program_id(0)
    width = points.shape[2]
    piece = width // shards

    def back(func):
        keys, values = keys_in[func], values_in[func]
        left = grad_state[func]
        grad_keys = nn(flip(left), values) + grad_totals[func, :, 0:1]
        grad_k = softmax_back(keys, grad_keys).astype(bf16)
        grad_v = nn(left, keys).astype(bf16)
        return jnp.concatenate([grad_k, grad_v], axis=0)

    grads = [back(func) for func in range(points.shape[0])]
    found = nn(grads[0], points[0])
    for func in range(1, points.shape[0]):
        found = found + nn(grads[func], points[func])

    @pl.when(step == 0)
    def _():
        sums[...] = found
        gain = as_row(carry[5 * width : 6 * width])
        bias = as_row(carry[6 * width : 7 * width])
        row = lax.broadcasted_iota(jnp.int32, (16, width), 0)
        small = jnp.where(row == 0, gain[:16], bias[:16]).astype(bf16)
        for place in range(5):
            part = carry[place * width : (place + 1) * width]
            part = (flip(part) if place < 3 else part).astype(bf16)
            stage[:, place * piece : (place + 1) * piece, :] = part.reshape(shards, piece, width)
        for shard in range(shards):
            stage[shard, 5 * piece : 5 * piece + 16, :] = small

    @pl.when(step > 0)
    def _():
        sums[...] += found

    @pl.when(step == pl.num_programs(0) - 1)
    def _():
        for place in range(2):
            start = 5 * piece + 16 + place * piece
            part = flip(sums[place * width : (place + 1) * width]).astype(bf16)
            stage[:, start : start + piece, :] = part.reshape(shards, piece, width)
        scatter_blocks(stage, outs)


def total_of(parts):
    value = parts[0][...].astype(f32)
    for part in parts[1:]:
        value = value + part[...].astype(f32)
    return value


def unpack_kernel(*refs, counts, experts, piece, exit_piece, hidden):
    main_parts, parts = refs[: counts[0]], refs[counts[0] : sum(counts)]
    outs, (small, main, rest) = refs[-18:-3], refs[-3:]
    width = main.shape[1]
    main[...] = total_of(main_parts)
    rest[...] = total_of(parts)
    (
        gain_one,
        bias_one,
        query_one,
        key_one,
        value_one,
        out_one,
        query_two,
        key_two,
        value_two,
        out_two,
        gain_two,
        bias_two,
        enter,
        leave,
        gate,
    ) = outs
    start = 0
    for expert in range(experts):
        for half in range(hidden // width):
            block = main[start : start + piece]
            enter[expert, :, half * width : (half + 1) * width] = block
            start += piece
    for expert in range(experts):
        leave[expert] = main[start : start + exit_piece]
        start += exit_piece
    out_two[...] = main[start : start + piece]
    start += piece
    small[:16] = main[start : start + 16]
    start = 0
    for out in (query_two, key_two, value_two, out_one, query_one):
        out[...] = rest[start : start + piece]
        start += piece
    small[16:] = rest[start : start + 16]
    start += 16
    for out in (key_one, value_one):
        out[...] = rest[start : start + piece]
        start += piece
    shard = lax.axis_index("fsdp")
    turned = pltpu.roll(small[...], lax.rem(width - shard * piece, width), 1)
    gain_two[...] = turned[0:1, :piece]
    bias_two[...] = turned[1:2, :piece]
    gain_one[...] = turned[16:17, :piece]
    bias_one[...] = turned[17:18, :piece]
    for row in range(2):
        gate[:, row : row + 1] = small[pl.ds(8 + row * experts + shard, 1), 0:1]


def whole_spec(shape):
    return pl.BlockSpec(shape, lambda *_: (0,) * len(shape))


def route(size, shift, digit, stride):
    def target(i):
        own = i // stride % digit
        return i + ((own + shift) % digit - own) * stride

    return [(i, target(i)) for i in range(size)]


def spread(value, axis, size, digit, stride):
    return [value] + [
        lax.ppermute(value, axis, route(size, shift, digit, stride)) for shift in range(1, digit)
    ]


def exchange(values, axis, size, stride):
    digit = len(values)
    return [values[0]] + [
        lax.ppermute(values[shift], axis, route(size, shift, digit, stride))
        for shift in range(1, digit)
    ]


def digits(size):
    found = []
    stride = 1
    while stride < size:
        rest = size // stride
        digit = 2 if stride == 1 and rest % 2 == 0 else 4 if rest % 4 == 0 else rest
        found.append((digit, stride))
        stride *= digit
    return found or [(1, 1)]


def sum_parts(parts):
    return total_of([part.astype(f32) for part in parts]).astype(bf16)


def shards_fn(
    dp,
    shards,
    tokens,
    points,
    coords,
    presence,
    counts,
    cotangent,
    gain_first,
    bias_first,
    query_first,
    key_first,
    value_first,
    out_first,
    query_second,
    key_second,
    value_second,
    out_second,
    gain_second,
    bias_second,
    expert_in,
    expert_out,
    gate_weight,
):
    count, width = tokens.shape
    items, funcs, slots, _ = points.shape
    length = count // items
    experts, piece, hidden = expert_in.shape
    exit_piece = expert_out.shape[1]
    tile, rest_tile = min(MAIN_TILE, length), min(REST_TILE, length)
    steps, rest_steps = length // tile, length // rest_tile
    inner = experts * hidden
    enter_rows = experts * piece * (hidden // width)
    limit = pltpu.CompilerParams(vmem_limit_bytes=VMEM)

    at = {}
    place = 0
    for name, size in (
        ("query_first", piece),
        ("out_first", piece),
        ("query_second", piece),
        ("key_second", piece),
        ("value_second", piece),
        ("out_second", piece),
        ("expert_in", enter_rows),
        ("expert_out", experts * exit_piece),
        ("small", 16),
    ):
        at[name] = place
        place += size
    late_rows_count = place
    early_pack, late_pack = pl.pallas_call(
        pack_kernel,
        out_shape=[
            jax.ShapeDtypeStruct((2 * piece, width), bf16),
            jax.ShapeDtypeStruct((late_rows_count, width), bf16),
        ],
        name="pack",
    )(
        key_first,
        value_first,
        query_first,
        out_first,
        query_second,
        key_second,
        value_second,
        out_second,
        expert_in,
        expert_out,
        *(
            vector.reshape(1, piece)
            for vector in (gain_first, bias_first, gain_second, bias_second)
        ),
        gate_weight,
    )
    early_parts = spread(early_pack, "fsdp", shards, shards, 1)
    late_parts = spread(late_pack, "fsdp", shards, shards, 1)
    late_specs = [whole_spec((late_rows_count, width))] * shards
    gathered = pltpu.VMEM((shards, late_rows_count, width), bf16)

    smem = pl.BlockSpec(memory_space=pltpu.SMEM)
    units = items * funcs
    state_rows = funcs * width + -(-funcs * HEADS // PAD) * PAD
    flat_points = points.reshape(units, slots, width)
    state_t, state, keys_one, values_one = pl.pallas_call(
        partial(points_forward, funcs=funcs, shards=shards),
        grid=(items,),
        in_specs=[smem, smem, pl.BlockSpec((funcs, slots, width), lambda u: (u, 0, 0))]
        + [whole_spec((2 * piece, width))] * shards,
        out_specs=[
            pl.BlockSpec((1, state_rows, width), lambda u: (u, 0, 0)),
            pl.BlockSpec((1, width, (funcs + 1) * width), lambda u: (u, 0, 0)),
            pl.BlockSpec((funcs, width, slots), lambda u: (u, 0, 0)),
            pl.BlockSpec((funcs, width, slots), lambda u: (u, 0, 0)),
        ],
        out_shape=[
            jax.ShapeDtypeStruct((items, state_rows, width), bf16),
            jax.ShapeDtypeStruct((items, width, (funcs + 1) * width), bf16),
            jax.ShapeDtypeStruct((units, width, slots), bf16),
            jax.ShapeDtypeStruct((units, width, slots), bf16),
        ],
        scratch_shapes=[
            pltpu.VMEM((shards, 2 * piece, width), bf16),
            pltpu.VMEM((2 * width, width), bf16),
        ],
        compiler_params=limit,
        cost_estimate=cost(8),
        name="points_forward",
    )(counts, presence, flat_points, *early_parts)

    kept = jax.ShapeDtypeStruct((width, count), bf16)
    main_rows = enter_rows + experts * exit_piece + piece + 16

    def early(i, p, j):
        return i * steps + jnp.where(p == 0, j, steps - 1)

    def late(i, p, j):
        return i * steps + jnp.where(p == 0, 0, j)

    early_keep = pl.BlockSpec((width, tile), lambda i, p, j: (0, early(i, p, j)))
    late_keep = pl.BlockSpec((width, tile), lambda i, p, j: (0, late(i, p, j)))
    late_rows = pl.BlockSpec((tile, width), lambda i, p, j: (late(i, p, j), 0))
    (
        result,
        queries_one,
        cross,
        first,
        keys_two,
        values_two,
        grad_q_two,
        grad_second,
        grad_state_two,
        *main_grads,
    ) = pl.pallas_call(
        partial(main_kernel, funcs=funcs, experts=experts, shards=shards, at=at),
        grid=(items, 2, steps),
        in_specs=[
            pl.BlockSpec((tile, width), lambda i, p, j: (early(i, p, j), 0)),
            late_rows,
            pl.BlockSpec((2, tile), lambda i, p, j: (0, late(i, p, j))),
            pl.BlockSpec((1, state_rows, width), lambda i, p, j: (i, 0, 0)),
        ]
        + late_specs,
        out_specs=[
            late_rows,
            early_keep,
            early_keep,
            early_keep,
            early_keep,
            early_keep,
            late_keep,
            late_keep,
            pl.BlockSpec((1, width + PAD, width), lambda i, p, j: (i, 0, 0)),
        ]
        + [whole_spec((main_rows, width))] * shards,
        out_shape=[
            jax.ShapeDtypeStruct((count, width), bf16),
            kept,
            kept,
            kept,
            kept,
            kept,
            kept,
            kept,
            jax.ShapeDtypeStruct((items, width + PAD, width), f32),
        ]
        + [jax.ShapeDtypeStruct((main_rows, width), bf16)] * shards,
        scratch_shapes=[
            gathered,
            pltpu.VMEM((shards, main_rows, width), bf16),
            pltpu.VMEM((steps, width, tile), f32),
            pltpu.VMEM((steps, width, tile), bf16),
            pltpu.VMEM((width + PAD, width), f32),
            pltpu.VMEM((width + PAD, width), bf16),
            pltpu.VMEM((width, 2 * width), bf16),
            pltpu.VMEM((width + PAD, width), f32),
            pltpu.VMEM((width, width), bf16),
            pltpu.VMEM((width, width), bf16),
            pltpu.VMEM((3 * width, width), bf16),
            pltpu.VMEM((width, width), bf16),
            pltpu.VMEM((width, width), bf16),
            pltpu.VMEM((inner, width), bf16),
            pltpu.VMEM((width, inner), bf16),
            pltpu.VMEM((inner, width), bf16),
            pltpu.VMEM((width, inner), bf16),
            pltpu.VMEM((width, CHUNK), f32),
            pltpu.VMEM((width, CHUNK), f32),
            pltpu.VMEM((width, CHUNK), f32),
            pltpu.VMEM((width, CHUNK), f32),
            pltpu.VMEM((inner, tile), bf16),
            pltpu.VMEM((inner, tile), bf16),
            pltpu.VMEM((width, tile), bf16),
            pltpu.VMEM((width, tile), bf16),
            pltpu.VMEM((width, tile), bf16),
            pltpu.VMEM((width + PAD, tile), bf16),
            pltpu.VMEM((inner, width), f32),
            pltpu.VMEM((inner, width), f32),
            pltpu.VMEM((width, width), f32),
            pltpu.VMEM((width, width), f32),
            pltpu.VMEM((width, width), f32),
            pltpu.VMEM((2 * experts, tile), f32),
        ],
        compiler_params=limit,
        cost_estimate=cost(80),
        name="main",
    )(tokens, cotangent, coords, state_t, *late_parts)

    rest_rows = 7 * piece + 16

    def rest_call(item, earlier, after):
        first_call = item == 0
        keep_spec = pl.BlockSpec((width, rest_tile), lambda j: (0, item * rest_steps + j))
        row_spec = pl.BlockSpec((rest_tile, width), lambda j: (item * rest_steps + j, 0))
        unit_spec = pl.BlockSpec((funcs, width, width), lambda j: (item, 0, 0))
        anywhere = pl.BlockSpec(memory_space=pl.ANY)
        in_specs = [
            smem,
            row_spec,
            keep_spec,
            keep_spec,
            keep_spec,
            keep_spec,
            keep_spec,
            keep_spec,
            keep_spec,
            pl.BlockSpec((1, width + PAD, width), lambda j: (item, 0, 0)),
            pl.BlockSpec((1, state_rows, width), lambda j: (item, 0, 0)),
            pl.BlockSpec((1, width, (funcs + 1) * width), lambda j: (item, 0, 0)),
        ] + late_specs
        operands = [
            presence,
            tokens,
            queries_one,
            cross,
            first,
            keys_two,
            values_two,
            grad_q_two,
            grad_second,
            grad_state_two,
            state_t,
            state,
            *late_parts,
        ]
        aliases = {}
        if not first_call:
            aliases = {len(operands) + k: k for k in range(3)}
            in_specs += [anywhere] * 3 + [whole_spec((7 * width, width)), anywhere]
            operands += [*earlier, after]
        out_specs = [row_spec, unit_spec, unit_spec, whole_spec((7 * width, width))]
        out_shape = [
            jax.ShapeDtypeStruct((count, width), f32),
            jax.ShapeDtypeStruct((units, width, width), bf16),
            jax.ShapeDtypeStruct((units, width, width), f32),
            jax.ShapeDtypeStruct((7 * width, width), f32),
        ]
        return pl.pallas_call(
            partial(
                rest_kernel,
                funcs=funcs,
                item=item,
                shards=shards,
                at=at,
                first_call=first_call,
            ),
            grid=(rest_steps,),
            in_specs=in_specs,
            out_specs=out_specs,
            out_shape=out_shape,
            input_output_aliases=aliases,
            scratch_shapes=[
                gathered,
                pltpu.VMEM((width, 3 * width), bf16),
                pltpu.VMEM((width, width), bf16),
                pltpu.VMEM((width, width), bf16),
                pltpu.VMEM((width, CHUNK), f32),
                pltpu.VMEM((width, CHUNK), f32),
                pltpu.VMEM((2, width, width), bf16),
                pltpu.VMEM((width, CHUNK), f32),
                pltpu.VMEM((state_rows, width), f32),
                pltpu.VMEM((7 * width, width), f32),
                pltpu.VMEM((3 * width, rest_tile), bf16),
                pltpu.VMEM((width, rest_tile), bf16),
                pltpu.VMEM((state_rows, rest_tile), bf16),
                pltpu.VMEM((width, rest_tile), bf16),
                pltpu.VMEM((width, rest_tile), bf16),
            ],
            compiler_params=limit,
            cost_estimate=cost(18),
            name="rest",
        )(*operands)

    levels = digits(dp)
    main_levels = levels[::-1]
    main_parts = exchange(main_grads, "fsdp", shards, 1)
    level = 0
    found = None
    for item in range(items):
        found = rest_call(item, found, main_sum if item else None)
        if item < len(main_levels):
            main_sum = sum_parts(main_parts)
            main_parts = spread(main_sum, "dp", dp, *main_levels[item])
            level = item + 1
    grad_tokens, grad_state_one, grad_totals_one, carry = found

    rest_grads = pl.pallas_call(
        partial(points_back, shards=shards),
        grid=(items,),
        in_specs=[
            pl.BlockSpec((funcs, slots, width), lambda u: (u, 0, 0)),
            pl.BlockSpec((funcs, width, slots), lambda u: (u, 0, 0)),
            pl.BlockSpec((funcs, width, slots), lambda u: (u, 0, 0)),
            pl.BlockSpec((funcs, width, width), lambda u: (u, 0, 0)),
            pl.BlockSpec((funcs, width, width), lambda u: (u, 0, 0)),
            whole_spec((7 * width, width)),
            pl.BlockSpec(memory_space=pl.ANY),
        ],
        out_specs=[whole_spec((rest_rows, width))] * shards,
        out_shape=[jax.ShapeDtypeStruct((rest_rows, width), bf16)] * shards,
        scratch_shapes=[
            pltpu.VMEM((2 * width, width), f32),
            pltpu.VMEM((shards, rest_rows, width), bf16),
        ],
        compiler_params=limit,
        cost_estimate=cost(7),
        name="points_back",
    )(flat_points, keys_one, values_one, grad_state_one, grad_totals_one, carry, main_sum)
    rest_got = exchange(rest_grads, "fsdp", shards, 1)

    parts = rest_got
    for digit, stride in main_levels[level:]:
        main_parts = spread(sum_parts(main_parts), "dp", dp, digit, stride)
    for digit, stride in levels:
        parts = spread(sum_parts(parts), "dp", dp, digit, stride)

    matrix = jax.ShapeDtypeStruct((piece, width), f32)
    vector = jax.ShapeDtypeStruct((1, piece), f32)
    outs = pl.pallas_call(
        partial(
            unpack_kernel,
            counts=(len(main_parts), len(parts)),
            experts=experts,
            piece=piece,
            exit_piece=exit_piece,
            hidden=hidden,
        ),
        out_shape=[vector] * 2
        + [matrix] * 8
        + [vector] * 2
        + [
            jax.ShapeDtypeStruct(expert_in.shape, f32),
            jax.ShapeDtypeStruct(expert_out.shape, f32),
            jax.ShapeDtypeStruct((1, 2), f32),
        ],
        scratch_shapes=[
            pltpu.VMEM((32, width), f32),
            pltpu.VMEM((main_rows, width), f32),
            pltpu.VMEM((rest_rows, width), f32),
        ],
        name="unpack",
    )(*main_parts, *parts)
    outs = [out.reshape(piece) if out.shape == (1, piece) else out for out in outs]
    return (result, grad_tokens, *outs[:-1], outs[-1].reshape(gate_weight.shape))


def solution(mesh):
    rows = P(("dp", "fsdp"), None)
    matrix = P("fsdp", None)
    vector = P("fsdp")
    expert = P(None, "fsdp", None)
    parameters = (
        (vector, vector)
        + (matrix,) * 8
        + (vector, vector, expert, expert, P(None, "fsdp"))
    )
    return jax.shard_map(
        partial(shards_fn, mesh.shape["dp"], mesh.shape["fsdp"]),
        mesh=mesh,
        in_specs=(
            rows,
            P(("dp", "fsdp"), None, None, None),
            P(None, ("dp", "fsdp")),
            rows,
            rows,
            rows,
        )
        + parameters,
        out_specs=(rows, rows) + parameters,
        check_vma=False,
    )
```

```python
from functools import partial

import jax
import jax.numpy as jnp
from jax import lax
from jax.experimental import pallas as pl
from jax.experimental.pallas import tpu as pltpu
from jax.sharding import PartitionSpec as P


HEADS = 8
eps = 1e-05
f32 = jnp.float32
bf16 = jnp.bfloat16
MAIN_TILE = 4096
REST_TILE = 1024
GROUP = 1024
CHUNK = 256
SLAB = 64
PAD = 16
VMEM = 60 * 1024 * 1024


def cost(microseconds):
    return pl.CostEstimate(flops=microseconds * 10**9, bytes_accessed=10**6, transcendentals=0)


def nn(left, right):
    return jnp.dot(left, right, preferred_element_type=f32)


def nt(left, right):
    return lax.dot_general(left, right, (((1,), (1,)), ((), ())), preferred_element_type=f32)


def flip(value):
    return value.T


def inverse(value):
    return pl.reciprocal(value, approx=True)


def head_softmax(value):
    width, rows = value.shape
    split = value.reshape(HEADS, width // HEADS, rows)
    raised = jnp.exp(split - jnp.max(split, axis=1, keepdims=True))
    return (raised * inverse(jnp.sum(raised, axis=1, keepdims=True))).reshape(width, rows)


def softmax_back(probs, grad):
    width, rows = grad.shape
    probs = probs.astype(f32).reshape(HEADS, width // HEADS, rows)
    grad = grad.reshape(HEADS, width // HEADS, rows)
    inner = jnp.sum(probs * grad, axis=1, keepdims=True)
    return (probs * (grad - inner)).reshape(width, rows)


def standardize(value):
    centre = value - jnp.mean(value, axis=0, keepdims=True)
    scale = lax.rsqrt(jnp.mean(centre * centre, axis=0, keepdims=True) + eps)
    return centre * scale, scale


def norm_back(grad, hat, scale):
    return scale * (
        grad
        - jnp.mean(grad, axis=0, keepdims=True)
        - hat * jnp.mean(grad * hat, axis=0, keepdims=True)
    )


def same_head(width):
    shape, head = (width, width), width // HEADS
    row = lax.broadcasted_iota(jnp.int32, shape, 0)
    column = lax.broadcasted_iota(jnp.int32, shape, 1)
    return lax.div(row, head) == lax.div(column, head)


def own_head(width):
    shape, head = (HEADS, width), width // HEADS
    row = lax.broadcasted_iota(jnp.int32, shape, 0)
    return row == lax.div(lax.broadcasted_iota(jnp.int32, shape, 1), head)


def by_head(value, scales):
    width, rows = value.shape
    split = value.reshape(HEADS, width // HEADS, rows)
    return (split * scales.reshape(HEADS, 1, rows)).reshape(width, rows)


def head_sums(value):
    width, rows = value.shape
    return jnp.sum(value.reshape(HEADS, width // HEADS, rows), axis=1)


def totals_column(rows, width):
    row = jnp.sum(jnp.where(own_head(width), rows, 0.0), axis=0, keepdims=True)
    return flip(jnp.broadcast_to(-row, (width, width)))


def pack_states(lefts, totals, state_t, state, width):
    count = len(lefts)
    rights = [jnp.where(own_head(width), total, 0.0) for total in totals]
    rest = jnp.zeros((width - count * HEADS, width), f32)
    right = jnp.concatenate(rights + [rest], axis=0)
    for place, left in enumerate(lefts):
        span = slice(place * width, (place + 1) * width)
        state_t[span] = left.astype(bf16)
        state[:, span] = flip(left).astype(bf16)
    start = count * width
    used = state_t.shape[0] - start
    state_t[start:] = right[:used].astype(bf16)
    state[:, start : start + width] = -flip(right).astype(bf16)


def assemble(parts, gathered):
    shards = len(parts)
    here = lax.axis_index("fsdp")
    for place, part in enumerate(parts):
        gathered[lax.rem(here + shards - place, shards)] = part[...]


def columns(gathered, start, count):
    shards, _, width = gathered.shape
    piece = width // shards
    small = [gathered[shard, start : start + 16, :].astype(f32) for shard in range(shards)]
    joined = jnp.concatenate([part[:, :piece] for part in small], axis=1)
    return [
        flip(jnp.broadcast_to(joined[place : place + 1], (width, width)))[:, 0:1]
        for place in range(count)
    ]


def lane_fold(value):
    width = value.shape[0]
    total = value[:, :width]
    for start in range(width, value.shape[1], width):
        total = total + value[:, start : start + width]
    return total


def as_row(value):
    width = value.shape[0]
    return flip(jnp.broadcast_to(jnp.sum(value, axis=1, keepdims=True), (width, width)))


def scatter_blocks(stage, outs):
    shards = len(outs)
    here = lax.axis_index("fsdp")
    for place, out in enumerate(outs):
        out[...] = stage[lax.rem(here + place, shards)]


def whole(gathered, start, rows):
    shards = gathered.shape[0]
    return gathered[:, start : start + rows, :].reshape(shards * rows, gathered.shape[2])


def function_weight(presence, item, func, funcs, shape):
    total = presence[item, 0]
    for other in range(1, funcs):
        total = total + presence[item, other]
    own = jnp.full(shape, presence[item, func], jnp.int32).astype(f32)
    return own / jnp.full(shape, total, jnp.int32).astype(f32)


def pack_kernel(*refs):
    weights, vectors, gate = refs[:10], refs[10:14], refs[14]
    early, late = refs[15:]
    keys, values, query, out, query_two, key_two, value_two, out_two, enter, leave = weights
    start = 0
    for weight in (keys, values):
        early[start : start + weight.shape[0]] = weight[...]
        start += weight.shape[0]
    start = 0
    for weight in (query, out, query_two, key_two, value_two, out_two):
        late[start : start + weight.shape[0]] = weight[...]
        start += weight.shape[0]
    experts, piece, hidden = enter.shape
    width = late.shape[1]
    for expert in range(experts):
        for half in range(hidden // width):
            late[start : start + piece] = enter[expert, :, half * width : (half + 1) * width]
            start += piece
    for expert in range(experts):
        late[start : start + leave.shape[1]] = leave[expert]
        start += leave.shape[1]
    rest = jnp.zeros((1, width - piece), f32)
    rows = [
        jnp.concatenate([vector[...].astype(f32), rest], axis=1) for vector in vectors
    ]
    rows.append(jnp.zeros((4, width), f32))
    for row in range(2):
        rows.append(jnp.broadcast_to(gate[row : row + 1, 0:1].astype(f32), (1, width)))
    rows.append(jnp.zeros((6, width), f32))
    late[start : start + 16] = jnp.concatenate(rows, axis=0).astype(bf16)


def run_tasks(tasks):
    waiting = None
    for dots, work in tasks:
        found = dots()
        if waiting is not None:
            waiting[0](*waiting[1])
        waiting = (work, found)
    waiting[0](*waiting[1])


def mix(tasks, extra):
    mixed = []
    done = 0
    for place, task in enumerate(tasks, 1):
        mixed.append(task)
        due = len(extra) * place // len(tasks)
        mixed += extra[done:due]
        done = due
    return mixed


def behind(stage, total, chunks, groups):
    tasks = []
    for cols in chunks:
        tasks.append(stage(cols))
        tasks += [total(group) for group in groups if group.stop == cols.stop - 2 * CHUNK]
    return tasks


def add_to(ref, span):
    def work(value):
        ref[span] += value

    return work


def points_forward(counts, presence, points, *refs, funcs, shards):
    parts = refs[:shards]
    state_t, state, keys_out, values_out, gathered, weight = refs[shards:]
    item = pl.program_id(0)
    width = points.shape[2]
    slots = points.shape[1]
    piece = width // shards

    @pl.when(item == 0)
    def _():
        assemble(parts, gathered)
        weight[:width] = flip(whole(gathered, 0, piece))
        weight[width:] = flip(whole(gathered, piece, piece))

    chunks = [slice(start, start + CHUNK) for start in range(0, slots, CHUNK)]

    def project(func, cols):
        def dots():
            return (nt(weight[...], points[func, cols, :]),)

        def work(both):
            slot = cols.start + lax.broadcasted_iota(jnp.int32, (1, CHUNK), 1)
            probs = head_softmax(both[:width])
            keys = jnp.where(slot < counts[item, func], probs, 0.0)
            keys_out[func, :, cols] = keys.astype(bf16)
            values_out[func, :, cols] = both[width:].astype(bf16)

        return dots, work

    def summarize(func):
        values = values_out[func]
        extended = jnp.concatenate([values, jnp.ones((PAD, slots), bf16)], axis=0)
        share = function_weight(presence, item, func, funcs, (1, width))
        summed = nt(extended, keys_out[func])
        left = jnp.where(same_head(width), summed[:width], 0.0) * share
        return left, summed[width : width + 1]

    run_tasks([project(func, cols) for func in range(funcs) for cols in chunks])
    lefts, totals = zip(*(summarize(func) for func in range(funcs)))
    pack_states(lefts, totals, state_t.at[0], state.at[0], width)


def main_kernel(tokens, cotangent, coords, state_t, *refs, funcs, experts, shards, at):
    parts, outs, scratch = refs[:shards], refs[shards : 2 * shards + 11], refs[2 * shards + 11 :]
    (
        result,
        queries_out,
        cross_out,
        first_out,
        keys_out,
        values_out,
        grad_q_out,
        grad_second_out,
        grad_state_out,
        rest_weights,
        rest_vectors,
    ) = outs[:11]
    grads_out = outs[11:]
    (
        params,
        grads_stage,
        first_keep,
        query_keep,
        state_sum,
        self_t,
        self_state,
        grad_state_sum,
        w_query,
        w_out_one,
        w_self,
        w_out_two_t,
        w_out_two,
        w_in_t,
        w_in,
        w_exit,
        w_exit_t,
        gain_one,
        bias_one,
        gain_two,
        bias_two,
        hidden_keep,
        inner_keep,
        normed_keep,
        normed_rows,
        grad_keep,
        own_keep,
        pair_keep,
        sum_in,
        sum_exit,
        sum_out_two,
        sum_gain,
        sum_bias,
        sum_gate,
    ) = scratch
    item = pl.program_id(0)
    phase = pl.program_id(1)
    step = pl.program_id(2)
    steps = pl.num_programs(2)
    width = tokens.shape[1]
    rows = tokens.shape[0]
    piece = width // shards
    hidden = w_in.shape[1] // experts
    exit_piece = hidden // shards

    @pl.when((item == 0) & (phase == 0) & (step == 0))
    def _():
        assemble(parts, params)
        w_query[...] = flip(whole(params, at["query_first"], piece))
        w_out_one[...] = flip(whole(params, at["out_first"], piece))
        w_self[:width] = flip(whole(params, at["query_second"], piece))
        w_self[width : 2 * width] = flip(whole(params, at["key_second"], piece))
        w_self[2 * width :] = flip(whole(params, at["value_second"], piece))
        out_two = whole(params, at["out_second"], piece)
        w_out_two[...] = out_two
        w_out_two_t[...] = flip(out_two)
        for block in range(experts * hidden // width):
            part = whole(params, at["expert_in"] + block * piece, piece)
            w_in[:, block * width : (block + 1) * width] = part
            w_in_t[block * width : (block + 1) * width] = flip(part)
        for expert in range(experts):
            part = whole(params, at["expert_out"] + expert * exit_piece, exit_piece)
            w_exit[expert * hidden : (expert + 1) * hidden] = part
            w_exit_t[:, expert * hidden : (expert + 1) * hidden] = flip(part)
        names = ("query_second", "key_second", "value_second", "out_first", "query_first")
        for place, name in enumerate(names):
            rest_weights[:, place * width : (place + 1) * width] = whole(params, at[name], piece)
        found = columns(params, at["small"], 4)
        rest_vectors[0] = jnp.broadcast_to(found[0], rest_vectors.shape[1:])
        rest_vectors[1] = jnp.broadcast_to(found[1], rest_vectors.shape[1:])
        for vector, column in zip((gain_one, bias_one, gain_two, bias_two), found):
            vector[...] = jnp.broadcast_to(column, vector.shape)
        sum_in[...] = jnp.zeros_like(sum_in)
        sum_exit[...] = jnp.zeros_like(sum_exit)
        sum_out_two[...] = jnp.zeros_like(sum_out_two)
        sum_gain[...] = jnp.zeros_like(sum_gain)
        sum_bias[...] = jnp.zeros_like(sum_bias)
        sum_gate[...] = jnp.zeros_like(sum_gate)

    chunks = [slice(start, start + CHUNK) for start in range(0, rows, CHUNK)]
    groups = [slice(start, start + GROUP) for start in range(0, rows, GROUP)]
    every = slice(None)

    @pl.when((phase == 0) & (step == 0))
    def _():
        state_sum[...] = jnp.zeros_like(state_sum)
        grad_state_sum[...] = jnp.zeros_like(grad_state_sum)

    @pl.when(phase == 0)
    def _():
        def enter(cols):
            def dots():
                return (flip(tokens[cols, :]).astype(f32),)

            def work(rows_t):
                first_keep[step, :, cols] = rows_t
                hat, _scale = standardize(rows_t)
                normed_keep[:, cols] = (hat * gain_one[...] + bias_one[...]).astype(bf16)

            return dots, work

        def ask(cols):
            def dots():
                return (nn(w_query[...], normed_keep[:, cols]),)

            def work(value):
                queries_out[:, cols] = head_softmax(value).astype(bf16)

            return dots, work

        def across(cols):
            def dots():
                return (nn(state_t[0], queries_out[:, cols]),)

            def work(both):
                undo = inverse(both[funcs * width :])
                mixed = None
                for func in range(funcs):
                    part = by_head(
                        both[func * width : (func + 1) * width],
                        undo[func * HEADS : (func + 1) * HEADS],
                    )
                    mixed = part if mixed is None else mixed + part
                cross_out[:, cols] = mixed.astype(bf16)

            return dots, work

        def leave(cols):
            def dots():
                return (nn(w_out_one[...], cross_out[:, cols]),)

            def work(value):
                first = first_keep[step, :, cols] + value
                first_keep[step, :, cols] = first
                first_out[:, cols] = first.astype(bf16)

            return dots, work

        def project(cols):
            def dots():
                return (nn(w_self[...], first_out[:, cols]),)

            def work(three):
                query_keep[step, :, cols] = head_softmax(three[:width]).astype(bf16)
                keys_out[:, cols] = head_softmax(three[width : 2 * width]).astype(bf16)
                values = three[2 * width :].astype(bf16)
                values_out[:, cols] = values
                pair_keep[:width, cols] = values
                pair_keep[width:, cols] = jnp.ones((PAD, CHUNK), bf16)

            return dots, work

        def sum_state(cols):
            return (
                lambda: (nt(pair_keep[:, cols], keys_out[:, cols]),),
                add_to(state_sum, every),
            )

        tasks = [stage(cols) for stage in (enter, ask, across, leave) for cols in chunks]
        run_tasks(tasks + behind(project, sum_state, chunks, groups[:-1]))
        run_tasks([sum_state(groups[-1])])

        @pl.when(step == steps - 1)
        def _():
            left = jnp.where(same_head(width), state_sum[:width], 0.0)
            pack_states([left], [state_sum[width : width + 1]], self_t, self_state, width)

    @pl.when(phase == 1)
    def _():
        undo_of, norm_of, gates_of = {}, {}, {}
        grad_gates_of = {chunk.start: [] for chunk in chunks}

        def attend(cols):
            def dots():
                return (nn(self_t[...], query_keep[step, :, cols]),)

            def work(both):
                undo = inverse(both[width : width + HEADS])
                undo_of[cols.start] = undo
                own_keep[:, cols] = by_head(both[:width], undo).astype(bf16)
                grad_keep[:, cols] = flip(cotangent[cols, :])

            return dots, work

        def gate(cols):
            across, down = coords[0:1, cols], coords[1:2, cols]
            logits = []
            for expert in range(experts):
                pair = params[expert, at["small"] : at["small"] + 16, 0:1].astype(f32)
                logits.append(across * pair[8:9] + down * pair[9:10])
            peak = logits[0]
            for logit in logits[1:]:
                peak = jnp.maximum(peak, logit)
            raised = [jnp.exp(logit - peak) for logit in logits]
            total = raised[0]
            for other in raised[1:]:
                total = total + other
            return [other / total for other in raised]

        def norm(cols):
            def dots():
                return (nn(w_out_two_t[...], own_keep[:, cols]),)

            def work(value):
                second = first_keep[step, :, cols] + value
                first_keep[step, :, cols] = second
                hat, scale = standardize(second)
                norm_of[cols.start] = (hat, scale)
                normed = (hat * gain_two[...] + bias_two[...]).astype(bf16)
                normed_keep[:, cols] = normed
                normed_rows[cols, :] = flip(normed)
                gates_of[cols.start] = gate(cols)

            return dots, work

        def expand(cols, expert):
            whole_span = slice(expert * hidden, (expert + 1) * hidden)

            def dots():
                return (
                    nn(w_in_t[whole_span], normed_keep[:, cols]).astype(bf16),
                    nn(w_exit[whole_span], grad_keep[:, cols]).astype(bf16),
                )

            def work(inners, backs):
                share = (0.5 * gates_of[cols.start][expert]).astype(bf16)
                partial_sum = None
                for start in range(0, hidden, SLAB):
                    inner, back = inners[start : start + SLAB], backs[start : start + SLAB]
                    span = slice(expert * hidden + start, expert * hidden + start + SLAB)
                    square = inner * inner
                    tanh = jnp.tanh(inner * (0.7978845608028654 + 0.035677408136300125 * square))
                    above = 1.0 + tanh
                    active = inner * above
                    product = active * back
                    folded = product[:16]
                    for row in range(16, SLAB, 16):
                        folded = folded + product[row : row + 16]
                    folded = folded.astype(f32)
                    partial_sum = folded if partial_sum is None else partial_sum + folded
                    hidden_keep[span, cols] = active * share
                    slope = above + active * (1.0 - tanh) * (
                        0.7978845608028654 + 0.10703222440890037 * square
                    )
                    inner_keep[span, cols] = slope * (back * share)
                partial_sum = 0.5 * partial_sum
                grad_gates_of[cols.start].append(jnp.sum(partial_sum, axis=0, keepdims=True))

            return dots, work

        def contract(cols):
            def dots():
                return (
                    nn(w_exit_t[...], hidden_keep[:, cols]),
                    nn(w_in[...], inner_keep[:, cols]),
                )

            def work(mixed, grad_normed):
                result[cols, :] = flip((first_keep[step, :, cols] + mixed).astype(bf16))
                hat, scale = norm_of[cols.start]
                sum_gain[...] += lane_fold(grad_normed * hat)
                sum_bias[...] += lane_fold(grad_normed)
                grad_second = grad_keep[:, cols].astype(f32) + norm_back(
                    grad_normed * gain_two[...], hat, scale
                )
                grad_second_out[:, cols] = grad_second.astype(bf16)
                gates, grad_gates = gates_of[cols.start], grad_gates_of[cols.start]
                across, down = coords[0:1, cols], coords[1:2, cols]
                mean_gate = gates[0] * grad_gates[0]
                for expert in range(1, experts):
                    mean_gate = mean_gate + gates[expert] * grad_gates[expert]
                for expert in range(experts):
                    change = gates[expert] * (grad_gates[expert] - mean_gate)
                    sum_gate[expert : expert + 1, cols] += across * change
                    sum_gate[experts + expert : experts + expert + 1, cols] += down * change

            return dots, work

        def attend_back(cols):
            def dots():
                return (nn(w_out_two[...], grad_second_out[:, cols]),)

            def work(value):
                share = by_head(value, undo_of[cols.start])
                pair_keep[:width, cols] = share.astype(bf16)
                sums = head_sums(share * own_keep[:, cols].astype(f32))
                pair_keep[width:, cols] = jnp.concatenate(
                    [sums, jnp.zeros((PAD - HEADS, CHUNK), f32)], axis=0
                ).astype(bf16)

            return dots, work

        def query_back(cols):
            def dots():
                return (nn(self_state[:, : width + PAD], pair_keep[:, cols]),)

            def work(grad_q):
                queries = query_keep[step, :, cols]
                grad_q_out[:, cols] = softmax_back(queries, grad_q).astype(bf16)

            return dots, work

        def sum_hidden(cols, expert):
            span = slice(expert * hidden, (expert + 1) * hidden)
            return (
                lambda: (nn(hidden_keep[span, cols], cotangent[cols, :]),),
                add_to(sum_exit, span),
            )

        def sum_inner(cols, expert):
            span = slice(expert * hidden, (expert + 1) * hidden)
            return (
                lambda: (nn(inner_keep[span, cols], normed_rows[cols, :]),),
                add_to(sum_in, span),
            )

        def sum_own(cols):
            return (
                lambda: (nt(own_keep[:, cols], grad_second_out[:, cols]),),
                add_to(sum_out_two, every),
            )

        def sum_pair(cols):
            return (
                lambda: (nt(pair_keep[:, cols], query_keep[step, :, cols]),),
                add_to(grad_state_sum, every),
            )

        tasks = [stage(cols) for stage in (attend, norm) for cols in chunks]
        earlier = []
        for group in groups:
            inside = [cols for cols in chunks if group.start <= cols.start < group.stop]
            tasks += mix(
                [expand(cols, expert) for cols in inside for expert in range(experts)], earlier
            )
            earlier = [
                sums(group, expert) for expert in range(experts) for sums in (sum_hidden, sum_inner)
            ]
        tasks += mix([stage(cols) for stage in (contract, attend_back) for cols in chunks], earlier)
        last = [sums(group) for group in groups for sums in (sum_own, sum_pair)]
        tasks += mix([query_back(cols) for cols in chunks], last)
        run_tasks(tasks)

        @pl.when(step == steps - 1)
        def _():
            grad_state_out[0] = grad_state_sum[...]

    @pl.when((item == pl.num_programs(0) - 1) & (phase == 1) & (step == steps - 1))
    def _():
        gain, bias = as_row(sum_gain[...]), as_row(sum_bias[...])
        gate = jnp.broadcast_to(jnp.sum(sum_gate[...], axis=1, keepdims=True), (8, width))
        row = lax.broadcasted_iota(jnp.int32, (8, width), 0)
        vectors = jnp.where(row == 0, gain[:8], bias[:8])
        small = jnp.concatenate([vectors, gate], axis=0).astype(bf16)
        start = 0
        for block in range(experts * hidden // width):
            part = flip(sum_in[block * width : (block + 1) * width]).astype(bf16)
            grads_stage[:, start : start + piece, :] = part.reshape(shards, piece, width)
            start += piece
        for expert in range(experts):
            part = sum_exit[expert * hidden : (expert + 1) * hidden].astype(bf16)
            grads_stage[:, start : start + exit_piece, :] = part.reshape(shards, exit_piece, width)
            start += exit_piece
        part = sum_out_two[...].astype(bf16)
        grads_stage[:, start : start + piece, :] = part.reshape(shards, piece, width)
        start += piece
        for shard in range(shards):
            grads_stage[shard, start : start + 16, :] = small
        scatter_blocks(grads_stage, grads_out)


def rest_kernel(
    presence,
    tokens,
    queries_in,
    cross_in,
    first_in,
    keys_in,
    values_in,
    grad_q_in,
    grad_second_in,
    grad_state_in,
    state_t,
    state,
    weights,
    vectors,
    *refs,
    funcs,
    item,
    first_call,
):
    if not first_call:
        carry, refs = refs[3], refs[5:]
    (
        grad_tokens,
        grad_cross_state_out,
        grad_totals_out,
        sums_out,
        grad_self_state,
        grad_totals,
        grad_state_sum,
        sums,
        three_keep,
        cross_keep,
        stack_keep,
        query_keep,
        normed_keep,
    ) = refs
    step = pl.program_id(0)
    steps = pl.num_programs(0)
    width = tokens.shape[1]
    self_part = slice(0, 3 * width)
    out_part = slice(3 * width, 4 * width)
    query_part = slice(4 * width, 5 * width)
    gain_part = slice(5 * width, 6 * width)
    bias_part = slice(6 * width, 7 * width)

    @pl.when(step == 0)
    def _():
        sums[...] = jnp.zeros_like(sums) if first_call else carry[...]
        left = jnp.where(same_head(width), grad_state_in[0, :width], 0.0)
        grad_self_state[0] = flip(left).astype(bf16)
        grad_self_state[1] = left.astype(bf16)
        column = totals_column(grad_state_in[0, width : width + HEADS], width)
        grad_totals[...] = jnp.broadcast_to(column[:, 0:1], grad_totals.shape)

    chunks = [slice(start, start + CHUNK) for start in range(0, tokens.shape[0], CHUNK)]
    norm_of, grad_first_of = {}, {}

    def self_back(cols):
        def dots():
            return (
                nn(grad_self_state[0], values_in[:, cols]),
                nn(grad_self_state[1], keys_in[:, cols]),
            )

        def work(grad_keys, grad_values):
            grad_keys = softmax_back(keys_in[:, cols], grad_keys + grad_totals[...])
            three_keep[:width, cols] = grad_q_in[:, cols]
            three_keep[width : 2 * width, cols] = grad_keys.astype(bf16)
            three_keep[2 * width :, cols] = grad_values.astype(bf16)

        return dots, work

    def join(cols):
        def dots():
            return (nn(weights[:, self_part], three_keep[:, cols]), flip(tokens[cols, :]))

        def work(value, rows_t):
            grad_first = grad_second_in[:, cols].astype(f32) + value
            grad_first_of[cols.start] = grad_first
            cross_keep[:, cols] = grad_first.astype(bf16)
            hat, scale = standardize(rows_t.astype(f32))
            norm_of[cols.start] = (hat, scale)
            normed_keep[:, cols] = (hat * vectors[0] + vectors[1]).astype(bf16)

        return dots, work

    def cross_back(cols):
        def dots():
            return nn(weights[:, out_part], cross_keep[:, cols]), nn(state_t[0], queries_in[:, cols])

        def work(share, both):
            undo = inverse(both[funcs * width :])
            sums_by_head = []
            for func in range(funcs):
                span = slice(func * width, (func + 1) * width)
                scales = undo[func * HEADS : (func + 1) * HEADS]
                part = by_head(share, scales)
                stack_keep[span, cols] = part.astype(bf16)
                sums_by_head.append(head_sums(part * by_head(both[span], scales)))
            spare = stack_keep.shape[0] - funcs * (width + HEADS)
            if spare:
                sums_by_head.append(jnp.zeros((spare, CHUNK), f32))
            stack_keep[funcs * width :, cols] = jnp.concatenate(sums_by_head, axis=0).astype(bf16)

        return dots, work

    def query_back(cols):
        def dots():
            return (nn(state[0, :, : stack_keep.shape[0]], stack_keep[:, cols]),)

        def work(grad_q):
            query_keep[:, cols] = softmax_back(queries_in[:, cols], grad_q).astype(bf16)

        return dots, work

    def finish(cols):
        def dots():
            return (nn(weights[:, query_part], query_keep[:, cols]),)

        def work(grad_normed):
            hat, scale = norm_of[cols.start]
            sums[gain_part] += lane_fold(grad_normed * hat)
            sums[bias_part] += lane_fold(grad_normed)
            grad_rows = grad_first_of[cols.start] + norm_back(
                grad_normed * vectors[0], hat, scale
            )
            grad_tokens[cols, :] = flip(grad_rows)

        return dots, work

    @pl.when(step == 0)
    def _():
        grad_state_sum[...] = jnp.zeros_like(grad_state_sum)

    every = slice(None)
    sum_self = (lambda: (nt(three_keep[...], first_in[...]),), add_to(sums, self_part))
    sum_out = (lambda: (nt(cross_in[...], cross_keep[...]),), add_to(sums, out_part))
    sum_state = (lambda: (nt(stack_keep[...], queries_in[...]),), add_to(grad_state_sum, every))
    sum_query = (lambda: (nt(normed_keep[...], query_keep[...]),), add_to(sums, query_part))
    tasks = [stage(cols) for stage in (self_back, join) for cols in chunks]
    tasks += mix([cross_back(cols) for cols in chunks], [sum_self])
    tasks += mix([query_back(cols) for cols in chunks], [sum_out])
    tasks += mix([finish(cols) for cols in chunks], [sum_state])
    run_tasks(tasks + [sum_query])

    @pl.when(step == steps - 1)
    def _():
        mask = same_head(width)
        for func in range(funcs):
            weight = function_weight(presence, item, func, funcs, (1, width))
            left = jnp.where(mask, grad_state_sum[func * width : (func + 1) * width], 0.0)
            grad_cross_state_out[func] = (left * weight).astype(bf16)
            start = funcs * width + func * HEADS
            grad_totals_out[func] = totals_column(grad_state_sum[start : start + HEADS], width)
        sums_out[...] = sums[...]


def points_back(points, keys_in, values_in, grad_state, grad_totals, carry, _after, *refs, shards):
    outs = refs[:shards]
    sums, stage, grads = refs[shards:]
    step = pl.program_id(0)
    width = points.shape[2]
    piece = width // shards

    funcs, slots, _ = points.shape
    chunks = [slice(start, start + CHUNK) for start in range(0, slots, CHUNK)]
    turned = [flip(grad_state[func]) for func in range(funcs)]

    def back(func, cols):
        def dots():
            return (
                nn(turned[func], values_in[func, :, cols]),
                nn(grad_state[func], keys_in[func, :, cols]),
            )

        def work(grad_keys, grad_values):
            grad_keys = grad_keys + grad_totals[func, :, 0:1]
            grad_k = softmax_back(keys_in[func, :, cols], grad_keys)
            grads[func, :width, cols] = grad_k.astype(bf16)
            grads[func, width:, cols] = grad_values.astype(bf16)

        return dots, work

    run_tasks([back(func, cols) for func in range(funcs) for cols in chunks])
    found = nn(grads[0], points[0])
    for func in range(1, funcs):
        found = found + nn(grads[func], points[func])

    @pl.when(step == 0)
    def _():
        sums[...] = found
        gain = as_row(carry[5 * width : 6 * width])
        bias = as_row(carry[6 * width : 7 * width])
        row = lax.broadcasted_iota(jnp.int32, (16, width), 0)
        small = jnp.where(row == 0, gain[:16], bias[:16]).astype(bf16)
        for place in range(5):
            part = carry[place * width : (place + 1) * width]
            part = (flip(part) if place < 3 else part).astype(bf16)
            stage[:, place * piece : (place + 1) * piece, :] = part.reshape(shards, piece, width)
        for shard in range(shards):
            stage[shard, 5 * piece : 5 * piece + 16, :] = small

    @pl.when(step > 0)
    def _():
        sums[...] += found

    @pl.when(step == pl.num_programs(0) - 1)
    def _():
        for place in range(2):
            start = 5 * piece + 16 + place * piece
            part = flip(sums[place * width : (place + 1) * width]).astype(bf16)
            stage[:, start : start + piece, :] = part.reshape(shards, piece, width)
        scatter_blocks(stage, outs)


def total_of(parts):
    value = parts[0][...].astype(f32)
    for part in parts[1:]:
        value = value + part[...].astype(f32)
    return value


def unpack_kernel(*refs, counts, experts, piece, exit_piece, hidden):
    main_parts, parts = refs[: counts[0]], refs[counts[0] : sum(counts)]
    outs, (small, main, rest) = refs[-18:-3], refs[-3:]
    width = main.shape[1]
    main[...] = total_of(main_parts)
    rest[...] = total_of(parts)
    (
        gain_one,
        bias_one,
        query_one,
        key_one,
        value_one,
        out_one,
        query_two,
        key_two,
        value_two,
        out_two,
        gain_two,
        bias_two,
        enter,
        leave,
        gate,
    ) = outs
    start = 0
    for expert in range(experts):
        for half in range(hidden // width):
            block = main[start : start + piece]
            enter[expert, :, half * width : (half + 1) * width] = block
            start += piece
    for expert in range(experts):
        leave[expert] = main[start : start + exit_piece]
        start += exit_piece
    out_two[...] = main[start : start + piece]
    start += piece
    small[:16] = main[start : start + 16]
    start = 0
    for out in (query_two, key_two, value_two, out_one, query_one):
        out[...] = rest[start : start + piece]
        start += piece
    small[16:] = rest[start : start + 16]
    start += 16
    for out in (key_one, value_one):
        out[...] = rest[start : start + piece]
        start += piece
    shard = lax.axis_index("fsdp")
    turned = pltpu.roll(small[...], lax.rem(width - shard * piece, width), 1)
    gain_two[...] = turned[0:1, :piece]
    bias_two[...] = turned[1:2, :piece]
    gain_one[...] = turned[16:17, :piece]
    bias_one[...] = turned[17:18, :piece]
    for row in range(2):
        gate[:, row : row + 1] = small[pl.ds(8 + row * experts + shard, 1), 0:1]


def whole_spec(shape):
    return pl.BlockSpec(shape, lambda *_: (0,) * len(shape))


def route(size, shift, digit, stride):
    def target(i):
        own = i // stride % digit
        return i + ((own + shift) % digit - own) * stride

    return [(i, target(i)) for i in range(size)]


def spread(value, axis, size, digit, stride):
    return [value] + [
        lax.ppermute(value, axis, route(size, shift, digit, stride)) for shift in range(1, digit)
    ]


def exchange(values, axis, size, stride):
    digit = len(values)
    return [values[0]] + [
        lax.ppermute(values[shift], axis, route(size, shift, digit, stride))
        for shift in range(1, digit)
    ]


def digits(size):
    found = []
    stride = 1
    while stride < size:
        rest = size // stride
        digit = 2 if stride == 1 and rest % 2 == 0 else 4 if rest % 4 == 0 else rest
        found.append((digit, stride))
        stride *= digit
    return found or [(1, 1)]


def sum_parts(parts):
    return total_of([part.astype(f32) for part in parts]).astype(bf16)


def shards_fn(
    dp,
    shards,
    tokens,
    points,
    coords,
    presence,
    counts,
    cotangent,
    gain_first,
    bias_first,
    query_first,
    key_first,
    value_first,
    out_first,
    query_second,
    key_second,
    value_second,
    out_second,
    gain_second,
    bias_second,
    expert_in,
    expert_out,
    gate_weight,
):
    count, width = tokens.shape
    items, funcs, slots, _ = points.shape
    length = count // items
    experts, piece, hidden = expert_in.shape
    exit_piece = expert_out.shape[1]
    tile, rest_tile = min(MAIN_TILE, length), min(REST_TILE, length)
    steps, rest_steps = length // tile, length // rest_tile
    inner = experts * hidden
    enter_rows = experts * piece * (hidden // width)
    limit = pltpu.CompilerParams(vmem_limit_bytes=VMEM)

    at = {}
    place = 0
    for name, size in (
        ("query_first", piece),
        ("out_first", piece),
        ("query_second", piece),
        ("key_second", piece),
        ("value_second", piece),
        ("out_second", piece),
        ("expert_in", enter_rows),
        ("expert_out", experts * exit_piece),
        ("small", 16),
    ):
        at[name] = place
        place += size
    late_rows_count = place
    early_pack, late_pack = pl.pallas_call(
        pack_kernel,
        out_shape=[
            jax.ShapeDtypeStruct((2 * piece, width), bf16),
            jax.ShapeDtypeStruct((late_rows_count, width), bf16),
        ],
        name="pack",
    )(
        key_first,
        value_first,
        query_first,
        out_first,
        query_second,
        key_second,
        value_second,
        out_second,
        expert_in,
        expert_out,
        *(
            vector.reshape(1, piece)
            for vector in (gain_first, bias_first, gain_second, bias_second)
        ),
        gate_weight,
    )
    early_parts = spread(early_pack, "fsdp", shards, shards, 1)
    late_parts = spread(late_pack, "fsdp", shards, shards, 1)
    late_specs = [whole_spec((late_rows_count, width))] * shards
    gathered = pltpu.VMEM((shards, late_rows_count, width), bf16)

    smem = pl.BlockSpec(memory_space=pltpu.SMEM)
    units = items * funcs
    state_rows = funcs * width + -(-funcs * HEADS // PAD) * PAD
    flat_points = points.reshape(units, slots, width)
    state_t, state, keys_one, values_one = pl.pallas_call(
        partial(points_forward, funcs=funcs, shards=shards),
        grid=(items,),
        in_specs=[smem, smem, pl.BlockSpec((funcs, slots, width), lambda u: (u, 0, 0))]
        + [whole_spec((2 * piece, width))] * shards,
        out_specs=[
            pl.BlockSpec((1, state_rows, width), lambda u: (u, 0, 0)),
            pl.BlockSpec((1, width, (funcs + 1) * width), lambda u: (u, 0, 0)),
            pl.BlockSpec((funcs, width, slots), lambda u: (u, 0, 0)),
            pl.BlockSpec((funcs, width, slots), lambda u: (u, 0, 0)),
        ],
        out_shape=[
            jax.ShapeDtypeStruct((items, state_rows, width), bf16),
            jax.ShapeDtypeStruct((items, width, (funcs + 1) * width), bf16),
            jax.ShapeDtypeStruct((units, width, slots), bf16),
            jax.ShapeDtypeStruct((units, width, slots), bf16),
        ],
        scratch_shapes=[
            pltpu.VMEM((shards, 2 * piece, width), bf16),
            pltpu.VMEM((2 * width, width), bf16),
        ],
        compiler_params=limit,
        cost_estimate=cost(8),
        name="points_forward",
    )(counts, presence, flat_points, *early_parts)

    kept = jax.ShapeDtypeStruct((width, count), bf16)
    main_rows = enter_rows + experts * exit_piece + piece + 16

    def early(i, p, j):
        return i * steps + jnp.where(p == 0, j, steps - 1)

    def late(i, p, j):
        return i * steps + jnp.where(p == 0, 0, j)

    early_keep = pl.BlockSpec((width, tile), lambda i, p, j: (0, early(i, p, j)))
    late_keep = pl.BlockSpec((width, tile), lambda i, p, j: (0, late(i, p, j)))
    late_rows = pl.BlockSpec((tile, width), lambda i, p, j: (late(i, p, j), 0))
    (
        result,
        queries_one,
        cross,
        first,
        keys_two,
        values_two,
        grad_q_two,
        grad_second,
        grad_state_two,
        rest_weights,
        rest_vectors,
        *main_grads,
    ) = pl.pallas_call(
        partial(main_kernel, funcs=funcs, experts=experts, shards=shards, at=at),
        grid=(items, 2, steps),
        in_specs=[
            pl.BlockSpec((tile, width), lambda i, p, j: (early(i, p, j), 0)),
            late_rows,
            pl.BlockSpec((2, tile), lambda i, p, j: (0, late(i, p, j))),
            pl.BlockSpec((1, state_rows, width), lambda i, p, j: (i, 0, 0)),
        ]
        + late_specs,
        out_specs=[
            late_rows,
            early_keep,
            early_keep,
            early_keep,
            early_keep,
            early_keep,
            late_keep,
            late_keep,
            pl.BlockSpec((1, width + PAD, width), lambda i, p, j: (i, 0, 0)),
            whole_spec((width, 5 * width)),
            whole_spec((2, width, CHUNK)),
        ]
        + [whole_spec((main_rows, width))] * shards,
        out_shape=[
            jax.ShapeDtypeStruct((count, width), bf16),
            kept,
            kept,
            kept,
            kept,
            kept,
            kept,
            kept,
            jax.ShapeDtypeStruct((items, width + PAD, width), f32),
            jax.ShapeDtypeStruct((width, 5 * width), bf16),
            jax.ShapeDtypeStruct((2, width, CHUNK), f32),
        ]
        + [jax.ShapeDtypeStruct((main_rows, width), bf16)] * shards,
        scratch_shapes=[
            gathered,
            pltpu.VMEM((shards, main_rows, width), bf16),
            pltpu.VMEM((steps, width, tile), f32),
            pltpu.VMEM((steps, width, tile), bf16),
            pltpu.VMEM((width + PAD, width), f32),
            pltpu.VMEM((width + PAD, width), bf16),
            pltpu.VMEM((width, 2 * width), bf16),
            pltpu.VMEM((width + PAD, width), f32),
            pltpu.VMEM((width, width), bf16),
            pltpu.VMEM((width, width), bf16),
            pltpu.VMEM((3 * width, width), bf16),
            pltpu.VMEM((width, width), bf16),
            pltpu.VMEM((width, width), bf16),
            pltpu.VMEM((inner, width), bf16),
            pltpu.VMEM((width, inner), bf16),
            pltpu.VMEM((inner, width), bf16),
            pltpu.VMEM((width, inner), bf16),
            pltpu.VMEM((width, CHUNK), f32),
            pltpu.VMEM((width, CHUNK), f32),
            pltpu.VMEM((width, CHUNK), f32),
            pltpu.VMEM((width, CHUNK), f32),
            pltpu.VMEM((inner, tile), bf16),
            pltpu.VMEM((inner, tile), bf16),
            pltpu.VMEM((width, tile), bf16),
            pltpu.VMEM((tile, width), bf16),
            pltpu.VMEM((width, tile), bf16),
            pltpu.VMEM((width, tile), bf16),
            pltpu.VMEM((width + PAD, tile), bf16),
            pltpu.VMEM((inner, width), f32),
            pltpu.VMEM((inner, width), f32),
            pltpu.VMEM((width, width), f32),
            pltpu.VMEM((width, width), f32),
            pltpu.VMEM((width, width), f32),
            pltpu.VMEM((2 * experts, tile), f32),
        ],
        compiler_params=limit,
        cost_estimate=cost(80),
        name="main",
    )(tokens, cotangent, coords, state_t, *late_parts)

    rest_rows = 7 * piece + 16

    def rest_call(item, earlier, after):
        first_call = item == 0
        keep_spec = pl.BlockSpec((width, rest_tile), lambda j: (0, item * rest_steps + j))
        row_spec = pl.BlockSpec((rest_tile, width), lambda j: (item * rest_steps + j, 0))
        unit_spec = pl.BlockSpec((funcs, width, width), lambda j: (item, 0, 0))
        anywhere = pl.BlockSpec(memory_space=pl.ANY)
        in_specs = [
            smem,
            row_spec,
            keep_spec,
            keep_spec,
            keep_spec,
            keep_spec,
            keep_spec,
            keep_spec,
            keep_spec,
            pl.BlockSpec((1, width + PAD, width), lambda j: (item, 0, 0)),
            pl.BlockSpec((1, state_rows, width), lambda j: (item, 0, 0)),
            pl.BlockSpec((1, width, (funcs + 1) * width), lambda j: (item, 0, 0)),
            whole_spec((width, 5 * width)),
            whole_spec((2, width, CHUNK)),
        ]
        operands = [
            presence,
            tokens,
            queries_one,
            cross,
            first,
            keys_two,
            values_two,
            grad_q_two,
            grad_second,
            grad_state_two,
            state_t,
            state,
            rest_weights,
            rest_vectors,
        ]
        aliases = {}
        if not first_call:
            aliases = {len(operands) + k: k for k in range(3)}
            in_specs += [anywhere] * 3 + [whole_spec((7 * width, width)), anywhere]
            operands += [*earlier, after]
        out_specs = [row_spec, unit_spec, unit_spec, whole_spec((7 * width, width))]
        out_shape = [
            jax.ShapeDtypeStruct((count, width), f32),
            jax.ShapeDtypeStruct((units, width, width), bf16),
            jax.ShapeDtypeStruct((units, width, width), f32),
            jax.ShapeDtypeStruct((7 * width, width), f32),
        ]
        return pl.pallas_call(
            partial(
                rest_kernel,
                funcs=funcs,
                item=item,
                first_call=first_call,
            ),
            grid=(rest_steps,),
            in_specs=in_specs,
            out_specs=out_specs,
            out_shape=out_shape,
            input_output_aliases=aliases,
            scratch_shapes=[
                pltpu.VMEM((2, width, width), bf16),
                pltpu.VMEM((width, CHUNK), f32),
                pltpu.VMEM((state_rows, width), f32),
                pltpu.VMEM((7 * width, width), f32),
                pltpu.VMEM((3 * width, rest_tile), bf16),
                pltpu.VMEM((width, rest_tile), bf16),
                pltpu.VMEM((state_rows, rest_tile), bf16),
                pltpu.VMEM((width, rest_tile), bf16),
                pltpu.VMEM((width, rest_tile), bf16),
            ],
            compiler_params=limit,
            cost_estimate=cost(18),
            name="rest",
        )(*operands)

    levels = digits(dp)
    main_levels = levels[::-1]
    main_parts = exchange(main_grads, "fsdp", shards, 1)
    level = 0
    found = None
    for item in range(items):
        found = rest_call(item, found, main_sum if item else None)
        if item < len(main_levels):
            main_sum = sum_parts(main_parts)
            main_parts = spread(main_sum, "dp", dp, *main_levels[item])
            level = item + 1
    grad_tokens, grad_state_one, grad_totals_one, carry = found

    rest_grads = pl.pallas_call(
        partial(points_back, shards=shards),
        grid=(items,),
        in_specs=[
            pl.BlockSpec((funcs, slots, width), lambda u: (u, 0, 0)),
            pl.BlockSpec((funcs, width, slots), lambda u: (u, 0, 0)),
            pl.BlockSpec((funcs, width, slots), lambda u: (u, 0, 0)),
            pl.BlockSpec((funcs, width, width), lambda u: (u, 0, 0)),
            pl.BlockSpec((funcs, width, width), lambda u: (u, 0, 0)),
            whole_spec((7 * width, width)),
            pl.BlockSpec(memory_space=pl.ANY),
        ],
        out_specs=[whole_spec((rest_rows, width))] * shards,
        out_shape=[jax.ShapeDtypeStruct((rest_rows, width), bf16)] * shards,
        scratch_shapes=[
            pltpu.VMEM((2 * width, width), f32),
            pltpu.VMEM((shards, rest_rows, width), bf16),
            pltpu.VMEM((funcs, 2 * width, slots), bf16),
        ],
        compiler_params=limit,
        cost_estimate=cost(7),
        name="points_back",
    )(flat_points, keys_one, values_one, grad_state_one, grad_totals_one, carry, main_sum)
    rest_got = exchange(rest_grads, "fsdp", shards, 1)

    parts = rest_got
    for digit, stride in main_levels[level:]:
        main_parts = spread(sum_parts(main_parts), "dp", dp, digit, stride)
    for digit, stride in levels:
        parts = spread(sum_parts(parts), "dp", dp, digit, stride)

    matrix = jax.ShapeDtypeStruct((piece, width), f32)
    vector = jax.ShapeDtypeStruct((1, piece), f32)
    outs = pl.pallas_call(
        partial(
            unpack_kernel,
            counts=(len(main_parts), len(parts)),
            experts=experts,
            piece=piece,
            exit_piece=exit_piece,
            hidden=hidden,
        ),
        out_shape=[vector] * 2
        + [matrix] * 8
        + [vector] * 2
        + [
            jax.ShapeDtypeStruct(expert_in.shape, f32),
            jax.ShapeDtypeStruct(expert_out.shape, f32),
            jax.ShapeDtypeStruct((1, 2), f32),
        ],
        scratch_shapes=[
            pltpu.VMEM((32, width), f32),
            pltpu.VMEM((main_rows, width), f32),
            pltpu.VMEM((rest_rows, width), f32),
        ],
        name="unpack",
    )(*main_parts, *parts)
    outs = [out.reshape(piece) if out.shape == (1, piece) else out for out in outs]
    return (result, grad_tokens, *outs[:-1], outs[-1].reshape(gate_weight.shape))


def solution(mesh):
    rows = P(("dp", "fsdp"), None)
    matrix = P("fsdp", None)
    vector = P("fsdp")
    expert = P(None, "fsdp", None)
    parameters = (
        (vector, vector)
        + (matrix,) * 8
        + (vector, vector, expert, expert, P(None, "fsdp"))
    )
    return jax.shard_map(
        partial(shards_fn, mesh.shape["dp"], mesh.shape["fsdp"]),
        mesh=mesh,
        in_specs=(
            rows,
            P(("dp", "fsdp"), None, None, None),
            P(None, ("dp", "fsdp")),
            rows,
            rows,
            rows,
        )
        + parameters,
        out_specs=(rows, rows) + parameters,
        check_vma=False,
    )
```

```python
from functools import partial

import jax
import jax.numpy as jnp
from jax import lax
from jax.experimental import pallas as pl
from jax.experimental.pallas import tpu as pltpu
from jax.sharding import PartitionSpec as P


HEADS = 8
eps = 1e-05
f32 = jnp.float32
bf16 = jnp.bfloat16
MAIN_TILE = 4096
REST_TILE = 1024
GROUP = 1024
STRIP = 128
CHUNK = 256
SLAB = 64
PAD = 16
VMEM = 60 * 1024 * 1024


def cost(microseconds):
    return pl.CostEstimate(flops=microseconds * 10**9, bytes_accessed=10**6, transcendentals=0)


def nn(left, right):
    return jnp.dot(left, right, preferred_element_type=f32)


def nt(left, right):
    return lax.dot_general(left, right, (((1,), (1,)), ((), ())), preferred_element_type=f32)


def flip(value):
    return value.T


def inverse(value):
    return pl.reciprocal(value, approx=True)


def head_softmax(value):
    width, rows = value.shape
    split = value.reshape(HEADS, width // HEADS, rows)
    raised = jnp.exp(split - jnp.max(split, axis=1, keepdims=True))
    return (raised * inverse(jnp.sum(raised, axis=1, keepdims=True))).reshape(width, rows)


def softmax_back(probs, grad):
    width, rows = grad.shape
    probs = probs.astype(f32).reshape(HEADS, width // HEADS, rows)
    grad = grad.reshape(HEADS, width // HEADS, rows)
    inner = jnp.sum(probs * grad, axis=1, keepdims=True)
    return (probs * (grad - inner)).reshape(width, rows)


def standardize(value):
    centre = value - jnp.mean(value, axis=0, keepdims=True)
    scale = lax.rsqrt(jnp.mean(centre * centre, axis=0, keepdims=True) + eps)
    return centre * scale, scale


def norm_back(grad, hat, scale):
    return scale * (
        grad
        - jnp.mean(grad, axis=0, keepdims=True)
        - hat * jnp.mean(grad * hat, axis=0, keepdims=True)
    )


def same_head(width):
    shape, head = (width, width), width // HEADS
    row = lax.broadcasted_iota(jnp.int32, shape, 0)
    column = lax.broadcasted_iota(jnp.int32, shape, 1)
    return lax.div(row, head) == lax.div(column, head)


def own_head(width):
    shape, head = (HEADS, width), width // HEADS
    row = lax.broadcasted_iota(jnp.int32, shape, 0)
    return row == lax.div(lax.broadcasted_iota(jnp.int32, shape, 1), head)


def by_head(value, scales):
    width, rows = value.shape
    split = value.reshape(HEADS, width // HEADS, rows)
    return (split * scales.reshape(HEADS, 1, rows)).reshape(width, rows)


def head_sums(value):
    width, rows = value.shape
    return jnp.sum(value.reshape(HEADS, width // HEADS, rows), axis=1)


def totals_column(rows, width):
    row = jnp.sum(jnp.where(own_head(width), rows, 0.0), axis=0, keepdims=True)
    return flip(jnp.broadcast_to(-row, (width, width)))


def pack_states(lefts, totals, state_t, state, width):
    count = len(lefts)
    rights = [jnp.where(own_head(width), total, 0.0) for total in totals]
    rest = jnp.zeros((width - count * HEADS, width), f32)
    right = jnp.concatenate(rights + [rest], axis=0)
    for place, left in enumerate(lefts):
        span = slice(place * width, (place + 1) * width)
        state_t[span] = left.astype(bf16)
        state[:, span] = flip(left).astype(bf16)
    start = count * width
    used = state_t.shape[0] - start
    state_t[start:] = right[:used].astype(bf16)
    state[:, start : start + width] = -flip(right).astype(bf16)


def assemble(parts, gathered):
    shards = len(parts)
    here = lax.axis_index("fsdp")
    for place, part in enumerate(parts):
        gathered[lax.rem(here + shards - place, shards)] = part[...]


def columns(gathered, start, count):
    shards, _, width = gathered.shape
    piece = width // shards
    small = [gathered[shard, start : start + 16, :].astype(f32) for shard in range(shards)]
    joined = jnp.concatenate([part[:, :piece] for part in small], axis=1)
    return [
        flip(jnp.broadcast_to(joined[place : place + 1], (width, width)))[:, 0:1]
        for place in range(count)
    ]


def lane_fold(value):
    width = value.shape[0]
    total = value[:, :width]
    for start in range(width, value.shape[1], width):
        total = total + value[:, start : start + width]
    return total


def as_row(value):
    width = value.shape[0]
    return flip(jnp.broadcast_to(jnp.sum(value, axis=1, keepdims=True), (width, width)))


def scatter_blocks(stage, outs):
    shards = len(outs)
    here = lax.axis_index("fsdp")
    for place, out in enumerate(outs):
        out[...] = stage[lax.rem(here + place, shards)]


def whole(gathered, start, rows):
    shards = gathered.shape[0]
    return gathered[:, start : start + rows, :].reshape(shards * rows, gathered.shape[2])


def function_weight(presence, item, func, funcs, shape):
    total = presence[item, 0]
    for other in range(1, funcs):
        total = total + presence[item, other]
    own = jnp.full(shape, presence[item, func], jnp.int32).astype(f32)
    return own / jnp.full(shape, total, jnp.int32).astype(f32)


def pack_kernel(*refs):
    weights, vectors, gate = refs[:10], refs[10:14], refs[14]
    early, late = refs[15:]
    keys, values, query, out, query_two, key_two, value_two, out_two, enter, leave = weights
    start = 0
    for weight in (keys, values):
        early[start : start + weight.shape[0]] = weight[...]
        start += weight.shape[0]
    start = 0
    for weight in (query, out, query_two, key_two, value_two, out_two):
        late[start : start + weight.shape[0]] = weight[...]
        start += weight.shape[0]
    experts, piece, hidden = enter.shape
    width = late.shape[1]
    for expert in range(experts):
        for half in range(hidden // width):
            late[start : start + piece] = enter[expert, :, half * width : (half + 1) * width]
            start += piece
    for expert in range(experts):
        late[start : start + leave.shape[1]] = leave[expert]
        start += leave.shape[1]
    rest = jnp.zeros((1, width - piece), f32)
    rows = [
        jnp.concatenate([vector[...].astype(f32), rest], axis=1) for vector in vectors
    ]
    rows.append(jnp.zeros((4, width), f32))
    for row in range(2):
        rows.append(jnp.broadcast_to(gate[row : row + 1, 0:1].astype(f32), (1, width)))
    rows.append(jnp.zeros((6, width), f32))
    late[start : start + 16] = jnp.concatenate(rows, axis=0).astype(bf16)


def run_tasks(tasks):
    waiting = None
    for dots, work in tasks:
        found = dots()
        if waiting is not None:
            waiting[0](*waiting[1])
        waiting = (work, found)
    waiting[0](*waiting[1])


def mix(tasks, extra):
    mixed = []
    done = 0
    for place, task in enumerate(tasks, 1):
        mixed.append(task)
        due = len(extra) * place // len(tasks)
        mixed += extra[done:due]
        done = due
    return mixed


def behind(stage, total, chunks, groups):
    tasks = []
    for cols in chunks:
        tasks.append(stage(cols))
        tasks += [total(group) for group in groups if group.stop == cols.stop - 2 * CHUNK]
    return tasks


def add_to(ref, span):
    def work(value):
        ref[span] += value

    return work


def points_forward(counts, presence, points, *refs, funcs, shards):
    parts = refs[:shards]
    state_t, state, keys_out, values_out, gathered, weight = refs[shards:]
    item = pl.program_id(0)
    width = points.shape[2]
    slots = points.shape[1]
    piece = width // shards

    @pl.when(item == 0)
    def _():
        assemble(parts, gathered)
        weight[:width] = flip(whole(gathered, 0, piece))
        weight[width:] = flip(whole(gathered, piece, piece))

    chunks = [slice(start, start + CHUNK) for start in range(0, slots, CHUNK)]

    def project(func, cols):
        def dots():
            return (nt(weight[...], points[func, cols, :]),)

        def work(both):
            slot = cols.start + lax.broadcasted_iota(jnp.int32, (1, CHUNK), 1)
            probs = head_softmax(both[:width])
            keys = jnp.where(slot < counts[item, func], probs, 0.0)
            keys_out[func, :, cols] = keys.astype(bf16)
            values_out[func, :, cols] = both[width:].astype(bf16)

        return dots, work

    def summarize(func):
        values = values_out[func]
        extended = jnp.concatenate([values, jnp.ones((PAD, slots), bf16)], axis=0)
        share = function_weight(presence, item, func, funcs, (1, width))
        summed = nt(extended, keys_out[func])
        left = jnp.where(same_head(width), summed[:width], 0.0) * share
        return left, summed[width : width + 1]

    run_tasks([project(func, cols) for func in range(funcs) for cols in chunks])
    lefts, totals = zip(*(summarize(func) for func in range(funcs)))
    pack_states(lefts, totals, state_t.at[0], state.at[0], width)


def main_kernel(tokens, cotangent, coords, state_t, *refs, funcs, experts, shards, at):
    parts, outs, scratch = refs[:shards], refs[shards : 2 * shards + 14], refs[2 * shards + 14 :]
    (
        result,
        queries_out,
        cross_out,
        first_out,
        keys_out,
        values_out,
        grad_q_out,
        grad_second_out,
        grad_state_out,
        rest_weights,
        rest_vectors,
        normed_out,
        hat_out,
        scale_out,
    ) = outs[:14]
    grads_out = outs[14:]
    (
        params,
        grads_stage,
        first_keep,
        query_keep,
        state_sum,
        self_t,
        self_state,
        grad_state_sum,
        w_query,
        w_out_one,
        w_self,
        w_out_two_t,
        w_out_two,
        w_in_t,
        w_in,
        w_exit,
        w_exit_t,
        gain_one,
        bias_one,
        gain_two,
        bias_two,
        hidden_keep,
        inner_keep,
        normed_keep,
        grad_keep,
        own_keep,
        pair_keep,
        sum_in,
        sum_exit,
        sum_out_two,
        sum_gain,
        sum_bias,
        sum_gate,
    ) = scratch
    item = pl.program_id(0)
    phase = pl.program_id(1)
    step = pl.program_id(2)
    steps = pl.num_programs(2)
    width = tokens.shape[1]
    rows = tokens.shape[0]
    piece = width // shards
    hidden = w_in.shape[1] // experts
    exit_piece = hidden // shards

    @pl.when((item == 0) & (phase == 0) & (step == 0))
    def _():
        assemble(parts, params)
        w_query[...] = flip(whole(params, at["query_first"], piece))
        w_out_one[...] = flip(whole(params, at["out_first"], piece))
        w_self[:width] = flip(whole(params, at["query_second"], piece))
        w_self[width : 2 * width] = flip(whole(params, at["key_second"], piece))
        w_self[2 * width :] = flip(whole(params, at["value_second"], piece))
        out_two = whole(params, at["out_second"], piece)
        w_out_two[...] = out_two
        w_out_two_t[...] = flip(out_two)
        for block in range(experts * hidden // width):
            part = whole(params, at["expert_in"] + block * piece, piece)
            w_in[:, block * width : (block + 1) * width] = part
            w_in_t[block * width : (block + 1) * width] = flip(part)
        for expert in range(experts):
            part = whole(params, at["expert_out"] + expert * exit_piece, exit_piece)
            w_exit[expert * hidden : (expert + 1) * hidden] = part
            w_exit_t[:, expert * hidden : (expert + 1) * hidden] = flip(part)
        names = ("query_second", "key_second", "value_second", "out_first", "query_first")
        for place, name in enumerate(names):
            rest_weights[:, place * width : (place + 1) * width] = whole(params, at[name], piece)
        found = columns(params, at["small"], 4)
        rest_vectors[...] = jnp.broadcast_to(found[0], rest_vectors.shape)
        for vector, column in zip((gain_one, bias_one, gain_two, bias_two), found):
            vector[...] = jnp.broadcast_to(column, vector.shape)
        sum_in[...] = jnp.zeros_like(sum_in)
        sum_exit[...] = jnp.zeros_like(sum_exit)
        sum_out_two[...] = jnp.zeros_like(sum_out_two)
        sum_gain[...] = jnp.zeros_like(sum_gain)
        sum_bias[...] = jnp.zeros_like(sum_bias)
        sum_gate[...] = jnp.zeros_like(sum_gate)

    chunks = [slice(start, start + CHUNK) for start in range(0, rows, CHUNK)]
    groups = [slice(start, start + GROUP) for start in range(0, rows, GROUP)]
    every = slice(None)

    @pl.when((phase == 0) & (step == 0))
    def _():
        state_sum[...] = jnp.zeros_like(state_sum)
        grad_state_sum[...] = jnp.zeros_like(grad_state_sum)

    @pl.when(phase == 0)
    def _():
        def enter(cols):
            def dots():
                return (flip(tokens[cols, :]).astype(f32),)

            def work(rows_t):
                first_keep[step, :, cols] = rows_t
                hat, scale = standardize(rows_t)
                hat_out[:, cols] = hat.astype(bf16)
                scale_out[:, cols] = jnp.broadcast_to(scale, (8, CHUNK))
                normed_out[:, cols] = (hat * gain_one[...] + bias_one[...]).astype(bf16)

            return dots, work

        def ask(cols):
            def dots():
                return (nn(w_query[...], normed_out[:, cols]),)

            def work(value):
                queries_out[:, cols] = head_softmax(value).astype(bf16)

            return dots, work

        def across(cols):
            def dots():
                return (nn(state_t[0], queries_out[:, cols]),)

            def work(both):
                undo = inverse(both[funcs * width :])
                mixed = None
                for func in range(funcs):
                    part = by_head(
                        both[func * width : (func + 1) * width],
                        undo[func * HEADS : (func + 1) * HEADS],
                    )
                    mixed = part if mixed is None else mixed + part
                cross_out[:, cols] = mixed.astype(bf16)

            return dots, work

        def leave(cols):
            def dots():
                return (nn(w_out_one[...], cross_out[:, cols]),)

            def work(value):
                first = first_keep[step, :, cols] + value
                first_keep[step, :, cols] = first
                first_out[:, cols] = first.astype(bf16)

            return dots, work

        def project(cols):
            def dots():
                return (nn(w_self[...], first_out[:, cols]),)

            def work(three):
                query_keep[step, :, cols] = head_softmax(three[:width]).astype(bf16)
                keys_out[:, cols] = head_softmax(three[width : 2 * width]).astype(bf16)
                values = three[2 * width :].astype(bf16)
                values_out[:, cols] = values
                pair_keep[:width, cols] = values
                pair_keep[width:, cols] = jnp.ones((PAD, CHUNK), bf16)

            return dots, work

        def sum_state(cols):
            return (
                lambda: (nt(pair_keep[:, cols], keys_out[:, cols]),),
                add_to(state_sum, every),
            )

        tasks = [stage(cols) for stage in (enter, ask, across, leave) for cols in chunks]
        run_tasks(tasks + behind(project, sum_state, chunks, groups[:-1]))
        run_tasks([sum_state(groups[-1])])

        @pl.when(step == steps - 1)
        def _():
            left = jnp.where(same_head(width), state_sum[:width], 0.0)
            pack_states([left], [state_sum[width : width + 1]], self_t, self_state, width)

    @pl.when(phase == 1)
    def _():
        undo_of, norm_of, gates_of = {}, {}, {}
        grad_gates_of = {chunk.start: [] for chunk in chunks}

        def attend(cols):
            def dots():
                return (nn(self_t[...], query_keep[step, :, cols]),)

            def work(both):
                undo = inverse(both[width : width + HEADS])
                undo_of[cols.start] = undo
                own_keep[:, cols] = by_head(both[:width], undo).astype(bf16)
                grad_keep[:, cols] = flip(cotangent[cols, :])

            return dots, work

        def gate(cols):
            across, down = coords[0:1, cols], coords[1:2, cols]
            logits = []
            for expert in range(experts):
                pair = params[expert, at["small"] : at["small"] + 16, 0:1].astype(f32)
                logits.append(across * pair[8:9] + down * pair[9:10])
            peak = logits[0]
            for logit in logits[1:]:
                peak = jnp.maximum(peak, logit)
            raised = [jnp.exp(logit - peak) for logit in logits]
            total = raised[0]
            for other in raised[1:]:
                total = total + other
            return [other / total for other in raised]

        def norm(cols):
            def dots():
                return (nn(w_out_two_t[...], own_keep[:, cols]),)

            def work(value):
                second = first_keep[step, :, cols] + value
                first_keep[step, :, cols] = second
                hat, scale = standardize(second)
                norm_of[cols.start] = (hat, scale)
                normed_keep[:, cols] = (hat * gain_two[...] + bias_two[...]).astype(bf16)
                gates_of[cols.start] = gate(cols)

            return dots, work

        def ring(cols):
            start = cols.start % (2 * GROUP)
            return slice(start, start + cols.stop - cols.start)

        def expand(cols, first):
            expert = first // hidden
            strip = slice(first, first + STRIP)

            def dots():
                return (
                    nn(w_in_t[strip], normed_keep[:, cols]).astype(bf16),
                    nn(w_exit[strip], grad_keep[:, cols]).astype(bf16),
                )

            def work(inners, backs):
                share = (0.5 * gates_of[cols.start][expert]).astype(bf16)
                partial_sum = None
                for start in range(0, STRIP, SLAB):
                    inner, back = inners[start : start + SLAB], backs[start : start + SLAB]
                    span = slice(first + start, first + start + SLAB)
                    square = inner * inner
                    tanh = jnp.tanh(inner * (0.7978845608028654 + 0.035677408136300125 * square))
                    above = 1.0 + tanh
                    active = inner * above
                    product = active * back
                    folded = product[:16]
                    for row in range(16, SLAB, 16):
                        folded = folded + product[row : row + 16]
                    folded = folded.astype(f32)
                    partial_sum = folded if partial_sum is None else partial_sum + folded
                    hidden_keep[span, ring(cols)] = active * share
                    slope = above + active * (1.0 - tanh) * (
                        0.7978845608028654 + 0.10703222440890037 * square
                    )
                    inner_keep[span, ring(cols)] = slope * (back * share)
                found = jnp.sum(0.5 * partial_sum, axis=0, keepdims=True)
                if first % hidden:
                    grad_gates_of[cols.start][expert] += found
                else:
                    grad_gates_of[cols.start].append(found)

            return dots, work

        def contract(cols):
            def dots():
                return (
                    nn(w_exit_t[...], hidden_keep[:, ring(cols)]),
                    nn(w_in[...], inner_keep[:, ring(cols)]),
                )

            def work(mixed, grad_normed):
                result[cols, :] = flip((first_keep[step, :, cols] + mixed).astype(bf16))
                hat, scale = norm_of[cols.start]
                sum_gain[...] += lane_fold(grad_normed * hat)
                sum_bias[...] += lane_fold(grad_normed)
                grad_second = grad_keep[:, cols].astype(f32) + norm_back(
                    grad_normed * gain_two[...], hat, scale
                )
                grad_second_out[:, cols] = grad_second.astype(bf16)
                gates, grad_gates = gates_of[cols.start], grad_gates_of[cols.start]
                across, down = coords[0:1, cols], coords[1:2, cols]
                mean_gate = gates[0] * grad_gates[0]
                for expert in range(1, experts):
                    mean_gate = mean_gate + gates[expert] * grad_gates[expert]
                for expert in range(experts):
                    change = gates[expert] * (grad_gates[expert] - mean_gate)
                    sum_gate[expert : expert + 1, cols] += across * change
                    sum_gate[experts + expert : experts + expert + 1, cols] += down * change

            return dots, work

        def attend_back(cols):
            def dots():
                return (nn(w_out_two[...], grad_second_out[:, cols]),)

            def work(value):
                share = by_head(value, undo_of[cols.start])
                pair_keep[:width, cols] = share.astype(bf16)
                sums = head_sums(share * own_keep[:, cols].astype(f32))
                pair_keep[width:, cols] = jnp.concatenate(
                    [sums, jnp.zeros((PAD - HEADS, CHUNK), f32)], axis=0
                ).astype(bf16)

            return dots, work

        def query_back(cols):
            def dots():
                return (nn(self_state[:, : width + PAD], pair_keep[:, cols]),)

            def work(grad_q):
                queries = query_keep[step, :, cols]
                grad_q_out[:, cols] = softmax_back(queries, grad_q).astype(bf16)

            return dots, work

        def sum_hidden(cols, expert):
            span = slice(expert * hidden, (expert + 1) * hidden)
            return (
                lambda: (nn(hidden_keep[span, ring(cols)], cotangent[cols, :]),),
                add_to(sum_exit, span),
            )

        def sum_inner(cols, expert):
            span = slice(expert * hidden, (expert + 1) * hidden)
            return (
                lambda: (nt(inner_keep[span, ring(cols)], normed_keep[:, cols]),),
                add_to(sum_in, span),
            )

        def sum_own(cols):
            return (
                lambda: (nt(own_keep[:, cols], grad_second_out[:, cols]),),
                add_to(sum_out_two, every),
            )

        def sum_pair(cols):
            return (
                lambda: (nt(pair_keep[:, cols], query_keep[step, :, cols]),),
                add_to(grad_state_sum, every),
            )

        tasks = [stage(cols) for stage in (attend, norm) for cols in chunks]
        sums, contracts = [], []
        for group in groups:
            inside = [cols for cols in chunks if group.start <= cols.start < group.stop]
            expands = [
                expand(cols, first) for cols in inside for first in range(0, experts * hidden, STRIP)
            ]
            tasks += mix(expands, mix(sums, contracts) if sums else [])
            contracts = [contract(cols) for cols in inside]
            sums = [
                total(group, expert) for expert in range(experts) for total in (sum_hidden, sum_inner)
            ]
        tasks += mix(contracts + [attend_back(cols) for cols in chunks], sums)
        last = [total(group) for group in groups for total in (sum_own, sum_pair)]
        tasks += mix([query_back(cols) for cols in chunks], last)
        run_tasks(tasks)

        @pl.when(step == steps - 1)
        def _():
            grad_state_out[0] = grad_state_sum[...]

    @pl.when((item == pl.num_programs(0) - 1) & (phase == 1) & (step == steps - 1))
    def _():
        gain, bias = as_row(sum_gain[...]), as_row(sum_bias[...])
        gate = jnp.broadcast_to(jnp.sum(sum_gate[...], axis=1, keepdims=True), (8, width))
        row = lax.broadcasted_iota(jnp.int32, (8, width), 0)
        vectors = jnp.where(row == 0, gain[:8], bias[:8])
        small = jnp.concatenate([vectors, gate], axis=0).astype(bf16)
        start = 0
        for block in range(experts * hidden // width):
            part = flip(sum_in[block * width : (block + 1) * width]).astype(bf16)
            grads_stage[:, start : start + piece, :] = part.reshape(shards, piece, width)
            start += piece
        for expert in range(experts):
            part = sum_exit[expert * hidden : (expert + 1) * hidden].astype(bf16)
            grads_stage[:, start : start + exit_piece, :] = part.reshape(shards, exit_piece, width)
            start += exit_piece
        part = sum_out_two[...].astype(bf16)
        grads_stage[:, start : start + piece, :] = part.reshape(shards, piece, width)
        start += piece
        for shard in range(shards):
            grads_stage[shard, start : start + 16, :] = small
        scatter_blocks(grads_stage, grads_out)


def rest_kernel(
    presence,
    hat_in,
    scale_in,
    normed_in,
    queries_in,
    cross_in,
    first_in,
    keys_in,
    values_in,
    grad_q_in,
    grad_second_in,
    grad_state_in,
    state_t,
    state,
    weights,
    gain_one,
    *refs,
    funcs,
    item,
    first_call,
):
    if not first_call:
        carry, refs = refs[3], refs[5:]
    (
        grad_tokens,
        grad_cross_state_out,
        grad_totals_out,
        sums_out,
        grad_self_state,
        grad_totals,
        grad_state_sum,
        sums,
        three_keep,
        cross_keep,
        stack_keep,
        query_keep,
    ) = refs
    step = pl.program_id(0)
    steps = pl.num_programs(0)
    width = hat_in.shape[0]
    self_part = slice(0, 3 * width)
    out_part = slice(3 * width, 4 * width)
    query_part = slice(4 * width, 5 * width)
    gain_part = slice(5 * width, 6 * width)
    bias_part = slice(6 * width, 7 * width)

    @pl.when(step == 0)
    def _():
        sums[...] = jnp.zeros_like(sums) if first_call else carry[...]
        left = jnp.where(same_head(width), grad_state_in[0, :width], 0.0)
        grad_self_state[0] = flip(left).astype(bf16)
        grad_self_state[1] = left.astype(bf16)
        column = totals_column(grad_state_in[0, width : width + HEADS], width)
        grad_totals[...] = jnp.broadcast_to(column[:, 0:1], grad_totals.shape)

    chunks = [slice(start, start + CHUNK) for start in range(0, hat_in.shape[1], CHUNK)]
    grad_first_of = {}

    def self_back(cols):
        def dots():
            return (
                nn(grad_self_state[0], values_in[:, cols]),
                nn(grad_self_state[1], keys_in[:, cols]),
            )

        def work(grad_keys, grad_values):
            grad_keys = softmax_back(keys_in[:, cols], grad_keys + grad_totals[...])
            three_keep[:width, cols] = grad_q_in[:, cols]
            three_keep[width : 2 * width, cols] = grad_keys.astype(bf16)
            three_keep[2 * width :, cols] = grad_values.astype(bf16)

        return dots, work

    def join(cols):
        def dots():
            return (nn(weights[:, self_part], three_keep[:, cols]),)

        def work(value):
            grad_first = grad_second_in[:, cols].astype(f32) + value
            grad_first_of[cols.start] = grad_first
            cross_keep[:, cols] = grad_first.astype(bf16)

        return dots, work

    def cross_back(cols):
        def dots():
            return nn(weights[:, out_part], cross_keep[:, cols]), nn(state_t[0], queries_in[:, cols])

        def work(share, both):
            undo = inverse(both[funcs * width :])
            sums_by_head = []
            for func in range(funcs):
                span = slice(func * width, (func + 1) * width)
                scales = undo[func * HEADS : (func + 1) * HEADS]
                part = by_head(share, scales)
                stack_keep[span, cols] = part.astype(bf16)
                sums_by_head.append(head_sums(part * by_head(both[span], scales)))
            spare = stack_keep.shape[0] - funcs * (width + HEADS)
            if spare:
                sums_by_head.append(jnp.zeros((spare, CHUNK), f32))
            stack_keep[funcs * width :, cols] = jnp.concatenate(sums_by_head, axis=0).astype(bf16)

        return dots, work

    def query_back(cols):
        def dots():
            return (nn(state[0, :, : stack_keep.shape[0]], stack_keep[:, cols]),)

        def work(grad_q):
            query_keep[:, cols] = softmax_back(queries_in[:, cols], grad_q).astype(bf16)

        return dots, work

    def finish(cols):
        def dots():
            return (nn(weights[:, query_part], query_keep[:, cols]),)

        def work(grad_normed):
            hat, scale = hat_in[:, cols].astype(f32), scale_in[0:1, cols]
            sums[gain_part] += lane_fold(grad_normed * hat)
            sums[bias_part] += lane_fold(grad_normed)
            grad_rows = grad_first_of[cols.start] + norm_back(
                grad_normed * gain_one[...], hat, scale
            )
            grad_tokens[cols, :] = flip(grad_rows)

        return dots, work

    @pl.when(step == 0)
    def _():
        grad_state_sum[...] = jnp.zeros_like(grad_state_sum)

    every = slice(None)
    sum_self = (lambda: (nt(three_keep[...], first_in[...]),), add_to(sums, self_part))
    sum_out = (lambda: (nt(cross_in[...], cross_keep[...]),), add_to(sums, out_part))
    sum_state = (lambda: (nt(stack_keep[...], queries_in[...]),), add_to(grad_state_sum, every))
    sum_query = (lambda: (nt(normed_in[...], query_keep[...]),), add_to(sums, query_part))
    tasks = [stage(cols) for stage in (self_back, join) for cols in chunks]
    tasks += mix([cross_back(cols) for cols in chunks], [sum_self])
    tasks += mix([query_back(cols) for cols in chunks], [sum_out])
    tasks += mix([finish(cols) for cols in chunks], [sum_state])
    run_tasks(tasks + [sum_query])

    @pl.when(step == steps - 1)
    def _():
        mask = same_head(width)
        for func in range(funcs):
            weight = function_weight(presence, item, func, funcs, (1, width))
            left = jnp.where(mask, grad_state_sum[func * width : (func + 1) * width], 0.0)
            grad_cross_state_out[func] = (left * weight).astype(bf16)
            start = funcs * width + func * HEADS
            grad_totals_out[func] = totals_column(grad_state_sum[start : start + HEADS], width)
        sums_out[...] = sums[...]


def points_back(points, keys_in, values_in, grad_state, grad_totals, carry, _after, *refs, shards):
    outs = refs[:shards]
    sums, stage, grads = refs[shards:]
    step = pl.program_id(0)
    width = points.shape[2]
    piece = width // shards

    funcs, slots, _ = points.shape
    chunks = [slice(start, start + CHUNK) for start in range(0, slots, CHUNK)]
    turned = [flip(grad_state[func]) for func in range(funcs)]

    def back(func, cols):
        def dots():
            return (
                nn(turned[func], values_in[func, :, cols]),
                nn(grad_state[func], keys_in[func, :, cols]),
            )

        def work(grad_keys, grad_values):
            grad_keys = grad_keys + grad_totals[func, :, 0:1]
            grad_k = softmax_back(keys_in[func, :, cols], grad_keys)
            grads[func, :width, cols] = grad_k.astype(bf16)
            grads[func, width:, cols] = grad_values.astype(bf16)

        return dots, work

    run_tasks([back(func, cols) for func in range(funcs) for cols in chunks])
    found = nn(grads[0], points[0])
    for func in range(1, funcs):
        found = found + nn(grads[func], points[func])

    @pl.when(step == 0)
    def _():
        sums[...] = found
        gain = as_row(carry[5 * width : 6 * width])
        bias = as_row(carry[6 * width : 7 * width])
        row = lax.broadcasted_iota(jnp.int32, (16, width), 0)
        small = jnp.where(row == 0, gain[:16], bias[:16]).astype(bf16)
        for place in range(5):
            part = carry[place * width : (place + 1) * width]
            part = (flip(part) if place < 3 else part).astype(bf16)
            stage[:, place * piece : (place + 1) * piece, :] = part.reshape(shards, piece, width)
        for shard in range(shards):
            stage[shard, 5 * piece : 5 * piece + 16, :] = small

    @pl.when(step > 0)
    def _():
        sums[...] += found

    @pl.when(step == pl.num_programs(0) - 1)
    def _():
        for place in range(2):
            start = 5 * piece + 16 + place * piece
            part = flip(sums[place * width : (place + 1) * width]).astype(bf16)
            stage[:, start : start + piece, :] = part.reshape(shards, piece, width)
        scatter_blocks(stage, outs)


def total_of(parts):
    value = parts[0][...].astype(f32)
    for part in parts[1:]:
        value = value + part[...].astype(f32)
    return value


def unpack_kernel(*refs, counts, experts, piece, exit_piece, hidden):
    main_parts, parts = refs[: counts[0]], refs[counts[0] : sum(counts)]
    outs, (small, main, rest) = refs[-18:-3], refs[-3:]
    width = main.shape[1]
    main[...] = total_of(main_parts)
    rest[...] = total_of(parts)
    (
        gain_one,
        bias_one,
        query_one,
        key_one,
        value_one,
        out_one,
        query_two,
        key_two,
        value_two,
        out_two,
        gain_two,
        bias_two,
        enter,
        leave,
        gate,
    ) = outs
    start = 0
    for expert in range(experts):
        for half in range(hidden // width):
            block = main[start : start + piece]
            enter[expert, :, half * width : (half + 1) * width] = block
            start += piece
    for expert in range(experts):
        leave[expert] = main[start : start + exit_piece]
        start += exit_piece
    out_two[...] = main[start : start + piece]
    start += piece
    small[:16] = main[start : start + 16]
    start = 0
    for out in (query_two, key_two, value_two, out_one, query_one):
        out[...] = rest[start : start + piece]
        start += piece
    small[16:] = rest[start : start + 16]
    start += 16
    for out in (key_one, value_one):
        out[...] = rest[start : start + piece]
        start += piece
    shard = lax.axis_index("fsdp")
    turned = pltpu.roll(small[...], lax.rem(width - shard * piece, width), 1)
    gain_two[...] = turned[0:1, :piece]
    bias_two[...] = turned[1:2, :piece]
    gain_one[...] = turned[16:17, :piece]
    bias_one[...] = turned[17:18, :piece]
    for row in range(2):
        gate[:, row : row + 1] = small[pl.ds(8 + row * experts + shard, 1), 0:1]


def whole_spec(shape):
    return pl.BlockSpec(shape, lambda *_: (0,) * len(shape))


def route(size, shift, digit, stride):
    def target(i):
        own = i // stride % digit
        return i + ((own + shift) % digit - own) * stride

    return [(i, target(i)) for i in range(size)]


def spread(value, axis, size, digit, stride):
    return [value] + [
        lax.ppermute(value, axis, route(size, shift, digit, stride)) for shift in range(1, digit)
    ]


def exchange(values, axis, size, stride):
    digit = len(values)
    return [values[0]] + [
        lax.ppermute(values[shift], axis, route(size, shift, digit, stride))
        for shift in range(1, digit)
    ]


def digits(size):
    found = []
    stride = 1
    while stride < size:
        rest = size // stride
        digit = 2 if stride == 1 and rest % 2 == 0 else 4 if rest % 4 == 0 else rest
        found.append((digit, stride))
        stride *= digit
    return found or [(1, 1)]


def sum_parts(parts):
    return total_of([part.astype(f32) for part in parts]).astype(bf16)


def shards_fn(
    dp,
    shards,
    tokens,
    points,
    coords,
    presence,
    counts,
    cotangent,
    gain_first,
    bias_first,
    query_first,
    key_first,
    value_first,
    out_first,
    query_second,
    key_second,
    value_second,
    out_second,
    gain_second,
    bias_second,
    expert_in,
    expert_out,
    gate_weight,
):
    count, width = tokens.shape
    items, funcs, slots, _ = points.shape
    length = count // items
    experts, piece, hidden = expert_in.shape
    exit_piece = expert_out.shape[1]
    tile, rest_tile = min(MAIN_TILE, length), min(REST_TILE, length)
    steps, rest_steps = length // tile, length // rest_tile
    inner = experts * hidden
    enter_rows = experts * piece * (hidden // width)
    limit = pltpu.CompilerParams(vmem_limit_bytes=VMEM)

    at = {}
    place = 0
    for name, size in (
        ("query_first", piece),
        ("out_first", piece),
        ("query_second", piece),
        ("key_second", piece),
        ("value_second", piece),
        ("out_second", piece),
        ("expert_in", enter_rows),
        ("expert_out", experts * exit_piece),
        ("small", 16),
    ):
        at[name] = place
        place += size
    late_rows_count = place
    early_pack, late_pack = pl.pallas_call(
        pack_kernel,
        out_shape=[
            jax.ShapeDtypeStruct((2 * piece, width), bf16),
            jax.ShapeDtypeStruct((late_rows_count, width), bf16),
        ],
        name="pack",
    )(
        key_first,
        value_first,
        query_first,
        out_first,
        query_second,
        key_second,
        value_second,
        out_second,
        expert_in,
        expert_out,
        *(
            vector.reshape(1, piece)
            for vector in (gain_first, bias_first, gain_second, bias_second)
        ),
        gate_weight,
    )
    early_parts = spread(early_pack, "fsdp", shards, shards, 1)
    late_parts = spread(late_pack, "fsdp", shards, shards, 1)
    late_specs = [whole_spec((late_rows_count, width))] * shards
    gathered = pltpu.VMEM((shards, late_rows_count, width), bf16)

    smem = pl.BlockSpec(memory_space=pltpu.SMEM)
    units = items * funcs
    state_rows = funcs * width + -(-funcs * HEADS // PAD) * PAD
    flat_points = points.reshape(units, slots, width)
    state_t, state, keys_one, values_one = pl.pallas_call(
        partial(points_forward, funcs=funcs, shards=shards),
        grid=(items,),
        in_specs=[smem, smem, pl.BlockSpec((funcs, slots, width), lambda u: (u, 0, 0))]
        + [whole_spec((2 * piece, width))] * shards,
        out_specs=[
            pl.BlockSpec((1, state_rows, width), lambda u: (u, 0, 0)),
            pl.BlockSpec((1, width, (funcs + 1) * width), lambda u: (u, 0, 0)),
            pl.BlockSpec((funcs, width, slots), lambda u: (u, 0, 0)),
            pl.BlockSpec((funcs, width, slots), lambda u: (u, 0, 0)),
        ],
        out_shape=[
            jax.ShapeDtypeStruct((items, state_rows, width), bf16),
            jax.ShapeDtypeStruct((items, width, (funcs + 1) * width), bf16),
            jax.ShapeDtypeStruct((units, width, slots), bf16),
            jax.ShapeDtypeStruct((units, width, slots), bf16),
        ],
        scratch_shapes=[
            pltpu.VMEM((shards, 2 * piece, width), bf16),
            pltpu.VMEM((2 * width, width), bf16),
        ],
        compiler_params=limit,
        cost_estimate=cost(8),
        name="points_forward",
    )(counts, presence, flat_points, *early_parts)

    kept = jax.ShapeDtypeStruct((width, count), bf16)
    main_rows = enter_rows + experts * exit_piece + piece + 16

    def early(i, p, j):
        return i * steps + jnp.where(p == 0, j, steps - 1)

    def late(i, p, j):
        return i * steps + jnp.where(p == 0, 0, j)

    early_keep = pl.BlockSpec((width, tile), lambda i, p, j: (0, early(i, p, j)))
    late_keep = pl.BlockSpec((width, tile), lambda i, p, j: (0, late(i, p, j)))
    late_rows = pl.BlockSpec((tile, width), lambda i, p, j: (late(i, p, j), 0))
    (
        result,
        queries_one,
        cross,
        first,
        keys_two,
        values_two,
        grad_q_two,
        grad_second,
        grad_state_two,
        rest_weights,
        rest_vectors,
        normed_one,
        hat_one,
        scale_one,
        *main_grads,
    ) = pl.pallas_call(
        partial(main_kernel, funcs=funcs, experts=experts, shards=shards, at=at),
        grid=(items, 2, steps),
        in_specs=[
            pl.BlockSpec((tile, width), lambda i, p, j: (early(i, p, j), 0)),
            late_rows,
            pl.BlockSpec((2, tile), lambda i, p, j: (0, late(i, p, j))),
            pl.BlockSpec((1, state_rows, width), lambda i, p, j: (i, 0, 0)),
        ]
        + late_specs,
        out_specs=[
            late_rows,
            early_keep,
            early_keep,
            early_keep,
            early_keep,
            early_keep,
            late_keep,
            late_keep,
            pl.BlockSpec((1, width + PAD, width), lambda i, p, j: (i, 0, 0)),
            whole_spec((width, 5 * width)),
            whole_spec((width, CHUNK)),
            early_keep,
            early_keep,
            pl.BlockSpec((8, tile), lambda i, p, j: (0, early(i, p, j))),
        ]
        + [whole_spec((main_rows, width))] * shards,
        out_shape=[
            jax.ShapeDtypeStruct((count, width), bf16),
            kept,
            kept,
            kept,
            kept,
            kept,
            kept,
            kept,
            jax.ShapeDtypeStruct((items, width + PAD, width), f32),
            jax.ShapeDtypeStruct((width, 5 * width), bf16),
            jax.ShapeDtypeStruct((width, CHUNK), f32),
            kept,
            kept,
            jax.ShapeDtypeStruct((8, count), f32),
        ]
        + [jax.ShapeDtypeStruct((main_rows, width), bf16)] * shards,
        scratch_shapes=[
            gathered,
            pltpu.VMEM((shards, main_rows, width), bf16),
            pltpu.VMEM((steps, width, tile), f32),
            pltpu.VMEM((steps, width, tile), bf16),
            pltpu.VMEM((width + PAD, width), f32),
            pltpu.VMEM((width + PAD, width), bf16),
            pltpu.VMEM((width, 2 * width), bf16),
            pltpu.VMEM((width + PAD, width), f32),
            pltpu.VMEM((width, width), bf16),
            pltpu.VMEM((width, width), bf16),
            pltpu.VMEM((3 * width, width), bf16),
            pltpu.VMEM((width, width), bf16),
            pltpu.VMEM((width, width), bf16),
            pltpu.VMEM((inner, width), bf16),
            pltpu.VMEM((width, inner), bf16),
            pltpu.VMEM((inner, width), bf16),
            pltpu.VMEM((width, inner), bf16),
            pltpu.VMEM((width, CHUNK), f32),
            pltpu.VMEM((width, CHUNK), f32),
            pltpu.VMEM((width, CHUNK), f32),
            pltpu.VMEM((width, CHUNK), f32),
            pltpu.VMEM((inner, min(2 * GROUP, tile)), bf16),
            pltpu.VMEM((inner, min(2 * GROUP, tile)), bf16),
            pltpu.VMEM((width, tile), bf16),
            pltpu.VMEM((width, tile), bf16),
            pltpu.VMEM((width, tile), bf16),
            pltpu.VMEM((width + PAD, tile), bf16),
            pltpu.VMEM((inner, width), f32),
            pltpu.VMEM((inner, width), f32),
            pltpu.VMEM((width, width), f32),
            pltpu.VMEM((width, width), f32),
            pltpu.VMEM((width, width), f32),
            pltpu.VMEM((2 * experts, tile), f32),
        ],
        compiler_params=limit,
        cost_estimate=cost(80),
        name="main",
    )(tokens, cotangent, coords, state_t, *late_parts)

    rest_rows = 7 * piece + 16

    def rest_call(item, earlier, after):
        first_call = item == 0
        keep_spec = pl.BlockSpec((width, rest_tile), lambda j: (0, item * rest_steps + j))
        row_spec = pl.BlockSpec((rest_tile, width), lambda j: (item * rest_steps + j, 0))
        unit_spec = pl.BlockSpec((funcs, width, width), lambda j: (item, 0, 0))
        anywhere = pl.BlockSpec(memory_space=pl.ANY)
        in_specs = [
            smem,
            keep_spec,
            pl.BlockSpec((8, rest_tile), lambda j: (0, item * rest_steps + j)),
            keep_spec,
            keep_spec,
            keep_spec,
            keep_spec,
            keep_spec,
            keep_spec,
            keep_spec,
            keep_spec,
            pl.BlockSpec((1, width + PAD, width), lambda j: (item, 0, 0)),
            pl.BlockSpec((1, state_rows, width), lambda j: (item, 0, 0)),
            pl.BlockSpec((1, width, (funcs + 1) * width), lambda j: (item, 0, 0)),
            whole_spec((width, 5 * width)),
            whole_spec((width, CHUNK)),
        ]
        operands = [
            presence,
            hat_one,
            scale_one,
            normed_one,
            queries_one,
            cross,
            first,
            keys_two,
            values_two,
            grad_q_two,
            grad_second,
            grad_state_two,
            state_t,
            state,
            rest_weights,
            rest_vectors,
        ]
        aliases = {}
        if not first_call:
            aliases = {len(operands) + k: k for k in range(3)}
            in_specs += [anywhere] * 3 + [whole_spec((7 * width, width)), anywhere]
            operands += [*earlier, after]
        out_specs = [row_spec, unit_spec, unit_spec, whole_spec((7 * width, width))]
        out_shape = [
            jax.ShapeDtypeStruct((count, width), f32),
            jax.ShapeDtypeStruct((units, width, width), bf16),
            jax.ShapeDtypeStruct((units, width, width), f32),
            jax.ShapeDtypeStruct((7 * width, width), f32),
        ]
        return pl.pallas_call(
            partial(
                rest_kernel,
                funcs=funcs,
                item=item,
                first_call=first_call,
            ),
            grid=(rest_steps,),
            in_specs=in_specs,
            out_specs=out_specs,
            out_shape=out_shape,
            input_output_aliases=aliases,
            scratch_shapes=[
                pltpu.VMEM((2, width, width), bf16),
                pltpu.VMEM((width, CHUNK), f32),
                pltpu.VMEM((state_rows, width), f32),
                pltpu.VMEM((7 * width, width), f32),
                pltpu.VMEM((3 * width, rest_tile), bf16),
                pltpu.VMEM((width, rest_tile), bf16),
                pltpu.VMEM((state_rows, rest_tile), bf16),
                pltpu.VMEM((width, rest_tile), bf16),
            ],
            compiler_params=limit,
            cost_estimate=cost(18),
            name="rest",
        )(*operands)

    levels = digits(dp)
    main_levels = levels[::-1]
    main_parts = exchange(main_grads, "fsdp", shards, 1)
    level = 0
    found = None
    for item in range(items):
        found = rest_call(item, found, main_sum if item else None)
        if item < len(main_levels):
            main_sum = sum_parts(main_parts)
            main_parts = spread(main_sum, "dp", dp, *main_levels[item])
            level = item + 1
    grad_tokens, grad_state_one, grad_totals_one, carry = found

    rest_grads = pl.pallas_call(
        partial(points_back, shards=shards),
        grid=(items,),
        in_specs=[
            pl.BlockSpec((funcs, slots, width), lambda u: (u, 0, 0)),
            pl.BlockSpec((funcs, width, slots), lambda u: (u, 0, 0)),
            pl.BlockSpec((funcs, width, slots), lambda u: (u, 0, 0)),
            pl.BlockSpec((funcs, width, width), lambda u: (u, 0, 0)),
            pl.BlockSpec((funcs, width, width), lambda u: (u, 0, 0)),
            whole_spec((7 * width, width)),
            pl.BlockSpec(memory_space=pl.ANY),
        ],
        out_specs=[whole_spec((rest_rows, width))] * shards,
        out_shape=[jax.ShapeDtypeStruct((rest_rows, width), bf16)] * shards,
        scratch_shapes=[
            pltpu.VMEM((2 * width, width), f32),
            pltpu.VMEM((shards, rest_rows, width), bf16),
            pltpu.VMEM((funcs, 2 * width, slots), bf16),
        ],
        compiler_params=limit,
        cost_estimate=cost(7),
        name="points_back",
    )(flat_points, keys_one, values_one, grad_state_one, grad_totals_one, carry, main_sum)
    rest_got = exchange(rest_grads, "fsdp", shards, 1)

    parts = rest_got
    for digit, stride in main_levels[level:]:
        main_parts = spread(sum_parts(main_parts), "dp", dp, digit, stride)
    for digit, stride in levels:
        parts = spread(sum_parts(parts), "dp", dp, digit, stride)

    matrix = jax.ShapeDtypeStruct((piece, width), f32)
    vector = jax.ShapeDtypeStruct((1, piece), f32)
    outs = pl.pallas_call(
        partial(
            unpack_kernel,
            counts=(len(main_parts), len(parts)),
            experts=experts,
            piece=piece,
            exit_piece=exit_piece,
            hidden=hidden,
        ),
        out_shape=[vector] * 2
        + [matrix] * 8
        + [vector] * 2
        + [
            jax.ShapeDtypeStruct(expert_in.shape, f32),
            jax.ShapeDtypeStruct(expert_out.shape, f32),
            jax.ShapeDtypeStruct((1, 2), f32),
        ],
        scratch_shapes=[
            pltpu.VMEM((32, width), f32),
            pltpu.VMEM((main_rows, width), f32),
            pltpu.VMEM((rest_rows, width), f32),
        ],
        name="unpack",
    )(*main_parts, *parts)
    outs = [out.reshape(piece) if out.shape == (1, piece) else out for out in outs]
    return (result, grad_tokens, *outs[:-1], outs[-1].reshape(gate_weight.shape))


def solution(mesh):
    rows = P(("dp", "fsdp"), None)
    matrix = P("fsdp", None)
    vector = P("fsdp")
    expert = P(None, "fsdp", None)
    parameters = (
        (vector, vector)
        + (matrix,) * 8
        + (vector, vector, expert, expert, P(None, "fsdp"))
    )
    return jax.shard_map(
        partial(shards_fn, mesh.shape["dp"], mesh.shape["fsdp"]),
        mesh=mesh,
        in_specs=(
            rows,
            P(("dp", "fsdp"), None, None, None),
            P(None, ("dp", "fsdp")),
            rows,
            rows,
            rows,
        )
        + parameters,
        out_specs=(rows, rows) + parameters,
        check_vma=False,
    )
```

```python
from functools import partial

import jax
import jax.numpy as jnp
from jax import lax
from jax.experimental import pallas as pl
from jax.experimental.pallas import tpu as pltpu
from jax.sharding import PartitionSpec as P


HEADS = 8
eps = 1e-05
f32 = jnp.float32
bf16 = jnp.bfloat16
MAIN_TILE = 4096
REST_TILE = 1024
GROUP = 1024
STRIP = 256
CHUNK = 256
SLAB = 64
PAD = 16
VMEM = 60 * 1024 * 1024


def cost(microseconds):
    return pl.CostEstimate(flops=microseconds * 10**9, bytes_accessed=10**6, transcendentals=0)


def nn(left, right):
    return jnp.dot(left, right, preferred_element_type=f32)


def nt(left, right):
    return lax.dot_general(left, right, (((1,), (1,)), ((), ())), preferred_element_type=f32)


def flip(value):
    return value.T


def inverse(value):
    return pl.reciprocal(value, approx=True)


def head_softmax(value):
    width, rows = value.shape
    split = value.reshape(HEADS, width // HEADS, rows)
    raised = jnp.exp(split - jnp.max(split, axis=1, keepdims=True))
    return (raised * inverse(jnp.sum(raised, axis=1, keepdims=True))).reshape(width, rows)


def softmax_back(probs, grad):
    width, rows = grad.shape
    probs = probs.astype(f32).reshape(HEADS, width // HEADS, rows)
    grad = grad.reshape(HEADS, width // HEADS, rows)
    inner = jnp.sum(probs * grad, axis=1, keepdims=True)
    return (probs * (grad - inner)).reshape(width, rows)


def standardize(value):
    centre = value - jnp.mean(value, axis=0, keepdims=True)
    scale = lax.rsqrt(jnp.mean(centre * centre, axis=0, keepdims=True) + eps)
    return centre * scale, scale


def norm_back(grad, hat, scale):
    return scale * (
        grad
        - jnp.mean(grad, axis=0, keepdims=True)
        - hat * jnp.mean(grad * hat, axis=0, keepdims=True)
    )


def same_head(width):
    shape, head = (width, width), width // HEADS
    row = lax.broadcasted_iota(jnp.int32, shape, 0)
    column = lax.broadcasted_iota(jnp.int32, shape, 1)
    return lax.div(row, head) == lax.div(column, head)


def own_head(width):
    shape, head = (HEADS, width), width // HEADS
    row = lax.broadcasted_iota(jnp.int32, shape, 0)
    return row == lax.div(lax.broadcasted_iota(jnp.int32, shape, 1), head)


def by_head(value, scales):
    width, rows = value.shape
    split = value.reshape(HEADS, width // HEADS, rows)
    return (split * scales.reshape(HEADS, 1, rows)).reshape(width, rows)


def head_sums(value):
    width, rows = value.shape
    return jnp.sum(value.reshape(HEADS, width // HEADS, rows), axis=1)


def totals_column(rows, width):
    row = jnp.sum(jnp.where(own_head(width), rows, 0.0), axis=0, keepdims=True)
    return flip(jnp.broadcast_to(-row, (width, width)))


def pack_states(lefts, totals, state_t, state, width):
    count = len(lefts)
    rights = [jnp.where(own_head(width), total, 0.0) for total in totals]
    rest = jnp.zeros((width - count * HEADS, width), f32)
    right = jnp.concatenate(rights + [rest], axis=0)
    for place, left in enumerate(lefts):
        span = slice(place * width, (place + 1) * width)
        state_t[span] = left.astype(bf16)
        state[:, span] = flip(left).astype(bf16)
    start = count * width
    used = state_t.shape[0] - start
    state_t[start:] = right[:used].astype(bf16)
    state[:, start : start + width] = -flip(right).astype(bf16)


def assemble(parts, gathered):
    shards = len(parts)
    here = lax.axis_index("fsdp")
    for place, part in enumerate(parts):
        gathered[lax.rem(here + shards - place, shards)] = part[...]


def columns(gathered, start, count):
    shards, _, width = gathered.shape
    piece = width // shards
    small = [gathered[shard, start : start + 16, :].astype(f32) for shard in range(shards)]
    joined = jnp.concatenate([part[:, :piece] for part in small], axis=1)
    return [
        flip(jnp.broadcast_to(joined[place : place + 1], (width, width)))[:, 0:1]
        for place in range(count)
    ]


def lane_fold(value):
    width = value.shape[0]
    total = value[:, :width]
    for start in range(width, value.shape[1], width):
        total = total + value[:, start : start + width]
    return total


def as_row(value):
    width = value.shape[0]
    return flip(jnp.broadcast_to(jnp.sum(value, axis=1, keepdims=True), (width, width)))


def scatter_blocks(stage, outs):
    shards = len(outs)
    here = lax.axis_index("fsdp")
    for place, out in enumerate(outs):
        out[...] = stage[lax.rem(here + place, shards)]


def whole(gathered, start, rows):
    shards = gathered.shape[0]
    return gathered[:, start : start + rows, :].reshape(shards * rows, gathered.shape[2])


def function_weight(presence, item, func, funcs, shape):
    total = presence[item, 0]
    for other in range(1, funcs):
        total = total + presence[item, other]
    own = jnp.full(shape, presence[item, func], jnp.int32).astype(f32)
    return own / jnp.full(shape, total, jnp.int32).astype(f32)


def pack_kernel(*refs):
    weights, vectors, gate = refs[:10], refs[10:14], refs[14]
    early, late = refs[15:]
    keys, values, query, out, query_two, key_two, value_two, out_two, enter, leave = weights
    start = 0
    for weight in (keys, values):
        early[start : start + weight.shape[0]] = weight[...]
        start += weight.shape[0]
    start = 0
    for weight in (query, out, query_two, key_two, value_two, out_two):
        late[start : start + weight.shape[0]] = weight[...]
        start += weight.shape[0]
    experts, piece, hidden = enter.shape
    width = late.shape[1]
    for expert in range(experts):
        for half in range(hidden // width):
            late[start : start + piece] = enter[expert, :, half * width : (half + 1) * width]
            start += piece
    for expert in range(experts):
        late[start : start + leave.shape[1]] = leave[expert]
        start += leave.shape[1]
    rest = jnp.zeros((1, width - piece), f32)
    rows = [
        jnp.concatenate([vector[...].astype(f32), rest], axis=1) for vector in vectors
    ]
    rows.append(jnp.zeros((4, width), f32))
    for row in range(2):
        rows.append(jnp.broadcast_to(gate[row : row + 1, 0:1].astype(f32), (1, width)))
    rows.append(jnp.zeros((6, width), f32))
    late[start : start + 16] = jnp.concatenate(rows, axis=0).astype(bf16)


def run_tasks(tasks):
    waiting = None
    for dots, work in tasks:
        found = dots()
        if waiting is not None:
            waiting[0](*waiting[1])
        waiting = (work, found)
    waiting[0](*waiting[1])


def mix(tasks, extra):
    mixed = []
    done = 0
    for place, task in enumerate(tasks, 1):
        mixed.append(task)
        due = len(extra) * place // len(tasks)
        mixed += extra[done:due]
        done = due
    return mixed


def behind(stage, total, chunks, groups):
    tasks = []
    for cols in chunks:
        tasks.append(stage(cols))
        tasks += [total(group) for group in groups if group.stop == cols.stop - 2 * CHUNK]
    return tasks


def add_to(ref, span):
    def work(value):
        ref[span] += value

    return work


def points_forward(counts, presence, points, *refs, funcs, shards):
    parts = refs[:shards]
    state_t, state, keys_out, values_out, gathered, weight = refs[shards:]
    item = pl.program_id(0)
    width = points.shape[2]
    slots = points.shape[1]
    piece = width // shards

    @pl.when(item == 0)
    def _():
        assemble(parts, gathered)
        weight[:width] = flip(whole(gathered, 0, piece))
        weight[width:] = flip(whole(gathered, piece, piece))

    chunks = [slice(start, start + CHUNK) for start in range(0, slots, CHUNK)]

    def project(func, cols):
        def dots():
            return (nt(weight[...], points[func, cols, :]),)

        def work(both):
            slot = cols.start + lax.broadcasted_iota(jnp.int32, (1, CHUNK), 1)
            probs = head_softmax(both[:width])
            keys = jnp.where(slot < counts[item, func], probs, 0.0)
            keys_out[func, :, cols] = keys.astype(bf16)
            values_out[func, :, cols] = both[width:].astype(bf16)

        return dots, work

    def summarize(func):
        values = values_out[func]
        extended = jnp.concatenate([values, jnp.ones((PAD, slots), bf16)], axis=0)
        share = function_weight(presence, item, func, funcs, (1, width))
        summed = nt(extended, keys_out[func])
        left = jnp.where(same_head(width), summed[:width], 0.0) * share
        return left, summed[width : width + 1]

    run_tasks([project(func, cols) for func in range(funcs) for cols in chunks])
    lefts, totals = zip(*(summarize(func) for func in range(funcs)))
    pack_states(lefts, totals, state_t.at[0], state.at[0], width)


def main_kernel(tokens, cotangent, coords, state_t, *refs, funcs, experts, shards, at):
    parts, outs, scratch = refs[:shards], refs[shards : 2 * shards + 14], refs[2 * shards + 14 :]
    (
        result,
        queries_out,
        cross_out,
        first_out,
        keys_out,
        values_out,
        grad_q_out,
        grad_second_out,
        grad_state_out,
        rest_weights,
        rest_vectors,
        normed_out,
        hat_out,
        scale_out,
    ) = outs[:14]
    grads_out = outs[14:]
    (
        params,
        grads_stage,
        first_keep,
        query_keep,
        state_sum,
        self_t,
        self_state,
        grad_state_sum,
        w_query,
        w_out_one,
        w_self,
        w_out_two_t,
        w_out_two,
        w_in_t,
        w_in,
        w_exit,
        w_exit_t,
        gain_one,
        bias_one,
        gain_two,
        bias_two,
        hidden_keep,
        inner_keep,
        normed_keep,
        grad_keep,
        own_keep,
        pair_keep,
        sum_in,
        sum_exit,
        sum_out_two,
        sum_gain,
        sum_bias,
        sum_gate,
    ) = scratch
    item = pl.program_id(0)
    phase = pl.program_id(1)
    step = pl.program_id(2)
    steps = pl.num_programs(2)
    width = tokens.shape[1]
    rows = tokens.shape[0]
    piece = width // shards
    hidden = w_in.shape[1] // experts
    exit_piece = hidden // shards

    @pl.when((item == 0) & (phase == 0) & (step == 0))
    def _():
        assemble(parts, params)
        w_query[...] = flip(whole(params, at["query_first"], piece))
        w_out_one[...] = flip(whole(params, at["out_first"], piece))
        w_self[:width] = flip(whole(params, at["query_second"], piece))
        w_self[width : 2 * width] = flip(whole(params, at["key_second"], piece))
        w_self[2 * width :] = flip(whole(params, at["value_second"], piece))
        out_two = whole(params, at["out_second"], piece)
        w_out_two[...] = out_two
        w_out_two_t[...] = flip(out_two)
        for block in range(experts * hidden // width):
            part = whole(params, at["expert_in"] + block * piece, piece)
            w_in[:, block * width : (block + 1) * width] = part
            w_in_t[block * width : (block + 1) * width] = flip(part)
        for expert in range(experts):
            part = whole(params, at["expert_out"] + expert * exit_piece, exit_piece)
            w_exit[expert * hidden : (expert + 1) * hidden] = part
            w_exit_t[:, expert * hidden : (expert + 1) * hidden] = flip(part)
        names = ("query_second", "key_second", "value_second", "out_first", "query_first")
        for place, name in enumerate(names):
            rest_weights[:, place * width : (place + 1) * width] = whole(params, at[name], piece)
        found = columns(params, at["small"], 4)
        rest_vectors[...] = jnp.broadcast_to(found[0], rest_vectors.shape)
        for vector, column in zip((gain_one, bias_one, gain_two, bias_two), found):
            vector[...] = jnp.broadcast_to(column, vector.shape)
        sum_in[...] = jnp.zeros_like(sum_in)
        sum_exit[...] = jnp.zeros_like(sum_exit)
        sum_out_two[...] = jnp.zeros_like(sum_out_two)
        sum_gain[...] = jnp.zeros_like(sum_gain)
        sum_bias[...] = jnp.zeros_like(sum_bias)
        sum_gate[...] = jnp.zeros_like(sum_gate)

    chunks = [slice(start, start + CHUNK) for start in range(0, rows, CHUNK)]
    groups = [slice(start, start + GROUP) for start in range(0, rows, GROUP)]
    every = slice(None)

    @pl.when((phase == 0) & (step == 0))
    def _():
        state_sum[...] = jnp.zeros_like(state_sum)
        grad_state_sum[...] = jnp.zeros_like(grad_state_sum)

    @pl.when(phase == 0)
    def _():
        def enter(cols):
            def dots():
                return (flip(tokens[cols, :]).astype(f32),)

            def work(rows_t):
                first_keep[step, :, cols] = rows_t
                hat, scale = standardize(rows_t)
                hat_out[:, cols] = hat.astype(bf16)
                scale_out[:, cols] = jnp.broadcast_to(scale, (8, CHUNK))
                normed_out[:, cols] = (hat * gain_one[...] + bias_one[...]).astype(bf16)

            return dots, work

        def ask(cols):
            def dots():
                return (nn(w_query[...], normed_out[:, cols]),)

            def work(value):
                queries_out[:, cols] = head_softmax(value).astype(bf16)

            return dots, work

        def across(cols):
            def dots():
                return (nn(state_t[0], queries_out[:, cols]),)

            def work(both):
                undo = inverse(both[funcs * width :])
                mixed = None
                for func in range(funcs):
                    part = by_head(
                        both[func * width : (func + 1) * width],
                        undo[func * HEADS : (func + 1) * HEADS],
                    )
                    mixed = part if mixed is None else mixed + part
                cross_out[:, cols] = mixed.astype(bf16)

            return dots, work

        def leave(cols):
            def dots():
                return (nn(w_out_one[...], cross_out[:, cols]),)

            def work(value):
                first = first_keep[step, :, cols] + value
                first_keep[step, :, cols] = first
                first_out[:, cols] = first.astype(bf16)

            return dots, work

        def project(cols):
            def dots():
                return (nn(w_self[...], first_out[:, cols]),)

            def work(three):
                query_keep[step, :, cols] = head_softmax(three[:width]).astype(bf16)
                keys_out[:, cols] = head_softmax(three[width : 2 * width]).astype(bf16)
                values = three[2 * width :].astype(bf16)
                values_out[:, cols] = values
                pair_keep[:width, cols] = values
                pair_keep[width:, cols] = jnp.ones((PAD, CHUNK), bf16)

            return dots, work

        def sum_state(cols):
            return (
                lambda: (nt(pair_keep[:, cols], keys_out[:, cols]),),
                add_to(state_sum, every),
            )

        tasks = [stage(cols) for stage in (enter, ask, across, leave) for cols in chunks]
        run_tasks(tasks + behind(project, sum_state, chunks, groups[:-1]))
        run_tasks([sum_state(groups[-1])])

        @pl.when(step == steps - 1)
        def _():
            left = jnp.where(same_head(width), state_sum[:width], 0.0)
            pack_states([left], [state_sum[width : width + 1]], self_t, self_state, width)

    @pl.when(phase == 1)
    def _():
        undo_of, norm_of, gates_of = {}, {}, {}
        grad_gates_of = {chunk.start: [] for chunk in chunks}

        def attend(cols):
            def dots():
                return (nn(self_t[...], query_keep[step, :, cols]),)

            def work(both):
                undo = inverse(both[width : width + HEADS])
                undo_of[cols.start] = undo
                own_keep[:, cols] = by_head(both[:width], undo).astype(bf16)
                grad_keep[:, cols] = flip(cotangent[cols, :])

            return dots, work

        def gate(cols):
            across, down = coords[0:1, cols], coords[1:2, cols]
            logits = []
            for expert in range(experts):
                pair = params[expert, at["small"] : at["small"] + 16, 0:1].astype(f32)
                logits.append(across * pair[8:9] + down * pair[9:10])
            peak = logits[0]
            for logit in logits[1:]:
                peak = jnp.maximum(peak, logit)
            raised = [jnp.exp(logit - peak) for logit in logits]
            total = raised[0]
            for other in raised[1:]:
                total = total + other
            return [other / total for other in raised]

        def norm(cols):
            def dots():
                return (nn(w_out_two_t[...], own_keep[:, cols]),)

            def work(value):
                second = first_keep[step, :, cols] + value
                first_keep[step, :, cols] = second
                hat, scale = standardize(second)
                norm_of[cols.start] = (hat, scale)
                normed_keep[:, cols] = (hat * gain_two[...] + bias_two[...]).astype(bf16)
                gates_of[cols.start] = gate(cols)

            return dots, work

        def ring(cols):
            start = cols.start % (2 * GROUP)
            return slice(start, start + cols.stop - cols.start)

        def expand(cols, first):
            expert = first // hidden
            strip = slice(first, first + STRIP)

            def dots():
                return (
                    nn(w_in_t[strip], normed_keep[:, cols]).astype(bf16),
                    nn(w_exit[strip], grad_keep[:, cols]).astype(bf16),
                )

            def work(inners, backs):
                share = (0.5 * gates_of[cols.start][expert]).astype(bf16)
                partial_sum = None
                for start in range(0, STRIP, SLAB):
                    inner, back = inners[start : start + SLAB], backs[start : start + SLAB]
                    span = slice(first + start, first + start + SLAB)
                    square = inner * inner
                    tanh = jnp.tanh(inner * (0.7978845608028654 + 0.035677408136300125 * square))
                    above = 1.0 + tanh
                    active = inner * above
                    product = active * back
                    folded = product[:16]
                    for row in range(16, SLAB, 16):
                        folded = folded + product[row : row + 16]
                    folded = folded.astype(f32)
                    partial_sum = folded if partial_sum is None else partial_sum + folded
                    hidden_keep[span, ring(cols)] = active * share
                    slope = above + active * (1.0 - tanh) * (
                        0.7978845608028654 + 0.10703222440890037 * square
                    )
                    inner_keep[span, ring(cols)] = slope * (back * share)
                found = jnp.sum(0.5 * partial_sum, axis=0, keepdims=True)
                if first % hidden:
                    grad_gates_of[cols.start][expert] += found
                else:
                    grad_gates_of[cols.start].append(found)

            return dots, work

        def contract(cols):
            def dots():
                return (
                    nn(w_exit_t[...], hidden_keep[:, ring(cols)]),
                    nn(w_in[...], inner_keep[:, ring(cols)]),
                )

            def work(mixed, grad_normed):
                result[cols, :] = flip((first_keep[step, :, cols] + mixed).astype(bf16))
                hat, scale = norm_of[cols.start]
                sum_gain[...] += lane_fold(grad_normed * hat)
                sum_bias[...] += lane_fold(grad_normed)
                grad_second = grad_keep[:, cols].astype(f32) + norm_back(
                    grad_normed * gain_two[...], hat, scale
                )
                grad_second_out[:, cols] = grad_second.astype(bf16)
                gates, grad_gates = gates_of[cols.start], grad_gates_of[cols.start]
                across, down = coords[0:1, cols], coords[1:2, cols]
                mean_gate = gates[0] * grad_gates[0]
                for expert in range(1, experts):
                    mean_gate = mean_gate + gates[expert] * grad_gates[expert]
                for expert in range(experts):
                    change = gates[expert] * (grad_gates[expert] - mean_gate)
                    sum_gate[expert : expert + 1, cols] += across * change
                    sum_gate[experts + expert : experts + expert + 1, cols] += down * change

            return dots, work

        def attend_back(cols):
            def dots():
                return (nn(w_out_two[...], grad_second_out[:, cols]),)

            def work(value):
                share = by_head(value, undo_of[cols.start])
                pair_keep[:width, cols] = share.astype(bf16)
                sums = head_sums(share * own_keep[:, cols].astype(f32))
                pair_keep[width:, cols] = jnp.concatenate(
                    [sums, jnp.zeros((PAD - HEADS, CHUNK), f32)], axis=0
                ).astype(bf16)

            return dots, work

        def query_back(cols):
            def dots():
                return (nn(self_state[:, : width + PAD], pair_keep[:, cols]),)

            def work(grad_q):
                queries = query_keep[step, :, cols]
                grad_q_out[:, cols] = softmax_back(queries, grad_q).astype(bf16)

            return dots, work

        def sum_hidden(cols, expert):
            span = slice(expert * hidden, (expert + 1) * hidden)
            return (
                lambda: (nn(hidden_keep[span, ring(cols)], cotangent[cols, :]),),
                add_to(sum_exit, span),
            )

        def sum_inner(cols, expert):
            span = slice(expert * hidden, (expert + 1) * hidden)
            return (
                lambda: (nt(inner_keep[span, ring(cols)], normed_keep[:, cols]),),
                add_to(sum_in, span),
            )

        def sum_own(cols):
            return (
                lambda: (nt(own_keep[:, cols], grad_second_out[:, cols]),),
                add_to(sum_out_two, every),
            )

        def sum_pair(cols):
            return (
                lambda: (nt(pair_keep[:, cols], query_keep[step, :, cols]),),
                add_to(grad_state_sum, every),
            )

        tasks = [stage(cols) for stage in (attend, norm) for cols in chunks]
        sums, contracts = [], []
        for group in groups:
            inside = [cols for cols in chunks if group.start <= cols.start < group.stop]
            expands = [
                expand(cols, first) for cols in inside for first in range(0, experts * hidden, STRIP)
            ]
            tasks += mix(expands, mix(sums, contracts) if sums else [])
            contracts = [contract(cols) for cols in inside]
            sums = [
                total(group, expert) for expert in range(experts) for total in (sum_hidden, sum_inner)
            ]
        tasks += mix(contracts + [attend_back(cols) for cols in chunks], sums)
        last = [total(group) for group in groups for total in (sum_own, sum_pair)]
        tasks += mix([query_back(cols) for cols in chunks], last)
        run_tasks(tasks)

        @pl.when(step == steps - 1)
        def _():
            grad_state_out[0] = grad_state_sum[...]

    @pl.when((item == pl.num_programs(0) - 1) & (phase == 1) & (step == steps - 1))
    def _():
        gain, bias = as_row(sum_gain[...]), as_row(sum_bias[...])
        gate = jnp.broadcast_to(jnp.sum(sum_gate[...], axis=1, keepdims=True), (8, width))
        row = lax.broadcasted_iota(jnp.int32, (8, width), 0)
        vectors = jnp.where(row == 0, gain[:8], bias[:8])
        small = jnp.concatenate([vectors, gate], axis=0).astype(bf16)
        start = 0
        for block in range(experts * hidden // width):
            part = flip(sum_in[block * width : (block + 1) * width]).astype(bf16)
            grads_stage[:, start : start + piece, :] = part.reshape(shards, piece, width)
            start += piece
        for expert in range(experts):
            part = sum_exit[expert * hidden : (expert + 1) * hidden].astype(bf16)
            grads_stage[:, start : start + exit_piece, :] = part.reshape(shards, exit_piece, width)
            start += exit_piece
        part = sum_out_two[...].astype(bf16)
        grads_stage[:, start : start + piece, :] = part.reshape(shards, piece, width)
        start += piece
        for shard in range(shards):
            grads_stage[shard, start : start + 16, :] = small
        scatter_blocks(grads_stage, grads_out)


def rest_kernel(
    presence,
    hat_in,
    scale_in,
    normed_in,
    queries_in,
    cross_in,
    first_in,
    keys_in,
    values_in,
    grad_q_in,
    grad_second_in,
    grad_state_in,
    state_t,
    state,
    weights,
    gain_one,
    *refs,
    funcs,
    item,
    first_call,
):
    if not first_call:
        carry, refs = refs[3], refs[5:]
    (
        grad_tokens,
        grad_cross_state_out,
        grad_totals_out,
        sums_out,
        grad_self_state,
        grad_totals,
        grad_state_sum,
        sums,
        three_keep,
        cross_keep,
        stack_keep,
        query_keep,
    ) = refs
    step = pl.program_id(0)
    steps = pl.num_programs(0)
    width = hat_in.shape[0]
    self_part = slice(0, 3 * width)
    out_part = slice(3 * width, 4 * width)
    query_part = slice(4 * width, 5 * width)
    gain_part = slice(5 * width, 6 * width)
    bias_part = slice(6 * width, 7 * width)

    @pl.when(step == 0)
    def _():
        sums[...] = jnp.zeros_like(sums) if first_call else carry[...]
        left = jnp.where(same_head(width), grad_state_in[0, :width], 0.0)
        grad_self_state[0] = flip(left).astype(bf16)
        grad_self_state[1] = left.astype(bf16)
        column = totals_column(grad_state_in[0, width : width + HEADS], width)
        grad_totals[...] = jnp.broadcast_to(column[:, 0:1], grad_totals.shape)

    chunks = [slice(start, start + CHUNK) for start in range(0, hat_in.shape[1], CHUNK)]
    grad_first_of = {}

    def self_back(cols):
        def dots():
            return (
                nn(grad_self_state[0], values_in[:, cols]),
                nn(grad_self_state[1], keys_in[:, cols]),
            )

        def work(grad_keys, grad_values):
            grad_keys = softmax_back(keys_in[:, cols], grad_keys + grad_totals[...])
            three_keep[:width, cols] = grad_q_in[:, cols]
            three_keep[width : 2 * width, cols] = grad_keys.astype(bf16)
            three_keep[2 * width :, cols] = grad_values.astype(bf16)

        return dots, work

    def join(cols):
        def dots():
            return (nn(weights[:, self_part], three_keep[:, cols]),)

        def work(value):
            grad_first = grad_second_in[:, cols].astype(f32) + value
            grad_first_of[cols.start] = grad_first
            cross_keep[:, cols] = grad_first.astype(bf16)

        return dots, work

    def cross_back(cols):
        def dots():
            return nn(weights[:, out_part], cross_keep[:, cols]), nn(state_t[0], queries_in[:, cols])

        def work(share, both):
            undo = inverse(both[funcs * width :])
            sums_by_head = []
            for func in range(funcs):
                span = slice(func * width, (func + 1) * width)
                scales = undo[func * HEADS : (func + 1) * HEADS]
                part = by_head(share, scales)
                stack_keep[span, cols] = part.astype(bf16)
                sums_by_head.append(head_sums(part * by_head(both[span], scales)))
            spare = stack_keep.shape[0] - funcs * (width + HEADS)
            if spare:
                sums_by_head.append(jnp.zeros((spare, CHUNK), f32))
            stack_keep[funcs * width :, cols] = jnp.concatenate(sums_by_head, axis=0).astype(bf16)

        return dots, work

    def query_back(cols):
        def dots():
            return (nn(state[0, :, : stack_keep.shape[0]], stack_keep[:, cols]),)

        def work(grad_q):
            query_keep[:, cols] = softmax_back(queries_in[:, cols], grad_q).astype(bf16)

        return dots, work

    def finish(cols):
        def dots():
            return (nn(weights[:, query_part], query_keep[:, cols]),)

        def work(grad_normed):
            hat, scale = hat_in[:, cols].astype(f32), scale_in[0:1, cols]
            sums[gain_part] += lane_fold(grad_normed * hat)
            sums[bias_part] += lane_fold(grad_normed)
            grad_rows = grad_first_of[cols.start] + norm_back(
                grad_normed * gain_one[...], hat, scale
            )
            grad_tokens[cols, :] = flip(grad_rows)

        return dots, work

    @pl.when(step == 0)
    def _():
        grad_state_sum[...] = jnp.zeros_like(grad_state_sum)

    every = slice(None)
    sum_self = (lambda: (nt(three_keep[...], first_in[...]),), add_to(sums, self_part))
    sum_out = (lambda: (nt(cross_in[...], cross_keep[...]),), add_to(sums, out_part))
    sum_state = (lambda: (nt(stack_keep[...], queries_in[...]),), add_to(grad_state_sum, every))
    sum_query = (lambda: (nt(normed_in[...], query_keep[...]),), add_to(sums, query_part))
    tasks = [stage(cols) for stage in (self_back, join) for cols in chunks]
    tasks += mix([cross_back(cols) for cols in chunks], [sum_self])
    tasks += mix([query_back(cols) for cols in chunks], [sum_out])
    tasks += mix([finish(cols) for cols in chunks], [sum_state])
    run_tasks(tasks + [sum_query])

    @pl.when(step == steps - 1)
    def _():
        mask = same_head(width)
        for func in range(funcs):
            weight = function_weight(presence, item, func, funcs, (1, width))
            left = jnp.where(mask, grad_state_sum[func * width : (func + 1) * width], 0.0)
            grad_cross_state_out[func] = (left * weight).astype(bf16)
            start = funcs * width + func * HEADS
            grad_totals_out[func] = totals_column(grad_state_sum[start : start + HEADS], width)
        sums_out[...] = sums[...]


def points_back(points, keys_in, values_in, grad_state, grad_totals, carry, _after, *refs, shards):
    outs = refs[:shards]
    sums, stage, grads = refs[shards:]
    step = pl.program_id(0)
    width = points.shape[2]
    piece = width // shards

    funcs, slots, _ = points.shape
    chunks = [slice(start, start + CHUNK) for start in range(0, slots, CHUNK)]
    turned = [flip(grad_state[func]) for func in range(funcs)]

    def back(func, cols):
        def dots():
            return (
                nn(turned[func], values_in[func, :, cols]),
                nn(grad_state[func], keys_in[func, :, cols]),
            )

        def work(grad_keys, grad_values):
            grad_keys = grad_keys + grad_totals[func, :, 0:1]
            grad_k = softmax_back(keys_in[func, :, cols], grad_keys)
            grads[func, :width, cols] = grad_k.astype(bf16)
            grads[func, width:, cols] = grad_values.astype(bf16)

        return dots, work

    run_tasks([back(func, cols) for func in range(funcs) for cols in chunks])
    found = nn(grads[0], points[0])
    for func in range(1, funcs):
        found = found + nn(grads[func], points[func])

    @pl.when(step == 0)
    def _():
        sums[...] = found
        gain = as_row(carry[5 * width : 6 * width])
        bias = as_row(carry[6 * width : 7 * width])
        row = lax.broadcasted_iota(jnp.int32, (16, width), 0)
        small = jnp.where(row == 0, gain[:16], bias[:16]).astype(bf16)
        for place in range(5):
            part = carry[place * width : (place + 1) * width]
            part = (flip(part) if place < 3 else part).astype(bf16)
            stage[:, place * piece : (place + 1) * piece, :] = part.reshape(shards, piece, width)
        for shard in range(shards):
            stage[shard, 5 * piece : 5 * piece + 16, :] = small

    @pl.when(step > 0)
    def _():
        sums[...] += found

    @pl.when(step == pl.num_programs(0) - 1)
    def _():
        for place in range(2):
            start = 5 * piece + 16 + place * piece
            part = flip(sums[place * width : (place + 1) * width]).astype(bf16)
            stage[:, start : start + piece, :] = part.reshape(shards, piece, width)
        scatter_blocks(stage, outs)


def total_of(parts):
    value = parts[0][...].astype(f32)
    for part in parts[1:]:
        value = value + part[...].astype(f32)
    return value


def unpack_kernel(*refs, counts, experts, piece, exit_piece, hidden):
    main_parts, parts = refs[: counts[0]], refs[counts[0] : sum(counts)]
    outs, (small, main, rest) = refs[-18:-3], refs[-3:]
    width = main.shape[1]
    main[...] = total_of(main_parts)
    rest[...] = total_of(parts)
    (
        gain_one,
        bias_one,
        query_one,
        key_one,
        value_one,
        out_one,
        query_two,
        key_two,
        value_two,
        out_two,
        gain_two,
        bias_two,
        enter,
        leave,
        gate,
    ) = outs
    start = 0
    for expert in range(experts):
        for half in range(hidden // width):
            block = main[start : start + piece]
            enter[expert, :, half * width : (half + 1) * width] = block
            start += piece
    for expert in range(experts):
        leave[expert] = main[start : start + exit_piece]
        start += exit_piece
    out_two[...] = main[start : start + piece]
    start += piece
    small[:16] = main[start : start + 16]
    start = 0
    for out in (query_two, key_two, value_two, out_one, query_one):
        out[...] = rest[start : start + piece]
        start += piece
    small[16:] = rest[start : start + 16]
    start += 16
    for out in (key_one, value_one):
        out[...] = rest[start : start + piece]
        start += piece
    shard = lax.axis_index("fsdp")
    turned = pltpu.roll(small[...], lax.rem(width - shard * piece, width), 1)
    gain_two[...] = turned[0:1, :piece]
    bias_two[...] = turned[1:2, :piece]
    gain_one[...] = turned[16:17, :piece]
    bias_one[...] = turned[17:18, :piece]
    for row in range(2):
        gate[:, row : row + 1] = small[pl.ds(8 + row * experts + shard, 1), 0:1]


def whole_spec(shape):
    return pl.BlockSpec(shape, lambda *_: (0,) * len(shape))


def route(size, shift, digit, stride):
    def target(i):
        own = i // stride % digit
        return i + ((own + shift) % digit - own) * stride

    return [(i, target(i)) for i in range(size)]


def spread(value, axis, size, digit, stride):
    return [value] + [
        lax.ppermute(value, axis, route(size, shift, digit, stride)) for shift in range(1, digit)
    ]


def exchange(values, axis, size, stride):
    digit = len(values)
    return [values[0]] + [
        lax.ppermute(values[shift], axis, route(size, shift, digit, stride))
        for shift in range(1, digit)
    ]


def digits(size):
    found = []
    stride = 1
    while stride < size:
        rest = size // stride
        digit = 2 if stride == 1 and rest % 2 == 0 else 4 if rest % 4 == 0 else rest
        found.append((digit, stride))
        stride *= digit
    return found or [(1, 1)]


def sum_parts(parts):
    return total_of([part.astype(f32) for part in parts]).astype(bf16)


def shards_fn(
    dp,
    shards,
    tokens,
    points,
    coords,
    presence,
    counts,
    cotangent,
    gain_first,
    bias_first,
    query_first,
    key_first,
    value_first,
    out_first,
    query_second,
    key_second,
    value_second,
    out_second,
    gain_second,
    bias_second,
    expert_in,
    expert_out,
    gate_weight,
):
    count, width = tokens.shape
    items, funcs, slots, _ = points.shape
    length = count // items
    experts, piece, hidden = expert_in.shape
    exit_piece = expert_out.shape[1]
    tile, rest_tile = min(MAIN_TILE, length), min(REST_TILE, length)
    steps, rest_steps = length // tile, length // rest_tile
    inner = experts * hidden
    enter_rows = experts * piece * (hidden // width)
    limit = pltpu.CompilerParams(vmem_limit_bytes=VMEM)

    at = {}
    place = 0
    for name, size in (
        ("query_first", piece),
        ("out_first", piece),
        ("query_second", piece),
        ("key_second", piece),
        ("value_second", piece),
        ("out_second", piece),
        ("expert_in", enter_rows),
        ("expert_out", experts * exit_piece),
        ("small", 16),
    ):
        at[name] = place
        place += size
    late_rows_count = place
    early_pack, late_pack = pl.pallas_call(
        pack_kernel,
        out_shape=[
            jax.ShapeDtypeStruct((2 * piece, width), bf16),
            jax.ShapeDtypeStruct((late_rows_count, width), bf16),
        ],
        name="pack",
    )(
        key_first,
        value_first,
        query_first,
        out_first,
        query_second,
        key_second,
        value_second,
        out_second,
        expert_in,
        expert_out,
        *(
            vector.reshape(1, piece)
            for vector in (gain_first, bias_first, gain_second, bias_second)
        ),
        gate_weight,
    )
    early_parts = spread(early_pack, "fsdp", shards, shards, 1)
    late_parts = spread(late_pack, "fsdp", shards, shards, 1)
    late_specs = [whole_spec((late_rows_count, width))] * shards
    gathered = pltpu.VMEM((shards, late_rows_count, width), bf16)

    smem = pl.BlockSpec(memory_space=pltpu.SMEM)
    units = items * funcs
    state_rows = funcs * width + -(-funcs * HEADS // PAD) * PAD
    flat_points = points.reshape(units, slots, width)
    state_t, state, keys_one, values_one = pl.pallas_call(
        partial(points_forward, funcs=funcs, shards=shards),
        grid=(items,),
        in_specs=[smem, smem, pl.BlockSpec((funcs, slots, width), lambda u: (u, 0, 0))]
        + [whole_spec((2 * piece, width))] * shards,
        out_specs=[
            pl.BlockSpec((1, state_rows, width), lambda u: (u, 0, 0)),
            pl.BlockSpec((1, width, (funcs + 1) * width), lambda u: (u, 0, 0)),
            pl.BlockSpec((funcs, width, slots), lambda u: (u, 0, 0)),
            pl.BlockSpec((funcs, width, slots), lambda u: (u, 0, 0)),
        ],
        out_shape=[
            jax.ShapeDtypeStruct((items, state_rows, width), bf16),
            jax.ShapeDtypeStruct((items, width, (funcs + 1) * width), bf16),
            jax.ShapeDtypeStruct((units, width, slots), bf16),
            jax.ShapeDtypeStruct((units, width, slots), bf16),
        ],
        scratch_shapes=[
            pltpu.VMEM((shards, 2 * piece, width), bf16),
            pltpu.VMEM((2 * width, width), bf16),
        ],
        compiler_params=pltpu.CompilerParams(vmem_limit_bytes=VMEM * 2 // 5),
        cost_estimate=cost(8),
        name="points_forward",
    )(counts, presence, flat_points, *early_parts)

    kept = jax.ShapeDtypeStruct((width, count), bf16)
    main_rows = enter_rows + experts * exit_piece + piece + 16

    def early(i, p, j):
        return i * steps + jnp.where(p == 0, j, steps - 1)

    def late(i, p, j):
        return i * steps + jnp.where(p == 0, 0, j)

    early_keep = pl.BlockSpec((width, tile), lambda i, p, j: (0, early(i, p, j)))
    late_keep = pl.BlockSpec((width, tile), lambda i, p, j: (0, late(i, p, j)))
    late_rows = pl.BlockSpec((tile, width), lambda i, p, j: (late(i, p, j), 0))
    (
        result,
        queries_one,
        cross,
        first,
        keys_two,
        values_two,
        grad_q_two,
        grad_second,
        grad_state_two,
        rest_weights,
        rest_vectors,
        normed_one,
        hat_one,
        scale_one,
        *main_grads,
    ) = pl.pallas_call(
        partial(main_kernel, funcs=funcs, experts=experts, shards=shards, at=at),
        grid=(items, 2, steps),
        in_specs=[
            pl.BlockSpec((tile, width), lambda i, p, j: (early(i, p, j), 0)),
            late_rows,
            pl.BlockSpec((2, tile), lambda i, p, j: (0, late(i, p, j))),
            pl.BlockSpec((1, state_rows, width), lambda i, p, j: (i, 0, 0)),
        ]
        + late_specs,
        out_specs=[
            late_rows,
            early_keep,
            early_keep,
            early_keep,
            early_keep,
            early_keep,
            late_keep,
            late_keep,
            pl.BlockSpec((1, width + PAD, width), lambda i, p, j: (i, 0, 0)),
            whole_spec((width, 5 * width)),
            whole_spec((width, CHUNK)),
            early_keep,
            early_keep,
            pl.BlockSpec((8, tile), lambda i, p, j: (0, early(i, p, j))),
        ]
        + [whole_spec((main_rows, width))] * shards,
        out_shape=[
            jax.ShapeDtypeStruct((count, width), bf16),
            kept,
            kept,
            kept,
            kept,
            kept,
            kept,
            kept,
            jax.ShapeDtypeStruct((items, width + PAD, width), f32),
            jax.ShapeDtypeStruct((width, 5 * width), bf16),
            jax.ShapeDtypeStruct((width, CHUNK), f32),
            kept,
            kept,
            jax.ShapeDtypeStruct((8, count), f32),
        ]
        + [jax.ShapeDtypeStruct((main_rows, width), bf16)] * shards,
        scratch_shapes=[
            gathered,
            pltpu.VMEM((shards, main_rows, width), bf16),
            pltpu.VMEM((steps, width, tile), f32),
            pltpu.VMEM((steps, width, tile), bf16),
            pltpu.VMEM((width + PAD, width), f32),
            pltpu.VMEM((width + PAD, width), bf16),
            pltpu.VMEM((width, 2 * width), bf16),
            pltpu.VMEM((width + PAD, width), f32),
            pltpu.VMEM((width, width), bf16),
            pltpu.VMEM((width, width), bf16),
            pltpu.VMEM((3 * width, width), bf16),
            pltpu.VMEM((width, width), bf16),
            pltpu.VMEM((width, width), bf16),
            pltpu.VMEM((inner, width), bf16),
            pltpu.VMEM((width, inner), bf16),
            pltpu.VMEM((inner, width), bf16),
            pltpu.VMEM((width, inner), bf16),
            pltpu.VMEM((width, CHUNK), f32),
            pltpu.VMEM((width, CHUNK), f32),
            pltpu.VMEM((width, CHUNK), f32),
            pltpu.VMEM((width, CHUNK), f32),
            pltpu.VMEM((inner, min(2 * GROUP, tile)), bf16),
            pltpu.VMEM((inner, min(2 * GROUP, tile)), bf16),
            pltpu.VMEM((width, tile), bf16),
            pltpu.VMEM((width, tile), bf16),
            pltpu.VMEM((width, tile), bf16),
            pltpu.VMEM((width + PAD, tile), bf16),
            pltpu.VMEM((inner, width), f32),
            pltpu.VMEM((inner, width), f32),
            pltpu.VMEM((width, width), f32),
            pltpu.VMEM((width, width), f32),
            pltpu.VMEM((width, width), f32),
            pltpu.VMEM((2 * experts, tile), f32),
        ],
        compiler_params=limit,
        cost_estimate=cost(80),
        name="main",
    )(tokens, cotangent, coords, state_t, *late_parts)

    rest_rows = 7 * piece + 16

    def rest_call(item, earlier, after):
        first_call = item == 0
        keep_spec = pl.BlockSpec((width, rest_tile), lambda j: (0, item * rest_steps + j))
        row_spec = pl.BlockSpec((rest_tile, width), lambda j: (item * rest_steps + j, 0))
        unit_spec = pl.BlockSpec((funcs, width, width), lambda j: (item, 0, 0))
        anywhere = pl.BlockSpec(memory_space=pl.ANY)
        in_specs = [
            smem,
            keep_spec,
            pl.BlockSpec((8, rest_tile), lambda j: (0, item * rest_steps + j)),
            keep_spec,
            keep_spec,
            keep_spec,
            keep_spec,
            keep_spec,
            keep_spec,
            keep_spec,
            keep_spec,
            pl.BlockSpec((1, width + PAD, width), lambda j: (item, 0, 0)),
            pl.BlockSpec((1, state_rows, width), lambda j: (item, 0, 0)),
            pl.BlockSpec((1, width, (funcs + 1) * width), lambda j: (item, 0, 0)),
            whole_spec((width, 5 * width)),
            whole_spec((width, CHUNK)),
        ]
        operands = [
            presence,
            hat_one,
            scale_one,
            normed_one,
            queries_one,
            cross,
            first,
            keys_two,
            values_two,
            grad_q_two,
            grad_second,
            grad_state_two,
            state_t,
            state,
            rest_weights,
            rest_vectors,
        ]
        aliases = {}
        if not first_call:
            aliases = {len(operands) + k: k for k in range(3)}
            in_specs += [anywhere] * 3 + [whole_spec((7 * width, width)), anywhere]
            operands += [*earlier, after]
        out_specs = [row_spec, unit_spec, unit_spec, whole_spec((7 * width, width))]
        out_shape = [
            jax.ShapeDtypeStruct((count, width), f32),
            jax.ShapeDtypeStruct((units, width, width), bf16),
            jax.ShapeDtypeStruct((units, width, width), f32),
            jax.ShapeDtypeStruct((7 * width, width), f32),
        ]
        return pl.pallas_call(
            partial(
                rest_kernel,
                funcs=funcs,
                item=item,
                first_call=first_call,
            ),
            grid=(rest_steps,),
            in_specs=in_specs,
            out_specs=out_specs,
            out_shape=out_shape,
            input_output_aliases=aliases,
            scratch_shapes=[
                pltpu.VMEM((2, width, width), bf16),
                pltpu.VMEM((width, CHUNK), f32),
                pltpu.VMEM((state_rows, width), f32),
                pltpu.VMEM((7 * width, width), f32),
                pltpu.VMEM((3 * width, rest_tile), bf16),
                pltpu.VMEM((width, rest_tile), bf16),
                pltpu.VMEM((state_rows, rest_tile), bf16),
                pltpu.VMEM((width, rest_tile), bf16),
            ],
            compiler_params=limit,
            cost_estimate=cost(18),
            name="rest",
        )(*operands)

    levels = digits(dp)
    main_levels = levels[::-1]
    main_parts = exchange(main_grads, "fsdp", shards, 1)
    level = 0
    found = None
    for item in range(items):
        found = rest_call(item, found, main_sum if item else None)
        if item < len(main_levels):
            main_sum = sum_parts(main_parts)
            main_parts = spread(main_sum, "dp", dp, *main_levels[item])
            level = item + 1
    grad_tokens, grad_state_one, grad_totals_one, carry = found

    rest_grads = pl.pallas_call(
        partial(points_back, shards=shards),
        grid=(items,),
        in_specs=[
            pl.BlockSpec((funcs, slots, width), lambda u: (u, 0, 0)),
            pl.BlockSpec((funcs, width, slots), lambda u: (u, 0, 0)),
            pl.BlockSpec((funcs, width, slots), lambda u: (u, 0, 0)),
            pl.BlockSpec((funcs, width, width), lambda u: (u, 0, 0)),
            pl.BlockSpec((funcs, width, width), lambda u: (u, 0, 0)),
            whole_spec((7 * width, width)),
            pl.BlockSpec(memory_space=pl.ANY),
        ],
        out_specs=[whole_spec((rest_rows, width))] * shards,
        out_shape=[jax.ShapeDtypeStruct((rest_rows, width), bf16)] * shards,
        scratch_shapes=[
            pltpu.VMEM((2 * width, width), f32),
            pltpu.VMEM((shards, rest_rows, width), bf16),
            pltpu.VMEM((funcs, 2 * width, slots), bf16),
        ],
        compiler_params=limit,
        cost_estimate=cost(7),
        name="points_back",
    )(flat_points, keys_one, values_one, grad_state_one, grad_totals_one, carry, main_sum)
    rest_got = exchange(rest_grads, "fsdp", shards, 1)

    parts = rest_got
    for digit, stride in main_levels[level:]:
        main_parts = spread(sum_parts(main_parts), "dp", dp, digit, stride)
    for digit, stride in levels:
        parts = spread(sum_parts(parts), "dp", dp, digit, stride)

    matrix = jax.ShapeDtypeStruct((piece, width), f32)
    vector = jax.ShapeDtypeStruct((1, piece), f32)
    outs = pl.pallas_call(
        partial(
            unpack_kernel,
            counts=(len(main_parts), len(parts)),
            experts=experts,
            piece=piece,
            exit_piece=exit_piece,
            hidden=hidden,
        ),
        out_shape=[vector] * 2
        + [matrix] * 8
        + [vector] * 2
        + [
            jax.ShapeDtypeStruct(expert_in.shape, f32),
            jax.ShapeDtypeStruct(expert_out.shape, f32),
            jax.ShapeDtypeStruct((1, 2), f32),
        ],
        scratch_shapes=[
            pltpu.VMEM((32, width), f32),
            pltpu.VMEM((main_rows, width), f32),
            pltpu.VMEM((rest_rows, width), f32),
        ],
        compiler_params=pltpu.CompilerParams(vmem_limit_bytes=VMEM // 8),
        name="unpack",
    )(*main_parts, *parts)
    outs = [out.reshape(piece) if out.shape == (1, piece) else out for out in outs]
    return (result, grad_tokens, *outs[:-1], outs[-1].reshape(gate_weight.shape))


def solution(mesh):
    rows = P(("dp", "fsdp"), None)
    matrix = P("fsdp", None)
    vector = P("fsdp")
    expert = P(None, "fsdp", None)
    parameters = (
        (vector, vector)
        + (matrix,) * 8
        + (vector, vector, expert, expert, P(None, "fsdp"))
    )
    return jax.shard_map(
        partial(shards_fn, mesh.shape["dp"], mesh.shape["fsdp"]),
        mesh=mesh,
        in_specs=(
            rows,
            P(("dp", "fsdp"), None, None, None),
            P(None, ("dp", "fsdp")),
            rows,
            rows,
            rows,
        )
        + parameters,
        out_specs=(rows, rows) + parameters,
        check_vma=False,
    )
```

```python
from functools import partial

import jax
import jax.numpy as jnp
from jax import lax
from jax.experimental import pallas as pl
from jax.experimental.pallas import tpu as pltpu
from jax.sharding import PartitionSpec as P


HEADS = 8
eps = 1e-05
f32 = jnp.float32
bf16 = jnp.bfloat16
MAIN_TILE = 4096
REST_TILE = 1024
GROUP = 1024
STRIP = 128
CHUNK = 256
SLAB = 64
PAD = 16
VMEM = 60 * 1024 * 1024


def cost(microseconds):
    return pl.CostEstimate(flops=microseconds * 10**9, bytes_accessed=10**6, transcendentals=0)


def nn(left, right):
    return jnp.dot(left, right, preferred_element_type=f32)


def nt(left, right):
    return lax.dot_general(left, right, (((1,), (1,)), ((), ())), preferred_element_type=f32)


def flip(value):
    return value.T


def inverse(value):
    return pl.reciprocal(value, approx=True)


def head_softmax(value):
    width, rows = value.shape
    split = value.reshape(HEADS, width // HEADS, rows)
    raised = jnp.exp(split - jnp.max(split, axis=1, keepdims=True))
    return (raised * inverse(jnp.sum(raised, axis=1, keepdims=True))).reshape(width, rows)


def softmax_back(probs, grad):
    width, rows = grad.shape
    probs = probs.astype(f32).reshape(HEADS, width // HEADS, rows)
    grad = grad.reshape(HEADS, width // HEADS, rows)
    inner = jnp.sum(probs * grad, axis=1, keepdims=True)
    return (probs * (grad - inner)).reshape(width, rows)


def standardize(value):
    centre = value - jnp.mean(value, axis=0, keepdims=True)
    scale = lax.rsqrt(jnp.mean(centre * centre, axis=0, keepdims=True) + eps)
    return centre * scale, scale


def norm_back(grad, hat, scale):
    return scale * (
        grad
        - jnp.mean(grad, axis=0, keepdims=True)
        - hat * jnp.mean(grad * hat, axis=0, keepdims=True)
    )


def same_head(width):
    shape, head = (width, width), width // HEADS
    row = lax.broadcasted_iota(jnp.int32, shape, 0)
    column = lax.broadcasted_iota(jnp.int32, shape, 1)
    return lax.div(row, head) == lax.div(column, head)


def own_head(width):
    shape, head = (HEADS, width), width // HEADS
    row = lax.broadcasted_iota(jnp.int32, shape, 0)
    return row == lax.div(lax.broadcasted_iota(jnp.int32, shape, 1), head)


def by_head(value, scales):
    width, rows = value.shape
    split = value.reshape(HEADS, width // HEADS, rows)
    return (split * scales.reshape(HEADS, 1, rows)).reshape(width, rows)


def head_sums(value):
    width, rows = value.shape
    return jnp.sum(value.reshape(HEADS, width // HEADS, rows), axis=1)


def totals_column(rows, width):
    row = jnp.sum(jnp.where(own_head(width), rows, 0.0), axis=0, keepdims=True)
    return flip(jnp.broadcast_to(-row, (width, width)))


def pack_states(lefts, totals, state_t, state, width):
    count = len(lefts)
    rights = [jnp.where(own_head(width), total, 0.0) for total in totals]
    rest = jnp.zeros((width - count * HEADS, width), f32)
    right = jnp.concatenate(rights + [rest], axis=0)
    for place, left in enumerate(lefts):
        span = slice(place * width, (place + 1) * width)
        state_t[span] = left.astype(bf16)
        state[:, span] = flip(left).astype(bf16)
    start = count * width
    used = state_t.shape[0] - start
    state_t[start:] = right[:used].astype(bf16)
    state[:, start : start + width] = -flip(right).astype(bf16)


def assemble(parts, gathered):
    shards = len(parts)
    here = lax.axis_index("fsdp")
    for place, part in enumerate(parts):
        gathered[lax.rem(here + shards - place, shards)] = part[...]


def columns(gathered, start, count):
    shards, _, width = gathered.shape
    piece = width // shards
    small = [gathered[shard, start : start + 16, :].astype(f32) for shard in range(shards)]
    joined = jnp.concatenate([part[:, :piece] for part in small], axis=1)
    return [
        flip(jnp.broadcast_to(joined[place : place + 1], (width, width)))[:, 0:1]
        for place in range(count)
    ]


def lane_fold(value):
    width = value.shape[0]
    total = value[:, :width]
    for start in range(width, value.shape[1], width):
        total = total + value[:, start : start + width]
    return total


def as_row(value):
    width = value.shape[0]
    return flip(jnp.broadcast_to(jnp.sum(value, axis=1, keepdims=True), (width, width)))


def scatter_blocks(stage, outs):
    shards = len(outs)
    here = lax.axis_index("fsdp")
    for place, out in enumerate(outs):
        out[...] = stage[lax.rem(here + place, shards)]


def whole(gathered, start, rows):
    shards = gathered.shape[0]
    return gathered[:, start : start + rows, :].reshape(shards * rows, gathered.shape[2])


def function_weight(presence, item, func, funcs, shape):
    total = presence[item, 0]
    for other in range(1, funcs):
        total = total + presence[item, other]
    own = jnp.full(shape, presence[item, func], jnp.int32).astype(f32)
    return own / jnp.full(shape, total, jnp.int32).astype(f32)


def pack_kernel(*refs):
    weights, vectors, gate = refs[:10], refs[10:14], refs[14]
    early, late = refs[15:]
    keys, values, query, out, query_two, key_two, value_two, out_two, enter, leave = weights
    start = 0
    for weight in (keys, values):
        early[start : start + weight.shape[0]] = weight[...]
        start += weight.shape[0]
    start = 0
    for weight in (query, out, query_two, key_two, value_two, out_two):
        late[start : start + weight.shape[0]] = weight[...]
        start += weight.shape[0]
    experts, piece, hidden = enter.shape
    width = late.shape[1]
    for expert in range(experts):
        for half in range(hidden // width):
            late[start : start + piece] = enter[expert, :, half * width : (half + 1) * width]
            start += piece
    for expert in range(experts):
        late[start : start + leave.shape[1]] = leave[expert]
        start += leave.shape[1]
    rest = jnp.zeros((1, width - piece), f32)
    rows = [
        jnp.concatenate([vector[...].astype(f32), rest], axis=1) for vector in vectors
    ]
    rows.append(jnp.zeros((4, width), f32))
    for row in range(2):
        rows.append(jnp.broadcast_to(gate[row : row + 1, 0:1].astype(f32), (1, width)))
    rows.append(jnp.zeros((6, width), f32))
    late[start : start + 16] = jnp.concatenate(rows, axis=0).astype(bf16)


def run_tasks(tasks):
    waiting = None
    for dots, work in tasks:
        found = dots()
        if waiting is not None:
            waiting[0](*waiting[1])
        waiting = (work, found)
    waiting[0](*waiting[1])


def mix(tasks, extra):
    mixed = []
    done = 0
    for place, task in enumerate(tasks, 1):
        mixed.append(task)
        due = len(extra) * place // len(tasks)
        mixed += extra[done:due]
        done = due
    return mixed


def behind(stage, total, chunks, groups):
    tasks = []
    for cols in chunks:
        tasks.append(stage(cols))
        tasks += [total(group) for group in groups if group.stop == cols.stop - 2 * CHUNK]
    return tasks


def add_to(ref, span):
    def work(value):
        ref[span] += value

    return work


def points_forward(counts, presence, points, *refs, funcs, shards):
    parts = refs[:shards]
    state_t, state, keys_out, values_out, gathered, weight = refs[shards:]
    item = pl.program_id(0)
    width = points.shape[2]
    slots = points.shape[1]
    piece = width // shards

    @pl.when(item == 0)
    def _():
        assemble(parts, gathered)
        weight[:width] = flip(whole(gathered, 0, piece))
        weight[width:] = flip(whole(gathered, piece, piece))

    chunks = [slice(start, start + CHUNK) for start in range(0, slots, CHUNK)]

    def project(func, cols):
        def dots():
            return (nt(weight[...], points[func, cols, :]),)

        def work(both):
            slot = cols.start + lax.broadcasted_iota(jnp.int32, (1, CHUNK), 1)
            probs = head_softmax(both[:width])
            keys = jnp.where(slot < counts[item, func], probs, 0.0)
            keys_out[func, :, cols] = keys.astype(bf16)
            values_out[func, :, cols] = both[width:].astype(bf16)

        return dots, work

    def summarize(func):
        values = values_out[func]
        extended = jnp.concatenate([values, jnp.ones((PAD, slots), bf16)], axis=0)
        share = function_weight(presence, item, func, funcs, (1, width))
        summed = nt(extended, keys_out[func])
        left = jnp.where(same_head(width), summed[:width], 0.0) * share
        return left, summed[width : width + 1]

    run_tasks([project(func, cols) for func in range(funcs) for cols in chunks])
    lefts, totals = zip(*(summarize(func) for func in range(funcs)))
    pack_states(lefts, totals, state_t.at[0], state.at[0], width)


def main_kernel(tokens, cotangent, coords, state_t, *refs, funcs, experts, shards, at):
    parts, outs, scratch = refs[:shards], refs[shards : 2 * shards + 14], refs[2 * shards + 14 :]
    (
        result,
        queries_out,
        cross_out,
        first_out,
        keys_out,
        values_out,
        grad_q_out,
        grad_second_out,
        grad_state_out,
        rest_weights,
        rest_vectors,
        normed_out,
        hat_out,
        scale_out,
    ) = outs[:14]
    grads_out = outs[14:]
    (
        params,
        grads_stage,
        first_keep,
        query_keep,
        state_sum,
        self_t,
        self_state,
        grad_state_sum,
        w_query,
        w_out_one,
        w_self,
        w_out_two_t,
        w_out_two,
        w_in_t,
        w_in,
        w_exit,
        w_exit_t,
        gain_one,
        bias_one,
        gain_two,
        bias_two,
        hidden_keep,
        inner_keep,
        normed_keep,
        grad_keep,
        own_keep,
        pair_keep,
        sum_in,
        sum_exit,
        sum_out_two,
        sum_gain,
        sum_bias,
        sum_gate,
    ) = scratch
    item = pl.program_id(0)
    phase = pl.program_id(1)
    step = pl.program_id(2)
    steps = pl.num_programs(2)
    width = tokens.shape[1]
    rows = tokens.shape[0]
    piece = width // shards
    hidden = w_in.shape[1] // experts
    exit_piece = hidden // shards

    @pl.when((item == 0) & (phase == 0) & (step == 0))
    def _():
        assemble(parts, params)
        w_query[...] = flip(whole(params, at["query_first"], piece))
        w_out_one[...] = flip(whole(params, at["out_first"], piece))
        w_self[:width] = flip(whole(params, at["query_second"], piece))
        w_self[width : 2 * width] = flip(whole(params, at["key_second"], piece))
        w_self[2 * width :] = flip(whole(params, at["value_second"], piece))
        out_two = whole(params, at["out_second"], piece)
        w_out_two[...] = out_two
        w_out_two_t[...] = flip(out_two)
        for block in range(experts * hidden // width):
            part = whole(params, at["expert_in"] + block * piece, piece)
            w_in[:, block * width : (block + 1) * width] = part
            w_in_t[block * width : (block + 1) * width] = flip(part)
        for expert in range(experts):
            part = whole(params, at["expert_out"] + expert * exit_piece, exit_piece)
            w_exit[expert * hidden : (expert + 1) * hidden] = part
            w_exit_t[:, expert * hidden : (expert + 1) * hidden] = flip(part)
        names = ("query_second", "key_second", "value_second", "out_first", "query_first")
        for place, name in enumerate(names):
            rest_weights[:, place * width : (place + 1) * width] = whole(params, at[name], piece)
        found = columns(params, at["small"], 4)
        rest_vectors[...] = jnp.broadcast_to(found[0], rest_vectors.shape)
        for vector, column in zip((gain_one, bias_one, gain_two, bias_two), found):
            vector[...] = jnp.broadcast_to(column, vector.shape)
        sum_in[...] = jnp.zeros_like(sum_in)
        sum_exit[...] = jnp.zeros_like(sum_exit)
        sum_out_two[...] = jnp.zeros_like(sum_out_two)
        sum_gain[...] = jnp.zeros_like(sum_gain)
        sum_bias[...] = jnp.zeros_like(sum_bias)
        sum_gate[...] = jnp.zeros_like(sum_gate)

    chunks = [slice(start, start + CHUNK) for start in range(0, rows, CHUNK)]
    groups = [slice(start, start + GROUP) for start in range(0, rows, GROUP)]
    every = slice(None)

    @pl.when((phase == 0) & (step == 0))
    def _():
        state_sum[...] = jnp.zeros_like(state_sum)
        grad_state_sum[...] = jnp.zeros_like(grad_state_sum)

    @pl.when(phase == 0)
    def _():
        def enter(cols):
            def dots():
                return (flip(tokens[cols, :]).astype(f32),)

            def work(rows_t):
                first_keep[step, :, cols] = rows_t
                hat, scale = standardize(rows_t)
                hat_out[:, cols] = hat.astype(bf16)
                scale_out[:, cols] = jnp.broadcast_to(scale, (8, CHUNK))
                normed_out[:, cols] = (hat * gain_one[...] + bias_one[...]).astype(bf16)

            return dots, work

        def ask(cols):
            def dots():
                return (nn(w_query[...], normed_out[:, cols]),)

            def work(value):
                queries_out[:, cols] = head_softmax(value).astype(bf16)

            return dots, work

        def across(cols):
            def dots():
                return (nn(state_t[0], queries_out[:, cols]),)

            def work(both):
                undo = inverse(both[funcs * width :])
                mixed = None
                for func in range(funcs):
                    part = by_head(
                        both[func * width : (func + 1) * width],
                        undo[func * HEADS : (func + 1) * HEADS],
                    )
                    mixed = part if mixed is None else mixed + part
                cross_out[:, cols] = mixed.astype(bf16)

            return dots, work

        def leave(cols):
            def dots():
                return (nn(w_out_one[...], cross_out[:, cols]),)

            def work(value):
                first = first_keep[step, :, cols] + value
                first_keep[step, :, cols] = first
                first_out[:, cols] = first.astype(bf16)

            return dots, work

        def project(cols):
            def dots():
                return (nn(w_self[...], first_out[:, cols]),)

            def work(three):
                query_keep[step, :, cols] = head_softmax(three[:width]).astype(bf16)
                keys_out[:, cols] = head_softmax(three[width : 2 * width]).astype(bf16)
                values = three[2 * width :].astype(bf16)
                values_out[:, cols] = values
                pair_keep[:width, cols] = values
                pair_keep[width:, cols] = jnp.ones((PAD, CHUNK), bf16)

            return dots, work

        def sum_state(cols):
            return (
                lambda: (nt(pair_keep[:, cols], keys_out[:, cols]),),
                add_to(state_sum, every),
            )

        tasks = [stage(cols) for stage in (enter, ask, across, leave) for cols in chunks]
        run_tasks(tasks + behind(project, sum_state, chunks, groups[:-1]))
        run_tasks([sum_state(groups[-1])])

        @pl.when(step == steps - 1)
        def _():
            left = jnp.where(same_head(width), state_sum[:width], 0.0)
            pack_states([left], [state_sum[width : width + 1]], self_t, self_state, width)

    @pl.when(phase == 1)
    def _():
        undo_of, norm_of, gates_of = {}, {}, {}
        grad_gates_of = {chunk.start: [] for chunk in chunks}

        def attend(cols):
            def dots():
                return (nn(self_t[...], query_keep[step, :, cols]),)

            def work(both):
                undo = inverse(both[width : width + HEADS])
                undo_of[cols.start] = undo
                own_keep[:, cols] = by_head(both[:width], undo).astype(bf16)
                grad_keep[:, cols] = flip(cotangent[cols, :])

            return dots, work

        def gate(cols):
            across, down = coords[0:1, cols], coords[1:2, cols]
            logits = []
            for expert in range(experts):
                pair = params[expert, at["small"] : at["small"] + 16, 0:1].astype(f32)
                logits.append(across * pair[8:9] + down * pair[9:10])
            peak = logits[0]
            for logit in logits[1:]:
                peak = jnp.maximum(peak, logit)
            raised = [jnp.exp(logit - peak) for logit in logits]
            total = raised[0]
            for other in raised[1:]:
                total = total + other
            return [other / total for other in raised]

        def norm(cols):
            def dots():
                return (nn(w_out_two_t[...], own_keep[:, cols]),)

            def work(value):
                second = first_keep[step, :, cols] + value
                first_keep[step, :, cols] = second
                hat, scale = standardize(second)
                norm_of[cols.start] = (hat, scale)
                normed_keep[:, cols] = (hat * gain_two[...] + bias_two[...]).astype(bf16)
                gates_of[cols.start] = gate(cols)

            return dots, work

        def ring(cols):
            start = cols.start % (2 * GROUP)
            return slice(start, start + cols.stop - cols.start)

        def expand(cols, first):
            expert = first // hidden
            strip = slice(first, first + STRIP)

            def dots():
                return (
                    nn(w_in_t[strip], normed_keep[:, cols]).astype(bf16),
                    nn(w_exit[strip], grad_keep[:, cols]).astype(bf16),
                )

            def work(inners, backs):
                share = (0.5 * gates_of[cols.start][expert]).astype(bf16)
                partial_sum = None
                for start in range(0, STRIP, SLAB):
                    inner, back = inners[start : start + SLAB], backs[start : start + SLAB]
                    span = slice(first + start, first + start + SLAB)
                    square = inner * inner
                    tanh = jnp.tanh(inner * (0.7978845608028654 + 0.035677408136300125 * square))
                    above = 1.0 + tanh
                    active = inner * above
                    product = active * back
                    folded = product[:16]
                    for row in range(16, SLAB, 16):
                        folded = folded + product[row : row + 16]
                    folded = folded.astype(f32)
                    partial_sum = folded if partial_sum is None else partial_sum + folded
                    hidden_keep[span, ring(cols)] = active * share
                    slope = above + active * (1.0 - tanh) * (
                        0.7978845608028654 + 0.10703222440890037 * square
                    )
                    inner_keep[span, ring(cols)] = slope * (back * share)
                found = jnp.sum(0.5 * partial_sum, axis=0, keepdims=True)
                if first % hidden:
                    grad_gates_of[cols.start][expert] += found
                else:
                    grad_gates_of[cols.start].append(found)

            return dots, work

        def contract(cols):
            def dots():
                return (
                    nn(w_exit_t[...], hidden_keep[:, ring(cols)]),
                    nn(w_in[...], inner_keep[:, ring(cols)]),
                )

            def work(mixed, grad_normed):
                result[cols, :] = flip((first_keep[step, :, cols] + mixed).astype(bf16))
                hat, scale = norm_of[cols.start]
                sum_gain[...] += lane_fold(grad_normed * hat)
                sum_bias[...] += lane_fold(grad_normed)
                grad_second = grad_keep[:, cols].astype(f32) + norm_back(
                    grad_normed * gain_two[...], hat, scale
                )
                grad_second_out[:, cols] = grad_second.astype(bf16)
                gates, grad_gates = gates_of[cols.start], grad_gates_of[cols.start]
                across, down = coords[0:1, cols], coords[1:2, cols]
                mean_gate = gates[0] * grad_gates[0]
                for expert in range(1, experts):
                    mean_gate = mean_gate + gates[expert] * grad_gates[expert]
                for expert in range(experts):
                    change = gates[expert] * (grad_gates[expert] - mean_gate)
                    sum_gate[expert : expert + 1, cols] += across * change
                    sum_gate[experts + expert : experts + expert + 1, cols] += down * change

            return dots, work

        def attend_back(cols):
            def dots():
                return (nn(w_out_two[...], grad_second_out[:, cols]),)

            def work(value):
                share = by_head(value, undo_of[cols.start])
                pair_keep[:width, cols] = share.astype(bf16)
                sums = head_sums(share * own_keep[:, cols].astype(f32))
                pair_keep[width:, cols] = jnp.concatenate(
                    [sums, jnp.zeros((PAD - HEADS, CHUNK), f32)], axis=0
                ).astype(bf16)

            return dots, work

        def query_back(cols):
            def dots():
                return (nn(self_state[:, : width + PAD], pair_keep[:, cols]),)

            def work(grad_q):
                queries = query_keep[step, :, cols]
                grad_q_out[:, cols] = softmax_back(queries, grad_q).astype(bf16)

            return dots, work

        def sum_hidden(cols, expert):
            span = slice(expert * hidden, (expert + 1) * hidden)
            return (
                lambda: (nn(hidden_keep[span, ring(cols)], cotangent[cols, :]),),
                add_to(sum_exit, span),
            )

        def sum_inner(cols, expert):
            span = slice(expert * hidden, (expert + 1) * hidden)
            return (
                lambda: (nt(inner_keep[span, ring(cols)], normed_keep[:, cols]),),
                add_to(sum_in, span),
            )

        def sum_own(cols):
            return (
                lambda: (nt(own_keep[:, cols], grad_second_out[:, cols]),),
                add_to(sum_out_two, every),
            )

        def sum_pair(cols):
            return (
                lambda: (nt(pair_keep[:, cols], query_keep[step, :, cols]),),
                add_to(grad_state_sum, every),
            )

        tasks = [stage(cols) for stage in (attend, norm) for cols in chunks]
        sums, contracts = [], []
        for group in groups:
            inside = [cols for cols in chunks if group.start <= cols.start < group.stop]
            expands = [
                expand(cols, first) for cols in inside for first in range(0, experts * hidden, STRIP)
            ]
            tasks += mix(expands, mix(sums, contracts) if sums else [])
            contracts = [contract(cols) for cols in inside]
            sums = [
                total(group, expert) for expert in range(experts) for total in (sum_hidden, sum_inner)
            ]
        tasks += mix(contracts + [attend_back(cols) for cols in chunks], sums)
        last = [total(group) for group in groups for total in (sum_own, sum_pair)]
        tasks += mix([query_back(cols) for cols in chunks], last)
        run_tasks(tasks)

        @pl.when(step == steps - 1)
        def _():
            grad_state_out[0] = grad_state_sum[...]

    @pl.when((item == pl.num_programs(0) - 1) & (phase == 1) & (step == steps - 1))
    def _():
        gain, bias = as_row(sum_gain[...]), as_row(sum_bias[...])
        gate = jnp.broadcast_to(jnp.sum(sum_gate[...], axis=1, keepdims=True), (8, width))
        row = lax.broadcasted_iota(jnp.int32, (8, width), 0)
        vectors = jnp.where(row == 0, gain[:8], bias[:8])
        small = jnp.concatenate([vectors, gate], axis=0).astype(bf16)
        start = 0
        for block in range(experts * hidden // width):
            part = flip(sum_in[block * width : (block + 1) * width]).astype(bf16)
            grads_stage[:, start : start + piece, :] = part.reshape(shards, piece, width)
            start += piece
        for expert in range(experts):
            part = sum_exit[expert * hidden : (expert + 1) * hidden].astype(bf16)
            grads_stage[:, start : start + exit_piece, :] = part.reshape(shards, exit_piece, width)
            start += exit_piece
        part = sum_out_two[...].astype(bf16)
        grads_stage[:, start : start + piece, :] = part.reshape(shards, piece, width)
        start += piece
        for shard in range(shards):
            grads_stage[shard, start : start + 16, :] = small
        scatter_blocks(grads_stage, grads_out)


def rest_kernel(
    presence,
    hat_in,
    scale_in,
    normed_in,
    queries_in,
    cross_in,
    first_in,
    keys_in,
    values_in,
    grad_q_in,
    grad_second_in,
    grad_state_in,
    state_t,
    state,
    weights,
    gain_one,
    *refs,
    funcs,
    item,
    first_call,
):
    if not first_call:
        carry, refs = refs[3], refs[5:]
    (
        grad_tokens,
        grad_cross_state_out,
        grad_totals_out,
        sums_out,
        grad_self_state,
        grad_totals,
        grad_state_sum,
        sums,
        three_keep,
        cross_keep,
        stack_keep,
        query_keep,
    ) = refs
    step = pl.program_id(0)
    steps = pl.num_programs(0)
    width = hat_in.shape[0]
    self_part = slice(0, 3 * width)
    out_part = slice(3 * width, 4 * width)
    query_part = slice(4 * width, 5 * width)
    gain_part = slice(5 * width, 6 * width)
    bias_part = slice(6 * width, 7 * width)

    @pl.when(step == 0)
    def _():
        sums[...] = jnp.zeros_like(sums) if first_call else carry[...]
        left = jnp.where(same_head(width), grad_state_in[0, :width], 0.0)
        grad_self_state[0] = flip(left).astype(bf16)
        grad_self_state[1] = left.astype(bf16)
        column = totals_column(grad_state_in[0, width : width + HEADS], width)
        grad_totals[...] = jnp.broadcast_to(column[:, 0:1], grad_totals.shape)

    chunks = [slice(start, start + CHUNK) for start in range(0, hat_in.shape[1], CHUNK)]
    grad_first_of = {}

    def self_back(cols):
        def dots():
            return (
                nn(grad_self_state[0], values_in[:, cols]),
                nn(grad_self_state[1], keys_in[:, cols]),
            )

        def work(grad_keys, grad_values):
            grad_keys = softmax_back(keys_in[:, cols], grad_keys + grad_totals[...])
            three_keep[:width, cols] = grad_q_in[:, cols]
            three_keep[width : 2 * width, cols] = grad_keys.astype(bf16)
            three_keep[2 * width :, cols] = grad_values.astype(bf16)

        return dots, work

    def join(cols):
        def dots():
            return (nn(weights[:, self_part], three_keep[:, cols]),)

        def work(value):
            grad_first = grad_second_in[:, cols].astype(f32) + value
            grad_first_of[cols.start] = grad_first
            cross_keep[:, cols] = grad_first.astype(bf16)

        return dots, work

    def cross_back(cols):
        def dots():
            return nn(weights[:, out_part], cross_keep[:, cols]), nn(state_t[0], queries_in[:, cols])

        def work(share, both):
            undo = inverse(both[funcs * width :])
            sums_by_head = []
            for func in range(funcs):
                span = slice(func * width, (func + 1) * width)
                scales = undo[func * HEADS : (func + 1) * HEADS]
                part = by_head(share, scales)
                stack_keep[span, cols] = part.astype(bf16)
                sums_by_head.append(head_sums(part * by_head(both[span], scales)))
            spare = stack_keep.shape[0] - funcs * (width + HEADS)
            if spare:
                sums_by_head.append(jnp.zeros((spare, CHUNK), f32))
            stack_keep[funcs * width :, cols] = jnp.concatenate(sums_by_head, axis=0).astype(bf16)

        return dots, work

    def query_back(cols):
        def dots():
            return (nn(state[0, :, : stack_keep.shape[0]], stack_keep[:, cols]),)

        def work(grad_q):
            query_keep[:, cols] = softmax_back(queries_in[:, cols], grad_q).astype(bf16)

        return dots, work

    def finish(cols):
        def dots():
            return (nn(weights[:, query_part], query_keep[:, cols]),)

        def work(grad_normed):
            hat, scale = hat_in[:, cols].astype(f32), scale_in[0:1, cols]
            sums[gain_part] += lane_fold(grad_normed * hat)
            sums[bias_part] += lane_fold(grad_normed)
            grad_rows = grad_first_of[cols.start] + norm_back(
                grad_normed * gain_one[...], hat, scale
            )
            grad_tokens[cols, :] = flip(grad_rows)

        return dots, work

    @pl.when(step == 0)
    def _():
        grad_state_sum[...] = jnp.zeros_like(grad_state_sum)

    every = slice(None)
    sum_self = (lambda: (nt(three_keep[...], first_in[...]),), add_to(sums, self_part))
    sum_out = (lambda: (nt(cross_in[...], cross_keep[...]),), add_to(sums, out_part))
    sum_state = (lambda: (nt(stack_keep[...], queries_in[...]),), add_to(grad_state_sum, every))
    sum_query = (lambda: (nt(normed_in[...], query_keep[...]),), add_to(sums, query_part))
    tasks = [stage(cols) for stage in (self_back, join) for cols in chunks]
    tasks += mix([cross_back(cols) for cols in chunks], [sum_self])
    tasks += mix([query_back(cols) for cols in chunks], [sum_out])
    tasks += mix([finish(cols) for cols in chunks], [sum_state])
    run_tasks(tasks + [sum_query])

    @pl.when(step == steps - 1)
    def _():
        mask = same_head(width)
        for func in range(funcs):
            weight = function_weight(presence, item, func, funcs, (1, width))
            left = jnp.where(mask, grad_state_sum[func * width : (func + 1) * width], 0.0)
            grad_cross_state_out[func] = (left * weight).astype(bf16)
            start = funcs * width + func * HEADS
            grad_totals_out[func] = totals_column(grad_state_sum[start : start + HEADS], width)
        sums_out[...] = sums[...]


def points_back(points, keys_in, values_in, grad_state, grad_totals, carry, _after, *refs, shards):
    outs = refs[:shards]
    sums, stage, grads = refs[shards:]
    step = pl.program_id(0)
    width = points.shape[2]
    piece = width // shards

    funcs, slots, _ = points.shape
    chunks = [slice(start, start + CHUNK) for start in range(0, slots, CHUNK)]
    turned = [flip(grad_state[func]) for func in range(funcs)]

    def back(func, cols):
        def dots():
            return (
                nn(turned[func], values_in[func, :, cols]),
                nn(grad_state[func], keys_in[func, :, cols]),
            )

        def work(grad_keys, grad_values):
            grad_keys = grad_keys + grad_totals[func, :, 0:1]
            grad_k = softmax_back(keys_in[func, :, cols], grad_keys)
            grads[func, :width, cols] = grad_k.astype(bf16)
            grads[func, width:, cols] = grad_values.astype(bf16)

        return dots, work

    run_tasks([back(func, cols) for func in range(funcs) for cols in chunks])
    found = nn(grads[0], points[0])
    for func in range(1, funcs):
        found = found + nn(grads[func], points[func])

    @pl.when(step == 0)
    def _():
        sums[...] = found
        gain = as_row(carry[5 * width : 6 * width])
        bias = as_row(carry[6 * width : 7 * width])
        row = lax.broadcasted_iota(jnp.int32, (16, width), 0)
        small = jnp.where(row == 0, gain[:16], bias[:16]).astype(bf16)
        for place in range(5):
            part = carry[place * width : (place + 1) * width]
            part = (flip(part) if place < 3 else part).astype(bf16)
            stage[:, place * piece : (place + 1) * piece, :] = part.reshape(shards, piece, width)
        for shard in range(shards):
            stage[shard, 5 * piece : 5 * piece + 16, :] = small

    @pl.when(step > 0)
    def _():
        sums[...] += found

    @pl.when(step == pl.num_programs(0) - 1)
    def _():
        for place in range(2):
            start = 5 * piece + 16 + place * piece
            part = flip(sums[place * width : (place + 1) * width]).astype(bf16)
            stage[:, start : start + piece, :] = part.reshape(shards, piece, width)
        scatter_blocks(stage, outs)


def total_of(parts):
    value = parts[0][...].astype(f32)
    for part in parts[1:]:
        value = value + part[...].astype(f32)
    return value


def unpack_kernel(*refs, counts, experts, piece, exit_piece, hidden):
    main_parts, parts = refs[: counts[0]], refs[counts[0] : sum(counts)]
    outs, (small, main, rest) = refs[-18:-3], refs[-3:]
    width = main.shape[1]
    main[...] = total_of(main_parts)
    rest[...] = total_of(parts)
    (
        gain_one,
        bias_one,
        query_one,
        key_one,
        value_one,
        out_one,
        query_two,
        key_two,
        value_two,
        out_two,
        gain_two,
        bias_two,
        enter,
        leave,
        gate,
    ) = outs
    start = 0
    for expert in range(experts):
        for half in range(hidden // width):
            block = main[start : start + piece]
            enter[expert, :, half * width : (half + 1) * width] = block
            start += piece
    for expert in range(experts):
        leave[expert] = main[start : start + exit_piece]
        start += exit_piece
    out_two[...] = main[start : start + piece]
    start += piece
    small[:16] = main[start : start + 16]
    start = 0
    for out in (query_two, key_two, value_two, out_one, query_one):
        out[...] = rest[start : start + piece]
        start += piece
    small[16:] = rest[start : start + 16]
    start += 16
    for out in (key_one, value_one):
        out[...] = rest[start : start + piece]
        start += piece
    shard = lax.axis_index("fsdp")
    turned = pltpu.roll(small[...], lax.rem(width - shard * piece, width), 1)
    gain_two[...] = turned[0:1, :piece]
    bias_two[...] = turned[1:2, :piece]
    gain_one[...] = turned[16:17, :piece]
    bias_one[...] = turned[17:18, :piece]
    for row in range(2):
        gate[:, row : row + 1] = small[pl.ds(8 + row * experts + shard, 1), 0:1]


def whole_spec(shape):
    return pl.BlockSpec(shape, lambda *_: (0,) * len(shape))


def route(size, shift, digit, stride):
    def target(i):
        own = i // stride % digit
        return i + ((own + shift) % digit - own) * stride

    return [(i, target(i)) for i in range(size)]


def spread(value, axis, size, digit, stride):
    return [value] + [
        lax.ppermute(value, axis, route(size, shift, digit, stride)) for shift in range(1, digit)
    ]


def exchange(values, axis, size, stride):
    digit = len(values)
    return [values[0]] + [
        lax.ppermute(values[shift], axis, route(size, shift, digit, stride))
        for shift in range(1, digit)
    ]


def digits(size):
    found = []
    stride = 1
    while stride < size:
        rest = size // stride
        digit = 2 if stride == 1 and rest % 2 == 0 else 4 if rest % 4 == 0 else rest
        found.append((digit, stride))
        stride *= digit
    return found or [(1, 1)]


def sum_parts(parts):
    return total_of([part.astype(f32) for part in parts]).astype(bf16)


def shards_fn(
    dp,
    shards,
    tokens,
    points,
    coords,
    presence,
    counts,
    cotangent,
    gain_first,
    bias_first,
    query_first,
    key_first,
    value_first,
    out_first,
    query_second,
    key_second,
    value_second,
    out_second,
    gain_second,
    bias_second,
    expert_in,
    expert_out,
    gate_weight,
):
    count, width = tokens.shape
    items, funcs, slots, _ = points.shape
    length = count // items
    experts, piece, hidden = expert_in.shape
    exit_piece = expert_out.shape[1]
    tile, rest_tile = min(MAIN_TILE, length), min(REST_TILE, length)
    steps, rest_steps = length // tile, length // rest_tile
    inner = experts * hidden
    enter_rows = experts * piece * (hidden // width)
    limit = pltpu.CompilerParams(vmem_limit_bytes=VMEM)

    at = {}
    place = 0
    for name, size in (
        ("query_first", piece),
        ("out_first", piece),
        ("query_second", piece),
        ("key_second", piece),
        ("value_second", piece),
        ("out_second", piece),
        ("expert_in", enter_rows),
        ("expert_out", experts * exit_piece),
        ("small", 16),
    ):
        at[name] = place
        place += size
    late_rows_count = place
    early_pack, late_pack = pl.pallas_call(
        pack_kernel,
        out_shape=[
            jax.ShapeDtypeStruct((2 * piece, width), bf16),
            jax.ShapeDtypeStruct((late_rows_count, width), bf16),
        ],
        name="pack",
    )(
        key_first,
        value_first,
        query_first,
        out_first,
        query_second,
        key_second,
        value_second,
        out_second,
        expert_in,
        expert_out,
        *(
            vector.reshape(1, piece)
            for vector in (gain_first, bias_first, gain_second, bias_second)
        ),
        gate_weight,
    )
    early_parts = spread(early_pack, "fsdp", shards, shards, 1)
    late_parts = spread(late_pack, "fsdp", shards, shards, 1)
    late_specs = [whole_spec((late_rows_count, width))] * shards
    gathered = pltpu.VMEM((shards, late_rows_count, width), bf16)

    smem = pl.BlockSpec(memory_space=pltpu.SMEM)
    units = items * funcs
    state_rows = funcs * width + -(-funcs * HEADS // PAD) * PAD
    flat_points = points.reshape(units, slots, width)
    state_t, state, keys_one, values_one = pl.pallas_call(
        partial(points_forward, funcs=funcs, shards=shards),
        grid=(items,),
        in_specs=[smem, smem, pl.BlockSpec((funcs, slots, width), lambda u: (u, 0, 0))]
        + [whole_spec((2 * piece, width))] * shards,
        out_specs=[
            pl.BlockSpec((1, state_rows, width), lambda u: (u, 0, 0)),
            pl.BlockSpec((1, width, (funcs + 1) * width), lambda u: (u, 0, 0)),
            pl.BlockSpec((funcs, width, slots), lambda u: (u, 0, 0)),
            pl.BlockSpec((funcs, width, slots), lambda u: (u, 0, 0)),
        ],
        out_shape=[
            jax.ShapeDtypeStruct((items, state_rows, width), bf16),
            jax.ShapeDtypeStruct((items, width, (funcs + 1) * width), bf16),
            jax.ShapeDtypeStruct((units, width, slots), bf16),
            jax.ShapeDtypeStruct((units, width, slots), bf16),
        ],
        scratch_shapes=[
            pltpu.VMEM((shards, 2 * piece, width), bf16),
            pltpu.VMEM((2 * width, width), bf16),
        ],
        compiler_params=limit,
        cost_estimate=cost(8),
        name="points_forward",
    )(counts, presence, flat_points, *early_parts)

    kept = jax.ShapeDtypeStruct((width, count), bf16)
    main_rows = enter_rows + experts * exit_piece + piece + 16

    def early(i, p, j):
        return i * steps + jnp.where(p == 0, j, steps - 1)

    def late(i, p, j):
        return i * steps + jnp.where(p == 0, 0, j)

    early_keep = pl.BlockSpec((width, tile), lambda i, p, j: (0, early(i, p, j)))
    late_keep = pl.BlockSpec((width, tile), lambda i, p, j: (0, late(i, p, j)))
    late_rows = pl.BlockSpec((tile, width), lambda i, p, j: (late(i, p, j), 0))
    (
        result,
        queries_one,
        cross,
        first,
        keys_two,
        values_two,
        grad_q_two,
        grad_second,
        grad_state_two,
        rest_weights,
        rest_vectors,
        normed_one,
        hat_one,
        scale_one,
        *main_grads,
    ) = pl.pallas_call(
        partial(main_kernel, funcs=funcs, experts=experts, shards=shards, at=at),
        grid=(items, 2, steps),
        in_specs=[
            pl.BlockSpec((tile, width), lambda i, p, j: (early(i, p, j), 0)),
            late_rows,
            pl.BlockSpec((2, tile), lambda i, p, j: (0, late(i, p, j))),
            pl.BlockSpec((1, state_rows, width), lambda i, p, j: (i, 0, 0)),
        ]
        + late_specs,
        out_specs=[
            late_rows,
            early_keep,
            early_keep,
            early_keep,
            early_keep,
            early_keep,
            late_keep,
            late_keep,
            pl.BlockSpec((1, width + PAD, width), lambda i, p, j: (i, 0, 0)),
            whole_spec((width, 5 * width)),
            whole_spec((width, CHUNK)),
            early_keep,
            early_keep,
            pl.BlockSpec((8, tile), lambda i, p, j: (0, early(i, p, j))),
        ]
        + [whole_spec((main_rows, width))] * shards,
        out_shape=[
            jax.ShapeDtypeStruct((count, width), bf16),
            kept,
            kept,
            kept,
            kept,
            kept,
            kept,
            kept,
            jax.ShapeDtypeStruct((items, width + PAD, width), f32),
            jax.ShapeDtypeStruct((width, 5 * width), bf16),
            jax.ShapeDtypeStruct((width, CHUNK), f32),
            kept,
            kept,
            jax.ShapeDtypeStruct((8, count), f32),
        ]
        + [jax.ShapeDtypeStruct((main_rows, width), bf16)] * shards,
        scratch_shapes=[
            gathered,
            pltpu.VMEM((shards, main_rows, width), bf16),
            pltpu.VMEM((steps, width, tile), f32),
            pltpu.VMEM((steps, width, tile), bf16),
            pltpu.VMEM((width + PAD, width), f32),
            pltpu.VMEM((width + PAD, width), bf16),
            pltpu.VMEM((width, 2 * width), bf16),
            pltpu.VMEM((width + PAD, width), f32),
            pltpu.VMEM((width, width), bf16),
            pltpu.VMEM((width, width), bf16),
            pltpu.VMEM((3 * width, width), bf16),
            pltpu.VMEM((width, width), bf16),
            pltpu.VMEM((width, width), bf16),
            pltpu.VMEM((inner, width), bf16),
            pltpu.VMEM((width, inner), bf16),
            pltpu.VMEM((inner, width), bf16),
            pltpu.VMEM((width, inner), bf16),
            pltpu.VMEM((width, CHUNK), f32),
            pltpu.VMEM((width, CHUNK), f32),
            pltpu.VMEM((width, CHUNK), f32),
            pltpu.VMEM((width, CHUNK), f32),
            pltpu.VMEM((inner, min(2 * GROUP, tile)), bf16),
            pltpu.VMEM((inner, min(2 * GROUP, tile)), bf16),
            pltpu.VMEM((width, tile), bf16),
            pltpu.VMEM((width, tile), bf16),
            pltpu.VMEM((width, tile), bf16),
            pltpu.VMEM((width + PAD, tile), bf16),
            pltpu.VMEM((inner, width), f32),
            pltpu.VMEM((inner, width), f32),
            pltpu.VMEM((width, width), f32),
            pltpu.VMEM((width, width), f32),
            pltpu.VMEM((width, width), f32),
            pltpu.VMEM((2 * experts, tile), f32),
        ],
        compiler_params=limit,
        cost_estimate=cost(80),
        name="main",
    )(tokens, cotangent, coords, state_t, *late_parts)

    rest_rows = 7 * piece + 16

    def rest_call(item, earlier, after):
        first_call = item == 0
        keep_spec = pl.BlockSpec((width, rest_tile), lambda j: (0, item * rest_steps + j))
        row_spec = pl.BlockSpec((rest_tile, width), lambda j: (item * rest_steps + j, 0))
        unit_spec = pl.BlockSpec((funcs, width, width), lambda j: (item, 0, 0))
        anywhere = pl.BlockSpec(memory_space=pl.ANY)
        in_specs = [
            smem,
            keep_spec,
            pl.BlockSpec((8, rest_tile), lambda j: (0, item * rest_steps + j)),
            keep_spec,
            keep_spec,
            keep_spec,
            keep_spec,
            keep_spec,
            keep_spec,
            keep_spec,
            keep_spec,
            pl.BlockSpec((1, width + PAD, width), lambda j: (item, 0, 0)),
            pl.BlockSpec((1, state_rows, width), lambda j: (item, 0, 0)),
            pl.BlockSpec((1, width, (funcs + 1) * width), lambda j: (item, 0, 0)),
            whole_spec((width, 5 * width)),
            whole_spec((width, CHUNK)),
        ]
        operands = [
            presence,
            hat_one,
            scale_one,
            normed_one,
            queries_one,
            cross,
            first,
            keys_two,
            values_two,
            grad_q_two,
            grad_second,
            grad_state_two,
            state_t,
            state,
            rest_weights,
            rest_vectors,
        ]
        aliases = {}
        if not first_call:
            aliases = {len(operands) + k: k for k in range(3)}
            in_specs += [anywhere] * 3 + [whole_spec((7 * width, width)), anywhere]
            operands += [*earlier, after]
        out_specs = [row_spec, unit_spec, unit_spec, whole_spec((7 * width, width))]
        out_shape = [
            jax.ShapeDtypeStruct((count, width), f32),
            jax.ShapeDtypeStruct((units, width, width), bf16),
            jax.ShapeDtypeStruct((units, width, width), f32),
            jax.ShapeDtypeStruct((7 * width, width), f32),
        ]
        return pl.pallas_call(
            partial(
                rest_kernel,
                funcs=funcs,
                item=item,
                first_call=first_call,
            ),
            grid=(rest_steps,),
            in_specs=in_specs,
            out_specs=out_specs,
            out_shape=out_shape,
            input_output_aliases=aliases,
            scratch_shapes=[
                pltpu.VMEM((2, width, width), bf16),
                pltpu.VMEM((width, CHUNK), f32),
                pltpu.VMEM((state_rows, width), f32),
                pltpu.VMEM((7 * width, width), f32),
                pltpu.VMEM((3 * width, rest_tile), bf16),
                pltpu.VMEM((width, rest_tile), bf16),
                pltpu.VMEM((state_rows, rest_tile), bf16),
                pltpu.VMEM((width, rest_tile), bf16),
            ],
            compiler_params=limit,
            cost_estimate=cost(18),
            name="rest",
        )(*operands)

    levels = digits(dp)
    main_levels = levels[::-1]
    main_parts = exchange(main_grads, "fsdp", shards, 1)
    level = 0
    found = None
    for item in range(items):
        found = rest_call(item, found, main_sum if item else None)
        if item < len(main_levels):
            main_sum = sum_parts(main_parts)
            main_parts = spread(main_sum, "dp", dp, *main_levels[item])
            level = item + 1
    grad_tokens, grad_state_one, grad_totals_one, carry = found

    rest_grads = pl.pallas_call(
        partial(points_back, shards=shards),
        grid=(items,),
        in_specs=[
            pl.BlockSpec((funcs, slots, width), lambda u: (u, 0, 0)),
            pl.BlockSpec((funcs, width, slots), lambda u: (u, 0, 0)),
            pl.BlockSpec((funcs, width, slots), lambda u: (u, 0, 0)),
            pl.BlockSpec((funcs, width, width), lambda u: (u, 0, 0)),
            pl.BlockSpec((funcs, width, width), lambda u: (u, 0, 0)),
            whole_spec((7 * width, width)),
            pl.BlockSpec(memory_space=pl.ANY),
        ],
        out_specs=[whole_spec((rest_rows, width))] * shards,
        out_shape=[jax.ShapeDtypeStruct((rest_rows, width), bf16)] * shards,
        scratch_shapes=[
            pltpu.VMEM((2 * width, width), f32),
            pltpu.VMEM((shards, rest_rows, width), bf16),
            pltpu.VMEM((funcs, 2 * width, slots), bf16),
        ],
        compiler_params=limit,
        cost_estimate=cost(7),
        name="points_back",
    )(flat_points, keys_one, values_one, grad_state_one, grad_totals_one, carry, main_sum)
    rest_got = exchange(rest_grads, "fsdp", shards, 1)

    parts = rest_got
    for digit, stride in main_levels[level:]:
        main_parts = spread(sum_parts(main_parts), "dp", dp, digit, stride)
    for digit, stride in levels:
        parts = spread(sum_parts(parts), "dp", dp, digit, stride)

    matrix = jax.ShapeDtypeStruct((piece, width), f32)
    vector = jax.ShapeDtypeStruct((1, piece), f32)
    outs = pl.pallas_call(
        partial(
            unpack_kernel,
            counts=(len(main_parts), len(parts)),
            experts=experts,
            piece=piece,
            exit_piece=exit_piece,
            hidden=hidden,
        ),
        out_shape=[vector] * 2
        + [matrix] * 8
        + [vector] * 2
        + [
            jax.ShapeDtypeStruct(expert_in.shape, f32),
            jax.ShapeDtypeStruct(expert_out.shape, f32),
            jax.ShapeDtypeStruct((1, 2), f32),
        ],
        scratch_shapes=[
            pltpu.VMEM((32, width), f32),
            pltpu.VMEM((main_rows, width), f32),
            pltpu.VMEM((rest_rows, width), f32),
        ],
        compiler_params=pltpu.CompilerParams(vmem_limit_bytes=VMEM // 8),
        name="unpack",
    )(*main_parts, *parts)
    outs = [out.reshape(piece) if out.shape == (1, piece) else out for out in outs]
    return (result, grad_tokens, *outs[:-1], outs[-1].reshape(gate_weight.shape))


def solution(mesh):
    rows = P(("dp", "fsdp"), None)
    matrix = P("fsdp", None)
    vector = P("fsdp")
    expert = P(None, "fsdp", None)
    parameters = (
        (vector, vector)
        + (matrix,) * 8
        + (vector, vector, expert, expert, P(None, "fsdp"))
    )
    return jax.shard_map(
        partial(shards_fn, mesh.shape["dp"], mesh.shape["fsdp"]),
        mesh=mesh,
        in_specs=(
            rows,
            P(("dp", "fsdp"), None, None, None),
            P(None, ("dp", "fsdp")),
            rows,
            rows,
            rows,
        )
        + parameters,
        out_specs=(rows, rows) + parameters,
        check_vma=False,
    )
```
